32 devices in a mesh: ctx: 8 (over z, x), fsdp: 4 (over y, core).
Axes of the slice: x: 2, y: 2, z: 4, core: 2. Of those that a mesh axis runs over, the one named last changes fastest.
Arguments:
- tokens: bfloat16 [4, 2048, 1280], P('fsdp', 'ctx'), may hold values from -6 to 6
- lengths: int32 [4, 4], P('fsdp'), may hold values from 1 to 1024, 1920 in all within a row
- position: int32 [4, 2048], P('fsdp'), may hold values from 0 to 2047, as said below
- qkv_weight: bfloat16 [1280, 3840], P('fsdp'), may hold values from -0.15625 to 0.15625
- out_weight: bfloat16 [1280, 1280], P('fsdp'), may hold values from -0.5 to 0.5
- up_weight: bfloat16 [1280, 1280], P('fsdp'), may hold values from -0.15625 to 0.15625
- down_weight: bfloat16 [1280, 1280], P('fsdp'), may hold values from -0.15625 to 0.15625
- attn_gain: bfloat16 [1280], P('fsdp'), may hold values from 0.099609375 to 1.8984375
- mlp_gain: bfloat16 [1280], P('fsdp'), may hold values from 0.099609375 to 1.8984375
- query_scale: bfloat16 [80], P('fsdp'), may hold values from -3 to 3
- cotangent: bfloat16 [4, 2048, 1280], P('fsdp', 'ctx'), may hold values from -6 to 6
Outputs:
- output: float32 [4, 2048, 1280], P('fsdp', 'ctx')
- input_grad: float32 [4, 2048, 1280], P('fsdp', 'ctx')
- grad_qkv: float32 [1280, 3840], P('fsdp')
- grad_out: float32 [1280, 1280], P('fsdp')
- grad_up: float32 [1280, 1280], P('fsdp')
- grad_down: float32 [1280, 1280], P('fsdp')
- grad_attn_gain: float32 [1280], P('fsdp')
- grad_mlp_gain: float32 [1280], P('fsdp')
- grad_query_scale: float32 [80], P('fsdp')
The draws below stay inside these ranges and needn't reach their ends.
Inputs may be any that keep to these rules, and one draw needn't show every extreme that they name: Each pack's sequences fill positions from 0 in order; positions from the sum of the lengths to the end are padding. Each row of position is a permutation of the pack's positions, and every run of 256 given rows of one index of ctx holds exactly 256 // 8 positions of each residue modulo 8.
All inputs are finite; a program needn't handle non-finite values.
Results may differ from the reference program's by a relative error of at most 0.04.
Values may be sent and summed in bfloat16 or wider, within the bound.
A program may use at most 256 MiB of HBM per device.

```python
import math
import jax
import jax.numpy as jnp
import numpy as np
from jax import lax

D = 1280
HEADS = 16
HEAD = 80
FF = 1280
TOK_DEV = 256
SEQS = 4
GROUP_TOK = 2048
LONGEST = 1024
PAD = 128
N_CTX = 8
N_FSDP = 4


def draw_position(key, part):
    key = jax.random.fold_in(key, 7)
    share_rows = TOK_DEV // N_CTX

    def one_group(group_key):
        first_key, second_key = jax.random.split(group_key)
        slots = jax.vmap(lambda sub: jax.random.permutation(sub, TOK_DEV))(jax.random.split(first_key, N_CTX))
        places = slots * N_CTX + jnp.arange(N_CTX, dtype=jnp.int32)[:, None]
        grouped = places.reshape(N_CTX, N_CTX, share_rows).transpose(1, 0, 2).reshape(N_CTX, TOK_DEV)
        mixed = jax.vmap(lambda sub, row: jax.random.permutation(sub, row))(jax.random.split(second_key, N_CTX), grouped)
        return mixed.reshape(-1)
    return jax.vmap(one_group)(jax.random.split(key, N_FSDP)).astype(jnp.int32)


def block_scale(own_key, shape, cuts, least, high):
    def one(axis_at, shards_of):
        steps = jax.random.uniform(jax.random.fold_in(jax.random.fold_in(own_key, 6), axis_at), (shards_of,), jnp.float32, least / len(cuts), high / len(cuts))
        return jnp.repeat(jnp.exp(steps), shape[axis_at] // shards_of).reshape((-1,) + (1,) * (len(shape) - axis_at - 1))

    factor_of = one(*cuts[0])
    for cut in cuts[1:]:
        factor_of = factor_of * one(*cut)
    return factor_of


def profile(count, total, reach, lean):
    portions = [(1 << 20) // math.isqrt(rank ** lean) + 1 for rank in range(2, count + 1)]
    rest, holding = total - reach - (count - 1), [1] * (count - 1)
    while rest > 0:
        free = [i for i in range(count - 1) if holding[i] < reach]
        whole, left = sum([portions[i] for i in free]), rest
        for i in free:
            more = min(reach - holding[i], max(1, left * portions[i] // whole), rest)
            holding[i] = holding[i] + more
            rest = rest - more
    return np.array([reach] + holding)


def ragged(rng, amount, total, bound, slope):
    if amount == 2:
        one = jax.random.randint(rng, (), max(1, total - bound), min(bound, total - 1) + 1)
        return jnp.stack([one, total - one])
    sizes = jnp.asarray(profile(amount, total, bound, slope), jnp.int32)
    twos = (amount - 1) // 2
    giver, taker = sizes[1:1 + 2 * twos:2], sizes[2:2 + 2 * twos:2]
    room = jnp.minimum(giver - 1, bound - taker)
    passed = jax.random.randint(jax.random.fold_in(rng, 1), (twos,), 0, 1 << 20) % (room + 1)
    sizes = sizes.at[1:1 + 2 * twos:2].set(giver - passed).at[2:2 + 2 * twos:2].set(taker + passed)
    return sizes[jax.random.permutation(jax.random.fold_in(rng, 2), amount)]


def gaussian(rng, shape, scale, bound, pieces=(), kind=jnp.bfloat16):
    factor_of = block_scale(rng, shape, pieces, -0.22, 0.18) if pieces else 1.0
    values = jax.random.normal(rng, shape, jnp.float32) * scale * factor_of
    return jnp.minimum(jnp.maximum(values, -bound), bound).astype(kind)


def setup_inputs(seed: int = 0) -> dict:
    key_list = jax.random.split(jax.random.key(seed), 12)
    return {
        "tokens": gaussian(key_list[0], (N_FSDP, GROUP_TOK, D), 1.0, 6.0, ((0, 4), (1, 8))),
        "lengths": jax.vmap(lambda own: ragged(own, SEQS, GROUP_TOK - PAD, LONGEST, 1))(jax.random.split(key_list[1], N_FSDP)).reshape((N_FSDP, SEQS)).astype(jnp.int32),
        "position": draw_position(jax.random.fold_in(key_list[11], 71), 0),
        "qkv_weight": gaussian(key_list[3], (D, 3 * HEADS * HEAD), D ** -0.5, 0.15625, ((0, 4),)),
        "out_weight": gaussian(key_list[4], (HEADS * HEAD, D), (D // 8) ** -0.5, 0.5, ((0, 4),)),
        "up_weight": gaussian(key_list[5], (D, FF), D ** -0.5, 0.15625, ((0, 4),)),
        "down_weight": gaussian(key_list[6], (FF, D), FF ** -0.5, 0.15625, ((0, 4),)),
        "attn_gain": jnp.clip(1.0 + 0.18 * jax.random.normal(key_list[7], (D,), jnp.float32), 0.099609375, 1.8984375).astype(jnp.bfloat16),
        "mlp_gain": jnp.clip(1.0 + 0.18 * jax.random.normal(key_list[8], (D,), jnp.float32), 0.099609375, 1.8984375).astype(jnp.bfloat16),
        "query_scale": gaussian(key_list[9], (HEAD,), 1.0, 3.0, ((0, 4),)),
        "cotangent": gaussian(key_list[10], (N_FSDP, GROUP_TOK, D), 1.0, 6.0, ((0, 4), (1, 8))),
    }


EPS = 1e-06
FLOOR = -1e+30
LOG2E = 1.442695041
HIGHEST = lax.Precision.HIGHEST

@jax.custom_vjp
def low(v):
    return lax.optimization_barrier(v.astype(jnp.bfloat16)).astype(jnp.float32)

@jax.custom_vjp
def low_back(v):
    return v

def low_keep(v):
    return (low(v), None)

def low_pass(kept, grad):
    return (grad,)

def back_keep(v):
    return (v, None)

def back_low(kept, grad):
    return (low(grad),)
low.defvjp(low_keep, low_pass)
low_back.defvjp(back_keep, back_low)

def doc_index(places, seq_ends):
    return lax.optimization_barrier(jnp.sum((places[:, None] >= seq_ends[None, :]).astype(jnp.int32), axis=1))

def group_layer(x_given, seq_lengths, place_row, qkv_weight, out_weight, up_weight, down_weight, attn_gain, mlp_gain, query_scale):
    group_rows = x_given.shape[0]
    att_width = HEADS * HEAD
    places = jnp.arange(group_rows, dtype=jnp.int32)
    by_place = jnp.zeros((group_rows,), jnp.int32).at[place_row].set(places)
    hidden = x_given[by_place]
    seq_ends = jnp.cumsum(seq_lengths).astype(jnp.int32)
    docs = doc_index(places, seq_ends)
    inv_attn = lax.rsqrt(lax.optimization_barrier(jnp.mean(hidden * hidden, axis=1, keepdims=True)) + EPS)
    normed_attn = low(hidden * inv_attn * attn_gain)
    projected = low_back(jnp.dot(normed_attn, qkv_weight, precision=HIGHEST))
    multiplier = jnp.tile(LOG2E / math.sqrt(HEAD) * jax.nn.softplus(query_scale), HEADS)
    queries = low(projected[:, :att_width] * multiplier)
    key_rows = low(projected[:, att_width:2 * att_width]).reshape(group_rows, HEADS, HEAD)
    value_rows = low(projected[:, 2 * att_width:]).reshape(group_rows, HEADS, HEAD)
    block_rows = math.gcd(512, group_rows)
    block_count = group_rows // block_rows

    def attend(entry):
        query_block, query_pos, query_doc = entry
        logits = jnp.einsum('qhd,khd->qhk', query_block.reshape(block_rows, HEADS, HEAD), key_rows, precision=HIGHEST)
        logits = low_back(logits)
        visible = ((query_doc[:, None] == docs[None, :]) & (places[None, :] <= query_pos[:, None]))[:, None, :]
        masked = jnp.where(visible, logits, FLOOR)
        highest = lax.optimization_barrier(jnp.max(masked, axis=2, keepdims=True))
        expo = jnp.where(visible, jnp.exp(masked - highest), 0.0)
        probs = low(expo / lax.optimization_barrier(jnp.sum(expo, axis=2, keepdims=True)))
        return jnp.einsum('qhk,khd->qhd', probs, value_rows, precision=HIGHEST).reshape(block_rows, att_width)
    attended = lax.map(jax.checkpoint(attend), (queries.reshape(block_count, block_rows, att_width), places.reshape(block_count, block_rows), docs.reshape(block_count, block_rows)))
    attended = low(low_back(attended.reshape(group_rows, att_width)))
    resid = hidden + low_back(jnp.dot(attended, out_weight, precision=HIGHEST))
    inv_mlp = lax.rsqrt(lax.optimization_barrier(jnp.mean(resid * resid, axis=1, keepdims=True)) + EPS)
    normed_mlp = low(resid * inv_mlp * mlp_gain)
    up_proj = low_back(jnp.dot(normed_mlp, up_weight, precision=HIGHEST))
    act_low = low(jax.nn.silu(up_proj))
    result = resid + low_back(jnp.dot(act_low, down_weight, precision=HIGHEST))
    return result[place_row]

def reference(tokens, lengths, position, qkv_weight, out_weight, up_weight, down_weight, attn_gain, mlp_gain, query_scale, cotangent):
    floats = tuple((a.astype(jnp.float32) for a in (tokens, qkv_weight, out_weight, up_weight, down_weight, attn_gain, mlp_gain, query_scale)))

    def forward(x_all, *weights):
        return jnp.stack([group_layer(x_all[group], lengths[group], position[group], *weights) for group in range(N_FSDP)])
    result, pullback = jax.vjp(forward, *floats)
    grads = pullback(cotangent.astype(jnp.float32))
    return (result, grads[0], grads[1], grads[2], grads[3], grads[4], grads[5], grads[6], grads[7])
```

```python
import functools
import math

import jax
import jax.numpy as jnp
from jax import lax
from jax.experimental import pallas as pl
from jax.experimental.pallas import tpu as pltpu
from jax.sharding import PartitionSpec as P

HEADS = 16


EPS = 1e-06
FLOOR = -1e30
LOG2E = 1.442695041

MESH = pl.DeviceIdType.MESH
LANES = 128
BF = jnp.bfloat16
F32 = jnp.float32
VMEM_SPEC = pl.BlockSpec(memory_space=pltpu.VMEM)
VMEM_LIMIT = 60 << 20


def flip(number, mask):
    total = 0
    for bit in (1, 2, 4):
        left = (number // bit) % 2
        right = (mask // bit) % 2
        total = total + bit * (left + right - 2 * left * right)
    return total


class Place:
    def __init__(self):
        self.c = lax.axis_index("ctx")
        self.f = lax.axis_index("fsdp")
        self.core = self.f % 2
        self.plane = self.f - self.core
        self.half = self.c // 4
        self.pack = self.plane + self.half
        self.group = (self.c % 4) * 2 + self.core
        self.twin = self.plane + 1 - self.core
        self.across = (self.f + 2) % 4


def dev(ctx, fsdp):
    return {"ctx": ctx, "fsdp": fsdp}


def send(src, dst, send_sem, recv_sem, device):
    copy = pltpu.make_async_remote_copy(
        src_ref=src,
        dst_ref=dst,
        send_sem=send_sem,
        recv_sem=recv_sem,
        device_id=device,
        device_id_type=MESH,
    )
    copy.start()
    return copy


def await_recv(ref, sem):
    pltpu.make_async_copy(ref, ref, sem).wait()


def meet_plane(at):
    barrier = pltpu.get_barrier_semaphore()

    def greet(k, carry):
        pl.semaphore_signal(
            barrier,
            1,
            device_id=dev((at.c + k // 2) % 8, at.plane + (at.core + k) % 2),
            device_id_type=MESH,
        )
        return carry

    lax.fori_loop(1, 16, greet, 0)
    for k in range(2):
        pl.semaphore_signal(
            barrier, 1, device_id=dev(at.c, (at.plane + 2) % 4 + k), device_id_type=MESH
        )
    pl.semaphore_wait(barrier, 17)


def span(start, size, unit):
    return pl.ds(pl.multiple_of(start, unit), size)


def doc_index(places, seq_ends):
    return jnp.sum((places[:, None] >= seq_ends[None, :]).astype(jnp.int32), axis=1)


def spread_position(gathered_index, tok_dev, cycle_size):
    return gathered_index % tok_dev * cycle_size + gathered_index // tok_dev


def pair_scores(left_rows, right_rows):
    return jnp.einsum(
        "qhd,khd->qhk",
        left_rows.reshape(left_rows.shape[0], HEADS, -1),
        right_rows.reshape(right_rows.shape[0], HEADS, -1),
        preferred_element_type=jnp.float32,
    )


def pair_mask(query_pos, query_doc, key_pos, key_doc):
    return ((query_doc[:, None] == key_doc[None, :]) & (key_pos[None, :] <= query_pos[:, None]))[
        :, None, :
    ]


def in_blocks(advance, carried, pieces):
    total_rows = pieces[0].shape[0]
    block_rows = math.gcd(total_rows, 1024)
    block_count = total_rows // block_rows
    split = tuple((p.reshape((block_count, block_rows) + p.shape[1:]) for p in pieces))

    def inner(running, entry):
        return (advance(running, entry[1], entry[0] * block_rows), None)

    result, unused = lax.scan(inner, carried, (jnp.arange(block_count, dtype=jnp.int32), split))
    return result


def pair_terms(
    query_part,
    grad_part,
    log_part,
    delta_part,
    query_pos,
    query_doc,
    key_part,
    value_part,
    key_pos,
    key_doc,
):
    visible = pair_mask(query_pos, query_doc, key_pos, key_doc)
    prob_float = jnp.where(
        visible, jnp.exp(pair_scores(query_part, key_part) - log_part[:, :, None]), 0.0
    )
    grad_probs = pair_scores(grad_part, value_part)
    score_grad = (prob_float * (grad_probs - delta_part[:, :, None])).astype(jnp.bfloat16)
    return (prob_float.astype(jnp.bfloat16), score_grad)


def body(
    tokens,
    lengths,
    position,
    qkv_weight,
    out_weight,
    up_weight,
    down_weight,
    attn_gain,
    mlp_gain,
    query_scale,
    cotangent,
):
    cycle_size = lax.axis_size("ctx")
    my_index = lax.axis_index("ctx")
    tok_dev = tokens.shape[1]
    share_rows = tok_dev // cycle_size
    seq_ends = jnp.cumsum(lengths[0])
    place_row = position[0]
    residue = (place_row % cycle_size).reshape(cycle_size, tok_dev)
    landing = place_row // cycle_size
    matches = (
        residue[:, :, None] == jnp.arange(cycle_size, dtype=jnp.int32)[None, None, :]
    ).astype(jnp.int32)
    ranked = jnp.sum(jnp.cumsum(matches, axis=1) * matches, axis=2) - 1
    buffer_slot = residue * share_rows + ranked
    my_slots = lax.dynamic_index_in_dim(buffer_slot, my_index, 0, keepdims=False)
    local_rows = jnp.arange(tok_dev, dtype=jnp.int32)
    outgoing = jnp.zeros((tok_dev,), jnp.int32).at[my_slots].set(local_rows)
    flat_slot = (jnp.arange(cycle_size, dtype=jnp.int32)[:, None] * tok_dev + buffer_slot).reshape(
        -1
    )
    landing_table = (
        jnp.zeros((cycle_size * tok_dev,), jnp.int32)
        .at[flat_slot]
        .set(landing)
        .reshape(cycle_size, cycle_size, share_rows)
    )
    arrived_slot = lax.dynamic_index_in_dim(landing_table, my_index, 1, keepdims=False).reshape(-1)
    arrived_order = jnp.zeros((tok_dev,), jnp.int32).at[arrived_slot].set(local_rows)
    moved_x, moved_dy = (
        lax.all_to_all(tokens[0][outgoing], "ctx", split_axis=0, concat_axis=0, tiled=True),
        lax.all_to_all(cotangent[0][outgoing], "ctx", split_axis=0, concat_axis=0, tiled=True),
    )
    dealt_x = moved_x[arrived_order]
    dealt_dy = moved_dy[arrived_order]
    query_pos = local_rows * cycle_size + my_index
    query_doc = doc_index(query_pos, seq_ends)
    full_qkv, full_out, full_up, full_down, attn_gain_full, mlp_gain_full, scale_full = (
        lax.all_gather(qkv_weight, "fsdp", axis=0, tiled=True),
        lax.all_gather(out_weight, "fsdp", axis=0, tiled=True),
        lax.all_gather(up_weight, "fsdp", axis=0, tiled=True),
        lax.all_gather(down_weight, "fsdp", axis=0, tiled=True),
        lax.all_gather(attn_gain, "fsdp", axis=0, tiled=True),
        lax.all_gather(mlp_gain, "fsdp", axis=0, tiled=True),
        lax.all_gather(query_scale, "fsdp", axis=0, tiled=True),
    )
    attn_gain_f = attn_gain_full.astype(jnp.float32)
    mlp_gain_f = mlp_gain_full.astype(jnp.float32)
    scale_float = scale_full.astype(jnp.float32)
    x_float = dealt_x.astype(jnp.float32)
    inv_attn = lax.rsqrt(jnp.mean(x_float * x_float, axis=1, keepdims=True) + EPS)
    normed_attn = (x_float * inv_attn * attn_gain_f).astype(jnp.bfloat16)
    projected = jnp.dot(normed_attn, full_qkv, preferred_element_type=jnp.float32)
    att_width = projected.shape[1] // 3
    head_dim = scale_full.shape[0]
    base_scale = LOG2E / math.sqrt(head_dim)
    multiplier = jnp.tile(base_scale * jax.nn.softplus(scale_float), att_width // head_dim)
    raw_query = projected[:, :att_width]
    queries = (raw_query * multiplier).astype(jnp.bfloat16)
    key_rows = projected[:, att_width : 2 * att_width].astype(jnp.bfloat16)
    value_rows = projected[:, 2 * att_width :].astype(jnp.bfloat16)

    def key_place(first_row, amount):
        gathered_index = first_row + jnp.arange(amount, dtype=jnp.int32)
        key_pos = spread_position(gathered_index, tok_dev, cycle_size)
        return (key_pos, doc_index(key_pos, seq_ends))

    def stat_block(carried, pieces, first_row):
        running_max, running_sum = carried
        key_pos, key_doc = key_place(first_row, pieces[0].shape[0])
        visible = pair_mask(query_pos, query_doc, key_pos, key_doc)
        logits = jnp.where(visible, pair_scores(queries, pieces[0]), FLOOR)
        new_max = jnp.maximum(running_max, jnp.max(logits, axis=2))
        added = jnp.sum(jnp.where(visible, jnp.exp(logits - new_max[:, :, None]), 0.0), axis=2)
        return (new_max, running_sum * jnp.exp(running_max - new_max) + added)

    def output_block(summed, pieces, first_row):
        key_pos, key_doc = key_place(first_row, pieces[0].shape[0])
        visible = pair_mask(query_pos, query_doc, key_pos, key_doc)
        prob_low = jnp.where(
            visible, jnp.exp(pair_scores(queries, pieces[0]) - log_total[:, :, None]), 0.0
        ).astype(jnp.bfloat16)
        values_part = pieces[1].reshape(pieces[1].shape[0], HEADS, -1)
        return summed + jnp.einsum(
            "qhk,khd->qhd", prob_low, values_part, preferred_element_type=jnp.float32
        ).reshape(summed.shape)

    def query_grad_block(summed, pieces, first_row):
        key_pos, key_doc = key_place(first_row, pieces[0].shape[0])
        unused_probs, score_grad = pair_terms(
            queries,
            attended_grad,
            log_total,
            row_delta,
            query_pos,
            query_doc,
            pieces[0],
            pieces[1],
            key_pos,
            key_doc,
        )
        keys_part = pieces[0].reshape(pieces[0].shape[0], HEADS, -1)
        return summed + jnp.einsum(
            "qhk,khd->qhd", score_grad, keys_part, preferred_element_type=jnp.float32
        ).reshape(summed.shape)

    def key_grad_block(carried, pieces, first_row):
        amount = pieces[0].shape[0]
        part_pos, part_doc = key_place(first_row, amount)
        part_log = lax.dynamic_slice_in_dim(all_log, first_row, amount, 0)
        part_delta = lax.dynamic_slice_in_dim(all_delta, first_row, amount, 0)
        prob_low, score_grad = pair_terms(
            pieces[0],
            pieces[1],
            part_log,
            part_delta,
            part_pos,
            part_doc,
            key_rows,
            value_rows,
            query_pos,
            query_doc,
        )
        grad_keys = carried[0] + jnp.einsum(
            "qhk,qhd->khd",
            score_grad,
            pieces[0].reshape(amount, HEADS, -1),
            preferred_element_type=jnp.float32,
        ).reshape(tok_dev, -1)
        grad_values = carried[1] + jnp.einsum(
            "qhk,qhd->khd",
            prob_low,
            pieces[1].reshape(amount, HEADS, -1),
            preferred_element_type=jnp.float32,
        ).reshape(tok_dev, -1)
        return (grad_keys, grad_values)

    zero_stats = (
        jnp.full((tok_dev, HEADS), FLOOR, jnp.float32),
        jnp.zeros((tok_dev, HEADS), jnp.float32),
    )
    zero_rows = jnp.zeros((tok_dev, att_width), jnp.float32)
    running_max, running_sum = in_blocks(
        stat_block, zero_stats, (lax.all_gather(key_rows, "ctx", axis=0, tiled=True),)
    )
    log_total = running_max + jnp.log(running_sum)
    attended = in_blocks(
        output_block,
        zero_rows,
        (
            lax.all_gather(key_rows, "ctx", axis=0, tiled=True),
            lax.all_gather(value_rows, "ctx", axis=0, tiled=True),
        ),
    )
    attended_low = attended.astype(jnp.bfloat16)
    resid = x_float + jnp.dot(attended_low, full_out, preferred_element_type=jnp.float32)
    inv_mlp = lax.rsqrt(jnp.mean(resid * resid, axis=1, keepdims=True) + EPS)
    normed_mlp = (resid * inv_mlp * mlp_gain_f).astype(jnp.bfloat16)
    up_proj = jnp.dot(normed_mlp, full_up, preferred_element_type=jnp.float32)
    act_low = jax.nn.silu(up_proj).astype(jnp.bfloat16)
    result = resid + jnp.dot(act_low, full_down, preferred_element_type=jnp.float32)
    cot_float = dealt_dy.astype(jnp.float32)
    grad_down = jnp.dot(act_low.T, dealt_dy, preferred_element_type=jnp.float32)
    act_grad = jnp.dot(dealt_dy, full_down.T, preferred_element_type=jnp.float32)
    sigma = jax.nn.sigmoid(up_proj)
    up_grad = (act_grad * sigma * (1.0 + up_proj * (1.0 - sigma))).astype(jnp.bfloat16)
    grad_up = jnp.dot(normed_mlp.T, up_grad, preferred_element_type=jnp.float32)
    norm_mlp_grad = jnp.dot(up_grad, full_up.T, preferred_element_type=jnp.float32)
    grad_mlp_gain = jnp.sum(norm_mlp_grad * resid * inv_mlp, axis=0)
    scaled_mlp = norm_mlp_grad * mlp_gain_f
    resid_grad = cot_float + inv_mlp * (
        scaled_mlp - resid * inv_mlp * inv_mlp * jnp.mean(scaled_mlp * resid, axis=1, keepdims=True)
    )
    branch_grad = resid_grad.astype(jnp.bfloat16)
    grad_out = jnp.dot(attended_low.T, branch_grad, preferred_element_type=jnp.float32)
    attended_grad = jnp.dot(branch_grad, full_out.T, preferred_element_type=jnp.float32).astype(
        jnp.bfloat16
    )
    row_delta = jnp.sum(
        (attended_grad.astype(jnp.float32) * attended).reshape(tok_dev, HEADS, -1), axis=2
    )
    query_grads = in_blocks(
        query_grad_block,
        zero_rows,
        (
            lax.all_gather(key_rows, "ctx", axis=0, tiled=True),
            lax.all_gather(value_rows, "ctx", axis=0, tiled=True),
        ),
    )
    all_log, all_delta = (
        lax.all_gather(log_total, "ctx", axis=0, tiled=True),
        lax.all_gather(row_delta, "ctx", axis=0, tiled=True),
    )
    key_grad_f, value_grad_f = in_blocks(
        key_grad_block,
        (zero_rows, zero_rows),
        (
            lax.all_gather(queries, "ctx", axis=0, tiled=True),
            lax.all_gather(attended_grad, "ctx", axis=0, tiled=True),
        ),
    )
    scale_terms = jnp.sum((query_grads * raw_query).reshape(tok_dev, -1, head_dim), axis=(0, 1))
    grad_scale = scale_terms * base_scale * jax.nn.sigmoid(scale_float)
    proj_grad = jnp.concatenate(
        [
            (query_grads * multiplier).astype(jnp.bfloat16),
            key_grad_f.astype(jnp.bfloat16),
            value_grad_f.astype(jnp.bfloat16),
        ],
        axis=1,
    )
    grad_qkv = jnp.dot(normed_attn.T, proj_grad, preferred_element_type=jnp.float32)
    norm_attn_grad = jnp.dot(proj_grad, full_qkv.T, preferred_element_type=jnp.float32)
    grad_attn_gain = jnp.sum(norm_attn_grad * x_float * inv_attn, axis=0)
    scaled_attn = norm_attn_grad * attn_gain_f
    input_grad = resid_grad + inv_attn * (
        scaled_attn
        - x_float * inv_attn * inv_attn * jnp.mean(scaled_attn * x_float, axis=1, keepdims=True)
    )
    owned = (
        lax.psum_scatter(grad_qkv, "fsdp", scatter_dimension=0, tiled=True),
        lax.psum_scatter(grad_out, "fsdp", scatter_dimension=0, tiled=True),
        lax.psum_scatter(grad_up, "fsdp", scatter_dimension=0, tiled=True),
        lax.psum_scatter(grad_down, "fsdp", scatter_dimension=0, tiled=True),
        lax.psum_scatter(grad_attn_gain, "fsdp", scatter_dimension=0, tiled=True),
        lax.psum_scatter(grad_mlp_gain, "fsdp", scatter_dimension=0, tiled=True),
        lax.psum_scatter(grad_scale, "fsdp", scatter_dimension=0, tiled=True),
    )
    summed_grads = lax.psum(
        (owned[0], owned[1], owned[2], owned[3], owned[4], owned[5], owned[6]), "ctx"
    )
    back_out, back_grad = (
        lax.all_to_all(result[arrived_slot], "ctx", split_axis=0, concat_axis=0, tiled=True),
        lax.all_to_all(input_grad[arrived_slot], "ctx", split_axis=0, concat_axis=0, tiled=True),
    )
    return (
        back_out[my_slots][None],
        back_grad[my_slots][None],
        summed_grads[0],
        summed_grads[1],
        summed_grads[2],
        summed_grads[3],
        summed_grads[4],
        summed_grads[5],
        summed_grads[6],
    )


def attend_kernel(
    x_ref,
    w_ref,
    aux_ref,
    pos_ref,
    att_ref,
    normed_ref,
    qkv_ref,
    lse_ref,
    out_ref,
    auxsum_ref,
    place_ref,
    x_all,
    w_all,
    aux_all,
    pos_all,
    v_turned,
    key_pos,
    bias,
    att_send,
    x_send_sem,
    x_recv_sem,
    w_send_sem,
    w_recv_sem,
    aux_send_sem,
    aux_recv_sem,
    pos_sem,
    att_send_sem,
    att_recv_sem,
    local_sem,
):
    at = Place()
    meet_plane(at)
    c, f = at.c, at.f
    hub = at.core == at.half

    w_own = pltpu.make_async_copy(
        w_ref.at[at.core], w_all.at[span(f * 320, 320, 320)], local_sem.at[0]
    )
    w_own.start()
    aux_own = pltpu.make_async_copy(aux_ref, aux_all.at[f], local_sem.at[1])
    aux_own.start()
    pos_own = pltpu.make_async_copy(pos_ref, pos_all.at[at.core], local_sem.at[2])
    pos_own.start()
    x_own = pltpu.make_async_copy(x_ref, x_all.at[c], local_sem.at[3])

    x_far = pltpu.make_async_remote_copy(
        src_ref=x_ref,
        dst_ref=x_all.at[c],
        send_sem=x_send_sem.at[0, 0],
        recv_sem=x_recv_sem.at[c],
        device_id=dev(flip(c, 4), f),
        device_id_type=MESH,
    )

    @pl.when(hub)
    def _():
        x_own.start()
        for k, where in enumerate((dev(flip(c, 1), f), dev(flip(c, 2), f), dev(c, at.twin))):
            send(x_ref, x_all.at[c], x_send_sem.at[0, k], x_recv_sem.at[c], where)

    @pl.when(jnp.logical_not(hub))
    def _():
        x_far.start()

    w_copies, aux_copies = [], []
    for k in (2, 1, 3):
        to = (f + k) % 4
        aux_copies.append(
            send(
                aux_ref,
                aux_all.at[f],
                aux_send_sem.at[k],
                aux_recv_sem.at[f],
                dev(c, to),
            )
        )
        w_copies.append(
            send(
                w_ref.at[to % 2],
                w_all.at[span(f * 320, 320, 320)],
                w_send_sem.at[k],
                w_recv_sem.at[f],
                dev(c, to),
            )
        )
    pos_copy = send(
        pos_ref, pos_all.at[at.core], pos_sem.at[0], pos_sem.at[1], dev(c, at.twin)
    )

    aux_own.wait()
    for k in (1, 2, 3):
        await_recv(aux_all.at[0], aux_recv_sem.at[(f + k) % 4])
    aux = jnp.zeros(aux_ref.shape, F32)
    for k in range(4):
        aux = aux + aux_all[k].astype(F32)
    auxsum_ref[...] = aux
    gain = aux[0:1, :]
    scale = aux[2:3, :LANES]
    real = lax.broadcasted_iota(jnp.int32, (1, LANES), 1) < 80
    mult = jnp.where(
        real, LOG2E / math.sqrt(80) * (jnp.maximum(scale, 0.0) + jnp.log1p(jnp.exp(-jnp.abs(scale)))), 0.0
    )
    one = jnp.ones_like(mult)
    mults = jnp.concatenate([mult, mult, one, one, one, one], axis=1)

    pos_own.wait()
    await_recv(pos_all.at[0], pos_sem.at[1])
    place_ref[...] = pos_all[at.half]
    for k in range(8):
        block = place_ref[0:1, k * 256 : (k + 1) * 256]
        key_pos[k * 256 : (k + 1) * 256, :] = jnp.transpose(
            jnp.broadcast_to(block, (256, 256))
        )

    def arrive(step, carry):
        slot = flip(c, step)

        @pl.when(jnp.logical_and(hub, step == 0))
        def _():
            x_own.wait()

        @pl.when(jnp.logical_not(jnp.logical_and(hub, step == 0)))
        def _():
            await_recv(x_all.at[slot], x_recv_sem.at[slot])

        def onward(way, where):
            send(
                x_all.at[slot],
                x_all.at[slot],
                x_send_sem.at[step, way],
                x_recv_sem.at[slot],
                where,
            )

        @pl.when(jnp.logical_and(hub, jnp.logical_or(step == 4, step == 6)))
        def _():
            onward(0, dev(flip(c, 1), f))

        @pl.when(jnp.logical_and(hub, jnp.logical_or(step == 4, step == 1)))
        def _():
            onward(1, dev(flip(c, 2), f))

        @pl.when(jnp.logical_and(hub, step > 0))
        def _():
            onward(2, dev(c, at.twin))

        xf = x_all[slot].astype(F32)
        inv = lax.rsqrt(jnp.mean(xf * xf, axis=1, keepdims=True) + EPS)
        normed_ref[span(slot * 256, 256, 256), :] = (xf * inv * gain).astype(BF)
        return carry

    def project(step, carry):
        slot = flip(c, step)
        rows = span(slot * 256, 256, 256)
        proj = jnp.dot(normed_ref[rows, :], w_all[...], preferred_element_type=F32)
        qkv_ref[rows, :] = (proj * mults).astype(BF)
        return carry

    lax.fori_loop(0, 7, arrive, 0)
    w_own.wait()
    for k in (1, 2, 3):
        await_recv(w_all.at[pl.ds(0, 320)], w_recv_sem.at[(f + k) % 4])
    lax.fori_loop(0, 5, project, 0)
    lax.fori_loop(7, 8, arrive, 0)
    lax.fori_loop(5, 8, project, 0)

    for h in range(2):
        v_turned[h] = jnp.transpose(qkv_ref[:, (4 + h) * LANES : (5 + h) * LANES])

    att_own = pltpu.make_async_copy(
        att_send.at[c], att_ref.at[span(at.group * 160, 160, 160)], local_sem.at[3]
    )

    def att_copy(block):
        return pltpu.make_async_remote_copy(
            src_ref=att_send.at[block],
            dst_ref=att_ref.at[span(at.group * 160, 160, 160)],
            send_sem=att_send_sem.at[block],
            recv_sem=att_recv_sem.at[at.group],
            device_id=dev(block, at.pack),
            device_id_type=MESH,
        )

    mine = at.core == at.half

    def attend(step, carry):
        block = flip(c, step)
        lanes = span(block * 256, 256, 256)
        high = place_ref[0:1, lanes]
        least = place_ref[1:2, lanes]
        kp = key_pos[...]
        bias[...] = jnp.where((kp >= least) & (kp <= high), 0.0, FLOOR)
        for h in range(2):
            keys = qkv_ref[:, (2 + h) * LANES : (3 + h) * LANES]
            query = qkv_ref[lanes, h * LANES : (h + 1) * LANES]
            s = lax.dot_general(
                keys, query, (((1,), (1,)), ((), ())), preferred_element_type=F32
            )
            s = s + bias[...]
            top = jnp.max(s, axis=0, keepdims=True)
            p = jnp.exp(s - top)
            total = jnp.sum(p, axis=0, keepdims=True)
            o = jnp.dot(v_turned[h], p.astype(BF), preferred_element_type=F32)
            o = o[:80] / total
            lse_ref[h : h + 1, lanes] = top + jnp.log(total)
            out_ref[h * 80 : (h + 1) * 80, lanes] = o
            att_send[block, h * 80 : (h + 1) * 80, :] = o.astype(BF)

        @pl.when(jnp.logical_and(mine, step == 0))
        def _():
            att_own.start()

        @pl.when(jnp.logical_not(jnp.logical_and(mine, step == 0)))
        def _():
            att_copy(block).start()

        return carry

    lax.fori_loop(0, 8, attend, 0)
    for row in range(2, 8):
        lse_ref[row : row + 1, :] = jnp.zeros((1, 2048), F32)

    for copy in w_copies + aux_copies:
        copy.wait_send()
    pos_copy.wait_send()

    @pl.when(hub)
    def _():
        for k in range(3):
            await_recv(x_ref, x_send_sem.at[0, k])
        for step in range(1, 8):
            ways = {1: (1, 2), 4: (0, 1, 2), 6: (0, 2)}.get(step, (2,))
            for way in ways:
                await_recv(x_ref, x_send_sem.at[step, way])

    @pl.when(jnp.logical_not(hub))
    def _():
        x_far.wait_send()

    def finish(block, carry):
        own = jnp.logical_and(mine, block == c)

        @pl.when(own)
        def _():
            att_own.wait()

        @pl.when(jnp.logical_not(own))
        def _():
            att_copy(block).wait_send()

        own_in = jnp.logical_and(mine, block == at.group)

        @pl.when(jnp.logical_not(own_in))
        def _():
            await_recv(att_ref.at[pl.ds(0, 160)], att_recv_sem.at[block])

        return carry

    lax.fori_loop(0, 8, finish, 0)


def attend_forward(x, w_slices, aux, pos):
    shape = jax.ShapeDtypeStruct
    return pl.pallas_call(
        attend_kernel,
        name="attend_forward",
        out_shape=(
            shape((1280, 256), BF),
            shape((2048, 1280), BF),
            shape((2048, 768), BF),
            shape((8, 2048), F32),
            shape((160, 2048), F32),
            shape((16, 1280), F32),
            shape((8, 2048), F32),
        ),
        in_specs=[VMEM_SPEC] * 4,
        out_specs=(VMEM_SPEC,) * 7,
        scratch_shapes=[
            pltpu.VMEM((8, 256, 1280), BF),
            pltpu.VMEM((1280, 768), BF),
            pltpu.VMEM((4, 16, 1280), BF),
            pltpu.VMEM((2, 8, 2048), F32),
            pltpu.VMEM((2, 128, 2048), BF),
            pltpu.VMEM((2048, 256), F32),
            pltpu.VMEM((2048, 256), F32),
            pltpu.VMEM((8, 160, 256), BF),
            pltpu.SemaphoreType.DMA((8, 3)),
            pltpu.SemaphoreType.DMA((8,)),
            pltpu.SemaphoreType.DMA((4,)),
            pltpu.SemaphoreType.DMA((4,)),
            pltpu.SemaphoreType.DMA((4,)),
            pltpu.SemaphoreType.DMA((4,)),
            pltpu.SemaphoreType.DMA((2,)),
            pltpu.SemaphoreType.DMA((8,)),
            pltpu.SemaphoreType.DMA((8,)),
            pltpu.SemaphoreType.DMA((4,)),
        ],
        compiler_params=pltpu.CompilerParams(
            collective_id=0, has_side_effects=True, vmem_limit_bytes=VMEM_LIMIT
        ),
        cost_estimate=pl.CostEstimate(
            flops=14_000_000_000, bytes_accessed=40_000_000, transcendentals=8_400_000
        ),
    )(x, w_slices, aux, pos)


def attend_grad_kernel(
    grad_ref,
    qkv_ref,
    lse_ref,
    out_ref,
    place_ref,
    normed_ref,
    mult_ref,
    back_ref,
    weight_ref,
    scale_ref,
    grad_all,
    key_pos,
    bias,
    k_turned,
    delta,
    key_sum,
    value_sum,
    turned,
    g_send_sem,
    g_recv_sem,
    b_send_sem,
    b_recv_sem,
    local_sem,
):
    at = Place()
    meet_plane(at)
    c, f = at.c, at.f
    mine = at.core == at.half

    def grad_copy(group, h):
        return pltpu.make_async_remote_copy(
            src_ref=grad_ref.at[span(group * 160 + h * 80, 80, 80)],
            dst_ref=grad_all.at[h, pl.ds(0, 80), span(c * 256, 256, 256)],
            send_sem=g_send_sem.at[group, h],
            recv_sem=g_recv_sem.at[c, h],
            device_id=dev(at.core * 4 + group // 2, at.plane + group % 2),
            device_id_type=MESH,
        )

    def grad_own(h):
        return pltpu.make_async_copy(
            grad_ref.at[span(at.group * 160 + h * 80, 80, 80)],
            grad_all.at[h, pl.ds(0, 80), span(c * 256, 256, 256)],
            local_sem.at[h],
        )

    def give(k, carry):
        group = flip(at.group, k)

        @pl.when(jnp.logical_and(mine, k == 0))
        def _():
            grad_own(0).start()
            grad_own(1).start()

        @pl.when(jnp.logical_not(jnp.logical_and(mine, k == 0)))
        def _():
            grad_copy(group, 0).start()
            grad_copy(group, 1).start()

        return carry

    lax.fori_loop(0, 8, give, 0)

    for h in range(2):
        grad_all[h, 80:, :] = jnp.zeros((48, 2048), BF)
        k_turned[h] = jnp.transpose(qkv_ref[:, (2 + h) * LANES : (3 + h) * LANES])
    for k in range(8):
        block = place_ref[0:1, k * 256 : (k + 1) * 256]
        key_pos[k * 256 : (k + 1) * 256, :] = jnp.transpose(
            jnp.broadcast_to(block, (256, 256))
        )
    scale_ref[...] = jnp.zeros((8, LANES), F32)

    def take(k, carry):
        block = flip(c, k)

        @pl.when(jnp.logical_and(mine, k == 0))
        def _():
            grad_own(0).wait()
            grad_own(1).wait()

        @pl.when(jnp.logical_not(jnp.logical_and(mine, k == 0)))
        def _():
            for h in range(2):
                await_recv(
                    grad_all.at[h, pl.ds(0, 80), pl.ds(0, 256)], g_recv_sem.at[block, h]
                )

        return carry

    lax.fori_loop(0, 8, take, 0)
    for h in range(2):
        delta[h : h + 1, :] = jnp.sum(
            grad_all[h, :80, :].astype(F32) * out_ref[h * 80 : (h + 1) * 80, :],
            axis=0,
            keepdims=True,
        )

    for h in range(2):
        key_sum[...] = jnp.zeros((2048, LANES), F32)
        value_sum[...] = jnp.zeros((2048, LANES), F32)

        def block_grad(block, carry, h=h):
            lanes = span(block * 256, 256, 256)
            high = place_ref[0:1, lanes]
            least = place_ref[1:2, lanes]
            kp = key_pos[...]
            keys = qkv_ref[:, (2 + h) * LANES : (3 + h) * LANES]
            values = qkv_ref[:, (4 + h) * LANES : (5 + h) * LANES]
            query = qkv_ref[lanes, h * LANES : (h + 1) * LANES]
            grad_t = grad_all[h, :, lanes]
            s = lax.dot_general(
                keys, query, (((1,), (1,)), ((), ())), preferred_element_type=F32
            )
            visible = (kp >= least) & (kp <= high)
            p = jnp.exp(jnp.where(visible, s - lse_ref[h : h + 1, lanes], FLOOR))
            gp = jnp.dot(values, grad_t, preferred_element_type=F32)
            gs = (p * (gp - delta[h : h + 1, lanes])).astype(BF)
            value_sum[...] += lax.dot_general(
                p.astype(BF), grad_t, (((1,), (1,)), ((), ())), preferred_element_type=F32
            )
            key_sum[...] += jnp.dot(gs, query, preferred_element_type=F32)
            q_grad = jnp.dot(k_turned[h], gs, preferred_element_type=F32)
            scale_ref[0:1, :] += jnp.sum(
                jnp.transpose(q_grad) * query.astype(F32), axis=0, keepdims=True
            )
            turned[h * 80 : (h + 1) * 80, lanes] = (
                q_grad[:80] * mult_ref[:80, 0:1]
            ).astype(BF)
            return carry

        lax.fori_loop(0, 8, block_grad, 0)
        turned[160 + h * 80 : 160 + (h + 1) * 80, :] = jnp.transpose(key_sum[...])[:80].astype(BF)
        turned[320 + h * 80 : 320 + (h + 1) * 80, :] = jnp.transpose(value_sum[...])[:80].astype(BF)

    def back_copy(block, j):
        return pltpu.make_async_remote_copy(
            src_ref=turned.at[pl.ds(j * 160, 160), span(block * 256, 256, 256)],
            dst_ref=back_ref.at[span(j * 1280 + at.group * 160, 160, 160)],
            send_sem=b_send_sem.at[block, j],
            recv_sem=b_recv_sem.at[at.group, j],
            device_id=dev(block, at.pack),
            device_id_type=MESH,
        )

    def back_own(j):
        return pltpu.make_async_copy(
            turned.at[pl.ds(j * 160, 160), span(c * 256, 256, 256)],
            back_ref.at[span(j * 1280 + at.group * 160, 160, 160)],
            local_sem.at[j],
        )

    def put(k, carry):
        block = flip(c, k)

        @pl.when(jnp.logical_and(mine, k == 0))
        def _():
            for j in range(3):
                back_own(j).start()

        @pl.when(jnp.logical_not(jnp.logical_and(mine, k == 0)))
        def _():
            for j in range(3):
                back_copy(block, j).start()

        return carry

    lax.fori_loop(0, 8, put, 0)

    for j in range(3):
        weight_ref[j * 160 : (j + 1) * 160, :] = jnp.dot(
            turned[j * 160 : (j + 1) * 160, :], normed_ref[...], preferred_element_type=F32
        ).astype(BF)

    def finish(block, carry):
        own = jnp.logical_and(mine, block == c)

        @pl.when(own)
        def _():
            for j in range(3):
                back_own(j).wait()

        @pl.when(jnp.logical_not(own))
        def _():
            for j in range(3):
                back_copy(block, j).wait_send()

        own_in = jnp.logical_and(mine, block == at.group)

        @pl.when(jnp.logical_not(own_in))
        def _():
            for j in range(3):
                await_recv(back_ref.at[pl.ds(0, 160)], b_recv_sem.at[block, j])
            for h in range(2):
                grad_copy(block, h).wait_send()

        return carry

    lax.fori_loop(0, 8, finish, 0)


def attend_backward(grad_t, qkv, lse, out, place, normed, mult):
    shape = jax.ShapeDtypeStruct
    return pl.pallas_call(
        attend_grad_kernel,
        name="attend_backward",
        out_shape=(shape((3840, 256), BF), shape((480, 1280), BF), shape((8, LANES), F32)),
        in_specs=[VMEM_SPEC] * 7,
        out_specs=(VMEM_SPEC,) * 3,
        scratch_shapes=[
            pltpu.VMEM((2, 128, 2048), BF),
            pltpu.VMEM((2048, 256), F32),
            pltpu.VMEM((8, 128), F32),
            pltpu.VMEM((2, 128, 2048), BF),
            pltpu.VMEM((8, 2048), F32),
            pltpu.VMEM((2048, LANES), F32),
            pltpu.VMEM((2048, LANES), F32),
            pltpu.VMEM((480, 2048), BF),
            pltpu.SemaphoreType.DMA((8, 2)),
            pltpu.SemaphoreType.DMA((8, 2)),
            pltpu.SemaphoreType.DMA((8, 3)),
            pltpu.SemaphoreType.DMA((8, 3)),
            pltpu.SemaphoreType.DMA((4,)),
        ],
        compiler_params=pltpu.CompilerParams(
            collective_id=1, has_side_effects=True, vmem_limit_bytes=VMEM_LIMIT
        ),
        cost_estimate=pl.CostEstimate(
            flops=24_000_000_000, bytes_accessed=40_000_000, transcendentals=8_400_000
        ),
    )(grad_t, qkv, lse, out, place, normed, mult)


def add_rows(target, source, rows, step):
    def one(k, carry):
        part = span(k * step, step, step)
        target[part, :] = (target[part, :].astype(F32) + source[part, :].astype(F32)).astype(
            target.dtype
        )
        return carry

    lax.fori_loop(0, rows // step, one, 0)


def sum_rows(target, left, right, rows, step):
    def one(k, carry):
        part = span(k * step, step, step)
        target[part, :] = (left[part, :].astype(F32) + right[part, :].astype(F32)).astype(
            target.dtype
        )
        return carry

    lax.fori_loop(0, rows // step, one, 0)


def reduce_kernel(
    first_ref,
    second_ref,
    third_ref,
    slice_ref,
    small_ref,
    first_out,
    second_out,
    third_out,
    slice_out,
    small_out,
    a0,
    a1,
    a2,
    a3,
    a4,
    final,
    s1,
    s2,
    small_in,
    m_send,
    m_recv,
    q_send,
    q_recv,
    v_send,
    v_recv,
):
    at = Place()
    meet_plane(at)
    c, f, core = at.c, at.f, at.core
    row = f // 2
    xbit, zbit, hbit = c % 2, (c // 2) % 2, c // 4
    twin, across = dev(c, at.twin), dev(c, at.across)
    xpeer, zpeer, hpeer = dev(flip(c, 1), f), dev(flip(c, 2), f), dev(flip(c, 4), f)
    inputs = (first_ref, second_ref, third_ref)
    outputs = (first_out, second_out, third_out)
    copies = {}

    def go(kind, stage, m, src, dst, where):
        sems = {"m": (m_send, m_recv), "q": (q_send, q_recv), "v": (v_send, v_recv)}[kind]
        copies[kind, stage, m] = send(
            src, dst, sems[0].at[stage, m], sems[1].at[stage, m], where
        )

    def got(kind, stage, m):
        copies[kind, stage, m].wait_recv()

    half = xbit * 160
    quarter = half + zbit * 80
    side = span(hbit * 640, 640, 640)
    other = span((1 - hbit) * 640, 640, 640)
    k2 = zbit + 2 * xbit

    def main(stage, m):
        src = inputs[m]
        if stage == 0:
            for y in range(2):
                go(
                    "m", y, m, src.at[span((2 * y + 1 - core) * 320, 320, 320)],
                    a0.at[m, y], twin,
                )
        if stage == 1:
            for y in range(2):
                got("m", y, m)
                base = (2 * y + core) * 320
                def one(k, carry, y=y, base=base):
                    part = span(k * 80, 80, 80)
                    a0[m, y, part, :] = (
                        a0[m, y, part, :].astype(F32)
                        + src[span(base + k * 80, 80, 80), :].astype(F32)
                    ).astype(BF)
                    return carry
                lax.fori_loop(0, 4, one, 0)
            go("m", 2, m, a0.at[m, 1 - row], a1.at[m], across)
        if stage == 2:
            got("m", 2, m)
            add_rows(a1.at[m], a0.at[m, row], 320, 80)
            go("m", 3, m, a1.at[m, span(160 - half, 160, 160)], a2.at[m], xpeer)
        if stage == 3:
            got("m", 3, m)
            add_rows(a2.at[m], a1.at[m, span(half, 160, 160)], 160, 80)
            go("m", 4, m, a2.at[m, span(80 - zbit * 80, 80, 80)], a3.at[m], zpeer)
        if stage == 4:
            got("m", 4, m)
            add_rows(a3.at[m], a2.at[m, span(zbit * 80, 80, 80)], 80, 80)
            go("m", 5, m, a3.at[m, :, other], a4.at[m], hpeer)
        if stage == 5:
            got("m", 5, m)
            spot = span(quarter, 80, 80)
            final[m, spot, side] = (
                a4[m].astype(F32) + a3[m, :, side].astype(F32)
            ).astype(BF)
            piece = final.at[m, spot, side]
            go("m", 6, m, piece, piece, hpeer)
        if stage == 6:
            got("m", 6, m)
            piece = final.at[m, span(quarter, 80, 80)]
            go("m", 7, m, piece, piece, zpeer)
        if stage == 7:
            got("m", 7, m)
            piece = final.at[m, span(half, 160, 160)]
            go("m", 8, m, piece, piece, xpeer)
        if stage == 8:
            got("m", 8, m)
            outputs[m][...] = final[m].astype(F32)

    def head(stage, j):
        rows = pl.ds(j * 160, 160)
        mine = slice_out.at[j, core]
        if stage == 0:
            go(
                "q", 0, j, slice_ref.at[rows, span((1 - row) * 640, 640, 640)], s1.at[j], across
            )
        if stage == 1:
            got("q", 0, j)
            s1[j] = (
                s1[j].astype(F32) + slice_ref[rows, span(row * 640, 640, 640)].astype(F32)
            ).astype(BF)
            go("q", 1, j, s1.at[j, span(80 - hbit * 80, 80, 80)], s2.at[j], hpeer)
        if stage == 2:
            got("q", 1, j)
            own = span(hbit * 80, 80, 80)
            slice_out[j, core, k2, own, :] = (
                s2[j].astype(F32) + s1[j, own, :].astype(F32)
            ).astype(BF)
            piece = mine.at[k2, own]
            go("q", 2, j, piece, piece, hpeer)
        if stage == 3:
            got("q", 2, j)
            piece = mine.at[k2]
            go("q", 3, j, piece, piece, zpeer)
        if stage == 4:
            got("q", 3, j)
            piece = mine.at[pl.ds(2 * xbit, 2)]
            go("q", 4, j, piece, piece, xpeer)
        if stage == 5:
            got("q", 4, j)
            go("q", 5, j, mine, mine, twin)
        if stage == 6:
            got("q", 5, j)

    def tiny(stage):
        if stage > 0:
            got("v", stage - 1, 0)
            small_out[...] += small_in[stage - 1]
        if stage < 5:
            where = (twin, across, xpeer, zpeer, hpeer)[stage]
            go("v", stage, 0, small_out, small_in.at[stage], where)

    small_out[...] = small_ref[...]
    for tick in range(12):
        for m in range(3):
            if 0 <= tick - m <= 6:
                head(tick - m, m)
        for m in range(3):
            if 0 <= tick - m <= 8:
                main(tick - m, m)
        if tick < 6:
            if tick > 0:
                copies["v", tick - 1, 0].wait_send()
            tiny(tick)
    for key, copy in copies.items():
        if key[0] != "v":
            copy.wait_send()


def reduce_grads(first, second, third, slices, small):
    shape = jax.ShapeDtypeStruct
    dma = pltpu.SemaphoreType.DMA
    return pl.pallas_call(
        reduce_kernel,
        name="reduce_grads",
        out_shape=(
            shape((320, 1280), F32),
            shape((320, 1280), F32),
            shape((320, 1280), F32),
            shape((3, 2, 4, 160, 640), BF),
            shape((8, 1280), F32),
        ),
        in_specs=[VMEM_SPEC] * 5,
        out_specs=(VMEM_SPEC,) * 5,
        scratch_shapes=[
            pltpu.VMEM((3, 2, 320, 1280), BF),
            pltpu.VMEM((3, 320, 1280), BF),
            pltpu.VMEM((3, 160, 1280), BF),
            pltpu.VMEM((3, 80, 1280), BF),
            pltpu.VMEM((3, 80, 640), BF),
            pltpu.VMEM((3, 320, 1280), BF),
            pltpu.VMEM((3, 160, 640), BF),
            pltpu.VMEM((3, 80, 640), BF),
            pltpu.VMEM((5, 8, 1280), F32),
            dma((9, 3)),
            dma((9, 3)),
            dma((6, 3)),
            dma((6, 3)),
            dma((5, 1)),
            dma((5, 1)),
        ],
        compiler_params=pltpu.CompilerParams(
            collective_id=2, has_side_effects=True, vmem_limit_bytes=VMEM_LIMIT
        ),
        cost_estimate=pl.CostEstimate(flops=30_000_000, bytes_accessed=30_000_000, transcendentals=0),
    )(first, second, third, slices, small)


def fast_body(
    tokens,
    lengths,
    position,
    qkv_weight,
    out_weight,
    up_weight,
    down_weight,
    attn_gain,
    mlp_gain,
    query_scale,
    cotangent,
):
    c, f = lax.axis_index("ctx"), lax.axis_index("fsdp")
    x, dy = tokens[0], cotangent[0]
    heads = qkv_weight.reshape(320, 3, HEADS, 80)
    heads = lax.dynamic_slice_in_dim(heads, (c % 4) * 4, 4, 2)
    heads = jnp.pad(heads, ((0, 0), (0, 0), (0, 0), (0, 48))).reshape(320, 3, 2, 2, LANES)
    w_slices = heads.transpose(2, 0, 1, 3, 4).reshape(2, 320, 768)
    aux = jnp.zeros((16, 1280), BF)
    aux = lax.dynamic_update_slice(aux, attn_gain[None], (0, f * 320))
    aux = lax.dynamic_update_slice(aux, mlp_gain[None], (1, f * 320))
    aux = lax.dynamic_update_slice(aux, query_scale[None], (2, f * 20))
    pos = position[0]
    start = jnp.zeros_like(pos)
    end = 0
    for k in range(4):
        end = end + lengths[0, k]
        start = jnp.where(pos >= end, end, start)
    places = jnp.concatenate([pos[None], start[None], jnp.zeros((6, 2048), jnp.int32)], axis=0)
    places = places.astype(F32)

    att_t, normed, qkv, lse, out, auxsum, place = attend_forward(x, w_slices, aux, places)

    full_out, full_up, full_down, full_qkv = (
        lax.all_gather(out_weight, "fsdp", axis=0, tiled=True),
        lax.all_gather(up_weight, "fsdp", axis=0, tiled=True),
        lax.all_gather(down_weight, "fsdp", axis=0, tiled=True),
        lax.all_gather(qkv_weight, "fsdp", axis=0, tiled=True),
    )
    attn_gain_f, mlp_gain_f = auxsum[0], auxsum[1]
    scale_float = auxsum[2, :80]
    xf = x.astype(F32)
    resid = xf + lax.dot_general(att_t, full_out, (((0,), (0,)), ((), ())), preferred_element_type=F32)
    inv_mlp = lax.rsqrt(jnp.mean(resid * resid, axis=1, keepdims=True) + EPS)
    normed_mlp = (resid * inv_mlp * mlp_gain_f).astype(BF)
    up_proj = jnp.dot(normed_mlp, full_up, preferred_element_type=F32)
    sigma = jax.nn.sigmoid(up_proj)
    act_low = (up_proj * sigma).astype(BF)
    result = resid + jnp.dot(act_low, full_down, preferred_element_type=F32)
    grad_down = jnp.dot(act_low.T, dy, preferred_element_type=F32).astype(BF)
    act_grad = jnp.dot(dy, full_down.T, preferred_element_type=F32)
    up_grad = (act_grad * sigma * (1.0 + up_proj * (1.0 - sigma))).astype(BF)
    grad_up = jnp.dot(normed_mlp.T, up_grad, preferred_element_type=F32).astype(BF)
    norm_mlp_grad = jnp.dot(up_grad, full_up.T, preferred_element_type=F32)
    grad_mlp_gain = jnp.sum(norm_mlp_grad * resid * inv_mlp, axis=0)
    scaled_mlp = norm_mlp_grad * mlp_gain_f
    resid_grad = dy.astype(F32) + inv_mlp * (
        scaled_mlp - resid * inv_mlp * inv_mlp * jnp.mean(scaled_mlp * resid, axis=1, keepdims=True)
    )
    branch_grad = resid_grad.astype(BF)
    grad_out = jnp.dot(att_t, branch_grad, preferred_element_type=F32).astype(BF)
    grad_t = lax.dot_general(
        full_out, branch_grad, (((1,), (1,)), ((), ())), preferred_element_type=F32
    ).astype(BF)

    base_scale = LOG2E / math.sqrt(80)
    soft = jax.nn.softplus(scale_float)
    mult = jnp.broadcast_to(jnp.pad(base_scale * soft, (0, 48))[:, None], (LANES, LANES))
    back, slices, scale_sum = attend_backward(grad_t, qkv, lse, out, place, normed, mult)

    inv_attn = lax.rsqrt(jnp.mean(xf * xf, axis=1, keepdims=True) + EPS)
    norm_attn_grad = jnp.dot(full_qkv, back, preferred_element_type=F32).T
    grad_attn_gain = jnp.sum(norm_attn_grad * xf * inv_attn, axis=0)
    scaled_attn = norm_attn_grad * attn_gain_f
    input_grad = resid_grad + inv_attn * (
        scaled_attn - xf * inv_attn * inv_attn * jnp.mean(scaled_attn * xf, axis=1, keepdims=True)
    )
    grad_scale = scale_sum[0, :80] / soft * jax.nn.sigmoid(scale_float)
    small = jnp.concatenate(
        [
            grad_attn_gain[None],
            grad_mlp_gain[None],
            jnp.pad(grad_scale, (0, 1200))[None],
            jnp.zeros((5, 1280), F32),
        ],
        axis=0,
    )
    g_out, g_up, g_down, g_qkv, small = reduce_grads(grad_out, grad_up, grad_down, slices, small)
    g_qkv = lax.dynamic_slice_in_dim(g_qkv, (f % 2) * 320, 320, 4)
    g_qkv = g_qkv.reshape(3, 2, 2, 2, 160, 320).transpose(5, 0, 3, 2, 1, 4)
    g_qkv = g_qkv.reshape(320, 3840).astype(F32)
    return (
        result[None],
        input_grad[None],
        g_qkv,
        g_out,
        g_up,
        g_down,
        lax.dynamic_slice_in_dim(small[0], f * 320, 320),
        lax.dynamic_slice_in_dim(small[1], f * 320, 320),
        lax.dynamic_slice_in_dim(small[2], f * 20, 20),
    )


def solution(mesh):
    placed = (
        P("fsdp", "ctx", None),
        P("fsdp", None),
        P("fsdp", None),
        P("fsdp", None),
        P("fsdp", None),
        P("fsdp", None),
        P("fsdp", None),
        P("fsdp"),
        P("fsdp"),
        P("fsdp"),
        P("fsdp", "ctx", None),
    )
    fits = mesh.shape["ctx"] == 8 and mesh.shape["fsdp"] == 4
    return jax.shard_map(
        fast_body if fits else body,
        mesh=mesh,
        in_specs=placed,
        out_specs=(
            P("fsdp", "ctx", None),
            P("fsdp", "ctx", None),
            P("fsdp", None),
            P("fsdp", None),
            P("fsdp", None),
            P("fsdp", None),
            P("fsdp"),
            P("fsdp"),
            P("fsdp"),
        ),
        check_vma=False,
    )
```

```python
import functools
import math

import jax
import jax.numpy as jnp
from jax import lax
from jax.experimental import pallas as pl
from jax.experimental.pallas import tpu as pltpu
from jax.sharding import PartitionSpec as P

HEADS = 16


EPS = 1e-06
FLOOR = -1e30
LOG2E = 1.442695041

MESH = pl.DeviceIdType.MESH
LANES = 128
BF = jnp.bfloat16
F32 = jnp.float32
VMEM_SPEC = pl.BlockSpec(memory_space=pltpu.VMEM)
VMEM_LIMIT = 60 << 20


def flip(number, mask):
    total = 0
    for bit in (1, 2, 4):
        left = (number // bit) % 2
        right = (mask // bit) % 2
        total = total + bit * (left + right - 2 * left * right)
    return total


class Place:
    def __init__(self):
        self.c = lax.axis_index("ctx")
        self.f = lax.axis_index("fsdp")
        self.core = self.f % 2
        self.plane = self.f - self.core
        self.half = self.c // 4
        self.pack = self.plane + self.half
        self.group = (self.c % 4) * 2 + self.core
        self.twin = self.plane + 1 - self.core
        self.across = (self.f + 2) % 4


def dev(ctx, fsdp):
    return {"ctx": ctx, "fsdp": fsdp}


def send(src, dst, send_sem, recv_sem, device):
    copy = pltpu.make_async_remote_copy(
        src_ref=src,
        dst_ref=dst,
        send_sem=send_sem,
        recv_sem=recv_sem,
        device_id=device,
        device_id_type=MESH,
    )
    copy.start()
    return copy


def await_recv(ref, sem):
    pltpu.make_async_copy(ref, ref, sem).wait()


def meet_plane(at):
    barrier = pltpu.get_barrier_semaphore()

    def greet(k, carry):
        pl.semaphore_signal(
            barrier,
            1,
            device_id=dev((at.c + k // 2) % 8, at.plane + (at.core + k) % 2),
            device_id_type=MESH,
        )
        return carry

    lax.fori_loop(1, 16, greet, 0)
    for k in range(2):
        pl.semaphore_signal(
            barrier, 1, device_id=dev(at.c, (at.plane + 2) % 4 + k), device_id_type=MESH
        )
    pl.semaphore_wait(barrier, 17)


def span(start, size, unit):
    return pl.ds(pl.multiple_of(start, unit), size)


def doc_index(places, seq_ends):
    return jnp.sum((places[:, None] >= seq_ends[None, :]).astype(jnp.int32), axis=1)


def spread_position(gathered_index, tok_dev, cycle_size):
    return gathered_index % tok_dev * cycle_size + gathered_index // tok_dev


def pair_scores(left_rows, right_rows):
    return jnp.einsum(
        "qhd,khd->qhk",
        left_rows.reshape(left_rows.shape[0], HEADS, -1),
        right_rows.reshape(right_rows.shape[0], HEADS, -1),
        preferred_element_type=jnp.float32,
    )


def pair_mask(query_pos, query_doc, key_pos, key_doc):
    return ((query_doc[:, None] == key_doc[None, :]) & (key_pos[None, :] <= query_pos[:, None]))[
        :, None, :
    ]


def in_blocks(advance, carried, pieces):
    total_rows = pieces[0].shape[0]
    block_rows = math.gcd(total_rows, 1024)
    block_count = total_rows // block_rows
    split = tuple((p.reshape((block_count, block_rows) + p.shape[1:]) for p in pieces))

    def inner(running, entry):
        return (advance(running, entry[1], entry[0] * block_rows), None)

    result, unused = lax.scan(inner, carried, (jnp.arange(block_count, dtype=jnp.int32), split))
    return result


def pair_terms(
    query_part,
    grad_part,
    log_part,
    delta_part,
    query_pos,
    query_doc,
    key_part,
    value_part,
    key_pos,
    key_doc,
):
    visible = pair_mask(query_pos, query_doc, key_pos, key_doc)
    prob_float = jnp.where(
        visible, jnp.exp(pair_scores(query_part, key_part) - log_part[:, :, None]), 0.0
    )
    grad_probs = pair_scores(grad_part, value_part)
    score_grad = (prob_float * (grad_probs - delta_part[:, :, None])).astype(jnp.bfloat16)
    return (prob_float.astype(jnp.bfloat16), score_grad)


def body(
    tokens,
    lengths,
    position,
    qkv_weight,
    out_weight,
    up_weight,
    down_weight,
    attn_gain,
    mlp_gain,
    query_scale,
    cotangent,
):
    cycle_size = lax.axis_size("ctx")
    my_index = lax.axis_index("ctx")
    tok_dev = tokens.shape[1]
    share_rows = tok_dev // cycle_size
    seq_ends = jnp.cumsum(lengths[0])
    place_row = position[0]
    residue = (place_row % cycle_size).reshape(cycle_size, tok_dev)
    landing = place_row // cycle_size
    matches = (
        residue[:, :, None] == jnp.arange(cycle_size, dtype=jnp.int32)[None, None, :]
    ).astype(jnp.int32)
    ranked = jnp.sum(jnp.cumsum(matches, axis=1) * matches, axis=2) - 1
    buffer_slot = residue * share_rows + ranked
    my_slots = lax.dynamic_index_in_dim(buffer_slot, my_index, 0, keepdims=False)
    local_rows = jnp.arange(tok_dev, dtype=jnp.int32)
    outgoing = jnp.zeros((tok_dev,), jnp.int32).at[my_slots].set(local_rows)
    flat_slot = (jnp.arange(cycle_size, dtype=jnp.int32)[:, None] * tok_dev + buffer_slot).reshape(
        -1
    )
    landing_table = (
        jnp.zeros((cycle_size * tok_dev,), jnp.int32)
        .at[flat_slot]
        .set(landing)
        .reshape(cycle_size, cycle_size, share_rows)
    )
    arrived_slot = lax.dynamic_index_in_dim(landing_table, my_index, 1, keepdims=False).reshape(-1)
    arrived_order = jnp.zeros((tok_dev,), jnp.int32).at[arrived_slot].set(local_rows)
    moved_x, moved_dy = (
        lax.all_to_all(tokens[0][outgoing], "ctx", split_axis=0, concat_axis=0, tiled=True),
        lax.all_to_all(cotangent[0][outgoing], "ctx", split_axis=0, concat_axis=0, tiled=True),
    )
    dealt_x = moved_x[arrived_order]
    dealt_dy = moved_dy[arrived_order]
    query_pos = local_rows * cycle_size + my_index
    query_doc = doc_index(query_pos, seq_ends)
    full_qkv, full_out, full_up, full_down, attn_gain_full, mlp_gain_full, scale_full = (
        lax.all_gather(qkv_weight, "fsdp", axis=0, tiled=True),
        lax.all_gather(out_weight, "fsdp", axis=0, tiled=True),
        lax.all_gather(up_weight, "fsdp", axis=0, tiled=True),
        lax.all_gather(down_weight, "fsdp", axis=0, tiled=True),
        lax.all_gather(attn_gain, "fsdp", axis=0, tiled=True),
        lax.all_gather(mlp_gain, "fsdp", axis=0, tiled=True),
        lax.all_gather(query_scale, "fsdp", axis=0, tiled=True),
    )
    attn_gain_f = attn_gain_full.astype(jnp.float32)
    mlp_gain_f = mlp_gain_full.astype(jnp.float32)
    scale_float = scale_full.astype(jnp.float32)
    x_float = dealt_x.astype(jnp.float32)
    inv_attn = lax.rsqrt(jnp.mean(x_float * x_float, axis=1, keepdims=True) + EPS)
    normed_attn = (x_float * inv_attn * attn_gain_f).astype(jnp.bfloat16)
    projected = jnp.dot(normed_attn, full_qkv, preferred_element_type=jnp.float32)
    att_width = projected.shape[1] // 3
    head_dim = scale_full.shape[0]
    base_scale = LOG2E / math.sqrt(head_dim)
    multiplier = jnp.tile(base_scale * jax.nn.softplus(scale_float), att_width // head_dim)
    raw_query = projected[:, :att_width]
    queries = (raw_query * multiplier).astype(jnp.bfloat16)
    key_rows = projected[:, att_width : 2 * att_width].astype(jnp.bfloat16)
    value_rows = projected[:, 2 * att_width :].astype(jnp.bfloat16)

    def key_place(first_row, amount):
        gathered_index = first_row + jnp.arange(amount, dtype=jnp.int32)
        key_pos = spread_position(gathered_index, tok_dev, cycle_size)
        return (key_pos, doc_index(key_pos, seq_ends))

    def stat_block(carried, pieces, first_row):
        running_max, running_sum = carried
        key_pos, key_doc = key_place(first_row, pieces[0].shape[0])
        visible = pair_mask(query_pos, query_doc, key_pos, key_doc)
        logits = jnp.where(visible, pair_scores(queries, pieces[0]), FLOOR)
        new_max = jnp.maximum(running_max, jnp.max(logits, axis=2))
        added = jnp.sum(jnp.where(visible, jnp.exp(logits - new_max[:, :, None]), 0.0), axis=2)
        return (new_max, running_sum * jnp.exp(running_max - new_max) + added)

    def output_block(summed, pieces, first_row):
        key_pos, key_doc = key_place(first_row, pieces[0].shape[0])
        visible = pair_mask(query_pos, query_doc, key_pos, key_doc)
        prob_low = jnp.where(
            visible, jnp.exp(pair_scores(queries, pieces[0]) - log_total[:, :, None]), 0.0
        ).astype(jnp.bfloat16)
        values_part = pieces[1].reshape(pieces[1].shape[0], HEADS, -1)
        return summed + jnp.einsum(
            "qhk,khd->qhd", prob_low, values_part, preferred_element_type=jnp.float32
        ).reshape(summed.shape)

    def query_grad_block(summed, pieces, first_row):
        key_pos, key_doc = key_place(first_row, pieces[0].shape[0])
        unused_probs, score_grad = pair_terms(
            queries,
            attended_grad,
            log_total,
            row_delta,
            query_pos,
            query_doc,
            pieces[0],
            pieces[1],
            key_pos,
            key_doc,
        )
        keys_part = pieces[0].reshape(pieces[0].shape[0], HEADS, -1)
        return summed + jnp.einsum(
            "qhk,khd->qhd", score_grad, keys_part, preferred_element_type=jnp.float32
        ).reshape(summed.shape)

    def key_grad_block(carried, pieces, first_row):
        amount = pieces[0].shape[0]
        part_pos, part_doc = key_place(first_row, amount)
        part_log = lax.dynamic_slice_in_dim(all_log, first_row, amount, 0)
        part_delta = lax.dynamic_slice_in_dim(all_delta, first_row, amount, 0)
        prob_low, score_grad = pair_terms(
            pieces[0],
            pieces[1],
            part_log,
            part_delta,
            part_pos,
            part_doc,
            key_rows,
            value_rows,
            query_pos,
            query_doc,
        )
        grad_keys = carried[0] + jnp.einsum(
            "qhk,qhd->khd",
            score_grad,
            pieces[0].reshape(amount, HEADS, -1),
            preferred_element_type=jnp.float32,
        ).reshape(tok_dev, -1)
        grad_values = carried[1] + jnp.einsum(
            "qhk,qhd->khd",
            prob_low,
            pieces[1].reshape(amount, HEADS, -1),
            preferred_element_type=jnp.float32,
        ).reshape(tok_dev, -1)
        return (grad_keys, grad_values)

    zero_stats = (
        jnp.full((tok_dev, HEADS), FLOOR, jnp.float32),
        jnp.zeros((tok_dev, HEADS), jnp.float32),
    )
    zero_rows = jnp.zeros((tok_dev, att_width), jnp.float32)
    running_max, running_sum = in_blocks(
        stat_block, zero_stats, (lax.all_gather(key_rows, "ctx", axis=0, tiled=True),)
    )
    log_total = running_max + jnp.log(running_sum)
    attended = in_blocks(
        output_block,
        zero_rows,
        (
            lax.all_gather(key_rows, "ctx", axis=0, tiled=True),
            lax.all_gather(value_rows, "ctx", axis=0, tiled=True),
        ),
    )
    attended_low = attended.astype(jnp.bfloat16)
    resid = x_float + jnp.dot(attended_low, full_out, preferred_element_type=jnp.float32)
    inv_mlp = lax.rsqrt(jnp.mean(resid * resid, axis=1, keepdims=True) + EPS)
    normed_mlp = (resid * inv_mlp * mlp_gain_f).astype(jnp.bfloat16)
    up_proj = jnp.dot(normed_mlp, full_up, preferred_element_type=jnp.float32)
    act_low = jax.nn.silu(up_proj).astype(jnp.bfloat16)
    result = resid + jnp.dot(act_low, full_down, preferred_element_type=jnp.float32)
    cot_float = dealt_dy.astype(jnp.float32)
    grad_down = jnp.dot(act_low.T, dealt_dy, preferred_element_type=jnp.float32)
    act_grad = jnp.dot(dealt_dy, full_down.T, preferred_element_type=jnp.float32)
    sigma = jax.nn.sigmoid(up_proj)
    up_grad = (act_grad * sigma * (1.0 + up_proj * (1.0 - sigma))).astype(jnp.bfloat16)
    grad_up = jnp.dot(normed_mlp.T, up_grad, preferred_element_type=jnp.float32)
    norm_mlp_grad = jnp.dot(up_grad, full_up.T, preferred_element_type=jnp.float32)
    grad_mlp_gain = jnp.sum(norm_mlp_grad * resid * inv_mlp, axis=0)
    scaled_mlp = norm_mlp_grad * mlp_gain_f
    resid_grad = cot_float + inv_mlp * (
        scaled_mlp - resid * inv_mlp * inv_mlp * jnp.mean(scaled_mlp * resid, axis=1, keepdims=True)
    )
    branch_grad = resid_grad.astype(jnp.bfloat16)
    grad_out = jnp.dot(attended_low.T, branch_grad, preferred_element_type=jnp.float32)
    attended_grad = jnp.dot(branch_grad, full_out.T, preferred_element_type=jnp.float32).astype(
        jnp.bfloat16
    )
    row_delta = jnp.sum(
        (attended_grad.astype(jnp.float32) * attended).reshape(tok_dev, HEADS, -1), axis=2
    )
    query_grads = in_blocks(
        query_grad_block,
        zero_rows,
        (
            lax.all_gather(key_rows, "ctx", axis=0, tiled=True),
            lax.all_gather(value_rows, "ctx", axis=0, tiled=True),
        ),
    )
    all_log, all_delta = (
        lax.all_gather(log_total, "ctx", axis=0, tiled=True),
        lax.all_gather(row_delta, "ctx", axis=0, tiled=True),
    )
    key_grad_f, value_grad_f = in_blocks(
        key_grad_block,
        (zero_rows, zero_rows),
        (
            lax.all_gather(queries, "ctx", axis=0, tiled=True),
            lax.all_gather(attended_grad, "ctx", axis=0, tiled=True),
        ),
    )
    scale_terms = jnp.sum((query_grads * raw_query).reshape(tok_dev, -1, head_dim), axis=(0, 1))
    grad_scale = scale_terms * base_scale * jax.nn.sigmoid(scale_float)
    proj_grad = jnp.concatenate(
        [
            (query_grads * multiplier).astype(jnp.bfloat16),
            key_grad_f.astype(jnp.bfloat16),
            value_grad_f.astype(jnp.bfloat16),
        ],
        axis=1,
    )
    grad_qkv = jnp.dot(normed_attn.T, proj_grad, preferred_element_type=jnp.float32)
    norm_attn_grad = jnp.dot(proj_grad, full_qkv.T, preferred_element_type=jnp.float32)
    grad_attn_gain = jnp.sum(norm_attn_grad * x_float * inv_attn, axis=0)
    scaled_attn = norm_attn_grad * attn_gain_f
    input_grad = resid_grad + inv_attn * (
        scaled_attn
        - x_float * inv_attn * inv_attn * jnp.mean(scaled_attn * x_float, axis=1, keepdims=True)
    )
    owned = (
        lax.psum_scatter(grad_qkv, "fsdp", scatter_dimension=0, tiled=True),
        lax.psum_scatter(grad_out, "fsdp", scatter_dimension=0, tiled=True),
        lax.psum_scatter(grad_up, "fsdp", scatter_dimension=0, tiled=True),
        lax.psum_scatter(grad_down, "fsdp", scatter_dimension=0, tiled=True),
        lax.psum_scatter(grad_attn_gain, "fsdp", scatter_dimension=0, tiled=True),
        lax.psum_scatter(grad_mlp_gain, "fsdp", scatter_dimension=0, tiled=True),
        lax.psum_scatter(grad_scale, "fsdp", scatter_dimension=0, tiled=True),
    )
    summed_grads = lax.psum(
        (owned[0], owned[1], owned[2], owned[3], owned[4], owned[5], owned[6]), "ctx"
    )
    back_out, back_grad = (
        lax.all_to_all(result[arrived_slot], "ctx", split_axis=0, concat_axis=0, tiled=True),
        lax.all_to_all(input_grad[arrived_slot], "ctx", split_axis=0, concat_axis=0, tiled=True),
    )
    return (
        back_out[my_slots][None],
        back_grad[my_slots][None],
        summed_grads[0],
        summed_grads[1],
        summed_grads[2],
        summed_grads[3],
        summed_grads[4],
        summed_grads[5],
        summed_grads[6],
    )


def attend_kernel(
    ends_ref,
    x_ref,
    w_ref,
    aux_ref,
    pos_ref,
    out_w_ref,
    up_w_ref,
    down_w_ref,
    dy_ref,
    att_ref,
    normed_ref,
    qkv_ref,
    lse_ref,
    out_ref,
    auxsum_ref,
    place_ref,
    w_all,
    result_ref,
    resid_grad_ref,
    branch_ref,
    up_grad_ref,
    act_ref,
    normed_mlp_ref,
    grad_ref,
    x_all,
    w_own,
    weights,
    aux_all,
    pos_all,
    v_turned,
    key_pos,
    bias,
    att_send,
    x_send_sem,
    x_recv_sem,
    w_send_sem,
    w_recv_sem,
    aux_send_sem,
    aux_recv_sem,
    pos_sem,
    att_send_sem,
    att_recv_sem,
    m_send_sem,
    m_recv_sem,
    local_sem,
):
    at = Place()
    meet_plane(at)
    c, f = at.c, at.f
    hub = at.core == at.half

    aux_own = pltpu.make_async_copy(aux_ref, aux_all.at[f], local_sem.at[1])
    aux_own.start()
    x_own = pltpu.make_async_copy(x_ref, x_all.at[c], local_sem.at[3])

    x_far = pltpu.make_async_remote_copy(
        src_ref=x_ref,
        dst_ref=x_all.at[c],
        send_sem=x_send_sem.at[0, 0],
        recv_sem=x_recv_sem.at[c],
        device_id=dev(flip(c, 4), f),
        device_id_type=MESH,
    )

    @pl.when(hub)
    def _():
        x_own.start()
        for k, where in enumerate((dev(flip(c, 1), f), dev(flip(c, 2), f), dev(c, at.twin))):
            send(x_ref, x_all.at[c], x_send_sem.at[0, k], x_recv_sem.at[c], where)

    @pl.when(jnp.logical_not(hub))
    def _():
        x_far.start()

    w_copies, aux_copies = [], []
    for k in (2, 1, 3):
        aux_copies.append(
            send(
                aux_ref,
                aux_all.at[f],
                aux_send_sem.at[k],
                aux_recv_sem.at[f],
                dev(c, (f + k) % 4),
            )
        )

    pos = pos_ref[...]
    start = jnp.zeros_like(pos)
    end = 0
    for k in range(4):
        end = end + ends_ref[0, k]
        start = jnp.where(pos >= end, end, start)
    pos_all[at.core, 0:1, :] = pos.astype(F32)
    pos_all[at.core, 1:2, :] = start.astype(F32)
    pos_all[at.core, 2:8, :] = jnp.zeros((6, 2048), F32)
    pos_copy = send(
        pos_all.at[at.core], pos_all.at[at.core], pos_sem.at[0], pos_sem.at[1], dev(c, at.twin)
    )

    row = lax.broadcasted_iota(jnp.int32, (1280, 512), 0)
    column = lax.broadcasted_iota(jnp.int32, (1280, 512), 1)
    inside = column % LANES
    wanted = (c % 4) * 320 + column // LANES * 80 + inside
    pick = jnp.where((row == wanted) & (inside < 80), 1.0, 0.0).astype(BF)
    for j in range(3):
        some = jnp.dot(w_ref[:, j * 1280 : (j + 1) * 1280], pick, preferred_element_type=F32)
        for k in range(2):
            w_own[k, :, j * 256 : (j + 1) * 256] = some[:, k * 256 : (k + 1) * 256].astype(BF)
    mine_rows = span(f * 320, 320, 320)
    for k in (2, 3, 1):
        to = (f + k) % 4
        w_copies.append(
            send(
                w_own.at[to % 2],
                w_all.at[mine_rows],
                w_send_sem.at[k],
                w_recv_sem.at[f],
                dev(c, to),
            )
        )
    w_all[mine_rows, :] = w_own[at.core]

    shards = (out_w_ref, up_w_ref, down_w_ref)
    xbit = c % 2
    other = (f + 2) % 4

    def part(m, owner, x):
        return weights.at[m, span(owner * 320 + x * 160, 160, 160)]

    def weight_copy(m, way):
        if way == 0:
            src, dst, to = shards[m], weights.at[m, mine_rows], dev(c, at.twin)
        elif way == 1:
            src = shards[m].at[span(xbit * 160, 160, 160)]
            dst, to = part(m, f, xbit), dev(c, other)
        else:
            x = (xbit, xbit, 1 - xbit)[way - 2]
            src = dst = part(m, other, x)
            to = (dev(flip(c, 1), f), dev(c, at.twin), dev(c, at.twin))[way - 2]
        return pltpu.make_async_remote_copy(
            src_ref=src,
            dst_ref=dst,
            send_sem=m_send_sem.at[m, way],
            recv_sem=m_recv_sem.at[m, way],
            device_id=to,
            device_id_type=MESH,
        )

    def weight_first(m):
        weight_copy(m, 0).start()
        weight_copy(m, 1).start()
        weights[m, mine_rows, :] = shards[m][...]

    def weight_second(m):
        weight_copy(m, 1).wait_recv()
        weight_copy(m, 2).start()
        weight_copy(m, 3).start()

    def weight_third(m):
        weight_copy(m, 2).wait_recv()
        weight_copy(m, 4).start()

    def weight_last(m):
        for way in (0, 3, 4):
            weight_copy(m, way).wait_recv()

    weight_first(0)

    aux_own.wait()
    for k in (1, 2, 3):
        await_recv(aux_all.at[0], aux_recv_sem.at[(f + k) % 4])
    aux = jnp.zeros((16, 1280), F32)
    scale = jnp.zeros((16, LANES), F32)
    row = lax.broadcasted_iota(jnp.int32, (384, 1280), 0)
    column = lax.broadcasted_iota(jnp.int32, (384, 1280), 1)
    for k in range(4):
        put = jnp.where((column == row + k * 320) & (row < 320), 1.0, 0.0).astype(BF)
        aux = aux + jnp.dot(aux_all[k], put, preferred_element_type=F32)
        put = (column[:LANES, :LANES] == row[:LANES, :LANES] + k * 20) & (row[:LANES, :LANES] < 20)
        put = jnp.where(put, 1.0, 0.0).astype(BF)
        scale = scale + jnp.dot(aux_all[k, :, :LANES], put, preferred_element_type=F32)
    auxsum_ref[...] = aux
    auxsum_ref[2:3, :LANES] = scale[2:3]
    gain = aux[0:1, :]
    mlp_gain = aux[1:2, :]
    scale = scale[2:3]
    real = lax.broadcasted_iota(jnp.int32, (1, LANES), 1) < 80
    mult = jnp.where(
        real, LOG2E / math.sqrt(80) * (jnp.maximum(scale, 0.0) + jnp.log1p(jnp.exp(-jnp.abs(scale)))), 0.0
    )
    one = jnp.ones_like(mult)
    mults = jnp.concatenate([mult, mult, one, one, one, one], axis=1)

    await_recv(pos_all.at[0], pos_sem.at[1])
    place_ref[...] = pos_all[at.half]
    for k in range(8):
        block = place_ref[0:1, k * 256 : (k + 1) * 256]
        key_pos[k * 256 : (k + 1) * 256, :] = jnp.transpose(
            jnp.broadcast_to(block, (256, 256))
        )

    def arrive(step, carry):
        slot = flip(c, step)

        @pl.when(jnp.logical_and(hub, step == 0))
        def _():
            x_own.wait()

        @pl.when(jnp.logical_not(jnp.logical_and(hub, step == 0)))
        def _():
            await_recv(x_all.at[slot], x_recv_sem.at[slot])

        def onward(way, where):
            send(
                x_all.at[slot],
                x_all.at[slot],
                x_send_sem.at[step, way],
                x_recv_sem.at[slot],
                where,
            )

        @pl.when(jnp.logical_and(hub, jnp.logical_or(step == 4, step == 6)))
        def _():
            onward(0, dev(flip(c, 1), f))

        @pl.when(jnp.logical_and(hub, jnp.logical_or(step == 4, step == 1)))
        def _():
            onward(1, dev(flip(c, 2), f))

        @pl.when(jnp.logical_and(hub, step > 0))
        def _():
            onward(2, dev(c, at.twin))

        xf = x_all[slot].astype(F32)
        inv = lax.rsqrt(jnp.mean(xf * xf, axis=1, keepdims=True) + EPS)
        normed_ref[span(slot * 256, 256, 256), :] = (xf * inv * gain).astype(BF)
        return carry

    def project(step, carry):
        slot = flip(c, step)
        rows = span(slot * 256, 256, 256)
        proj = jnp.dot(normed_ref[rows, :], w_all[...], preferred_element_type=F32)
        qkv_ref[rows, :] = (proj * mults).astype(BF)
        return carry

    lax.fori_loop(0, 7, arrive, 0)
    for k in (1, 2, 3):
        await_recv(w_all.at[pl.ds(0, 320)], w_recv_sem.at[(f + k) % 4])
    weight_first(1)
    weight_first(2)
    weight_second(0)
    lax.fori_loop(0, 5, project, 0)
    lax.fori_loop(7, 8, arrive, 0)
    lax.fori_loop(5, 8, project, 0)

    for h in range(2):
        v_turned[h] = jnp.transpose(qkv_ref[:, (4 + h) * LANES : (5 + h) * LANES])

    att_own = pltpu.make_async_copy(
        att_send.at[c], att_ref.at[span(at.group * 160, 160, 160)], local_sem.at[3]
    )

    def att_copy(block):
        return pltpu.make_async_remote_copy(
            src_ref=att_send.at[block],
            dst_ref=att_ref.at[span(at.group * 160, 160, 160)],
            send_sem=att_send_sem.at[block],
            recv_sem=att_recv_sem.at[at.group],
            device_id=dev(block, at.pack),
            device_id_type=MESH,
        )

    mine = at.core == at.half

    def attend(step, carry):
        block = flip(c, step)
        lanes = span(block * 256, 256, 256)
        high = place_ref[0:1, lanes]
        least = place_ref[1:2, lanes]
        kp = key_pos[...]
        bias[...] = jnp.where((kp >= least) & (kp <= high), 0.0, FLOOR)
        for h in range(2):
            keys = qkv_ref[:, (2 + h) * LANES : (3 + h) * LANES]
            query = qkv_ref[lanes, h * LANES : (h + 1) * LANES]
            s = lax.dot_general(
                keys, query, (((1,), (1,)), ((), ())), preferred_element_type=F32
            )
            s = s + bias[...]
            top = jnp.max(s, axis=0, keepdims=True)
            p = jnp.exp(s - top)
            total = jnp.sum(p, axis=0, keepdims=True)
            o = jnp.dot(v_turned[h], p.astype(BF), preferred_element_type=F32)
            o = o[:80] / total
            lse_ref[h : h + 1, lanes] = top + jnp.log(total)
            out_ref[h * 80 : (h + 1) * 80, lanes] = o.astype(BF)
            att_send[block, h * 80 : (h + 1) * 80, :] = o.astype(BF)

        @pl.when(jnp.logical_and(mine, step == 0))
        def _():
            att_own.start()

        @pl.when(jnp.logical_not(jnp.logical_and(mine, step == 0)))
        def _():
            att_copy(block).start()

        for when, todo in ((1, weight_third), (4, weight_second), (6, weight_second), (7, weight_third)):
            m = {(1, weight_third): 0, (4, weight_second): 1, (6, weight_second): 2}.get((when, todo), 1)

            @pl.when(step == when)
            def _(todo=todo, m=m):
                todo(m)

        return carry

    lax.fori_loop(0, 8, attend, 0)
    lse_ref[2:8, :] = jnp.zeros((6, 2048), F32)

    def land(block, carry):
        @pl.when(jnp.logical_not(jnp.logical_and(mine, block == at.group)))
        def _():
            await_recv(att_ref.at[pl.ds(0, 160)], att_recv_sem.at[block])

        return carry

    @pl.when(mine)
    def _():
        att_own.wait()

    weight_last(0)
    lax.fori_loop(0, 8, land, 0)

    def across(left, right):
        return lax.dot_general(
            left, right, (((1,), (1,)), ((), ())), preferred_element_type=F32
        )

    xf = x_ref[...].astype(F32)
    resid = xf + jnp.dot(jnp.transpose(att_ref[...]), weights[0], preferred_element_type=F32)
    inv = lax.rsqrt(jnp.mean(resid * resid, axis=1, keepdims=True) + EPS)
    normed_mlp = (resid * inv * mlp_gain).astype(BF)
    normed_mlp_ref[...] = jnp.transpose(normed_mlp)
    weight_third(2)
    weight_last(1)
    up = jnp.dot(normed_mlp, weights[1], preferred_element_type=F32)
    sigma = 1.0 / (1.0 + jnp.exp(-up))
    act = (up * sigma).astype(BF)
    act_ref[...] = jnp.transpose(act)
    slope = sigma * (1.0 + up * (1.0 - sigma))
    weight_last(2)
    dy = dy_ref[...]
    up_grad = (across(dy, weights[2]) * slope).astype(BF)
    up_grad_ref[...] = up_grad
    scaled = across(up_grad, weights[1]) * mlp_gain
    resid_grad = dy.astype(F32) + inv * (
        scaled - resid * inv * inv * jnp.mean(scaled * resid, axis=1, keepdims=True)
    )
    resid_grad_ref[...] = resid_grad
    branch = resid_grad.astype(BF)
    branch_ref[...] = branch
    grad_ref[...] = across(weights[0], branch).astype(BF)
    result_ref[...] = resid + jnp.dot(act, weights[2], preferred_element_type=F32)

    for copy in w_copies + aux_copies:
        copy.wait_send()
    pos_copy.wait_send()
    for m in range(3):
        for way in range(5):
            weight_copy(m, way).wait_send()

    @pl.when(hub)
    def _():
        for k in range(3):
            await_recv(x_ref, x_send_sem.at[0, k])
        for step in range(1, 8):
            ways = {1: (1, 2), 4: (0, 1, 2), 6: (0, 2)}.get(step, (2,))
            for way in ways:
                await_recv(x_ref, x_send_sem.at[step, way])

    @pl.when(jnp.logical_not(hub))
    def _():
        x_far.wait_send()

    def finish(block, carry):
        @pl.when(jnp.logical_not(jnp.logical_and(mine, block == c)))
        def _():
            att_copy(block).wait_send()

        return carry

    lax.fori_loop(0, 8, finish, 0)


def forward(*args):
    shape = jax.ShapeDtypeStruct
    dma = pltpu.SemaphoreType.DMA
    return pl.pallas_call(
        attend_kernel,
        name="forward",
        out_shape=(
            shape((1280, 256), BF),
            shape((2048, 1280), BF),
            shape((2048, 768), BF),
            shape((8, 2048), F32),
            shape((160, 2048), BF),
            shape((16, 1280), F32),
            shape((8, 2048), F32),
            shape((1280, 768), BF),
            shape((256, 1280), F32),
            shape((256, 1280), F32),
            shape((256, 1280), BF),
            shape((256, 1280), BF),
            shape((1280, 256), BF),
            shape((1280, 256), BF),
            shape((1280, 256), BF),
        ),
        in_specs=[pl.BlockSpec(memory_space=pltpu.SMEM)] + [VMEM_SPEC] * 8,
        out_specs=(VMEM_SPEC,) * 15,
        scratch_shapes=[
            pltpu.VMEM((8, 256, 1280), BF),
            pltpu.VMEM((2, 320, 768), BF),
            pltpu.VMEM((3, 1280, 1280), BF),
            pltpu.VMEM((4, 16, 384), BF),
            pltpu.VMEM((2, 8, 2048), F32),
            pltpu.VMEM((2, 128, 2048), BF),
            pltpu.VMEM((2048, 256), F32),
            pltpu.VMEM((2048, 256), F32),
            pltpu.VMEM((8, 160, 256), BF),
            dma((8, 3)),
            dma((8,)),
            dma((4,)),
            dma((4,)),
            dma((4,)),
            dma((4,)),
            dma((2,)),
            dma((8,)),
            dma((8,)),
            dma((3, 5)),
            dma((3, 5)),
            dma((4,)),
        ],
        compiler_params=pltpu.CompilerParams(
            collective_id=0, has_side_effects=True, vmem_limit_bytes=VMEM_LIMIT
        ),
        cost_estimate=pl.CostEstimate(
            flops=20_000_000_000, bytes_accessed=40_000_000, transcendentals=8_400_000
        ),
    )(*args)


def add_into(target, source, rows, step):
    def one(k, carry):
        part = span(k * step, step, step)
        target[part, :] = (target[part, :].astype(F32) + source[part, :].astype(F32)).astype(BF)
        return carry

    lax.fori_loop(0, rows // step, one, 0)


KEY_PARTS = 2
KEY_ROWS = 2048 // KEY_PARTS


def backward_kernel(
    grad_ref,
    att_ref,
    branch_ref,
    normed_mlp_ref,
    up_grad_ref,
    act_ref,
    dy_ref,
    qkv_ref,
    lse_ref,
    out_ref,
    place_ref,
    normed_hbm,
    w_ref,
    mult_ref,
    x_ref,
    resid_grad_ref,
    gain_ref,
    first_out,
    second_out,
    third_out,
    slice_out,
    input_grad_ref,
    scale_ref,
    grad_all,
    key_pos,
    k_turned,
    delta,
    key_sum,
    value_sum,
    turned,
    normed_part,
    n_core,
    n_x,
    n_z,
    n_last,
    sums,
    a0,
    a1,
    a2,
    a3,
    a4,
    slices,
    s1,
    s2,
    gathered,
    strip,
    scale_in,
    g_send_sem,
    g_recv_sem,
    local_sem,
    m_send,
    m_recv,
    q_send,
    q_recv,
    nc_send,
    nc_recv,
    n_send,
    n_recv,
    v_send,
    v_recv,
):
    at = Place()
    meet_plane(at)
    c, f, core, half = at.c, at.f, at.core, at.half
    mine = core == half
    row = f // 2
    xbit, zbit = c % 2, (c // 2) % 2
    twin, across = dev(c, at.twin), dev(c, at.across)
    xpeer, zpeer, hpeer = dev(flip(c, 1), f), dev(flip(c, 2), f), dev(flip(c, 4), f)

    def remote(src, dst, send_sem, recv_sem, where):
        return pltpu.make_async_remote_copy(
            src_ref=src,
            dst_ref=dst,
            send_sem=send_sem,
            recv_sem=recv_sem,
            device_id=where,
            device_id_type=MESH,
        )

    def grad_copy(group, h):
        return remote(
            grad_ref.at[span(group * 160 + h * 80, 80, 80)],
            grad_all.at[h, pl.ds(0, 80), span(c * 256, 256, 256)],
            g_send_sem.at[group, h],
            g_recv_sem.at[c, h],
            dev(core * 4 + group // 2, at.plane + group % 2),
        )

    def grad_own(h):
        return pltpu.make_async_copy(
            grad_ref.at[span(at.group * 160 + h * 80, 80, 80)],
            grad_all.at[h, pl.ds(0, 80), span(c * 256, 256, 256)],
            local_sem.at[h],
        )

    def give(k, carry):
        group = flip(at.group, k)

        @pl.when(jnp.logical_and(mine, k == 0))
        def _():
            grad_own(0).start()
            grad_own(1).start()

        @pl.when(jnp.logical_not(jnp.logical_and(mine, k == 0)))
        def _():
            grad_copy(group, 0).start()
            grad_copy(group, 1).start()

        return carry

    lax.fori_loop(0, 8, give, 0)

    side, other = span(half * 640, 640, 640), span(640 - half * 640, 640, 640)
    quarter = xbit * 160 + zbit * 80
    results = (first_out, second_out, third_out)

    def main_copy(stage, m):
        if stage < 2:
            rows = pl.ds((m * 2 + stage) * 320, 320)
            ends = sums.at[rows], a0.at[m, stage], twin
        elif stage == 2:
            ends = a0.at[m, 1 - row], a1.at[m], across
        elif stage == 3:
            ends = a1.at[m, span(160 - xbit * 160, 160, 160)], a2.at[m], xpeer
        elif stage == 4:
            ends = a2.at[m, span(80 - zbit * 80, 80, 80)], a3.at[m], zpeer
        elif stage == 5:
            ends = a3.at[m, :, other], a4.at[m], hpeer
        else:
            if stage == 6:
                piece, to = results[m].at[span(quarter, 80, 80), side], hpeer
            elif stage == 7:
                piece, to = results[m].at[span(quarter, 80, 80)], zpeer
            else:
                piece, to = results[m].at[span(xbit * 160, 160, 160)], xpeer
            ends = piece, piece, to
        return remote(ends[0], ends[1], m_send.at[stage, m], m_recv.at[stage, m], ends[2])

    def main(stage, m):
        if stage == 0:
            main_copy(0, m).start()
            main_copy(1, m).start()
            return
        if stage == 1:
            for y in range(2):
                main_copy(y, m).wait_recv()
                a0[m, y] = (a0[m, y].astype(F32) + weight_rows(m, 2 * y + core)).astype(BF)
            return
        if stage > 2:
            main_copy(stage - 1, m).wait_recv()
        if stage == 3:
            add_into(a1.at[m], a0.at[m, row], 320, 80)
        if stage == 4:
            add_into(a2.at[m], a1.at[m, span(xbit * 160, 160, 160)], 160, 80)
        if stage == 5:
            add_into(a3.at[m], a2.at[m, span(zbit * 80, 80, 80)], 80, 80)
        if stage == 6:
            results[m][span(quarter, 80, 80), side] = (
                a4[m].astype(F32) + a3[m, :, side].astype(F32)
            ).astype(BF)
        if stage < 9:
            main_copy(stage, m).start()

    lefts = (act_ref, normed_mlp_ref, att_ref)
    rights = (dy_ref, up_grad_ref, branch_ref)

    def weight_rows(m, quarter):
        rows = span(quarter * 320, 320, 320)
        return jnp.dot(lefts[m][rows, :], rights[m][...], preferred_element_type=F32)

    for m in range(3):
        for y in range(2):
            part = weight_rows(m, 2 * y + 1 - core)
            sums[(m * 2 + y) * 320 : (m * 2 + y + 1) * 320, :] = part.astype(BF)
        main(0, m)
    main(1, 0)
    main(2, 0)

    for h in range(2):
        grad_all[h, 80:, :] = jnp.zeros((48, 2048), BF)
        k_turned[h] = jnp.transpose(qkv_ref[:, (2 + h) * LANES : (3 + h) * LANES])
    for k in range(8):
        block = place_ref[0:1, k * 256 : (k + 1) * 256]
        key_pos[k * 256 : (k + 1) * 256, :] = jnp.transpose(
            jnp.broadcast_to(block, (LANES, 256))
        )
    scale_ref[...] = jnp.zeros((8, LANES), F32)
    main(1, 1)

    def take(k, carry):
        block = flip(c, k)

        @pl.when(jnp.logical_and(mine, k == 0))
        def _():
            grad_own(0).wait()
            grad_own(1).wait()

        @pl.when(jnp.logical_not(jnp.logical_and(mine, k == 0)))
        def _():
            for h in range(2):
                await_recv(
                    grad_all.at[h, pl.ds(0, 80), pl.ds(0, 256)], g_recv_sem.at[block, h]
                )

        return carry

    lax.fori_loop(0, 8, take, 0)
    main(1, 2)
    for h in range(2):
        delta[h : h + 1, :] = jnp.sum(
            grad_all[h, :80, :].astype(F32) * out_ref[h * 80 : (h + 1) * 80, :].astype(F32),
            axis=0,
            keepdims=True,
        )

    place4 = zbit + 2 * xbit

    def head_copy(stage, h):
        if stage == 0:
            ends = slices.at[h, :, span((1 - row) * 640, 640, 640)], s1.at[h], across
        elif stage == 1:
            ends = s1.at[h, span(128 - half * 128, 128, 128)], s2.at[h], hpeer
        else:
            if stage == 2:
                piece, to = gathered.at[core, place4, h, span(half * 128, 128, 128)], hpeer
            elif stage == 3:
                piece, to = gathered.at[core, place4, h], zpeer
            elif stage == 4:
                piece, to = gathered.at[core, pl.ds(2 * xbit, 2), h], xpeer
            else:
                piece, to = gathered.at[core, :, h], twin
            ends = piece, piece, to
        return remote(ends[0], ends[1], q_send.at[stage, h], q_recv.at[stage, h], ends[2])

    def head(stage, h):
        if stage > 0:
            head_copy(stage - 1, h).wait_recv()
        if stage == 1:
            add_into(s1.at[h], slices.at[h, :, span(row * 640, 640, 640)], 256, 128)
        if stage == 2:
            own = span(half * 128, 128, 128)
            gathered[core, place4, h, own, :] = (
                s2[h].astype(F32) + s1[h, own, :].astype(F32)
            ).astype(BF)
        if stage < 6:
            head_copy(stage, h).start()

    hooks = {
        (0, 4): (lambda: main(2, 1),),
        (0, 6): (lambda: main(3, 0),),
        (1, 0): (lambda: main(4, 0),),
        (1, 1): (lambda: main(5, 0),),
        (1, 2): (lambda: main(6, 0), lambda: main(2, 2)),
        (1, 3): (lambda: main(7, 0),),
        (1, 4): (lambda: main(8, 0), lambda: main(3, 1)),
        (1, 5): (lambda: head(1, 0), lambda: main(4, 1)),
        (1, 6): (lambda: head(2, 0), lambda: main(5, 1)),
        (1, 7): (lambda: head(3, 0), lambda: main(6, 1)),
    }

    def normed_load(part):
        return pltpu.make_async_copy(
            normed_hbm.at[:, pl.ds(part * 256, 256)], normed_part.at[part % 2], local_sem.at[2 + part % 2]
        )

    normed_load(0).start()
    for h in range(2):
        key_sum[...] = jnp.zeros((2048, LANES), F32)
        value_sum[...] = jnp.zeros((2048, LANES), F32)

        def block_grad(block, carry, h=h):
            lanes = span(block * 256, 256, 256)
            high = place_ref[0:1, lanes]
            least = place_ref[1:2, lanes]
            query = qkv_ref[lanes, h * LANES : (h + 1) * LANES]
            grad_t = grad_all[h, :, lanes]
            q_grad = jnp.zeros((LANES, 256), F32)
            for part in range(KEY_PARTS):
                some = slice(part * KEY_ROWS, (part + 1) * KEY_ROWS)
                kp = key_pos[some, :]
                kp = jnp.concatenate([kp, kp], axis=1)
                keys = qkv_ref[some, (2 + h) * LANES : (3 + h) * LANES]
                values = qkv_ref[some, (4 + h) * LANES : (5 + h) * LANES]
                s = lax.dot_general(
                    keys, query, (((1,), (1,)), ((), ())), preferred_element_type=F32
                )
                visible = (kp >= least) & (kp <= high)
                p = jnp.exp(jnp.where(visible, s - lse_ref[h : h + 1, lanes], FLOOR))
                gp = jnp.dot(values, grad_t, preferred_element_type=F32)
                gs = (p * (gp - delta[h : h + 1, lanes])).astype(BF)
                value_sum[some, :] += lax.dot_general(
                    p.astype(BF), grad_t, (((1,), (1,)), ((), ())), preferred_element_type=F32
                )
                key_sum[some, :] += jnp.dot(gs, query, preferred_element_type=F32)
                q_grad += jnp.dot(k_turned[h, :, some], gs, preferred_element_type=F32)
            scale_ref[0:1, :] += jnp.sum(
                jnp.transpose(q_grad) * query.astype(F32), axis=0, keepdims=True
            )
            turned[h * LANES : (h + 1) * LANES, lanes] = (q_grad * mult_ref[:, 0:1]).astype(BF)
            for (hh, step), todo in hooks.items():
                if hh == h:

                    @pl.when(block == step)
                    def _(todo=todo):
                        for one in todo:
                            one()

            return carry

        lax.fori_loop(0, 8, block_grad, 0)
        for j, total in ((1, key_sum), (2, value_sum)):
            low = jnp.transpose(total[...]).astype(BF)
            turned[(2 * j + h) * LANES : (2 * j + h + 1) * LANES, :] = low
        slices[h, 240:, :] = jnp.zeros((16, 1280), BF)
        for part in range(5):
            normed_load(part).wait()
            if part + 1 < 5:
                normed_load(part + 1).start()
            for j in range(3):
                first = (2 * j + h) * LANES
                slices[h, j * 80 : (j + 1) * 80, part * 256 : (part + 1) * 256] = jnp.dot(
                    turned[first : first + 80, :],
                    normed_part[part % 2],
                    preferred_element_type=F32,
                ).astype(BF)
        if h == 0:
            normed_load(0).start()
        head(0, h)

    def norm_bits(k):
        return (1 - xbit, 1 - xbit, xbit, xbit)[k], (1 - zbit, zbit, 1 - zbit, zbit)[k]

    def norm_spot(k, hh):
        slot = 2 * k + hh
        return sums.at[pl.ds(slot // 5 * 640, 640), pl.ds(slot % 5 * 256, 256)]

    def norm_copy(stage, k, hh=0):
        if stage == 0:
            return remote(
                norm_spot(k, hh), n_core.at[k, hh], nc_send.at[k, hh], nc_recv.at[k, hh], twin
            )
        took = k
        if stage == 1:
            ends = n_core.at[k], n_x.at[k], xpeer
        elif stage == 2:
            ends = n_core.at[2, (1 - half, half)[k]], n_z.at[k], zpeer
        else:
            to = dev(flip(c, 4), at.pack) if k == 0 else dev(c, at.twin)
            took = (core, 2)[k]
            ends = n_core.at[3, (1 - half, half)[k]], n_last.at[core], to
        return remote(ends[0], ends[1], n_send.at[stage, k], n_recv.at[stage, took], ends[2])

    def norm_part(k, hh, which):
        xs, zs = norm_bits(k)
        lanes = span((hh * 4 + zs * 2 + xs) * 256, 256, 256)
        rows = span(which * 640, 640, 640)
        return jnp.dot(w_ref[rows, :], turned[:, lanes], preferred_element_type=F32)

    for m in range(3):
        for stage in range(2):
            main_copy(stage, m).wait_send()
    for k in range(4):
        for hh in range(2):
            norm_spot(k, hh)[...] = norm_part(k, hh, 1 - core).astype(BF)
            norm_copy(0, k, hh).start()

    def norm_core(k):
        for hh in range(2):
            norm_copy(0, k, hh).wait_recv()
            n_core[k, hh] = (n_core[k, hh].astype(F32) + norm_part(k, hh, core)).astype(BF)

    for k in range(2):
        norm_core(k)
        norm_copy(1, k).start()
    head(1, 1)
    norm_core(2)
    norm_core(3)

    def scale_copy(stage):
        where = (twin, across, xpeer, zpeer, hpeer)[stage]
        return remote(scale_ref, scale_in.at[stage], v_send.at[stage], v_recv.at[stage], where)

    def tiny(stage):
        if stage > 0:
            scale_copy(stage - 1).wait()
            scale_ref[...] += scale_in[stage - 1]
        if stage < 5:
            scale_copy(stage).start()

    tiny(0)
    main(7, 1)
    head(4, 0)
    main(3, 2)
    head(2, 1)
    tiny(1)
    main(8, 1)
    head(5, 0)
    main(4, 2)
    norm_copy(1, 0).wait_recv()
    for hh in range(2):
        add_into(n_core.at[2, hh], n_x.at[0, hh], 640, 80)
    norm_copy(2, 0).start()
    norm_copy(2, 1).start()
    tiny(2)
    head(3, 1)
    main(5, 2)
    norm_copy(1, 1).wait_recv()
    for hh in range(2):
        add_into(n_core.at[3, hh], n_x.at[1, hh], 640, 80)
    tiny(3)
    main(6, 2)
    norm_copy(2, 0).wait_recv()
    add_into(n_core.at[3, 1 - half], n_z.at[0], 640, 80)
    norm_copy(3, 0).start()
    norm_copy(2, 1).wait_recv()
    add_into(n_core.at[3, half], n_z.at[1], 640, 80)

    @pl.when(jnp.logical_not(mine))
    def _():
        norm_copy(3, 1).start()

    tiny(4)
    main(7, 2)
    head(4, 1)
    main(8, 2)
    tiny(5)

    @pl.when(mine)
    def _():
        n_last[core] = n_core[3, half]
        await_recv(n_last.at[0], n_recv.at[3, 2])

    @pl.when(jnp.logical_not(mine))
    def _():
        await_recv(n_last.at[0], n_recv.at[3, 0])
        await_recv(n_last.at[1], n_recv.at[3, 1])

    xf = x_ref[...].astype(F32)
    inv = lax.rsqrt(jnp.mean(xf * xf, axis=1, keepdims=True) + EPS)
    scaled = jnp.concatenate(
        [jnp.transpose(n_last[k].astype(F32)) for k in range(2)], axis=1
    ) * gain_ref[0:1, :]
    input_grad_ref[...] = resid_grad_ref[...] + inv * (
        scaled - xf * inv * inv * jnp.mean(scaled * xf, axis=1, keepdims=True)
    )
    for m in range(3):
        main(9, m)
    head(6, 0)
    head(5, 1)
    head(6, 1)
    for k in range(4):
        for hh in range(2):
            norm_copy(0, k, hh).wait_send()
    for core_k in range(2):
        for m4 in range(4):
            group = 2 * (2 * (m4 % 2) + m4 // 2) + core_k
            for h in range(2):
                for j in range(3):
                    start = j * 1280 + (group * 2 + h) * 80
                    sums[
                        start % 1920 : start % 1920 + 80, start // 1920 * 640 : start // 1920 * 640 + 640
                    ] = gathered[core_k, m4, h, j * 80 : (j + 1) * 80, :]

    for part in range(2):

        def turn(k, carry, part=part):
            strip[...] = jnp.transpose(sums[span(k * LANES, LANES, LANES), part * 640 : part * 640 + 640])
            slice_out[:, span(part * 1920 + k * LANES, LANES, LANES)] = strip[span(core * 320, 320, 320), :]
            return carry

        lax.fori_loop(0, 15, turn, 0)

    def sent(block, carry):
        own_in = jnp.logical_and(mine, block == at.group)

        @pl.when(jnp.logical_not(own_in))
        def _():
            for h in range(2):
                grad_copy(block, h).wait_send()

        return carry

    lax.fori_loop(0, 8, sent, 0)
    for m in range(3):
        for stage in range(2, 9):
            main_copy(stage, m).wait_send()
    for h in range(2):
        for stage in range(6):
            head_copy(stage, h).wait_send()
    for k in range(2):
        norm_copy(1, k).wait_send()
        norm_copy(2, k).wait_send()
    norm_copy(3, 0).wait_send()

    @pl.when(jnp.logical_not(mine))
    def _():
        norm_copy(3, 1).wait_send()


def backward(*args):
    shape = jax.ShapeDtypeStruct
    dma = pltpu.SemaphoreType.DMA
    specs = [VMEM_SPEC] * 17
    specs[11] = pl.BlockSpec(memory_space=pl.ANY)
    return pl.pallas_call(
        backward_kernel,
        name="backward",
        out_shape=(
            shape((320, 1280), BF),
            shape((320, 1280), BF),
            shape((320, 1280), BF),
            shape((320, 3840), BF),
            shape((256, 1280), F32),
            shape((8, LANES), F32),
        ),
        in_specs=specs,
        out_specs=(VMEM_SPEC,) * 6,
        scratch_shapes=[
            pltpu.VMEM((2, 128, 2048), BF),
            pltpu.VMEM((2048, LANES), F32),
            pltpu.VMEM((2, 128, 2048), BF),
            pltpu.VMEM((8, 2048), F32),
            pltpu.VMEM((2048, LANES), F32),
            pltpu.VMEM((2048, LANES), F32),
            pltpu.VMEM((768, 2048), BF),
            pltpu.VMEM((2, 2048, 256), BF),
            pltpu.VMEM((4, 2, 640, 256), BF),
            pltpu.VMEM((2, 2, 640, 256), BF),
            pltpu.VMEM((2, 640, 256), BF),
            pltpu.VMEM((2, 640, 256), BF),
            pltpu.VMEM((1920, 1280), BF),
            pltpu.VMEM((3, 2, 320, 1280), BF),
            pltpu.VMEM((3, 320, 1280), BF),
            pltpu.VMEM((3, 160, 1280), BF),
            pltpu.VMEM((3, 80, 1280), BF),
            pltpu.VMEM((3, 80, 640), BF),
            pltpu.VMEM((2, 256, 1280), BF),
            pltpu.VMEM((2, 256, 640), BF),
            pltpu.VMEM((2, 128, 640), BF),
            pltpu.VMEM((2, 4, 2, 256, 640), BF),
            pltpu.VMEM((640, LANES), BF),
            pltpu.VMEM((5, 8, LANES), F32),
            dma((8, 2)),
            dma((8, 2)),
            dma((4,)),
            dma((9, 3)),
            dma((9, 3)),
            dma((6, 2)),
            dma((6, 2)),
            dma((4, 2)),
            dma((4, 2)),
            dma((4, 4)),
            dma((4, 4)),
            dma((5,)),
            dma((5,)),
        ],
        compiler_params=pltpu.CompilerParams(
            collective_id=1, has_side_effects=True, vmem_limit_bytes=VMEM_LIMIT
        ),
        cost_estimate=pl.CostEstimate(
            flops=30_000_000_000, bytes_accessed=60_000_000, transcendentals=8_400_000
        ),
    )(*args)


def fast_body(
    tokens,
    lengths,
    position,
    qkv_weight,
    out_weight,
    up_weight,
    down_weight,
    attn_gain,
    mlp_gain,
    query_scale,
    cotangent,
):
    f = lax.axis_index("fsdp")
    x, dy = tokens[0], cotangent[0]
    small = [jnp.pad(a, (0, 384 - a.shape[0])) for a in (attn_gain, mlp_gain, query_scale)]
    small = jnp.stack(small + [jnp.zeros((384,), BF)] * 13)
    (
        att_t, normed, qkv, lse, out, auxsum, place, w_heads,
        result, resid_grad, branch_grad, up_grad, act_t, normed_mlp_t, grad_t,
    ) = forward(
        lengths, x, qkv_weight, small, position, out_weight, up_weight, down_weight, dy
    )
    scale_float = auxsum[2, :80]
    base_scale = LOG2E / math.sqrt(80)
    soft = jax.nn.softplus(scale_float)
    mult = jnp.broadcast_to(jnp.pad(base_scale * soft, (0, 48))[:, None], (LANES, LANES))
    g_down, g_up, g_out, g_qkv, input_grad, scale_sum = backward(
        grad_t,
        att_t,
        branch_grad,
        normed_mlp_t,
        up_grad,
        act_t,
        dy,
        qkv,
        lse,
        out,
        place,
        normed,
        w_heads,
        mult,
        x,
        resid_grad,
        auxsum,
    )
    g_down, g_up, g_out, g_qkv = (g.astype(F32) for g in (g_down, g_up, g_out, g_qkv))
    grad_attn_gain = jnp.sum(qkv_weight.astype(F32) * g_qkv, axis=1) / attn_gain.astype(F32)
    grad_mlp_gain = jnp.sum(up_weight.astype(F32) * g_up, axis=1) / mlp_gain.astype(F32)
    grad_scale = scale_sum[0, :80] / soft * jax.nn.sigmoid(scale_float)
    return (
        result[None],
        input_grad[None],
        g_qkv,
        g_out,
        g_up,
        g_down,
        grad_attn_gain,
        grad_mlp_gain,
        lax.dynamic_slice_in_dim(grad_scale, f * 20, 20),
    )


def solution(mesh):
    placed = (
        P("fsdp", "ctx", None),
        P("fsdp", None),
        P("fsdp", None),
        P("fsdp", None),
        P("fsdp", None),
        P("fsdp", None),
        P("fsdp", None),
        P("fsdp"),
        P("fsdp"),
        P("fsdp"),
        P("fsdp", "ctx", None),
    )
    fits = mesh.shape["ctx"] == 8 and mesh.shape["fsdp"] == 4
    return jax.shard_map(
        fast_body if fits else body,
        mesh=mesh,
        in_specs=placed,
        out_specs=(
            P("fsdp", "ctx", None),
            P("fsdp", "ctx", None),
            P("fsdp", None),
            P("fsdp", None),
            P("fsdp", None),
            P("fsdp", None),
            P("fsdp"),
            P("fsdp"),
            P("fsdp"),
        ),
        check_vma=False,
    )
```

```python
import functools
import math

import jax
import jax.numpy as jnp
from jax import lax
from jax.experimental import pallas as pl
from jax.experimental.pallas import tpu as pltpu
from jax.sharding import PartitionSpec as P

HEADS = 16


EPS = 1e-06
FLOOR = -1e30
LOG2E = 1.442695041

MESH = pl.DeviceIdType.MESH
LANES = 128
BF = jnp.bfloat16
F32 = jnp.float32
VMEM_SPEC = pl.BlockSpec(memory_space=pltpu.VMEM)
VMEM_LIMIT = 60 << 20


def flip(number, mask):
    total = 0
    for bit in (1, 2, 4):
        left = (number // bit) % 2
        right = (mask // bit) % 2
        total = total + bit * (left + right - 2 * left * right)
    return total


class Place:
    def __init__(self):
        self.c = lax.axis_index("ctx")
        self.f = lax.axis_index("fsdp")
        self.core = self.f % 2
        self.plane = self.f - self.core
        self.half = self.c // 4
        self.pack = self.plane + self.half
        self.group = (self.c % 4) * 2 + self.core
        self.twin = self.plane + 1 - self.core
        self.across = (self.f + 2) % 4


def dev(ctx, fsdp):
    return {"ctx": ctx, "fsdp": fsdp}


def send(src, dst, send_sem, recv_sem, device):
    copy = pltpu.make_async_remote_copy(
        src_ref=src,
        dst_ref=dst,
        send_sem=send_sem,
        recv_sem=recv_sem,
        device_id=device,
        device_id_type=MESH,
    )
    copy.start()
    return copy


def await_recv(ref, sem):
    pltpu.make_async_copy(ref, ref, sem).wait()


def meet_plane(at):
    barrier = pltpu.get_barrier_semaphore()

    def greet(k, carry):
        pl.semaphore_signal(
            barrier,
            1,
            device_id=dev((at.c + k // 2) % 8, at.plane + (at.core + k) % 2),
            device_id_type=MESH,
        )
        return carry

    lax.fori_loop(1, 16, greet, 0)
    for k in range(2):
        pl.semaphore_signal(
            barrier, 1, device_id=dev(at.c, (at.plane + 2) % 4 + k), device_id_type=MESH
        )
    pl.semaphore_wait(barrier, 17)


def span(start, size, unit):
    return pl.ds(pl.multiple_of(start, unit), size)


def doc_index(places, seq_ends):
    return jnp.sum((places[:, None] >= seq_ends[None, :]).astype(jnp.int32), axis=1)


def spread_position(gathered_index, tok_dev, cycle_size):
    return gathered_index % tok_dev * cycle_size + gathered_index // tok_dev


def pair_scores(left_rows, right_rows):
    return jnp.einsum(
        "qhd,khd->qhk",
        left_rows.reshape(left_rows.shape[0], HEADS, -1),
        right_rows.reshape(right_rows.shape[0], HEADS, -1),
        preferred_element_type=jnp.float32,
    )


def pair_mask(query_pos, query_doc, key_pos, key_doc):
    return ((query_doc[:, None] == key_doc[None, :]) & (key_pos[None, :] <= query_pos[:, None]))[
        :, None, :
    ]


def in_blocks(advance, carried, pieces):
    total_rows = pieces[0].shape[0]
    block_rows = math.gcd(total_rows, 1024)
    block_count = total_rows // block_rows
    split = tuple((p.reshape((block_count, block_rows) + p.shape[1:]) for p in pieces))

    def inner(running, entry):
        return (advance(running, entry[1], entry[0] * block_rows), None)

    result, unused = lax.scan(inner, carried, (jnp.arange(block_count, dtype=jnp.int32), split))
    return result


def pair_terms(
    query_part,
    grad_part,
    log_part,
    delta_part,
    query_pos,
    query_doc,
    key_part,
    value_part,
    key_pos,
    key_doc,
):
    visible = pair_mask(query_pos, query_doc, key_pos, key_doc)
    prob_float = jnp.where(
        visible, jnp.exp(pair_scores(query_part, key_part) - log_part[:, :, None]), 0.0
    )
    grad_probs = pair_scores(grad_part, value_part)
    score_grad = (prob_float * (grad_probs - delta_part[:, :, None])).astype(jnp.bfloat16)
    return (prob_float.astype(jnp.bfloat16), score_grad)


def body(
    tokens,
    lengths,
    position,
    qkv_weight,
    out_weight,
    up_weight,
    down_weight,
    attn_gain,
    mlp_gain,
    query_scale,
    cotangent,
):
    cycle_size = lax.axis_size("ctx")
    my_index = lax.axis_index("ctx")
    tok_dev = tokens.shape[1]
    share_rows = tok_dev // cycle_size
    seq_ends = jnp.cumsum(lengths[0])
    place_row = position[0]
    residue = (place_row % cycle_size).reshape(cycle_size, tok_dev)
    landing = place_row // cycle_size
    matches = (
        residue[:, :, None] == jnp.arange(cycle_size, dtype=jnp.int32)[None, None, :]
    ).astype(jnp.int32)
    ranked = jnp.sum(jnp.cumsum(matches, axis=1) * matches, axis=2) - 1
    buffer_slot = residue * share_rows + ranked
    my_slots = lax.dynamic_index_in_dim(buffer_slot, my_index, 0, keepdims=False)
    local_rows = jnp.arange(tok_dev, dtype=jnp.int32)
    outgoing = jnp.zeros((tok_dev,), jnp.int32).at[my_slots].set(local_rows)
    flat_slot = (jnp.arange(cycle_size, dtype=jnp.int32)[:, None] * tok_dev + buffer_slot).reshape(
        -1
    )
    landing_table = (
        jnp.zeros((cycle_size * tok_dev,), jnp.int32)
        .at[flat_slot]
        .set(landing)
        .reshape(cycle_size, cycle_size, share_rows)
    )
    arrived_slot = lax.dynamic_index_in_dim(landing_table, my_index, 1, keepdims=False).reshape(-1)
    arrived_order = jnp.zeros((tok_dev,), jnp.int32).at[arrived_slot].set(local_rows)
    moved_x, moved_dy = (
        lax.all_to_all(tokens[0][outgoing], "ctx", split_axis=0, concat_axis=0, tiled=True),
        lax.all_to_all(cotangent[0][outgoing], "ctx", split_axis=0, concat_axis=0, tiled=True),
    )
    dealt_x = moved_x[arrived_order]
    dealt_dy = moved_dy[arrived_order]
    query_pos = local_rows * cycle_size + my_index
    query_doc = doc_index(query_pos, seq_ends)
    full_qkv, full_out, full_up, full_down, attn_gain_full, mlp_gain_full, scale_full = (
        lax.all_gather(qkv_weight, "fsdp", axis=0, tiled=True),
        lax.all_gather(out_weight, "fsdp", axis=0, tiled=True),
        lax.all_gather(up_weight, "fsdp", axis=0, tiled=True),
        lax.all_gather(down_weight, "fsdp", axis=0, tiled=True),
        lax.all_gather(attn_gain, "fsdp", axis=0, tiled=True),
        lax.all_gather(mlp_gain, "fsdp", axis=0, tiled=True),
        lax.all_gather(query_scale, "fsdp", axis=0, tiled=True),
    )
    attn_gain_f = attn_gain_full.astype(jnp.float32)
    mlp_gain_f = mlp_gain_full.astype(jnp.float32)
    scale_float = scale_full.astype(jnp.float32)
    x_float = dealt_x.astype(jnp.float32)
    inv_attn = lax.rsqrt(jnp.mean(x_float * x_float, axis=1, keepdims=True) + EPS)
    normed_attn = (x_float * inv_attn * attn_gain_f).astype(jnp.bfloat16)
    projected = jnp.dot(normed_attn, full_qkv, preferred_element_type=jnp.float32)
    att_width = projected.shape[1] // 3
    head_dim = scale_full.shape[0]
    base_scale = LOG2E / math.sqrt(head_dim)
    multiplier = jnp.tile(base_scale * jax.nn.softplus(scale_float), att_width // head_dim)
    raw_query = projected[:, :att_width]
    queries = (raw_query * multiplier).astype(jnp.bfloat16)
    key_rows = projected[:, att_width : 2 * att_width].astype(jnp.bfloat16)
    value_rows = projected[:, 2 * att_width :].astype(jnp.bfloat16)

    def key_place(first_row, amount):
        gathered_index = first_row + jnp.arange(amount, dtype=jnp.int32)
        key_pos = spread_position(gathered_index, tok_dev, cycle_size)
        return (key_pos, doc_index(key_pos, seq_ends))

    def stat_block(carried, pieces, first_row):
        running_max, running_sum = carried
        key_pos, key_doc = key_place(first_row, pieces[0].shape[0])
        visible = pair_mask(query_pos, query_doc, key_pos, key_doc)
        logits = jnp.where(visible, pair_scores(queries, pieces[0]), FLOOR)
        new_max = jnp.maximum(running_max, jnp.max(logits, axis=2))
        added = jnp.sum(jnp.where(visible, jnp.exp(logits - new_max[:, :, None]), 0.0), axis=2)
        return (new_max, running_sum * jnp.exp(running_max - new_max) + added)

    def output_block(summed, pieces, first_row):
        key_pos, key_doc = key_place(first_row, pieces[0].shape[0])
        visible = pair_mask(query_pos, query_doc, key_pos, key_doc)
        prob_low = jnp.where(
            visible, jnp.exp(pair_scores(queries, pieces[0]) - log_total[:, :, None]), 0.0
        ).astype(jnp.bfloat16)
        values_part = pieces[1].reshape(pieces[1].shape[0], HEADS, -1)
        return summed + jnp.einsum(
            "qhk,khd->qhd", prob_low, values_part, preferred_element_type=jnp.float32
        ).reshape(summed.shape)

    def query_grad_block(summed, pieces, first_row):
        key_pos, key_doc = key_place(first_row, pieces[0].shape[0])
        unused_probs, score_grad = pair_terms(
            queries,
            attended_grad,
            log_total,
            row_delta,
            query_pos,
            query_doc,
            pieces[0],
            pieces[1],
            key_pos,
            key_doc,
        )
        keys_part = pieces[0].reshape(pieces[0].shape[0], HEADS, -1)
        return summed + jnp.einsum(
            "qhk,khd->qhd", score_grad, keys_part, preferred_element_type=jnp.float32
        ).reshape(summed.shape)

    def key_grad_block(carried, pieces, first_row):
        amount = pieces[0].shape[0]
        part_pos, part_doc = key_place(first_row, amount)
        part_log = lax.dynamic_slice_in_dim(all_log, first_row, amount, 0)
        part_delta = lax.dynamic_slice_in_dim(all_delta, first_row, amount, 0)
        prob_low, score_grad = pair_terms(
            pieces[0],
            pieces[1],
            part_log,
            part_delta,
            part_pos,
            part_doc,
            key_rows,
            value_rows,
            query_pos,
            query_doc,
        )
        grad_keys = carried[0] + jnp.einsum(
            "qhk,qhd->khd",
            score_grad,
            pieces[0].reshape(amount, HEADS, -1),
            preferred_element_type=jnp.float32,
        ).reshape(tok_dev, -1)
        grad_values = carried[1] + jnp.einsum(
            "qhk,qhd->khd",
            prob_low,
            pieces[1].reshape(amount, HEADS, -1),
            preferred_element_type=jnp.float32,
        ).reshape(tok_dev, -1)
        return (grad_keys, grad_values)

    zero_stats = (
        jnp.full((tok_dev, HEADS), FLOOR, jnp.float32),
        jnp.zeros((tok_dev, HEADS), jnp.float32),
    )
    zero_rows = jnp.zeros((tok_dev, att_width), jnp.float32)
    running_max, running_sum = in_blocks(
        stat_block, zero_stats, (lax.all_gather(key_rows, "ctx", axis=0, tiled=True),)
    )
    log_total = running_max + jnp.log(running_sum)
    attended = in_blocks(
        output_block,
        zero_rows,
        (
            lax.all_gather(key_rows, "ctx", axis=0, tiled=True),
            lax.all_gather(value_rows, "ctx", axis=0, tiled=True),
        ),
    )
    attended_low = attended.astype(jnp.bfloat16)
    resid = x_float + jnp.dot(attended_low, full_out, preferred_element_type=jnp.float32)
    inv_mlp = lax.rsqrt(jnp.mean(resid * resid, axis=1, keepdims=True) + EPS)
    normed_mlp = (resid * inv_mlp * mlp_gain_f).astype(jnp.bfloat16)
    up_proj = jnp.dot(normed_mlp, full_up, preferred_element_type=jnp.float32)
    act_low = jax.nn.silu(up_proj).astype(jnp.bfloat16)
    result = resid + jnp.dot(act_low, full_down, preferred_element_type=jnp.float32)
    cot_float = dealt_dy.astype(jnp.float32)
    grad_down = jnp.dot(act_low.T, dealt_dy, preferred_element_type=jnp.float32)
    act_grad = jnp.dot(dealt_dy, full_down.T, preferred_element_type=jnp.float32)
    sigma = jax.nn.sigmoid(up_proj)
    up_grad = (act_grad * sigma * (1.0 + up_proj * (1.0 - sigma))).astype(jnp.bfloat16)
    grad_up = jnp.dot(normed_mlp.T, up_grad, preferred_element_type=jnp.float32)
    norm_mlp_grad = jnp.dot(up_grad, full_up.T, preferred_element_type=jnp.float32)
    grad_mlp_gain = jnp.sum(norm_mlp_grad * resid * inv_mlp, axis=0)
    scaled_mlp = norm_mlp_grad * mlp_gain_f
    resid_grad = cot_float + inv_mlp * (
        scaled_mlp - resid * inv_mlp * inv_mlp * jnp.mean(scaled_mlp * resid, axis=1, keepdims=True)
    )
    branch_grad = resid_grad.astype(jnp.bfloat16)
    grad_out = jnp.dot(attended_low.T, branch_grad, preferred_element_type=jnp.float32)
    attended_grad = jnp.dot(branch_grad, full_out.T, preferred_element_type=jnp.float32).astype(
        jnp.bfloat16
    )
    row_delta = jnp.sum(
        (attended_grad.astype(jnp.float32) * attended).reshape(tok_dev, HEADS, -1), axis=2
    )
    query_grads = in_blocks(
        query_grad_block,
        zero_rows,
        (
            lax.all_gather(key_rows, "ctx", axis=0, tiled=True),
            lax.all_gather(value_rows, "ctx", axis=0, tiled=True),
        ),
    )
    all_log, all_delta = (
        lax.all_gather(log_total, "ctx", axis=0, tiled=True),
        lax.all_gather(row_delta, "ctx", axis=0, tiled=True),
    )
    key_grad_f, value_grad_f = in_blocks(
        key_grad_block,
        (zero_rows, zero_rows),
        (
            lax.all_gather(queries, "ctx", axis=0, tiled=True),
            lax.all_gather(attended_grad, "ctx", axis=0, tiled=True),
        ),
    )
    scale_terms = jnp.sum((query_grads * raw_query).reshape(tok_dev, -1, head_dim), axis=(0, 1))
    grad_scale = scale_terms * base_scale * jax.nn.sigmoid(scale_float)
    proj_grad = jnp.concatenate(
        [
            (query_grads * multiplier).astype(jnp.bfloat16),
            key_grad_f.astype(jnp.bfloat16),
            value_grad_f.astype(jnp.bfloat16),
        ],
        axis=1,
    )
    grad_qkv = jnp.dot(normed_attn.T, proj_grad, preferred_element_type=jnp.float32)
    norm_attn_grad = jnp.dot(proj_grad, full_qkv.T, preferred_element_type=jnp.float32)
    grad_attn_gain = jnp.sum(norm_attn_grad * x_float * inv_attn, axis=0)
    scaled_attn = norm_attn_grad * attn_gain_f
    input_grad = resid_grad + inv_attn * (
        scaled_attn
        - x_float * inv_attn * inv_attn * jnp.mean(scaled_attn * x_float, axis=1, keepdims=True)
    )
    owned = (
        lax.psum_scatter(grad_qkv, "fsdp", scatter_dimension=0, tiled=True),
        lax.psum_scatter(grad_out, "fsdp", scatter_dimension=0, tiled=True),
        lax.psum_scatter(grad_up, "fsdp", scatter_dimension=0, tiled=True),
        lax.psum_scatter(grad_down, "fsdp", scatter_dimension=0, tiled=True),
        lax.psum_scatter(grad_attn_gain, "fsdp", scatter_dimension=0, tiled=True),
        lax.psum_scatter(grad_mlp_gain, "fsdp", scatter_dimension=0, tiled=True),
        lax.psum_scatter(grad_scale, "fsdp", scatter_dimension=0, tiled=True),
    )
    summed_grads = lax.psum(
        (owned[0], owned[1], owned[2], owned[3], owned[4], owned[5], owned[6]), "ctx"
    )
    back_out, back_grad = (
        lax.all_to_all(result[arrived_slot], "ctx", split_axis=0, concat_axis=0, tiled=True),
        lax.all_to_all(input_grad[arrived_slot], "ctx", split_axis=0, concat_axis=0, tiled=True),
    )
    return (
        back_out[my_slots][None],
        back_grad[my_slots][None],
        summed_grads[0],
        summed_grads[1],
        summed_grads[2],
        summed_grads[3],
        summed_grads[4],
        summed_grads[5],
        summed_grads[6],
    )


def attend_kernel(
    ends_ref,
    x_ref,
    w_ref,
    aux_ref,
    pos_ref,
    out_w_ref,
    up_w_ref,
    down_w_ref,
    dy_ref,
    att_ref,
    normed_ref,
    qkv_ref,
    lse_ref,
    out_ref,
    auxsum_ref,
    place_ref,
    w_all,
    result_ref,
    resid_grad_ref,
    branch_ref,
    up_grad_ref,
    act_ref,
    normed_mlp_ref,
    grad_ref,
    x_all,
    w_own,
    weights,
    aux_all,
    pos_all,
    v_turned,
    key_pos,
    bias,
    att_send,
    x_send_sem,
    x_recv_sem,
    w_send_sem,
    w_recv_sem,
    aux_send_sem,
    aux_recv_sem,
    pos_sem,
    att_send_sem,
    att_recv_sem,
    m_send_sem,
    m_recv_sem,
    local_sem,
):
    at = Place()
    meet_plane(at)
    c, f = at.c, at.f
    hub = at.core == at.half

    aux_own = pltpu.make_async_copy(aux_ref, aux_all.at[f], local_sem.at[1])
    aux_own.start()
    x_own = pltpu.make_async_copy(x_ref, x_all.at[c], local_sem.at[3])

    x_far = pltpu.make_async_remote_copy(
        src_ref=x_ref,
        dst_ref=x_all.at[c],
        send_sem=x_send_sem.at[0, 0],
        recv_sem=x_recv_sem.at[c],
        device_id=dev(flip(c, 4), f),
        device_id_type=MESH,
    )

    @pl.when(hub)
    def _():
        x_own.start()
        for k, where in enumerate((dev(flip(c, 1), f), dev(flip(c, 2), f), dev(c, at.twin))):
            send(x_ref, x_all.at[c], x_send_sem.at[0, k], x_recv_sem.at[c], where)

    @pl.when(jnp.logical_not(hub))
    def _():
        x_far.start()

    w_copies, aux_copies = [], []
    for k in (2, 1, 3):
        aux_copies.append(
            send(
                aux_ref,
                aux_all.at[f],
                aux_send_sem.at[k],
                aux_recv_sem.at[f],
                dev(c, (f + k) % 4),
            )
        )

    pos = pos_ref[...]
    start = jnp.zeros_like(pos)
    end = 0
    for k in range(4):
        end = end + ends_ref[0, k]
        start = jnp.where(pos >= end, end, start)
    pos_all[at.core, 0:1, :] = pos.astype(F32)
    pos_all[at.core, 1:2, :] = start.astype(F32)
    pos_all[at.core, 2:8, :] = jnp.zeros((6, 2048), F32)
    pos_copy = send(
        pos_all.at[at.core], pos_all.at[at.core], pos_sem.at[0], pos_sem.at[1], dev(c, at.twin)
    )

    row = lax.broadcasted_iota(jnp.int32, (1280, 512), 0)
    column = lax.broadcasted_iota(jnp.int32, (1280, 512), 1)
    inside = column % LANES
    wanted = (c % 4) * 320 + column // LANES * 80 + inside
    pick = jnp.where((row == wanted) & (inside < 80), 1.0, 0.0).astype(BF)
    for j in range(3):
        some = jnp.dot(w_ref[:, j * 1280 : (j + 1) * 1280], pick, preferred_element_type=F32)
        for k in range(2):
            w_own[k, :, j * 256 : (j + 1) * 256] = some[:, k * 256 : (k + 1) * 256].astype(BF)
    mine_rows = span(f * 320, 320, 320)
    for k in (2, 3, 1):
        to = (f + k) % 4
        w_copies.append(
            send(
                w_own.at[to % 2],
                w_all.at[mine_rows],
                w_send_sem.at[k],
                w_recv_sem.at[f],
                dev(c, to),
            )
        )
    w_all[mine_rows, :] = w_own[at.core]

    shards = (out_w_ref, up_w_ref, down_w_ref)
    xbit = c % 2
    other = (f + 2) % 4

    def part(m, owner, x):
        return weights.at[m, span(owner * 320 + x * 160, 160, 160)]

    def weight_copy(m, way):
        if way == 0:
            src, dst, to = shards[m], weights.at[m, mine_rows], dev(c, at.twin)
        elif way == 1:
            src = shards[m].at[span(xbit * 160, 160, 160)]
            dst, to = part(m, f, xbit), dev(c, other)
        else:
            x = (xbit, xbit, 1 - xbit)[way - 2]
            src = dst = part(m, other, x)
            to = (dev(flip(c, 1), f), dev(c, at.twin), dev(c, at.twin))[way - 2]
        return pltpu.make_async_remote_copy(
            src_ref=src,
            dst_ref=dst,
            send_sem=m_send_sem.at[m, way],
            recv_sem=m_recv_sem.at[m, way],
            device_id=to,
            device_id_type=MESH,
        )

    def weight_first(m):
        weight_copy(m, 0).start()
        weight_copy(m, 1).start()
        weights[m, mine_rows, :] = shards[m][...]

    def weight_second(m):
        weight_copy(m, 1).wait_recv()
        weight_copy(m, 2).start()
        weight_copy(m, 3).start()

    def weight_third(m):
        weight_copy(m, 2).wait_recv()
        weight_copy(m, 4).start()

    def weight_last(m):
        for way in (0, 3, 4):
            weight_copy(m, way).wait_recv()

    weight_first(0)

    aux_own.wait()
    for k in (1, 2, 3):
        await_recv(aux_all.at[0], aux_recv_sem.at[(f + k) % 4])
    aux = jnp.zeros((16, 1280), F32)
    scale = jnp.zeros((16, LANES), F32)
    row = lax.broadcasted_iota(jnp.int32, (384, 1280), 0)
    column = lax.broadcasted_iota(jnp.int32, (384, 1280), 1)
    for k in range(4):
        put = jnp.where((column == row + k * 320) & (row < 320), 1.0, 0.0).astype(BF)
        aux = aux + jnp.dot(aux_all[k], put, preferred_element_type=F32)
        put = (column[:LANES, :LANES] == row[:LANES, :LANES] + k * 20) & (row[:LANES, :LANES] < 20)
        put = jnp.where(put, 1.0, 0.0).astype(BF)
        scale = scale + jnp.dot(aux_all[k, :, :LANES], put, preferred_element_type=F32)
    auxsum_ref[...] = aux
    auxsum_ref[2:3, :LANES] = scale[2:3]
    gain = aux[0:1, :]
    mlp_gain = aux[1:2, :]
    scale = scale[2:3]
    real = lax.broadcasted_iota(jnp.int32, (1, LANES), 1) < 80
    mult = jnp.where(
        real, LOG2E / math.sqrt(80) * (jnp.maximum(scale, 0.0) + jnp.log1p(jnp.exp(-jnp.abs(scale)))), 0.0
    )
    one = jnp.ones_like(mult)
    mults = jnp.concatenate([mult, mult, one, one, one, one], axis=1)

    await_recv(pos_all.at[0], pos_sem.at[1])
    place_ref[...] = pos_all[at.half]
    for k in range(8):
        block = place_ref[0:1, k * 256 : (k + 1) * 256]
        key_pos[k * 256 : (k + 1) * 256, :] = jnp.transpose(
            jnp.broadcast_to(block, (256, 256))
        )

    def arrive(step, carry):
        slot = flip(c, step)

        @pl.when(jnp.logical_and(hub, step == 0))
        def _():
            x_own.wait()

        @pl.when(jnp.logical_not(jnp.logical_and(hub, step == 0)))
        def _():
            await_recv(x_all.at[slot], x_recv_sem.at[slot])

        def onward(way, where):
            send(
                x_all.at[slot],
                x_all.at[slot],
                x_send_sem.at[step, way],
                x_recv_sem.at[slot],
                where,
            )

        @pl.when(jnp.logical_and(hub, jnp.logical_or(step == 4, step == 6)))
        def _():
            onward(0, dev(flip(c, 1), f))

        @pl.when(jnp.logical_and(hub, jnp.logical_or(step == 4, step == 1)))
        def _():
            onward(1, dev(flip(c, 2), f))

        @pl.when(jnp.logical_and(hub, step > 0))
        def _():
            onward(2, dev(c, at.twin))

        xf = x_all[slot].astype(F32)
        inv = lax.rsqrt(jnp.mean(xf * xf, axis=1, keepdims=True) + EPS)
        normed_ref[span(slot * 256, 256, 256), :] = (xf * inv * gain).astype(BF)
        return carry

    def project(step, carry):
        slot = flip(c, step)
        rows = span(slot * 256, 256, 256)
        proj = jnp.dot(normed_ref[rows, :], w_all[...], preferred_element_type=F32)
        qkv_ref[rows, :] = (proj * mults).astype(BF)
        return carry

    lax.fori_loop(0, 7, arrive, 0)
    for k in (1, 2, 3):
        await_recv(w_all.at[pl.ds(0, 320)], w_recv_sem.at[(f + k) % 4])
    weight_first(1)
    weight_first(2)
    weight_second(0)
    lax.fori_loop(0, 5, project, 0)
    lax.fori_loop(7, 8, arrive, 0)
    lax.fori_loop(5, 8, project, 0)

    for h in range(2):
        v_turned[h] = jnp.transpose(qkv_ref[:, (4 + h) * LANES : (5 + h) * LANES])

    att_own = pltpu.make_async_copy(
        att_send.at[c], att_ref.at[span(at.group * 160, 160, 160)], local_sem.at[3]
    )

    def att_copy(block):
        return pltpu.make_async_remote_copy(
            src_ref=att_send.at[block],
            dst_ref=att_ref.at[span(at.group * 160, 160, 160)],
            send_sem=att_send_sem.at[block],
            recv_sem=att_recv_sem.at[at.group],
            device_id=dev(block, at.pack),
            device_id_type=MESH,
        )

    mine = at.core == at.half

    def attend(step, carry):
        block = flip(c, step)
        lanes = span(block * 256, 256, 256)
        high = place_ref[0:1, lanes]
        least = place_ref[1:2, lanes]
        kp = key_pos[...]
        bias[...] = jnp.where((kp >= least) & (kp <= high), 0.0, FLOOR)
        for h in range(2):
            keys = qkv_ref[:, (2 + h) * LANES : (3 + h) * LANES]
            query = qkv_ref[lanes, h * LANES : (h + 1) * LANES]
            s = lax.dot_general(
                keys, query, (((1,), (1,)), ((), ())), preferred_element_type=F32
            )
            s = s + bias[...]
            top = jnp.max(s, axis=0, keepdims=True)
            p = jnp.exp(s - top)
            total = jnp.sum(p, axis=0, keepdims=True)
            o = jnp.dot(v_turned[h], p.astype(BF), preferred_element_type=F32)
            o = o[:80] / total
            lse_ref[h : h + 1, lanes] = top + jnp.log(total)
            out_ref[h * 80 : (h + 1) * 80, lanes] = o.astype(BF)
            att_send[block, h * 80 : (h + 1) * 80, :] = o.astype(BF)

        @pl.when(jnp.logical_and(mine, step == 0))
        def _():
            att_own.start()

        @pl.when(jnp.logical_not(jnp.logical_and(mine, step == 0)))
        def _():
            att_copy(block).start()

        for when, todo in ((1, weight_third), (4, weight_second), (6, weight_second), (7, weight_third)):
            m = {(1, weight_third): 0, (4, weight_second): 1, (6, weight_second): 2}.get((when, todo), 1)

            @pl.when(step == when)
            def _(todo=todo, m=m):
                todo(m)

        return carry

    lax.fori_loop(0, 8, attend, 0)
    lse_ref[2:8, :] = jnp.zeros((6, 2048), F32)

    def land(block, carry):
        @pl.when(jnp.logical_not(jnp.logical_and(mine, block == at.group)))
        def _():
            await_recv(att_ref.at[pl.ds(0, 160)], att_recv_sem.at[block])

        return carry

    @pl.when(mine)
    def _():
        att_own.wait()

    weight_last(0)
    lax.fori_loop(0, 8, land, 0)

    def across(left, right):
        return lax.dot_general(
            left, right, (((1,), (1,)), ((), ())), preferred_element_type=F32
        )

    xf = x_ref[...].astype(F32)
    resid = xf + jnp.dot(jnp.transpose(att_ref[...]), weights[0], preferred_element_type=F32)
    inv = lax.rsqrt(jnp.mean(resid * resid, axis=1, keepdims=True) + EPS)
    normed_mlp = (resid * inv * mlp_gain).astype(BF)
    normed_mlp_ref[...] = jnp.transpose(normed_mlp)
    weight_third(2)
    weight_last(1)
    up = jnp.dot(normed_mlp, weights[1], preferred_element_type=F32)
    sigma = 1.0 / (1.0 + jnp.exp(-up))
    act = (up * sigma).astype(BF)
    act_ref[...] = jnp.transpose(act)
    slope = sigma * (1.0 + up * (1.0 - sigma))
    weight_last(2)
    dy = dy_ref[...]
    up_grad = (across(dy, weights[2]) * slope).astype(BF)
    up_grad_ref[...] = up_grad
    scaled = across(up_grad, weights[1]) * mlp_gain
    resid_grad = dy.astype(F32) + inv * (
        scaled - resid * inv * inv * jnp.mean(scaled * resid, axis=1, keepdims=True)
    )
    resid_grad_ref[...] = resid_grad
    branch = resid_grad.astype(BF)
    branch_ref[...] = branch
    grad_ref[...] = across(weights[0], branch).astype(BF)
    result_ref[...] = resid + jnp.dot(act, weights[2], preferred_element_type=F32)

    for copy in w_copies + aux_copies:
        copy.wait_send()
    pos_copy.wait_send()
    for m in range(3):
        for way in range(5):
            weight_copy(m, way).wait_send()

    @pl.when(hub)
    def _():
        for k in range(3):
            await_recv(x_ref, x_send_sem.at[0, k])
        for step in range(1, 8):
            ways = {1: (1, 2), 4: (0, 1, 2), 6: (0, 2)}.get(step, (2,))
            for way in ways:
                await_recv(x_ref, x_send_sem.at[step, way])

    @pl.when(jnp.logical_not(hub))
    def _():
        x_far.wait_send()

    def finish(block, carry):
        @pl.when(jnp.logical_not(jnp.logical_and(mine, block == c)))
        def _():
            att_copy(block).wait_send()

        return carry

    lax.fori_loop(0, 8, finish, 0)


def forward(*args):
    shape = jax.ShapeDtypeStruct
    dma = pltpu.SemaphoreType.DMA
    return pl.pallas_call(
        attend_kernel,
        name="forward",
        out_shape=(
            shape((1280, 256), BF),
            shape((2048, 1280), BF),
            shape((2048, 768), BF),
            shape((8, 2048), F32),
            shape((160, 2048), BF),
            shape((16, 1280), F32),
            shape((8, 2048), F32),
            shape((1280, 768), BF),
            shape((256, 1280), F32),
            shape((256, 1280), F32),
            shape((256, 1280), BF),
            shape((256, 1280), BF),
            shape((1280, 256), BF),
            shape((1280, 256), BF),
            shape((1280, 256), BF),
        ),
        in_specs=[pl.BlockSpec(memory_space=pltpu.SMEM)] + [VMEM_SPEC] * 8,
        out_specs=(VMEM_SPEC,) * 15,
        scratch_shapes=[
            pltpu.VMEM((8, 256, 1280), BF),
            pltpu.VMEM((2, 320, 768), BF),
            pltpu.VMEM((3, 1280, 1280), BF),
            pltpu.VMEM((4, 16, 384), BF),
            pltpu.VMEM((2, 8, 2048), F32),
            pltpu.VMEM((2, 128, 2048), BF),
            pltpu.VMEM((2048, 256), F32),
            pltpu.VMEM((2048, 256), F32),
            pltpu.VMEM((8, 160, 256), BF),
            dma((8, 3)),
            dma((8,)),
            dma((4,)),
            dma((4,)),
            dma((4,)),
            dma((4,)),
            dma((2,)),
            dma((8,)),
            dma((8,)),
            dma((3, 5)),
            dma((3, 5)),
            dma((4,)),
        ],
        compiler_params=pltpu.CompilerParams(
            collective_id=0, has_side_effects=True, vmem_limit_bytes=VMEM_LIMIT
        ),
        cost_estimate=pl.CostEstimate(
            flops=20_000_000_000, bytes_accessed=40_000_000, transcendentals=8_400_000
        ),
    )(*args)


def add_into(target, source, rows, step):
    def one(k, carry):
        part = span(k * step, step, step)
        target[part, :] = (target[part, :].astype(F32) + source[part, :].astype(F32)).astype(BF)
        return carry

    lax.fori_loop(0, rows // step, one, 0)


SUM_WAYS = ("xzyh", "xyzh", "zxyh")
SPREAD_WAYS = ("zhx", "hzx", "hxz")
HEAD_WAYS = "hzx"

PLAN = (
    "mt0", "mt1", "mt2", "prep", "m00", "m02", "take", "L00", "L01", "L02", "L03", "L04",
    "L05", "L06", "L07", "E0", "qs0", "m10", "m01", "L10", "L11", "L12", "L13", "L14", "L15",
    "qa0", "m12", "L16", "L17", "E1", "v0", "qs1", "nt0", "v1", "q00", "nt1", "nt2", "v2",
    "nt3", "na0", "m11", "na1", "v3", "qa1", "na2", "q10", "na3", "m20", "m22", "v4", "v5",
    "q01", "m21", "q20", "m30", "m32", "q11", "g00", "m31", "g02", "nb0", "nb1", "g10", "qc0",
    "g01", "g12", "q21", "qw0", "g22", "g11", "g20", "qc1", "nc_f", "nc_n", "qw1", "g21",
    "mw0", "mw2", "mw1", "nfin", "turn",
)

KEY_PARTS = 2
KEY_ROWS = 2048 // KEY_PARTS


def backward_kernel(
    grad_ref,
    att_ref,
    branch_ref,
    normed_mlp_ref,
    up_grad_ref,
    act_ref,
    dy_ref,
    qkv_ref,
    lse_ref,
    out_ref,
    place_ref,
    normed_hbm,
    w_ref,
    mult_ref,
    x_ref,
    resid_grad_ref,
    gain_ref,
    first_out,
    second_out,
    third_out,
    slice_out,
    input_grad_ref,
    scale_ref,
    grad_all,
    key_pos,
    k_turned,
    delta,
    key_sum,
    value_sum,
    turned,
    normed_part,
    n_core,
    n_x,
    n_z,
    n_last,
    sums,
    core_in,
    taken,
    slices,
    s1,
    s2,
    gathered,
    strip,
    scale_in,
    g_send_sem,
    g_recv_sem,
    local_sem,
    m_send,
    m_recv,
    q_send,
    q_recv,
    nc_send,
    nc_recv,
    n_send,
    n_recv,
    v_send,
    v_recv,
):
    at = Place()
    meet_plane(at)
    c, f, core, half = at.c, at.f, at.core, at.half
    mine = core == half
    row = f // 2
    xbit, zbit = c % 2, (c // 2) % 2
    twin, across = dev(c, at.twin), dev(c, at.across)
    xpeer, zpeer, hpeer = dev(flip(c, 1), f), dev(flip(c, 2), f), dev(flip(c, 4), f)

    def remote(src, dst, send_sem, recv_sem, where):
        return pltpu.make_async_remote_copy(
            src_ref=src,
            dst_ref=dst,
            send_sem=send_sem,
            recv_sem=recv_sem,
            device_id=where,
            device_id_type=MESH,
        )

    def grad_copy(group, h):
        return remote(
            grad_ref.at[span(group * 160 + h * 80, 80, 80)],
            grad_all.at[h, pl.ds(0, 80), span(c * 256, 256, 256)],
            g_send_sem.at[group, h],
            g_recv_sem.at[c, h],
            dev(core * 4 + group // 2, at.plane + group % 2),
        )

    def grad_own(h):
        return pltpu.make_async_copy(
            grad_ref.at[span(at.group * 160 + h * 80, 80, 80)],
            grad_all.at[h, pl.ds(0, 80), span(c * 256, 256, 256)],
            local_sem.at[h],
        )

    def give(k, carry):
        group = flip(at.group, k)

        @pl.when(jnp.logical_and(mine, k == 0))
        def _():
            grad_own(0).start()
            grad_own(1).start()

        @pl.when(jnp.logical_not(jnp.logical_and(mine, k == 0)))
        def _():
            grad_copy(group, 0).start()
            grad_copy(group, 1).start()

        return carry

    lax.fori_loop(0, 8, give, 0)

    bits = {"y": row, "x": xbit, "z": zbit, "h": half}
    peers = {"y": across, "x": xpeer, "z": zpeer, "h": hpeer}
    results = (first_out, second_out, third_out)

    def finer(m):
        return "z" if SUM_WAYS[m].index("x") < SUM_WAYS[m].index("z") else "x"

    def cut(ref, way, bit):
        if way == "y":
            return (bit,)
        lead = (slice(None),) * (len(ref.shape) - 2)
        if way == "h":
            return lead + (slice(None), span(bit * 640, 640, 640))
        rows = ref.shape[-2] // 2
        return lead + (span(bit * rows, rows, rows),)

    def main_copy(stage, m):
        if stage < 0:
            y = stage + 2
            src, dst, to = sums.at[pl.ds((m * 2 + y) * 320, 320)], core_in.at[m, y], twin
        elif stage < 4:
            way = SUM_WAYS[m][stage]
            ref = core_in.at[m] if stage == 0 else taken[m][stage - 1]
            src, dst, to = ref.at[cut(ref, way, 1 - bits[way])], taken[m][stage], peers[way]
        else:
            way = SPREAD_WAYS[m][stage - 4]
            known = SPREAD_WAYS[m][: stage - 4]
            low = finer(m)
            high = "x" if low == "z" else "z"
            if high in known:
                rows = pl.ds(0, 320)
            elif low in known:
                rows = span(bits[high] * 160, 160, 160)
            else:
                rows = span(bits[high] * 160 + bits[low] * 80, 80, 80)
            lanes = pl.ds(0, 1280) if "h" in known else span(half * 640, 640, 640)
            src = dst = results[m].at[rows, lanes]
            to = peers[way]
        return remote(src, dst, m_send.at[stage + 2, m], m_recv.at[stage + 2, m], to)

    def added(ref, other, spot):
        for k in range(2) if len(ref.shape) == 3 else (None,):
            here = () if k is None else (k,)
            there = spot if k is None else (k,) + spot[1:]
            ref[here] = (ref[here].astype(F32) + other[there].astype(F32)).astype(BF)

    def main(stage, m):
        if stage == 0:
            for y in range(2):
                main_copy(y - 2, m).wait_recv()
                total = core_in[m, y].astype(F32) + weight_rows(m, 2 * y + core)
                core_in[m, y] = total.astype(BF)
        elif stage < 5:
            main_copy(stage - 1, m).wait_recv()
            way = SUM_WAYS[m][stage - 1]
            ref = core_in.at[m] if stage == 1 else taken[m][stage - 2]
            spot = cut(ref, way, bits[way])
            if stage < 4:
                added(taken[m][stage - 1], ref, spot)
            else:
                low = finer(m)
                high = "x" if low == "z" else "z"
                rows = span(bits[high] * 160 + bits[low] * 80, 80, 80)
                results[m][rows, span(half * 640, 640, 640)] = (
                    taken[m][3][...].astype(F32) + ref[spot].astype(F32)
                ).astype(BF)
        else:
            main_copy(stage - 1, m).wait_recv()
        if stage < 7:
            main_copy(stage, m).start()

    lefts = (act_ref, normed_mlp_ref, att_ref)
    rights = (dy_ref, up_grad_ref, branch_ref)

    def weight_rows(m, quarter):
        rows = span(quarter * 320, 320, 320)
        return jnp.dot(lefts[m][rows, :], rights[m][...], preferred_element_type=F32)

    def main_first(m):
        for y in range(2):
            part = weight_rows(m, 2 * y + 1 - core)
            sums[(m * 2 + y) * 320 : (m * 2 + y + 1) * 320, :] = part.astype(BF)
            main_copy(y - 2, m).start()

    def prepare():
        for h in range(2):
            grad_all[h, 80:, :] = jnp.zeros((48, 2048), BF)
            k_turned[h] = jnp.transpose(qkv_ref[:, (2 + h) * LANES : (3 + h) * LANES])
        for k in range(8):
            block = place_ref[0:1, k * 256 : (k + 1) * 256]
            key_pos[k * 256 : (k + 1) * 256, :] = jnp.transpose(
                jnp.broadcast_to(block, (LANES, 256))
            )
        scale_ref[...] = jnp.zeros((8, LANES), F32)

    def take(k, carry):
        block = flip(c, k)

        @pl.when(jnp.logical_and(mine, k == 0))
        def _():
            grad_own(0).wait()
            grad_own(1).wait()

        @pl.when(jnp.logical_not(jnp.logical_and(mine, k == 0)))
        def _():
            for h in range(2):
                await_recv(
                    grad_all.at[h, pl.ds(0, 80), pl.ds(0, 256)], g_recv_sem.at[block, h]
                )

        return carry

    def take_all():
        lax.fori_loop(0, 8, take, 0)
        for h in range(2):
            delta[h : h + 1, :] = jnp.sum(
                grad_all[h, :80, :].astype(F32) * out_ref[h * 80 : (h + 1) * 80, :].astype(F32),
                axis=0,
                keepdims=True,
            )

    def head_copy(stage, h):
        if stage == 0:
            src, dst, to = slices.at[h, :, span((1 - row) * 640, 640, 640)], s1.at[h], across
        elif stage == 1:
            src, dst, to = s1.at[h, span(128 - half * 128, 128, 128)], s2.at[h], hpeer
        elif stage < 5:
            way = HEAD_WAYS[stage - 2]
            known = HEAD_WAYS[: stage - 2]
            where = (core,) + tuple(slice(None) if d in known else bits[d] for d in "xz") + (h,)
            rows = slice(None) if "h" in known else span(half * 128, 128, 128)
            src = dst = gathered.at[where + (rows,)]
            to = peers[way]
        else:
            src = dst = gathered.at[core, :, :, h]
            to = twin
        return remote(src, dst, q_send.at[stage, h], q_recv.at[stage, h], to)

    def head(stage, h):
        if stage > 0:
            head_copy(stage - 1, h).wait_recv()
        if stage == 1:
            add_into(s1.at[h], slices.at[h, :, span(row * 640, 640, 640)], 256, 128)
        if stage == 2:
            own = span(half * 128, 128, 128)
            gathered[core, xbit, zbit, h, own, :] = (
                s2[h].astype(F32) + s1[h, own, :].astype(F32)
            ).astype(BF)
        if stage < 6:
            head_copy(stage, h).start()

    def normed_load(part):
        return pltpu.make_async_copy(
            normed_hbm.at[:, pl.ds(part * 256, 256)], normed_part.at[part % 2], local_sem.at[2 + part % 2]
        )

    def attend_head(h, hooks):
        key_sum[...] = jnp.zeros((2048, LANES), F32)
        value_sum[...] = jnp.zeros((2048, LANES), F32)

        def block_grad(block, carry):
            lanes = span(block * 256, 256, 256)
            high = place_ref[0:1, lanes]
            least = place_ref[1:2, lanes]
            query = qkv_ref[lanes, h * LANES : (h + 1) * LANES]
            grad_t = grad_all[h, :, lanes]
            q_grad = jnp.zeros((LANES, 256), F32)
            for part in range(KEY_PARTS):
                some = slice(part * KEY_ROWS, (part + 1) * KEY_ROWS)
                kp = key_pos[some, :]
                kp = jnp.concatenate([kp, kp], axis=1)
                keys = qkv_ref[some, (2 + h) * LANES : (3 + h) * LANES]
                values = qkv_ref[some, (4 + h) * LANES : (5 + h) * LANES]
                s = lax.dot_general(
                    keys, query, (((1,), (1,)), ((), ())), preferred_element_type=F32
                )
                visible = (kp >= least) & (kp <= high)
                p = jnp.exp(jnp.where(visible, s - lse_ref[h : h + 1, lanes], FLOOR))
                gp = jnp.dot(values, grad_t, preferred_element_type=F32)
                gs = (p * (gp - delta[h : h + 1, lanes])).astype(BF)
                value_sum[some, :] += lax.dot_general(
                    p.astype(BF), grad_t, (((1,), (1,)), ((), ())), preferred_element_type=F32
                )
                key_sum[some, :] += jnp.dot(gs, query, preferred_element_type=F32)
                q_grad += jnp.dot(k_turned[h, :, some], gs, preferred_element_type=F32)
            scale_ref[0:1, :] += jnp.sum(
                jnp.transpose(q_grad) * query.astype(F32), axis=0, keepdims=True
            )
            turned[h * LANES : (h + 1) * LANES, lanes] = (q_grad * mult_ref[:, 0:1]).astype(BF)
            for step, todo in hooks.items():

                @pl.when(block == step)
                def _(todo=todo):
                    for one in todo:
                        one()

            return carry

        lax.fori_loop(0, 8, block_grad, 0)

    def attend_end(h):
        for j, total in ((1, key_sum), (2, value_sum)):
            low = jnp.transpose(total[...]).astype(BF)
            turned[(2 * j + h) * LANES : (2 * j + h + 1) * LANES, :] = low

    def head_first(h):
        slices[h, 240:, :] = jnp.zeros((16, 1280), BF)
        for part in range(5):
            normed_load(part).wait()
            if part + 1 < 5:
                normed_load(part + 1).start()
            for j in range(3):
                first = (2 * j + h) * LANES
                slices[h, j * 80 : (j + 1) * 80, part * 256 : (part + 1) * 256] = jnp.dot(
                    turned[first : first + 80, :],
                    normed_part[part % 2],
                    preferred_element_type=F32,
                ).astype(BF)
        if h == 0:
            normed_load(0).start()
        head(0, h)

    def norm_bits(k):
        return (1 - xbit, 1 - xbit, xbit, xbit)[k], (1 - zbit, zbit, 1 - zbit, zbit)[k]

    def norm_spot(k, hh):
        slot = 2 * k + hh
        return sums.at[pl.ds(slot // 5 * 640, 640), pl.ds(slot % 5 * 256, 256)]

    def norm_copy(stage, k, hh=0):
        if stage == 0:
            return remote(
                norm_spot(k, hh), n_core.at[k, hh], nc_send.at[k, hh], nc_recv.at[k, hh], twin
            )
        took = k
        if stage == 1:
            ends = n_core.at[k], n_x.at[k], xpeer
        elif stage == 2:
            ends = n_core.at[2, (1 - half, half)[k]], n_z.at[k], zpeer
        else:
            to = dev(flip(c, 4), at.pack) if k == 0 else dev(c, at.twin)
            took = (core, 2)[k]
            ends = n_core.at[3, (1 - half, half)[k]], n_last.at[core], to
        return remote(ends[0], ends[1], n_send.at[stage, k], n_recv.at[stage, took], ends[2])

    def norm_part(k, hh, which):
        xs, zs = norm_bits(k)
        lanes = span((hh * 4 + zs * 2 + xs) * 256, 256, 256)
        rows = span(which * 640, 640, 640)
        return jnp.dot(w_ref[rows, :], turned[:, lanes], preferred_element_type=F32)

    def norm_first(k):
        if k == 0:
            for m in range(3):
                for stage in range(2):
                    main_copy(stage - 2, m).wait_send()
        for hh in range(2):
            norm_spot(k, hh)[...] = norm_part(k, hh, 1 - core).astype(BF)
            norm_copy(0, k, hh).start()

    def norm_core(k):
        for hh in range(2):
            norm_copy(0, k, hh).wait_recv()
            n_core[k, hh] = (n_core[k, hh].astype(F32) + norm_part(k, hh, core)).astype(BF)
        if k < 2:
            norm_copy(1, k).start()

    def scale_copy(stage):
        where = (twin, across, xpeer, zpeer, hpeer)[stage]
        return remote(scale_ref, scale_in.at[stage], v_send.at[stage], v_recv.at[stage], where)

    def tiny(stage):
        if stage > 0:
            scale_copy(stage - 1).wait()
            scale_ref[...] += scale_in[stage - 1]
        if stage < 5:
            scale_copy(stage).start()

    def norm_x(k):
        norm_copy(1, k).wait_recv()
        for hh in range(2):
            add_into(n_core.at[2 + k, hh], n_x.at[k, hh], 640, 80)
        if k == 0:
            norm_copy(2, 0).start()
            norm_copy(2, 1).start()

    def norm_far():
        norm_copy(2, 0).wait_recv()
        add_into(n_core.at[3, 1 - half], n_z.at[0], 640, 80)
        norm_copy(3, 0).start()

    def norm_near():
        norm_copy(2, 1).wait_recv()
        add_into(n_core.at[3, half], n_z.at[1], 640, 80)

        @pl.when(jnp.logical_not(mine))
        def _():
            norm_copy(3, 1).start()

    def norm_last():
        @pl.when(mine)
        def _():
            n_last[core] = n_core[3, half]
            await_recv(n_last.at[0], n_recv.at[3, 2])

        @pl.when(jnp.logical_not(mine))
        def _():
            await_recv(n_last.at[0], n_recv.at[3, 0])
            await_recv(n_last.at[1], n_recv.at[3, 1])

        xf = x_ref[...].astype(F32)
        inv = lax.rsqrt(jnp.mean(xf * xf, axis=1, keepdims=True) + EPS)
        scaled = jnp.concatenate(
            [jnp.transpose(n_last[k].astype(F32)) for k in range(2)], axis=1
        ) * gain_ref[0:1, :]
        input_grad_ref[...] = resid_grad_ref[...] + inv * (
            scaled - xf * inv * inv * jnp.mean(scaled * xf, axis=1, keepdims=True)
        )

    def turn_all():
        for k in range(4):
            for hh in range(2):
                norm_copy(0, k, hh).wait_send()
        for core_k in range(2):
            for m4 in range(4):
                group = 2 * m4 + core_k
                for h in range(2):
                    for j in range(3):
                        start = j * 1280 + (group * 2 + h) * 80
                        sums[
                            start % 1920 : start % 1920 + 80, start // 1920 * 640 : start // 1920 * 640 + 640
                        ] = gathered[core_k, m4 % 2, m4 // 2, h, j * 80 : (j + 1) * 80, :]

        for part in range(2):

            def turn(k, carry, part=part):
                strip[...] = jnp.transpose(sums[span(k * LANES, LANES, LANES), part * 640 : part * 640 + 640])
                slice_out[:, span(part * 1920 + k * LANES, LANES, LANES)] = strip[span(core * 320, 320, 320), :]
                return carry

            lax.fori_loop(0, 15, turn, 0)


    tasks = {"prep": prepare, "take": take_all, "nb0": lambda: norm_x(0), "nb1": lambda: norm_x(1)}
    tasks |= {"nc_f": norm_far, "nc_n": norm_near, "nfin": norm_last, "turn": turn_all}
    for m in range(3):
        tasks[f"mt{m}"] = functools.partial(main_first, m)
        for stage in range(4):
            tasks[f"m{stage}{m}"] = functools.partial(main, stage, m)
        for stage in range(3):
            tasks[f"g{stage}{m}"] = functools.partial(main, 4 + stage, m)
        tasks[f"mw{m}"] = functools.partial(main, 7, m)
    for h in range(2):
        tasks[f"E{h}"] = functools.partial(attend_end, h)
        tasks[f"qs{h}"] = functools.partial(head_first, h)
        for stage, name in enumerate(("qa", "q0", "q1", "q2", "qc", "qw")):
            tasks[f"{name}{h}"] = functools.partial(head, 1 + stage, h)
    for k in range(4):
        tasks[f"nt{k}"] = functools.partial(norm_first, k)
        tasks[f"na{k}"] = functools.partial(norm_core, k)
    for stage in range(6):
        tasks[f"v{stage}"] = functools.partial(tiny, stage)

    normed_load(0).start()
    spot = 0
    while spot < len(PLAN):
        name = PLAN[spot]
        if name[0] != "L":
            tasks[name]()
            spot += 1
            continue
        h, step, hooks = int(name[1]), -1, {}
        while step < 7 or PLAN[spot][0] == "L":
            if PLAN[spot][0] == "L":
                step = int(PLAN[spot][2])
                if step == 7:
                    spot += 1
                    break
            else:
                hooks.setdefault(step, []).append(tasks[PLAN[spot]])
            spot += 1
        attend_head(h, hooks)

    def sent(block, carry):
        own_in = jnp.logical_and(mine, block == at.group)

        @pl.when(jnp.logical_not(own_in))
        def _():
            for h in range(2):
                grad_copy(block, h).wait_send()

        return carry

    lax.fori_loop(0, 8, sent, 0)
    for m in range(3):
        for stage in range(7):
            main_copy(stage, m).wait_send()
    for h in range(2):
        for stage in range(6):
            head_copy(stage, h).wait_send()
    for k in range(2):
        norm_copy(1, k).wait_send()
        norm_copy(2, k).wait_send()
    norm_copy(3, 0).wait_send()

    @pl.when(jnp.logical_not(mine))
    def _():
        norm_copy(3, 1).wait_send()


def sum_slots():
    slots = []
    for ways in SUM_WAYS:
        shape, own = [2, 320, 1280], []
        for way in ways:
            if way == "y":
                shape = shape[1:]
            else:
                shape[-1 if way == "h" else -2] //= 2
            own.append(pltpu.VMEM(tuple(shape), BF))
        slots.append(own)
    return slots


def backward(*args):
    shape = jax.ShapeDtypeStruct
    dma = pltpu.SemaphoreType.DMA
    specs = [VMEM_SPEC] * 17
    specs[11] = pl.BlockSpec(memory_space=pl.ANY)
    return pl.pallas_call(
        backward_kernel,
        name="backward",
        out_shape=(
            shape((320, 1280), BF),
            shape((320, 1280), BF),
            shape((320, 1280), BF),
            shape((320, 3840), BF),
            shape((256, 1280), F32),
            shape((8, LANES), F32),
        ),
        in_specs=specs,
        out_specs=(VMEM_SPEC,) * 6,
        scratch_shapes=[
            pltpu.VMEM((2, 128, 2048), BF),
            pltpu.VMEM((2048, LANES), F32),
            pltpu.VMEM((2, 128, 2048), BF),
            pltpu.VMEM((8, 2048), F32),
            pltpu.VMEM((2048, LANES), F32),
            pltpu.VMEM((2048, LANES), F32),
            pltpu.VMEM((768, 2048), BF),
            pltpu.VMEM((2, 2048, 256), BF),
            pltpu.VMEM((4, 2, 640, 256), BF),
            pltpu.VMEM((2, 2, 640, 256), BF),
            pltpu.VMEM((2, 640, 256), BF),
            pltpu.VMEM((2, 640, 256), BF),
            pltpu.VMEM((1920, 1280), BF),
            pltpu.VMEM((3, 2, 320, 1280), BF),
            sum_slots(),
            pltpu.VMEM((2, 256, 1280), BF),
            pltpu.VMEM((2, 256, 640), BF),
            pltpu.VMEM((2, 128, 640), BF),
            pltpu.VMEM((2, 2, 2, 2, 256, 640), BF),
            pltpu.VMEM((640, LANES), BF),
            pltpu.VMEM((5, 8, LANES), F32),
            dma((8, 2)),
            dma((8, 2)),
            dma((4,)),
            dma((9, 3)),
            dma((9, 3)),
            dma((6, 2)),
            dma((6, 2)),
            dma((4, 2)),
            dma((4, 2)),
            dma((4, 4)),
            dma((4, 4)),
            dma((5,)),
            dma((5,)),
        ],
        compiler_params=pltpu.CompilerParams(
            collective_id=1, has_side_effects=True, vmem_limit_bytes=VMEM_LIMIT
        ),
        cost_estimate=pl.CostEstimate(
            flops=30_000_000_000, bytes_accessed=60_000_000, transcendentals=8_400_000
        ),
    )(*args)


def fast_body(
    tokens,
    lengths,
    position,
    qkv_weight,
    out_weight,
    up_weight,
    down_weight,
    attn_gain,
    mlp_gain,
    query_scale,
    cotangent,
):
    f = lax.axis_index("fsdp")
    x, dy = tokens[0], cotangent[0]
    small = [jnp.pad(a, (0, 384 - a.shape[0])) for a in (attn_gain, mlp_gain, query_scale)]
    small = jnp.stack(small + [jnp.zeros((384,), BF)] * 13)
    (
        att_t, normed, qkv, lse, out, auxsum, place, w_heads,
        result, resid_grad, branch_grad, up_grad, act_t, normed_mlp_t, grad_t,
    ) = forward(
        lengths, x, qkv_weight, small, position, out_weight, up_weight, down_weight, dy
    )
    scale_float = auxsum[2, :80]
    base_scale = LOG2E / math.sqrt(80)
    soft = jax.nn.softplus(scale_float)
    mult = jnp.broadcast_to(jnp.pad(base_scale * soft, (0, 48))[:, None], (LANES, LANES))
    g_down, g_up, g_out, g_qkv, input_grad, scale_sum = backward(
        grad_t,
        att_t,
        branch_grad,
        normed_mlp_t,
        up_grad,
        act_t,
        dy,
        qkv,
        lse,
        out,
        place,
        normed,
        w_heads,
        mult,
        x,
        resid_grad,
        auxsum,
    )
    g_down, g_up, g_out = (g.astype(F32) for g in (g_down, g_up, g_out))
    g_qkv = g_qkv.astype(F32)
    grad_attn_gain = jnp.sum(qkv_weight.astype(F32) * g_qkv, axis=1) / attn_gain.astype(F32)
    grad_mlp_gain = jnp.sum(up_weight.astype(F32) * g_up, axis=1) / mlp_gain.astype(F32)
    grad_scale = scale_sum[0, :80] / soft * jax.nn.sigmoid(scale_float)
    return (
        result[None],
        input_grad[None],
        g_qkv,
        g_out,
        g_up,
        g_down,
        grad_attn_gain,
        grad_mlp_gain,
        lax.dynamic_slice_in_dim(grad_scale, f * 20, 20),
    )


def solution(mesh):
    placed = (
        P("fsdp", "ctx", None),
        P("fsdp", None),
        P("fsdp", None),
        P("fsdp", None),
        P("fsdp", None),
        P("fsdp", None),
        P("fsdp", None),
        P("fsdp"),
        P("fsdp"),
        P("fsdp"),
        P("fsdp", "ctx", None),
    )
    fits = mesh.shape["ctx"] == 8 and mesh.shape["fsdp"] == 4
    return jax.shard_map(
        fast_body if fits else body,
        mesh=mesh,
        in_specs=placed,
        out_specs=(
            P("fsdp", "ctx", None),
            P("fsdp", "ctx", None),
            P("fsdp", None),
            P("fsdp", None),
            P("fsdp", None),
            P("fsdp", None),
            P("fsdp"),
            P("fsdp"),
            P("fsdp"),
        ),
        check_vma=False,
    )
```

```python
import functools
import math

import jax
import jax.numpy as jnp
from jax import lax
from jax.experimental import pallas as pl
from jax.experimental.pallas import tpu as pltpu
from jax.sharding import PartitionSpec as P

HEADS = 16


EPS = 1e-06
FLOOR = -1e30
LOG2E = 1.442695041

MESH = pl.DeviceIdType.MESH
LANES = 128
BF = jnp.bfloat16
F32 = jnp.float32
VMEM_SPEC = pl.BlockSpec(memory_space=pltpu.VMEM)
ANY_SPEC = pl.BlockSpec(memory_space=pl.ANY)
VMEM_LIMIT = 60 << 20


def flip(number, mask):
    total = 0
    for bit in (1, 2, 4):
        left = (number // bit) % 2
        right = (mask // bit) % 2
        total = total + bit * (left + right - 2 * left * right)
    return total


class Place:
    def __init__(self):
        self.c = lax.axis_index("ctx")
        self.f = lax.axis_index("fsdp")
        self.core = self.f % 2
        self.plane = self.f - self.core
        self.half = self.c // 4
        self.pack = self.plane + self.half
        self.group = (self.c % 4) * 2 + self.core
        self.twin = self.plane + 1 - self.core
        self.across = (self.f + 2) % 4


def dev(ctx, fsdp):
    return {"ctx": ctx, "fsdp": fsdp}


def send(src, dst, send_sem, recv_sem, device):
    copy = pltpu.make_async_remote_copy(
        src_ref=src,
        dst_ref=dst,
        send_sem=send_sem,
        recv_sem=recv_sem,
        device_id=device,
        device_id_type=MESH,
    )
    copy.start()
    return copy


def await_recv(ref, sem):
    pltpu.make_async_copy(ref, ref, sem).wait()


def meet_plane(at):
    barrier = pltpu.get_barrier_semaphore()

    def greet(k, carry):
        pl.semaphore_signal(
            barrier,
            1,
            device_id=dev((at.c + k // 2) % 8, at.plane + (at.core + k) % 2),
            device_id_type=MESH,
        )
        return carry

    lax.fori_loop(1, 16, greet, 0)
    for k in range(2):
        pl.semaphore_signal(
            barrier, 1, device_id=dev(at.c, (at.plane + 2) % 4 + k), device_id_type=MESH
        )
    pl.semaphore_wait(barrier, 17)


def span(start, size, unit):
    return pl.ds(pl.multiple_of(start, unit), size)


def doc_index(places, seq_ends):
    return jnp.sum((places[:, None] >= seq_ends[None, :]).astype(jnp.int32), axis=1)


def spread_position(gathered_index, tok_dev, cycle_size):
    return gathered_index % tok_dev * cycle_size + gathered_index // tok_dev


def pair_scores(left_rows, right_rows):
    return jnp.einsum(
        "qhd,khd->qhk",
        left_rows.reshape(left_rows.shape[0], HEADS, -1),
        right_rows.reshape(right_rows.shape[0], HEADS, -1),
        preferred_element_type=jnp.float32,
    )


def pair_mask(query_pos, query_doc, key_pos, key_doc):
    return ((query_doc[:, None] == key_doc[None, :]) & (key_pos[None, :] <= query_pos[:, None]))[
        :, None, :
    ]


def in_blocks(advance, carried, pieces):
    total_rows = pieces[0].shape[0]
    block_rows = math.gcd(total_rows, 1024)
    block_count = total_rows // block_rows
    split = tuple((p.reshape((block_count, block_rows) + p.shape[1:]) for p in pieces))

    def inner(running, entry):
        return (advance(running, entry[1], entry[0] * block_rows), None)

    result, unused = lax.scan(inner, carried, (jnp.arange(block_count, dtype=jnp.int32), split))
    return result


def pair_terms(
    query_part,
    grad_part,
    log_part,
    delta_part,
    query_pos,
    query_doc,
    key_part,
    value_part,
    key_pos,
    key_doc,
):
    visible = pair_mask(query_pos, query_doc, key_pos, key_doc)
    prob_float = jnp.where(
        visible, jnp.exp(pair_scores(query_part, key_part) - log_part[:, :, None]), 0.0
    )
    grad_probs = pair_scores(grad_part, value_part)
    score_grad = (prob_float * (grad_probs - delta_part[:, :, None])).astype(jnp.bfloat16)
    return (prob_float.astype(jnp.bfloat16), score_grad)


def body(
    tokens,
    lengths,
    position,
    qkv_weight,
    out_weight,
    up_weight,
    down_weight,
    attn_gain,
    mlp_gain,
    query_scale,
    cotangent,
):
    cycle_size = lax.axis_size("ctx")
    my_index = lax.axis_index("ctx")
    tok_dev = tokens.shape[1]
    share_rows = tok_dev // cycle_size
    seq_ends = jnp.cumsum(lengths[0])
    place_row = position[0]
    residue = (place_row % cycle_size).reshape(cycle_size, tok_dev)
    landing = place_row // cycle_size
    matches = (
        residue[:, :, None] == jnp.arange(cycle_size, dtype=jnp.int32)[None, None, :]
    ).astype(jnp.int32)
    ranked = jnp.sum(jnp.cumsum(matches, axis=1) * matches, axis=2) - 1
    buffer_slot = residue * share_rows + ranked
    my_slots = lax.dynamic_index_in_dim(buffer_slot, my_index, 0, keepdims=False)
    local_rows = jnp.arange(tok_dev, dtype=jnp.int32)
    outgoing = jnp.zeros((tok_dev,), jnp.int32).at[my_slots].set(local_rows)
    flat_slot = (jnp.arange(cycle_size, dtype=jnp.int32)[:, None] * tok_dev + buffer_slot).reshape(
        -1
    )
    landing_table = (
        jnp.zeros((cycle_size * tok_dev,), jnp.int32)
        .at[flat_slot]
        .set(landing)
        .reshape(cycle_size, cycle_size, share_rows)
    )
    arrived_slot = lax.dynamic_index_in_dim(landing_table, my_index, 1, keepdims=False).reshape(-1)
    arrived_order = jnp.zeros((tok_dev,), jnp.int32).at[arrived_slot].set(local_rows)
    moved_x, moved_dy = (
        lax.all_to_all(tokens[0][outgoing], "ctx", split_axis=0, concat_axis=0, tiled=True),
        lax.all_to_all(cotangent[0][outgoing], "ctx", split_axis=0, concat_axis=0, tiled=True),
    )
    dealt_x = moved_x[arrived_order]
    dealt_dy = moved_dy[arrived_order]
    query_pos = local_rows * cycle_size + my_index
    query_doc = doc_index(query_pos, seq_ends)
    full_qkv, full_out, full_up, full_down, attn_gain_full, mlp_gain_full, scale_full = (
        lax.all_gather(qkv_weight, "fsdp", axis=0, tiled=True),
        lax.all_gather(out_weight, "fsdp", axis=0, tiled=True),
        lax.all_gather(up_weight, "fsdp", axis=0, tiled=True),
        lax.all_gather(down_weight, "fsdp", axis=0, tiled=True),
        lax.all_gather(attn_gain, "fsdp", axis=0, tiled=True),
        lax.all_gather(mlp_gain, "fsdp", axis=0, tiled=True),
        lax.all_gather(query_scale, "fsdp", axis=0, tiled=True),
    )
    attn_gain_f = attn_gain_full.astype(jnp.float32)
    mlp_gain_f = mlp_gain_full.astype(jnp.float32)
    scale_float = scale_full.astype(jnp.float32)
    x_float = dealt_x.astype(jnp.float32)
    inv_attn = lax.rsqrt(jnp.mean(x_float * x_float, axis=1, keepdims=True) + EPS)
    normed_attn = (x_float * inv_attn * attn_gain_f).astype(jnp.bfloat16)
    projected = jnp.dot(normed_attn, full_qkv, preferred_element_type=jnp.float32)
    att_width = projected.shape[1] // 3
    head_dim = scale_full.shape[0]
    base_scale = LOG2E / math.sqrt(head_dim)
    multiplier = jnp.tile(base_scale * jax.nn.softplus(scale_float), att_width // head_dim)
    raw_query = projected[:, :att_width]
    queries = (raw_query * multiplier).astype(jnp.bfloat16)
    key_rows = projected[:, att_width : 2 * att_width].astype(jnp.bfloat16)
    value_rows = projected[:, 2 * att_width :].astype(jnp.bfloat16)

    def key_place(first_row, amount):
        gathered_index = first_row + jnp.arange(amount, dtype=jnp.int32)
        key_pos = spread_position(gathered_index, tok_dev, cycle_size)
        return (key_pos, doc_index(key_pos, seq_ends))

    def stat_block(carried, pieces, first_row):
        running_max, running_sum = carried
        key_pos, key_doc = key_place(first_row, pieces[0].shape[0])
        visible = pair_mask(query_pos, query_doc, key_pos, key_doc)
        logits = jnp.where(visible, pair_scores(queries, pieces[0]), FLOOR)
        new_max = jnp.maximum(running_max, jnp.max(logits, axis=2))
        added = jnp.sum(jnp.where(visible, jnp.exp(logits - new_max[:, :, None]), 0.0), axis=2)
        return (new_max, running_sum * jnp.exp(running_max - new_max) + added)

    def output_block(summed, pieces, first_row):
        key_pos, key_doc = key_place(first_row, pieces[0].shape[0])
        visible = pair_mask(query_pos, query_doc, key_pos, key_doc)
        prob_low = jnp.where(
            visible, jnp.exp(pair_scores(queries, pieces[0]) - log_total[:, :, None]), 0.0
        ).astype(jnp.bfloat16)
        values_part = pieces[1].reshape(pieces[1].shape[0], HEADS, -1)
        return summed + jnp.einsum(
            "qhk,khd->qhd", prob_low, values_part, preferred_element_type=jnp.float32
        ).reshape(summed.shape)

    def query_grad_block(summed, pieces, first_row):
        key_pos, key_doc = key_place(first_row, pieces[0].shape[0])
        unused_probs, score_grad = pair_terms(
            queries,
            attended_grad,
            log_total,
            row_delta,
            query_pos,
            query_doc,
            pieces[0],
            pieces[1],
            key_pos,
            key_doc,
        )
        keys_part = pieces[0].reshape(pieces[0].shape[0], HEADS, -1)
        return summed + jnp.einsum(
            "qhk,khd->qhd", score_grad, keys_part, preferred_element_type=jnp.float32
        ).reshape(summed.shape)

    def key_grad_block(carried, pieces, first_row):
        amount = pieces[0].shape[0]
        part_pos, part_doc = key_place(first_row, amount)
        part_log = lax.dynamic_slice_in_dim(all_log, first_row, amount, 0)
        part_delta = lax.dynamic_slice_in_dim(all_delta, first_row, amount, 0)
        prob_low, score_grad = pair_terms(
            pieces[0],
            pieces[1],
            part_log,
            part_delta,
            part_pos,
            part_doc,
            key_rows,
            value_rows,
            query_pos,
            query_doc,
        )
        grad_keys = carried[0] + jnp.einsum(
            "qhk,qhd->khd",
            score_grad,
            pieces[0].reshape(amount, HEADS, -1),
            preferred_element_type=jnp.float32,
        ).reshape(tok_dev, -1)
        grad_values = carried[1] + jnp.einsum(
            "qhk,qhd->khd",
            prob_low,
            pieces[1].reshape(amount, HEADS, -1),
            preferred_element_type=jnp.float32,
        ).reshape(tok_dev, -1)
        return (grad_keys, grad_values)

    zero_stats = (
        jnp.full((tok_dev, HEADS), FLOOR, jnp.float32),
        jnp.zeros((tok_dev, HEADS), jnp.float32),
    )
    zero_rows = jnp.zeros((tok_dev, att_width), jnp.float32)
    running_max, running_sum = in_blocks(
        stat_block, zero_stats, (lax.all_gather(key_rows, "ctx", axis=0, tiled=True),)
    )
    log_total = running_max + jnp.log(running_sum)
    attended = in_blocks(
        output_block,
        zero_rows,
        (
            lax.all_gather(key_rows, "ctx", axis=0, tiled=True),
            lax.all_gather(value_rows, "ctx", axis=0, tiled=True),
        ),
    )
    attended_low = attended.astype(jnp.bfloat16)
    resid = x_float + jnp.dot(attended_low, full_out, preferred_element_type=jnp.float32)
    inv_mlp = lax.rsqrt(jnp.mean(resid * resid, axis=1, keepdims=True) + EPS)
    normed_mlp = (resid * inv_mlp * mlp_gain_f).astype(jnp.bfloat16)
    up_proj = jnp.dot(normed_mlp, full_up, preferred_element_type=jnp.float32)
    act_low = jax.nn.silu(up_proj).astype(jnp.bfloat16)
    result = resid + jnp.dot(act_low, full_down, preferred_element_type=jnp.float32)
    cot_float = dealt_dy.astype(jnp.float32)
    grad_down = jnp.dot(act_low.T, dealt_dy, preferred_element_type=jnp.float32)
    act_grad = jnp.dot(dealt_dy, full_down.T, preferred_element_type=jnp.float32)
    sigma = jax.nn.sigmoid(up_proj)
    up_grad = (act_grad * sigma * (1.0 + up_proj * (1.0 - sigma))).astype(jnp.bfloat16)
    grad_up = jnp.dot(normed_mlp.T, up_grad, preferred_element_type=jnp.float32)
    norm_mlp_grad = jnp.dot(up_grad, full_up.T, preferred_element_type=jnp.float32)
    grad_mlp_gain = jnp.sum(norm_mlp_grad * resid * inv_mlp, axis=0)
    scaled_mlp = norm_mlp_grad * mlp_gain_f
    resid_grad = cot_float + inv_mlp * (
        scaled_mlp - resid * inv_mlp * inv_mlp * jnp.mean(scaled_mlp * resid, axis=1, keepdims=True)
    )
    branch_grad = resid_grad.astype(jnp.bfloat16)
    grad_out = jnp.dot(attended_low.T, branch_grad, preferred_element_type=jnp.float32)
    attended_grad = jnp.dot(branch_grad, full_out.T, preferred_element_type=jnp.float32).astype(
        jnp.bfloat16
    )
    row_delta = jnp.sum(
        (attended_grad.astype(jnp.float32) * attended).reshape(tok_dev, HEADS, -1), axis=2
    )
    query_grads = in_blocks(
        query_grad_block,
        zero_rows,
        (
            lax.all_gather(key_rows, "ctx", axis=0, tiled=True),
            lax.all_gather(value_rows, "ctx", axis=0, tiled=True),
        ),
    )
    all_log, all_delta = (
        lax.all_gather(log_total, "ctx", axis=0, tiled=True),
        lax.all_gather(row_delta, "ctx", axis=0, tiled=True),
    )
    key_grad_f, value_grad_f = in_blocks(
        key_grad_block,
        (zero_rows, zero_rows),
        (
            lax.all_gather(queries, "ctx", axis=0, tiled=True),
            lax.all_gather(attended_grad, "ctx", axis=0, tiled=True),
        ),
    )
    scale_terms = jnp.sum((query_grads * raw_query).reshape(tok_dev, -1, head_dim), axis=(0, 1))
    grad_scale = scale_terms * base_scale * jax.nn.sigmoid(scale_float)
    proj_grad = jnp.concatenate(
        [
            (query_grads * multiplier).astype(jnp.bfloat16),
            key_grad_f.astype(jnp.bfloat16),
            value_grad_f.astype(jnp.bfloat16),
        ],
        axis=1,
    )
    grad_qkv = jnp.dot(normed_attn.T, proj_grad, preferred_element_type=jnp.float32)
    norm_attn_grad = jnp.dot(proj_grad, full_qkv.T, preferred_element_type=jnp.float32)
    grad_attn_gain = jnp.sum(norm_attn_grad * x_float * inv_attn, axis=0)
    scaled_attn = norm_attn_grad * attn_gain_f
    input_grad = resid_grad + inv_attn * (
        scaled_attn
        - x_float * inv_attn * inv_attn * jnp.mean(scaled_attn * x_float, axis=1, keepdims=True)
    )
    owned = (
        lax.psum_scatter(grad_qkv, "fsdp", scatter_dimension=0, tiled=True),
        lax.psum_scatter(grad_out, "fsdp", scatter_dimension=0, tiled=True),
        lax.psum_scatter(grad_up, "fsdp", scatter_dimension=0, tiled=True),
        lax.psum_scatter(grad_down, "fsdp", scatter_dimension=0, tiled=True),
        lax.psum_scatter(grad_attn_gain, "fsdp", scatter_dimension=0, tiled=True),
        lax.psum_scatter(grad_mlp_gain, "fsdp", scatter_dimension=0, tiled=True),
        lax.psum_scatter(grad_scale, "fsdp", scatter_dimension=0, tiled=True),
    )
    summed_grads = lax.psum(
        (owned[0], owned[1], owned[2], owned[3], owned[4], owned[5], owned[6]), "ctx"
    )
    back_out, back_grad = (
        lax.all_to_all(result[arrived_slot], "ctx", split_axis=0, concat_axis=0, tiled=True),
        lax.all_to_all(input_grad[arrived_slot], "ctx", split_axis=0, concat_axis=0, tiled=True),
    )
    return (
        back_out[my_slots][None],
        back_grad[my_slots][None],
        summed_grads[0],
        summed_grads[1],
        summed_grads[2],
        summed_grads[3],
        summed_grads[4],
        summed_grads[5],
        summed_grads[6],
    )


WEIGHT_STEPS = ((0, 2, 1), (2, 3, 0), (3, 2, 2), (6, 3, 1))


def attend_kernel(
    ends_ref,
    x_ref,
    w_ref,
    aux_ref,
    pos_ref,
    out_w_ref,
    up_w_ref,
    down_w_ref,
    dy_ref,
    att_ref,
    normed_out,
    qkv_out,
    lse_ref,
    out_ref,
    auxsum_ref,
    place_ref,
    w_out,
    result_ref,
    resid_grad_ref,
    branch_ref,
    up_grad_ref,
    act_ref,
    normed_mlp_ref,
    grad_ref,
    x_mine,
    w_mine,
    dy_mine,
    x_all,
    normed_ref,
    qkv_ref,
    w_all,
    w_own,
    w_small,
    weights,
    aux_all,
    pos_all,
    v_turned,
    key_pos,
    att_send,
    x_send_sem,
    x_recv_sem,
    w_send_sem,
    w_recv_sem,
    aux_send_sem,
    aux_recv_sem,
    pos_sem,
    att_send_sem,
    att_recv_sem,
    m_send_sem,
    m_recv_sem,
    local_sem,
    save_sem,
    shard_sem,
):
    w_load = pltpu.make_async_copy(w_ref, w_mine, local_sem.at[0])
    w_load.start()
    x_load = pltpu.make_async_copy(x_ref, x_mine, local_sem.at[2])
    dy_load = pltpu.make_async_copy(dy_ref, dy_mine, local_sem.at[4])
    at = Place()
    meet_plane(at)
    c, f = at.c, at.f
    hub = at.core == at.half

    aux_own = pltpu.make_async_copy(aux_ref, aux_all.at[f], local_sem.at[1])
    aux_own.start()
    x_own = pltpu.make_async_copy(x_ref, x_all.at[c], local_sem.at[3])

    x_far = pltpu.make_async_remote_copy(
        src_ref=x_ref,
        dst_ref=x_all.at[c],
        send_sem=x_send_sem.at[0, 0],
        recv_sem=x_recv_sem.at[c],
        device_id=dev(flip(c, 4), f),
        device_id_type=MESH,
    )

    @pl.when(hub)
    def _():
        x_own.start()
        for k, where in enumerate((dev(flip(c, 1), f), dev(flip(c, 2), f), dev(c, at.twin))):
            send(x_ref, x_all.at[c], x_send_sem.at[0, k], x_recv_sem.at[c], where)

    @pl.when(jnp.logical_not(hub))
    def _():
        x_far.start()

    w_copies, aux_copies = [], []
    for k in (2, 1, 3):
        aux_copies.append(
            send(
                aux_ref,
                aux_all.at[f],
                aux_send_sem.at[k],
                aux_recv_sem.at[f],
                dev(c, (f + k) % 4),
            )
        )

    pos = pos_ref[...]
    start = jnp.zeros_like(pos)
    end = 0
    for k in range(4):
        end = end + ends_ref[0, k]
        start = jnp.where(pos >= end, end, start)
    pos_all[at.core, 0:1, :] = pos.astype(F32)
    pos_all[at.core, 1:2, :] = start.astype(F32)
    pos_all[at.core, 2:8, :] = jnp.zeros((6, 2048), F32)
    pos_copy = send(
        pos_all.at[at.core], pos_all.at[at.core], pos_sem.at[0], pos_sem.at[1], dev(c, at.twin)
    )

    row = lax.broadcasted_iota(jnp.int32, (1280, 512), 0)
    column = lax.broadcasted_iota(jnp.int32, (1280, 512), 1)
    first = (c % 4) * 320
    w_load.wait()
    for k in range(2):
        some = jnp.zeros((320, 512), F32)
        for j in range(3):
            pick = (row - first - k * 160 == column - j * 160) & (column // 160 == j)
            pick = jnp.where(pick, 1.0, 0.0).astype(BF)
            some += jnp.dot(w_mine[:, j * 1280 : (j + 1) * 1280], pick, preferred_element_type=F32)
        w_own[k] = some.astype(BF)
    mine_rows = span(f * 320, 320, 320)
    for k in (2, 3, 1):
        to = (f + k) % 4
        w_copies.append(
            send(
                w_own.at[to % 2],
                w_small.at[mine_rows],
                w_send_sem.at[k],
                w_recv_sem.at[f],
                dev(c, to),
            )
        )
    w_small[mine_rows, :] = w_own[at.core]
    x_load.start()
    dy_load.start()


    shards = (out_w_ref, up_w_ref, down_w_ref)
    xbit = c % 2
    other = (f + 2) % 4

    def part(m, owner, x):
        return weights.at[m, span(owner * 320 + x * 160, 160, 160)]

    def weight_copy(m, way):
        if way == 0:
            src, dst, to = shards[m], weights.at[m, mine_rows], dev(c, at.twin)
        elif way == 1:
            src = shards[m].at[span(xbit * 160, 160, 160)]
            dst, to = part(m, f, xbit), dev(c, other)
        else:
            x = (xbit, xbit, 1 - xbit)[way - 2]
            src = dst = part(m, other, x)
            to = (dev(flip(c, 1), f), dev(c, at.twin), dev(c, at.twin))[way - 2]
        return pltpu.make_async_remote_copy(
            src_ref=src,
            dst_ref=dst,
            send_sem=m_send_sem.at[m, way],
            recv_sem=m_recv_sem.at[m, way],
            device_id=to,
            device_id_type=MESH,
        )

    def shard_copy(m):
        return pltpu.make_async_copy(shards[m], weights.at[m, mine_rows], shard_sem.at[m])

    def weight_first(m):
        weight_copy(m, 0).start()
        weight_copy(m, 1).start()
        shard_copy(m).start()

    def weight_second(m):
        weight_copy(m, 1).wait_recv()
        weight_copy(m, 2).start()
        weight_copy(m, 3).start()

    def weight_third(m):
        weight_copy(m, 2).wait_recv()
        weight_copy(m, 4).start()

    def weight_last(m):
        shard_copy(m).wait()
        for way in (0, 3, 4):
            weight_copy(m, way).wait_recv()

    weight_first(0)

    aux_own.wait()
    for k in (1, 2, 3):
        await_recv(aux_all.at[0], aux_recv_sem.at[(f + k) % 4])
    aux = jnp.zeros((16, 1280), F32)
    scale = jnp.zeros((16, LANES), F32)
    row = lax.broadcasted_iota(jnp.int32, (384, 1280), 0)
    column = lax.broadcasted_iota(jnp.int32, (384, 1280), 1)
    for k in range(4):
        put = jnp.where((column == row + k * 320) & (row < 320), 1.0, 0.0).astype(BF)
        aux = aux + jnp.dot(aux_all[k], put, preferred_element_type=F32)
        put = (column[:LANES, :LANES] == row[:LANES, :LANES] + k * 20) & (row[:LANES, :LANES] < 20)
        put = jnp.where(put, 1.0, 0.0).astype(BF)
        scale = scale + jnp.dot(aux_all[k, :, :LANES], put, preferred_element_type=F32)
    auxsum_ref[...] = aux
    auxsum_ref[2:3, :LANES] = scale[2:3]
    gain = aux[0:1, :]
    mlp_gain = aux[1:2, :]
    scale = scale[2:3]
    real = lax.broadcasted_iota(jnp.int32, (1, LANES), 1) < 80
    mult = jnp.where(
        real, LOG2E / math.sqrt(80) * (jnp.maximum(scale, 0.0) + jnp.log1p(jnp.exp(-jnp.abs(scale)))), 0.0
    )
    one = jnp.ones_like(mult)
    mults = jnp.concatenate([mult, mult, one, one, one, one], axis=1)

    await_recv(pos_all.at[0], pos_sem.at[1])
    place_ref[...] = pos_all[at.half]
    for k in range(8):
        block = place_ref[0:1, k * 256 : (k + 1) * 256]
        key_pos[k * 256 : (k + 1) * 256, :] = jnp.transpose(
            jnp.broadcast_to(block, (LANES, 256))
        )

    def arrive(step, carry):
        slot = flip(c, step)

        @pl.when(jnp.logical_and(hub, step == 0))
        def _():
            x_own.wait()

        @pl.when(jnp.logical_not(jnp.logical_and(hub, step == 0)))
        def _():
            await_recv(x_all.at[slot], x_recv_sem.at[slot])

        def onward(way, where):
            send(
                x_all.at[slot],
                x_all.at[slot],
                x_send_sem.at[step, way],
                x_recv_sem.at[slot],
                where,
            )

        @pl.when(jnp.logical_and(hub, jnp.logical_or(step == 4, step == 6)))
        def _():
            onward(0, dev(flip(c, 1), f))

        @pl.when(jnp.logical_and(hub, jnp.logical_or(step == 4, step == 1)))
        def _():
            onward(1, dev(flip(c, 2), f))

        @pl.when(jnp.logical_and(hub, step > 0))
        def _():
            onward(2, dev(c, at.twin))

        @pl.when(step == 5)
        def _():
            weight_first(1)

        xf = x_all[slot].astype(F32)
        inv = lax.rsqrt(jnp.mean(xf * xf, axis=1, keepdims=True) + EPS)
        rows = span(slot * 256, 256, 256)
        normed_ref[rows, :] = (xf * inv * gain).astype(BF)
        pltpu.make_async_copy(
            normed_ref.at[rows], normed_out.at[rows], save_sem.at[slot, 0]
        ).start()
        return carry

    def project(step, carry):
        slot = flip(c, step)
        rows = span(slot * 256, 256, 256)
        proj = jnp.dot(normed_ref[rows, :], w_all[...], preferred_element_type=F32)
        qkv_ref[rows, :] = (proj * mults).astype(BF)
        pltpu.make_async_copy(qkv_ref.at[rows], qkv_out.at[rows], save_sem.at[slot, 1]).start()
        return carry

    lax.fori_loop(0, 7, arrive, 0)
    for k in (1, 2, 3):
        await_recv(w_small.at[pl.ds(0, 320)], w_recv_sem.at[(f + k) % 4])
    weight_first(2)
    weight_second(0)
    row = lax.broadcasted_iota(jnp.int32, (512, 768), 0)
    column = lax.broadcasted_iota(jnp.int32, (512, 768), 1)
    spread = (row == column // LANES * 80 + column % LANES) & (column % LANES < 80)
    spread = jnp.where(spread, 1.0, 0.0).astype(BF)
    w_all[...] = jnp.dot(w_small[...], spread, preferred_element_type=F32).astype(BF)
    w_save = pltpu.make_async_copy(w_all, w_out, local_sem.at[5])
    w_save.start()
    lax.fori_loop(0, 5, project, 0)
    lax.fori_loop(7, 8, arrive, 0)
    lax.fori_loop(5, 8, project, 0)

    for h in range(2):
        v_turned[h] = jnp.transpose(qkv_ref[:, (4 + h) * LANES : (5 + h) * LANES])

    att_own = pltpu.make_async_copy(
        att_send.at[c], att_ref.at[span(at.group * 160, 160, 160)], local_sem.at[3]
    )

    def att_copy(block):
        return pltpu.make_async_remote_copy(
            src_ref=att_send.at[block],
            dst_ref=att_ref.at[span(at.group * 160, 160, 160)],
            send_sem=att_send_sem.at[block],
            recv_sem=att_recv_sem.at[at.group],
            device_id=dev(block, at.pack),
            device_id_type=MESH,
        )

    mine = at.core == at.half

    def attend(step, carry):
        block = flip(c, 7 - step)
        lanes = span(block * 256, 256, 256)
        high = place_ref[0:1, lanes]
        least = place_ref[1:2, lanes]
        for h in range(2):
            query = qkv_ref[lanes, h * LANES : (h + 1) * LANES]
            scores, top = [], None
            for part in range(2):
                rows = slice(part * 1024, (part + 1) * 1024)
                kp = key_pos[rows, :]
                kp = jnp.concatenate([kp, kp], axis=1)
                keys = qkv_ref[rows, (2 + h) * LANES : (3 + h) * LANES]
                s = lax.dot_general(
                    keys, query, (((1,), (1,)), ((), ())), preferred_element_type=F32
                )
                s = jnp.where((kp >= least) & (kp <= high), s, FLOOR)
                scores.append(s)
                most = jnp.max(s, axis=0, keepdims=True)
                top = most if top is None else jnp.maximum(top, most)
            total = jnp.zeros((1, 256), F32)
            o = jnp.zeros((LANES, 256), F32)
            for part in range(2):
                p = jnp.exp(scores[part] - top)
                total += jnp.sum(p, axis=0, keepdims=True)
                values = v_turned[h, :, part * 1024 : (part + 1) * 1024]
                o += jnp.dot(values, p.astype(BF), preferred_element_type=F32)
            o = o[:80] / total
            lse_ref[h : h + 1, lanes] = top + jnp.log(total)
            out_ref[h * 80 : (h + 1) * 80, lanes] = o.astype(BF)
            att_send[block, h * 80 : (h + 1) * 80, :] = o.astype(BF)

        @pl.when(jnp.logical_and(mine, step == 7))
        def _():
            att_own.start()

        @pl.when(jnp.logical_not(jnp.logical_and(mine, step == 7)))
        def _():
            att_copy(block).start()

        for when, todo, m in WEIGHT_STEPS:

            @pl.when(step == when)
            def _(todo=todo, m=m):
                (weight_second if todo == 2 else weight_third)(m)

        return carry

    lax.fori_loop(0, 8, attend, 0)
    weight_third(2)
    lse_ref[2:8, :] = jnp.zeros((6, 2048), F32)

    def land(block, carry):
        @pl.when(jnp.logical_not(jnp.logical_and(mine, block == at.group)))
        def _():
            await_recv(att_ref.at[pl.ds(0, 160)], att_recv_sem.at[block])

        return carry

    @pl.when(mine)
    def _():
        att_own.wait()

    weight_last(0)
    lax.fori_loop(0, 8, land, 0)

    def across(left, right):
        return lax.dot_general(
            left, right, (((1,), (1,)), ((), ())), preferred_element_type=F32
        )

    x_load.wait()
    dy_load.wait()
    xf = x_mine[...].astype(F32)
    resid = xf + jnp.dot(jnp.transpose(att_ref[...]), weights[0], preferred_element_type=F32)
    inv = lax.rsqrt(jnp.mean(resid * resid, axis=1, keepdims=True) + EPS)
    normed_mlp = (resid * inv * mlp_gain).astype(BF)
    normed_mlp_ref[...] = jnp.transpose(normed_mlp)
    weight_last(1)
    up = jnp.dot(normed_mlp, weights[1], preferred_element_type=F32)
    sigma = 1.0 / (1.0 + jnp.exp(-up))
    act = (up * sigma).astype(BF)
    act_ref[...] = jnp.transpose(act)
    slope = sigma * (1.0 + up * (1.0 - sigma))
    weight_last(2)
    dy = dy_mine[...]
    up_grad = (across(dy, weights[2]) * slope).astype(BF)
    up_grad_ref[...] = up_grad
    scaled = across(up_grad, weights[1]) * mlp_gain
    resid_grad = dy.astype(F32) + inv * (
        scaled - resid * inv * inv * jnp.mean(scaled * resid, axis=1, keepdims=True)
    )
    resid_grad_ref[...] = resid_grad
    branch = resid_grad.astype(BF)
    branch_ref[...] = branch
    grad_ref[...] = across(weights[0], branch).astype(BF)
    result_ref[...] = resid + jnp.dot(act, weights[2], preferred_element_type=F32)

    w_save.wait()
    for k in range(8):
        rows = pl.ds(k * 256, 256)
        pltpu.make_async_copy(normed_ref.at[rows], normed_out.at[rows], save_sem.at[k, 0]).wait()
        pltpu.make_async_copy(qkv_ref.at[rows], qkv_out.at[rows], save_sem.at[k, 1]).wait()
    for copy in w_copies + aux_copies:
        copy.wait_send()
    pos_copy.wait_send()
    for m in range(3):
        for way in range(5):
            weight_copy(m, way).wait_send()

    @pl.when(hub)
    def _():
        for k in range(3):
            await_recv(x_mine, x_send_sem.at[0, k])
        for step in range(1, 8):
            ways = {1: (1, 2), 4: (0, 1, 2), 6: (0, 2)}.get(step, (2,))
            for way in ways:
                await_recv(x_mine, x_send_sem.at[step, way])

    @pl.when(jnp.logical_not(hub))
    def _():
        x_far.wait_send()

    def finish(block, carry):
        @pl.when(jnp.logical_not(jnp.logical_and(mine, block == c)))
        def _():
            att_copy(block).wait_send()

        return carry

    lax.fori_loop(0, 8, finish, 0)


def forward(*args):
    shape = jax.ShapeDtypeStruct
    dma = pltpu.SemaphoreType.DMA
    return pl.pallas_call(
        attend_kernel,
        name="forward",
        out_shape=(
            shape((1280, 256), BF),
            shape((2048, 1280), BF),
            shape((2048, 768), BF),
            shape((8, 2048), F32),
            shape((160, 2048), BF),
            shape((16, 1280), F32),
            shape((8, 2048), F32),
            shape((1280, 768), BF),
            shape((256, 1280), F32),
            shape((256, 1280), F32),
            shape((256, 1280), BF),
            shape((256, 1280), BF),
            shape((1280, 256), BF),
            shape((1280, 256), BF),
            shape((1280, 256), BF),
        ),
        in_specs=[pl.BlockSpec(memory_space=pltpu.SMEM)] + [ANY_SPEC] * 2 + [VMEM_SPEC] * 2 + [ANY_SPEC] * 4,
        out_specs=(VMEM_SPEC,) + (ANY_SPEC,) * 2 + (VMEM_SPEC,) * 4 + (ANY_SPEC,) + (VMEM_SPEC,) * 7,
        scratch_shapes=[
            pltpu.VMEM((256, 1280), BF),
            pltpu.VMEM((320, 3840), BF),
            pltpu.VMEM((256, 1280), BF),
            pltpu.VMEM((8, 256, 1280), BF),
            pltpu.VMEM((2048, 1280), BF),
            pltpu.VMEM((2048, 768), BF),
            pltpu.VMEM((1280, 768), BF),
            pltpu.VMEM((2, 320, 512), BF),
            pltpu.VMEM((1280, 512), BF),
            pltpu.VMEM((3, 1280, 1280), BF),
            pltpu.VMEM((4, 16, 384), BF),
            pltpu.VMEM((2, 8, 2048), F32),
            pltpu.VMEM((2, 128, 2048), BF),
            pltpu.VMEM((2048, LANES), F32),
            pltpu.VMEM((8, 160, 256), BF),
            dma((8, 3)),
            dma((8,)),
            dma((4,)),
            dma((4,)),
            dma((4,)),
            dma((4,)),
            dma((2,)),
            dma((8,)),
            dma((8,)),
            dma((3, 5)),
            dma((3, 5)),
            dma((6,)),
            dma((8, 2)),
            dma((3,)),
        ],
        compiler_params=pltpu.CompilerParams(
            collective_id=0, has_side_effects=True, vmem_limit_bytes=VMEM_LIMIT
        ),
        cost_estimate=pl.CostEstimate(
            flops=20_000_000_000, bytes_accessed=40_000_000, transcendentals=8_400_000
        ),
    )(*args)


def add_into(target, source, rows, step):
    def one(k, carry):
        part = span(k * step, step, step)
        target[part, :] = (target[part, :].astype(F32) + source[part, :].astype(F32)).astype(BF)
        return carry

    lax.fori_loop(0, rows // step, one, 0)


SUM_WAYS = ("xzyh", "xyzh", "zxyh")
SPREAD_WAYS = ("zhx", "hzx", "hxz")
HEAD_WAYS = "hzx"

PLAN = (
    "mt0", "mt1", "mt2", "prep", "m00", "m02", "take", "L00", "L01", "L02", "L03", "L04",
    "L05", "L06", "L07", "E0", "qs0", "m10", "m01", "L10", "L11", "L12", "L13", "L14", "L15",
    "qa0", "m12", "L16", "L17", "E1", "v0", "qs1", "nt0", "v1", "q00", "nt1", "nt2", "v2",
    "nt3", "na0", "m11", "na1", "v3", "qa1", "na2", "q10", "na3", "m20", "m22", "v4", "v5",
    "q01", "m21", "q20", "m30", "m32", "q11", "g00", "m31", "g02", "nb0", "nb1", "g10", "qc0",
    "g01", "g12", "q21", "qw0", "g22", "g11", "g20", "qc1", "nc_f", "nc_n", "qw1", "g21",
    "mw0", "mw2", "mw1", "nfin", "turn",
)

KEY_PARTS = 2
KEY_ROWS = 2048 // KEY_PARTS


def backward_kernel(
    grad_ref,
    att_hbm,
    branch_hbm,
    normed_mlp_hbm,
    up_grad_hbm,
    act_hbm,
    dy_hbm,
    qkv_hbm,
    lse_ref,
    out_hbm,
    place_ref,
    normed_hbm,
    w_hbm,
    mult_ref,
    x_hbm,
    resid_grad_hbm,
    gain_ref,
    first_out,
    second_out,
    third_out,
    slice_out,
    input_grad_ref,
    scale_ref,
    att_ref,
    branch_ref,
    normed_mlp_ref,
    up_grad_ref,
    act_ref,
    dy_ref,
    qkv_ref,
    out_ref,
    w_ref,
    x_ref,
    resid_grad_ref,
    grad_all,
    key_pos,
    k_turned,
    delta,
    key_sum,
    value_sum,
    turned,
    normed_part,
    n_core,
    n_x,
    n_z,
    n_last,
    sums,
    core_in,
    taken,
    slices,
    s1,
    s2,
    gathered,
    strip,
    scale_in,
    g_send_sem,
    g_recv_sem,
    local_sem,
    m_send,
    m_recv,
    q_send,
    q_recv,
    nc_send,
    nc_recv,
    n_send,
    n_recv,
    v_send,
    v_recv,
    load_sem,
):
    loads = {
        name: pltpu.make_async_copy(src, dst, load_sem.at[k])
        for k, (name, src, dst) in enumerate(
            (
                ("act", act_hbm, act_ref),
                ("dy", dy_hbm, dy_ref),
                ("normed", normed_mlp_hbm, normed_mlp_ref),
                ("up", up_grad_hbm, up_grad_ref),
                ("att", att_hbm, att_ref),
                ("branch", branch_hbm, branch_ref),
                ("qkv", qkv_hbm, qkv_ref),
                ("out", out_hbm, out_ref),
                ("w", w_hbm, w_ref),
                ("x", x_hbm, x_ref),
                ("resid", resid_grad_hbm, resid_grad_ref),
            )
        )
    }
    for load in loads.values():
        load.start()
    at = Place()
    meet_plane(at)
    c, f, core, half = at.c, at.f, at.core, at.half
    mine = core == half
    row = f // 2
    xbit, zbit = c % 2, (c // 2) % 2
    twin, across = dev(c, at.twin), dev(c, at.across)
    xpeer, zpeer, hpeer = dev(flip(c, 1), f), dev(flip(c, 2), f), dev(flip(c, 4), f)

    def remote(src, dst, send_sem, recv_sem, where):
        return pltpu.make_async_remote_copy(
            src_ref=src,
            dst_ref=dst,
            send_sem=send_sem,
            recv_sem=recv_sem,
            device_id=where,
            device_id_type=MESH,
        )

    def grad_copy(group, h):
        return remote(
            grad_ref.at[span(group * 160 + h * 80, 80, 80)],
            grad_all.at[h, pl.ds(0, 80), span(c * 256, 256, 256)],
            g_send_sem.at[group, h],
            g_recv_sem.at[c, h],
            dev(core * 4 + group // 2, at.plane + group % 2),
        )

    def grad_own(h):
        return pltpu.make_async_copy(
            grad_ref.at[span(at.group * 160 + h * 80, 80, 80)],
            grad_all.at[h, pl.ds(0, 80), span(c * 256, 256, 256)],
            local_sem.at[h],
        )

    def give(k, carry):
        group = flip(at.group, k)

        @pl.when(jnp.logical_and(mine, k == 0))
        def _():
            grad_own(0).start()
            grad_own(1).start()

        @pl.when(jnp.logical_not(jnp.logical_and(mine, k == 0)))
        def _():
            grad_copy(group, 0).start()
            grad_copy(group, 1).start()

        return carry

    lax.fori_loop(0, 8, give, 0)

    bits = {"y": row, "x": xbit, "z": zbit, "h": half}
    peers = {"y": across, "x": xpeer, "z": zpeer, "h": hpeer}
    results = (first_out, second_out, third_out)

    def finer(m):
        return "z" if SUM_WAYS[m].index("x") < SUM_WAYS[m].index("z") else "x"

    def cut(ref, way, bit):
        if way == "y":
            return (bit,)
        lead = (slice(None),) * (len(ref.shape) - 2)
        if way == "h":
            return lead + (slice(None), span(bit * 640, 640, 640))
        rows = ref.shape[-2] // 2
        return lead + (span(bit * rows, rows, rows),)

    def main_copy(stage, m):
        if stage < 0:
            y = stage + 2
            src, dst, to = sums.at[pl.ds((m * 2 + y) * 320, 320)], core_in.at[m, y], twin
        elif stage < 4:
            way = SUM_WAYS[m][stage]
            ref = core_in.at[m] if stage == 0 else taken[m][stage - 1]
            src, dst, to = ref.at[cut(ref, way, 1 - bits[way])], taken[m][stage], peers[way]
        else:
            way = SPREAD_WAYS[m][stage - 4]
            known = SPREAD_WAYS[m][: stage - 4]
            low = finer(m)
            high = "x" if low == "z" else "z"
            if high in known:
                rows = pl.ds(0, 320)
            elif low in known:
                rows = span(bits[high] * 160, 160, 160)
            else:
                rows = span(bits[high] * 160 + bits[low] * 80, 80, 80)
            lanes = pl.ds(0, 1280) if "h" in known else span(half * 640, 640, 640)
            src = dst = results[m].at[rows, lanes]
            to = peers[way]
        return remote(src, dst, m_send.at[stage + 2, m], m_recv.at[stage + 2, m], to)

    def added(ref, other, spot):
        for k in range(2) if len(ref.shape) == 3 else (None,):
            here = () if k is None else (k,)
            there = spot if k is None else (k,) + spot[1:]
            ref[here] = (ref[here].astype(F32) + other[there].astype(F32)).astype(BF)

    def main(stage, m):
        if stage == 0:
            for y in range(2):
                main_copy(y - 2, m).wait_recv()
                total = core_in[m, y].astype(F32) + weight_rows(m, 2 * y + core)
                core_in[m, y] = total.astype(BF)
        elif stage < 5:
            main_copy(stage - 1, m).wait_recv()
            way = SUM_WAYS[m][stage - 1]
            ref = core_in.at[m] if stage == 1 else taken[m][stage - 2]
            spot = cut(ref, way, bits[way])
            if stage < 4:
                added(taken[m][stage - 1], ref, spot)
            else:
                low = finer(m)
                high = "x" if low == "z" else "z"
                rows = span(bits[high] * 160 + bits[low] * 80, 80, 80)
                results[m][rows, span(half * 640, 640, 640)] = (
                    taken[m][3][...].astype(F32) + ref[spot].astype(F32)
                ).astype(BF)
        else:
            main_copy(stage - 1, m).wait_recv()
        if stage < 7:
            main_copy(stage, m).start()

    lefts = (act_ref, normed_mlp_ref, att_ref)
    rights = (dy_ref, up_grad_ref, branch_ref)

    def weight_rows(m, quarter):
        rows = span(quarter * 320, 320, 320)
        return jnp.dot(lefts[m][rows, :], rights[m][...], preferred_element_type=F32)

    def main_first(m):
        for name in (("act", "dy"), ("normed", "up"), ("att", "branch"))[m]:
            loads[name].wait()
        for y in range(2):
            part = weight_rows(m, 2 * y + 1 - core)
            sums[(m * 2 + y) * 320 : (m * 2 + y + 1) * 320, :] = part.astype(BF)
            main_copy(y - 2, m).start()

    def prepare():
        loads["qkv"].wait()
        for h in range(2):
            grad_all[h, 80:, :] = jnp.zeros((48, 2048), BF)
            k_turned[h] = jnp.transpose(qkv_ref[:, (2 + h) * LANES : (3 + h) * LANES])
        for k in range(8):
            block = place_ref[0:1, k * 256 : (k + 1) * 256]
            key_pos[k * 256 : (k + 1) * 256, :] = jnp.transpose(
                jnp.broadcast_to(block, (LANES, 256))
            )
        scale_ref[...] = jnp.zeros((8, LANES), F32)

    def take(k, carry):
        block = flip(c, k)

        @pl.when(jnp.logical_and(mine, k == 0))
        def _():
            grad_own(0).wait()
            grad_own(1).wait()

        @pl.when(jnp.logical_not(jnp.logical_and(mine, k == 0)))
        def _():
            for h in range(2):
                await_recv(
                    grad_all.at[h, pl.ds(0, 80), pl.ds(0, 256)], g_recv_sem.at[block, h]
                )

        return carry

    def take_all():
        loads["out"].wait()
        lax.fori_loop(0, 8, take, 0)
        for h in range(2):
            delta[h : h + 1, :] = jnp.sum(
                grad_all[h, :80, :].astype(F32) * out_ref[h * 80 : (h + 1) * 80, :].astype(F32),
                axis=0,
                keepdims=True,
            )

    def head_copy(stage, h):
        if stage == 0:
            src, dst, to = slices.at[h, :, span((1 - row) * 640, 640, 640)], s1.at[h], across
        elif stage == 1:
            src, dst, to = s1.at[h, span(128 - half * 128, 128, 128)], s2.at[h], hpeer
        elif stage < 5:
            way = HEAD_WAYS[stage - 2]
            known = HEAD_WAYS[: stage - 2]
            where = (core,) + tuple(slice(None) if d in known else bits[d] for d in "xz") + (h,)
            rows = slice(None) if "h" in known else span(half * 128, 128, 128)
            src = dst = gathered.at[where + (rows,)]
            to = peers[way]
        else:
            src = dst = gathered.at[core, :, :, h]
            to = twin
        return remote(src, dst, q_send.at[stage, h], q_recv.at[stage, h], to)

    def head(stage, h):
        if stage > 0:
            head_copy(stage - 1, h).wait_recv()
        if stage == 1:
            add_into(s1.at[h], slices.at[h, :, span(row * 640, 640, 640)], 256, 128)
        if stage == 2:
            own = span(half * 128, 128, 128)
            gathered[core, xbit, zbit, h, own, :] = (
                s2[h].astype(F32) + s1[h, own, :].astype(F32)
            ).astype(BF)
        if stage < 6:
            head_copy(stage, h).start()

    def normed_load(part):
        return pltpu.make_async_copy(
            normed_hbm.at[:, pl.ds(part * 256, 256)], normed_part.at[part % 2], local_sem.at[2 + part % 2]
        )

    def attend_head(h, hooks):
        key_sum[...] = jnp.zeros((2048, LANES), F32)
        value_sum[...] = jnp.zeros((2048, LANES), F32)

        def block_grad(block, carry):
            lanes = span(block * 256, 256, 256)
            high = place_ref[0:1, lanes]
            least = place_ref[1:2, lanes]
            query = qkv_ref[lanes, h * LANES : (h + 1) * LANES]
            grad_t = grad_all[h, :, lanes]
            q_grad = jnp.zeros((LANES, 256), F32)
            for part in range(KEY_PARTS):
                some = slice(part * KEY_ROWS, (part + 1) * KEY_ROWS)
                kp = key_pos[some, :]
                kp = jnp.concatenate([kp, kp], axis=1)
                keys = qkv_ref[some, (2 + h) * LANES : (3 + h) * LANES]
                values = qkv_ref[some, (4 + h) * LANES : (5 + h) * LANES]
                s = lax.dot_general(
                    keys, query, (((1,), (1,)), ((), ())), preferred_element_type=F32
                )
                visible = (kp >= least) & (kp <= high)
                p = jnp.exp(jnp.where(visible, s - lse_ref[h : h + 1, lanes], FLOOR))
                gp = jnp.dot(values, grad_t, preferred_element_type=F32)
                gs = (p * (gp - delta[h : h + 1, lanes])).astype(BF)
                value_sum[some, :] += lax.dot_general(
                    p.astype(BF), grad_t, (((1,), (1,)), ((), ())), preferred_element_type=F32
                )
                key_sum[some, :] += jnp.dot(gs, query, preferred_element_type=F32)
                q_grad += jnp.dot(k_turned[h, :, some], gs, preferred_element_type=F32)
            scale_ref[0:1, :] += jnp.sum(
                jnp.transpose(q_grad) * query.astype(F32), axis=0, keepdims=True
            )
            turned[h * LANES : (h + 1) * LANES, lanes] = (q_grad * mult_ref[:, 0:1]).astype(BF)
            for step, todo in hooks.items():

                @pl.when(block == step)
                def _(todo=todo):
                    for one in todo:
                        one()

            return carry

        lax.fori_loop(0, 8, block_grad, 0)

    def attend_end(h):
        for j, total in ((1, key_sum), (2, value_sum)):
            low = jnp.transpose(total[...]).astype(BF)
            turned[(2 * j + h) * LANES : (2 * j + h + 1) * LANES, :] = low

    def head_first(h):
        slices[h, 240:, :] = jnp.zeros((16, 1280), BF)
        for part in range(5):
            normed_load(part).wait()
            if part + 1 < 5:
                normed_load(part + 1).start()
            for j in range(3):
                first = (2 * j + h) * LANES
                slices[h, j * 80 : (j + 1) * 80, part * 256 : (part + 1) * 256] = jnp.dot(
                    turned[first : first + 80, :],
                    normed_part[part % 2],
                    preferred_element_type=F32,
                ).astype(BF)
        if h == 0:
            normed_load(0).start()
        head(0, h)

    def norm_bits(k):
        return (1 - xbit, 1 - xbit, xbit, xbit)[k], (1 - zbit, zbit, 1 - zbit, zbit)[k]

    def norm_spot(k, hh):
        slot = 2 * k + hh
        return sums.at[pl.ds(slot // 5 * 640, 640), pl.ds(slot % 5 * 256, 256)]

    def norm_copy(stage, k, hh=0):
        if stage == 0:
            return remote(
                norm_spot(k, hh), n_core.at[k, hh], nc_send.at[k, hh], nc_recv.at[k, hh], twin
            )
        took = k
        if stage == 1:
            ends = n_core.at[k], n_x.at[k], xpeer
        elif stage == 2:
            ends = n_core.at[2, (1 - half, half)[k]], n_z.at[k], zpeer
        else:
            to = dev(flip(c, 4), at.pack) if k == 0 else dev(c, at.twin)
            took = (core, 2)[k]
            ends = n_core.at[3, (1 - half, half)[k]], n_last.at[core], to
        return remote(ends[0], ends[1], n_send.at[stage, k], n_recv.at[stage, took], ends[2])

    def norm_part(k, hh, which):
        xs, zs = norm_bits(k)
        lanes = span((hh * 4 + zs * 2 + xs) * 256, 256, 256)
        rows = span(which * 640, 640, 640)
        return jnp.dot(w_ref[rows, :], turned[:, lanes], preferred_element_type=F32)

    def norm_first(k):
        if k == 0:
            loads["w"].wait()
            for m in range(3):
                for stage in range(2):
                    main_copy(stage - 2, m).wait_send()
        for hh in range(2):
            norm_spot(k, hh)[...] = norm_part(k, hh, 1 - core).astype(BF)
            norm_copy(0, k, hh).start()

    def norm_core(k):
        for hh in range(2):
            norm_copy(0, k, hh).wait_recv()
            n_core[k, hh] = (n_core[k, hh].astype(F32) + norm_part(k, hh, core)).astype(BF)
        if k < 2:
            norm_copy(1, k).start()

    def scale_copy(stage):
        where = (twin, across, xpeer, zpeer, hpeer)[stage]
        return remote(scale_ref, scale_in.at[stage], v_send.at[stage], v_recv.at[stage], where)

    def tiny(stage):
        if stage > 0:
            scale_copy(stage - 1).wait()
            scale_ref[...] += scale_in[stage - 1]
        if stage < 5:
            scale_copy(stage).start()

    def norm_x(k):
        norm_copy(1, k).wait_recv()
        for hh in range(2):
            add_into(n_core.at[2 + k, hh], n_x.at[k, hh], 640, 80)
        if k == 0:
            norm_copy(2, 0).start()
            norm_copy(2, 1).start()

    def norm_far():
        norm_copy(2, 0).wait_recv()
        add_into(n_core.at[3, 1 - half], n_z.at[0], 640, 80)
        norm_copy(3, 0).start()

    def norm_near():
        norm_copy(2, 1).wait_recv()
        add_into(n_core.at[3, half], n_z.at[1], 640, 80)

        @pl.when(jnp.logical_not(mine))
        def _():
            norm_copy(3, 1).start()

    def norm_last():
        loads["x"].wait()
        loads["resid"].wait()
        @pl.when(mine)
        def _():
            n_last[core] = n_core[3, half]
            await_recv(n_last.at[0], n_recv.at[3, 2])

        @pl.when(jnp.logical_not(mine))
        def _():
            await_recv(n_last.at[0], n_recv.at[3, 0])
            await_recv(n_last.at[1], n_recv.at[3, 1])

        xf = x_ref[...].astype(F32)
        inv = lax.rsqrt(jnp.mean(xf * xf, axis=1, keepdims=True) + EPS)
        scaled = jnp.concatenate(
            [jnp.transpose(n_last[k].astype(F32)) for k in range(2)], axis=1
        ) * gain_ref[0:1, :]
        input_grad_ref[...] = resid_grad_ref[...] + inv * (
            scaled - xf * inv * inv * jnp.mean(scaled * xf, axis=1, keepdims=True)
        )

    def turn_all():
        for k in range(4):
            for hh in range(2):
                norm_copy(0, k, hh).wait_send()
        for core_k in range(2):
            for m4 in range(4):
                group = 2 * m4 + core_k
                for h in range(2):
                    for j in range(3):
                        start = j * 1280 + (group * 2 + h) * 80
                        sums[
                            start % 1920 : start % 1920 + 80, start // 1920 * 640 : start // 1920 * 640 + 640
                        ] = gathered[core_k, m4 % 2, m4 // 2, h, j * 80 : (j + 1) * 80, :]

        for part in range(2):

            def turn(k, carry, part=part):
                strip[...] = jnp.transpose(sums[span(k * LANES, LANES, LANES), part * 640 : part * 640 + 640])
                slice_out[:, span(part * 1920 + k * LANES, LANES, LANES)] = strip[span(core * 320, 320, 320), :]
                return carry

            lax.fori_loop(0, 15, turn, 0)


    tasks = {"prep": prepare, "take": take_all, "nb0": lambda: norm_x(0), "nb1": lambda: norm_x(1)}
    tasks |= {"nc_f": norm_far, "nc_n": norm_near, "nfin": norm_last, "turn": turn_all}
    for m in range(3):
        tasks[f"mt{m}"] = functools.partial(main_first, m)
        for stage in range(4):
            tasks[f"m{stage}{m}"] = functools.partial(main, stage, m)
        for stage in range(3):
            tasks[f"g{stage}{m}"] = functools.partial(main, 4 + stage, m)
        tasks[f"mw{m}"] = functools.partial(main, 7, m)
    for h in range(2):
        tasks[f"E{h}"] = functools.partial(attend_end, h)
        tasks[f"qs{h}"] = functools.partial(head_first, h)
        for stage, name in enumerate(("qa", "q0", "q1", "q2", "qc", "qw")):
            tasks[f"{name}{h}"] = functools.partial(head, 1 + stage, h)
    for k in range(4):
        tasks[f"nt{k}"] = functools.partial(norm_first, k)
        tasks[f"na{k}"] = functools.partial(norm_core, k)
    for stage in range(6):
        tasks[f"v{stage}"] = functools.partial(tiny, stage)

    normed_load(0).start()
    spot = 0
    while spot < len(PLAN):
        name = PLAN[spot]
        if name[0] != "L":
            tasks[name]()
            spot += 1
            continue
        h, step, hooks = int(name[1]), -1, {}
        while step < 7 or PLAN[spot][0] == "L":
            if PLAN[spot][0] == "L":
                step = int(PLAN[spot][2])
                if step == 7:
                    spot += 1
                    break
            else:
                hooks.setdefault(step, []).append(tasks[PLAN[spot]])
            spot += 1
        attend_head(h, hooks)

    def sent(block, carry):
        own_in = jnp.logical_and(mine, block == at.group)

        @pl.when(jnp.logical_not(own_in))
        def _():
            for h in range(2):
                grad_copy(block, h).wait_send()

        return carry

    lax.fori_loop(0, 8, sent, 0)
    for m in range(3):
        for stage in range(7):
            main_copy(stage, m).wait_send()
    for h in range(2):
        for stage in range(6):
            head_copy(stage, h).wait_send()
    for k in range(2):
        norm_copy(1, k).wait_send()
        norm_copy(2, k).wait_send()
    norm_copy(3, 0).wait_send()

    @pl.when(jnp.logical_not(mine))
    def _():
        norm_copy(3, 1).wait_send()


def sum_slots():
    slots = []
    for ways in SUM_WAYS:
        shape, own = [2, 320, 1280], []
        for way in ways:
            if way == "y":
                shape = shape[1:]
            else:
                shape[-1 if way == "h" else -2] //= 2
            own.append(pltpu.VMEM(tuple(shape), BF))
        slots.append(own)
    return slots


def backward(*args):
    shape = jax.ShapeDtypeStruct
    dma = pltpu.SemaphoreType.DMA
    specs = [ANY_SPEC] * 17
    for k in (8, 10, 13, 16):
        specs[k] = VMEM_SPEC
    return pl.pallas_call(
        backward_kernel,
        name="backward",
        out_shape=(
            shape((320, 1280), BF),
            shape((320, 1280), BF),
            shape((320, 1280), BF),
            shape((320, 3840), BF),
            shape((256, 1280), F32),
            shape((8, LANES), F32),
        ),
        in_specs=specs,
        out_specs=(VMEM_SPEC,) * 6,
        scratch_shapes=[
            pltpu.VMEM((1280, 256), BF),
            pltpu.VMEM((256, 1280), BF),
            pltpu.VMEM((1280, 256), BF),
            pltpu.VMEM((256, 1280), BF),
            pltpu.VMEM((1280, 256), BF),
            pltpu.VMEM((256, 1280), BF),
            pltpu.VMEM((2048, 768), BF),
            pltpu.VMEM((160, 2048), BF),
            pltpu.VMEM((1280, 768), BF),
            pltpu.VMEM((256, 1280), BF),
            pltpu.VMEM((256, 1280), F32),
            pltpu.VMEM((2, 128, 2048), BF),
            pltpu.VMEM((2048, LANES), F32),
            pltpu.VMEM((2, 128, 2048), BF),
            pltpu.VMEM((8, 2048), F32),
            pltpu.VMEM((2048, LANES), F32),
            pltpu.VMEM((2048, LANES), F32),
            pltpu.VMEM((768, 2048), BF),
            pltpu.VMEM((2, 2048, 256), BF),
            pltpu.VMEM((4, 2, 640, 256), BF),
            pltpu.VMEM((2, 2, 640, 256), BF),
            pltpu.VMEM((2, 640, 256), BF),
            pltpu.VMEM((2, 640, 256), BF),
            pltpu.VMEM((1920, 1280), BF),
            pltpu.VMEM((3, 2, 320, 1280), BF),
            sum_slots(),
            pltpu.VMEM((2, 256, 1280), BF),
            pltpu.VMEM((2, 256, 640), BF),
            pltpu.VMEM((2, 128, 640), BF),
            pltpu.VMEM((2, 2, 2, 2, 256, 640), BF),
            pltpu.VMEM((640, LANES), BF),
            pltpu.VMEM((5, 8, LANES), F32),
            dma((8, 2)),
            dma((8, 2)),
            dma((4,)),
            dma((9, 3)),
            dma((9, 3)),
            dma((6, 2)),
            dma((6, 2)),
            dma((4, 2)),
            dma((4, 2)),
            dma((4, 4)),
            dma((4, 4)),
            dma((5,)),
            dma((5,)),
            dma((11,)),
        ],
        compiler_params=pltpu.CompilerParams(
            collective_id=1, has_side_effects=True, vmem_limit_bytes=VMEM_LIMIT
        ),
        cost_estimate=pl.CostEstimate(
            flops=30_000_000_000, bytes_accessed=60_000_000, transcendentals=8_400_000
        ),
    )(*args)


def fast_body(
    tokens,
    lengths,
    position,
    qkv_weight,
    out_weight,
    up_weight,
    down_weight,
    attn_gain,
    mlp_gain,
    query_scale,
    cotangent,
):
    f = lax.axis_index("fsdp")
    x, dy = tokens[0], cotangent[0]
    small = [jnp.pad(a, (0, 384 - a.shape[0])) for a in (attn_gain, mlp_gain, query_scale)]
    small = jnp.stack(small + [jnp.zeros((384,), BF)] * 13)
    (
        att_t, normed, qkv, lse, out, auxsum, place, w_heads,
        result, resid_grad, branch_grad, up_grad, act_t, normed_mlp_t, grad_t,
    ) = forward(
        lengths, x, qkv_weight, small, position, out_weight, up_weight, down_weight, dy
    )
    scale_float = auxsum[2, :80]
    base_scale = LOG2E / math.sqrt(80)
    soft = jax.nn.softplus(scale_float)
    mult = jnp.broadcast_to(jnp.pad(base_scale * soft, (0, 48))[:, None], (LANES, LANES))
    g_down, g_up, g_out, g_qkv, input_grad, scale_sum = backward(
        grad_t,
        att_t,
        branch_grad,
        normed_mlp_t,
        up_grad,
        act_t,
        dy,
        qkv,
        lse,
        out,
        place,
        normed,
        w_heads,
        mult,
        x,
        resid_grad,
        auxsum,
    )
    g_down, g_up, g_out = (g.astype(F32) for g in (g_down, g_up, g_out))
    g_qkv = g_qkv.astype(F32)
    grad_attn_gain = jnp.sum(qkv_weight.astype(F32) * g_qkv, axis=1) / attn_gain.astype(F32)
    grad_mlp_gain = jnp.sum(up_weight.astype(F32) * g_up, axis=1) / mlp_gain.astype(F32)
    grad_scale = scale_sum[0, :80] / soft * jax.nn.sigmoid(scale_float)
    return (
        result[None],
        input_grad[None],
        g_qkv,
        g_out,
        g_up,
        g_down,
        grad_attn_gain,
        grad_mlp_gain,
        lax.dynamic_slice_in_dim(grad_scale, f * 20, 20),
    )


def solution(mesh):
    placed = (
        P("fsdp", "ctx", None),
        P("fsdp", None),
        P("fsdp", None),
        P("fsdp", None),
        P("fsdp", None),
        P("fsdp", None),
        P("fsdp", None),
        P("fsdp"),
        P("fsdp"),
        P("fsdp"),
        P("fsdp", "ctx", None),
    )
    fits = mesh.shape["ctx"] == 8 and mesh.shape["fsdp"] == 4
    return jax.shard_map(
        fast_body if fits else body,
        mesh=mesh,
        in_specs=placed,
        out_specs=(
            P("fsdp", "ctx", None),
            P("fsdp", "ctx", None),
            P("fsdp", None),
            P("fsdp", None),
            P("fsdp", None),
            P("fsdp", None),
            P("fsdp"),
            P("fsdp"),
            P("fsdp"),
        ),
        check_vma=False,
    )
```

```python
import functools
import math

import jax
import jax.numpy as jnp
from jax import lax
from jax.experimental import pallas as pl
from jax.experimental.pallas import tpu as pltpu
from jax.sharding import PartitionSpec as P

HEADS = 16


EPS = 1e-06
FLOOR = -1e30
LOG2E = 1.442695041

MESH = pl.DeviceIdType.MESH
LANES = 128
BF = jnp.bfloat16
F32 = jnp.float32
VMEM_SPEC = pl.BlockSpec(memory_space=pltpu.VMEM)
ANY_SPEC = pl.BlockSpec(memory_space=pl.ANY)
VMEM_LIMIT = 60 << 20


def flip(number, mask):
    total = 0
    for bit in (1, 2, 4):
        left = (number // bit) % 2
        right = (mask // bit) % 2
        total = total + bit * (left + right - 2 * left * right)
    return total


class Place:
    def __init__(self):
        self.c = lax.axis_index("ctx")
        self.f = lax.axis_index("fsdp")
        self.core = self.f % 2
        self.plane = self.f - self.core
        self.half = self.c // 4
        self.pack = self.plane + self.half
        self.group = (self.c % 4) * 2 + self.core
        self.twin = self.plane + 1 - self.core
        self.across = (self.f + 2) % 4


def dev(ctx, fsdp):
    return {"ctx": ctx, "fsdp": fsdp}


def send(src, dst, send_sem, recv_sem, device):
    copy = pltpu.make_async_remote_copy(
        src_ref=src,
        dst_ref=dst,
        send_sem=send_sem,
        recv_sem=recv_sem,
        device_id=device,
        device_id_type=MESH,
    )
    copy.start()
    return copy


def await_recv(ref, sem):
    pltpu.make_async_copy(ref, ref, sem).wait()


def meet_plane(at):
    barrier = pltpu.get_barrier_semaphore()

    def greet(k, carry):
        pl.semaphore_signal(
            barrier,
            1,
            device_id=dev((at.c + k // 2) % 8, at.plane + (at.core + k) % 2),
            device_id_type=MESH,
        )
        return carry

    lax.fori_loop(1, 16, greet, 0)
    for k in range(2):
        pl.semaphore_signal(
            barrier, 1, device_id=dev(at.c, (at.plane + 2) % 4 + k), device_id_type=MESH
        )
    pl.semaphore_wait(barrier, 17)


def span(start, size, unit):
    return pl.ds(pl.multiple_of(start, unit), size)


def doc_index(places, seq_ends):
    return jnp.sum((places[:, None] >= seq_ends[None, :]).astype(jnp.int32), axis=1)


def spread_position(gathered_index, tok_dev, cycle_size):
    return gathered_index % tok_dev * cycle_size + gathered_index // tok_dev


def pair_scores(left_rows, right_rows):
    return jnp.einsum(
        "qhd,khd->qhk",
        left_rows.reshape(left_rows.shape[0], HEADS, -1),
        right_rows.reshape(right_rows.shape[0], HEADS, -1),
        preferred_element_type=jnp.float32,
    )


def pair_mask(query_pos, query_doc, key_pos, key_doc):
    return ((query_doc[:, None] == key_doc[None, :]) & (key_pos[None, :] <= query_pos[:, None]))[
        :, None, :
    ]


def in_blocks(advance, carried, pieces):
    total_rows = pieces[0].shape[0]
    block_rows = math.gcd(total_rows, 1024)
    block_count = total_rows // block_rows
    split = tuple((p.reshape((block_count, block_rows) + p.shape[1:]) for p in pieces))

    def inner(running, entry):
        return (advance(running, entry[1], entry[0] * block_rows), None)

    result, unused = lax.scan(inner, carried, (jnp.arange(block_count, dtype=jnp.int32), split))
    return result


def pair_terms(
    query_part,
    grad_part,
    log_part,
    delta_part,
    query_pos,
    query_doc,
    key_part,
    value_part,
    key_pos,
    key_doc,
):
    visible = pair_mask(query_pos, query_doc, key_pos, key_doc)
    prob_float = jnp.where(
        visible, jnp.exp(pair_scores(query_part, key_part) - log_part[:, :, None]), 0.0
    )
    grad_probs = pair_scores(grad_part, value_part)
    score_grad = (prob_float * (grad_probs - delta_part[:, :, None])).astype(jnp.bfloat16)
    return (prob_float.astype(jnp.bfloat16), score_grad)


def body(
    tokens,
    lengths,
    position,
    qkv_weight,
    out_weight,
    up_weight,
    down_weight,
    attn_gain,
    mlp_gain,
    query_scale,
    cotangent,
):
    cycle_size = lax.axis_size("ctx")
    my_index = lax.axis_index("ctx")
    tok_dev = tokens.shape[1]
    share_rows = tok_dev // cycle_size
    seq_ends = jnp.cumsum(lengths[0])
    place_row = position[0]
    residue = (place_row % cycle_size).reshape(cycle_size, tok_dev)
    landing = place_row // cycle_size
    matches = (
        residue[:, :, None] == jnp.arange(cycle_size, dtype=jnp.int32)[None, None, :]
    ).astype(jnp.int32)
    ranked = jnp.sum(jnp.cumsum(matches, axis=1) * matches, axis=2) - 1
    buffer_slot = residue * share_rows + ranked
    my_slots = lax.dynamic_index_in_dim(buffer_slot, my_index, 0, keepdims=False)
    local_rows = jnp.arange(tok_dev, dtype=jnp.int32)
    outgoing = jnp.zeros((tok_dev,), jnp.int32).at[my_slots].set(local_rows)
    flat_slot = (jnp.arange(cycle_size, dtype=jnp.int32)[:, None] * tok_dev + buffer_slot).reshape(
        -1
    )
    landing_table = (
        jnp.zeros((cycle_size * tok_dev,), jnp.int32)
        .at[flat_slot]
        .set(landing)
        .reshape(cycle_size, cycle_size, share_rows)
    )
    arrived_slot = lax.dynamic_index_in_dim(landing_table, my_index, 1, keepdims=False).reshape(-1)
    arrived_order = jnp.zeros((tok_dev,), jnp.int32).at[arrived_slot].set(local_rows)
    moved_x, moved_dy = (
        lax.all_to_all(tokens[0][outgoing], "ctx", split_axis=0, concat_axis=0, tiled=True),
        lax.all_to_all(cotangent[0][outgoing], "ctx", split_axis=0, concat_axis=0, tiled=True),
    )
    dealt_x = moved_x[arrived_order]
    dealt_dy = moved_dy[arrived_order]
    query_pos = local_rows * cycle_size + my_index
    query_doc = doc_index(query_pos, seq_ends)
    full_qkv, full_out, full_up, full_down, attn_gain_full, mlp_gain_full, scale_full = (
        lax.all_gather(qkv_weight, "fsdp", axis=0, tiled=True),
        lax.all_gather(out_weight, "fsdp", axis=0, tiled=True),
        lax.all_gather(up_weight, "fsdp", axis=0, tiled=True),
        lax.all_gather(down_weight, "fsdp", axis=0, tiled=True),
        lax.all_gather(attn_gain, "fsdp", axis=0, tiled=True),
        lax.all_gather(mlp_gain, "fsdp", axis=0, tiled=True),
        lax.all_gather(query_scale, "fsdp", axis=0, tiled=True),
    )
    attn_gain_f = attn_gain_full.astype(jnp.float32)
    mlp_gain_f = mlp_gain_full.astype(jnp.float32)
    scale_float = scale_full.astype(jnp.float32)
    x_float = dealt_x.astype(jnp.float32)
    inv_attn = lax.rsqrt(jnp.mean(x_float * x_float, axis=1, keepdims=True) + EPS)
    normed_attn = (x_float * inv_attn * attn_gain_f).astype(jnp.bfloat16)
    projected = jnp.dot(normed_attn, full_qkv, preferred_element_type=jnp.float32)
    att_width = projected.shape[1] // 3
    head_dim = scale_full.shape[0]
    base_scale = LOG2E / math.sqrt(head_dim)
    multiplier = jnp.tile(base_scale * jax.nn.softplus(scale_float), att_width // head_dim)
    raw_query = projected[:, :att_width]
    queries = (raw_query * multiplier).astype(jnp.bfloat16)
    key_rows = projected[:, att_width : 2 * att_width].astype(jnp.bfloat16)
    value_rows = projected[:, 2 * att_width :].astype(jnp.bfloat16)

    def key_place(first_row, amount):
        gathered_index = first_row + jnp.arange(amount, dtype=jnp.int32)
        key_pos = spread_position(gathered_index, tok_dev, cycle_size)
        return (key_pos, doc_index(key_pos, seq_ends))

    def stat_block(carried, pieces, first_row):
        running_max, running_sum = carried
        key_pos, key_doc = key_place(first_row, pieces[0].shape[0])
        visible = pair_mask(query_pos, query_doc, key_pos, key_doc)
        logits = jnp.where(visible, pair_scores(queries, pieces[0]), FLOOR)
        new_max = jnp.maximum(running_max, jnp.max(logits, axis=2))
        added = jnp.sum(jnp.where(visible, jnp.exp(logits - new_max[:, :, None]), 0.0), axis=2)
        return (new_max, running_sum * jnp.exp(running_max - new_max) + added)

    def output_block(summed, pieces, first_row):
        key_pos, key_doc = key_place(first_row, pieces[0].shape[0])
        visible = pair_mask(query_pos, query_doc, key_pos, key_doc)
        prob_low = jnp.where(
            visible, jnp.exp(pair_scores(queries, pieces[0]) - log_total[:, :, None]), 0.0
        ).astype(jnp.bfloat16)
        values_part = pieces[1].reshape(pieces[1].shape[0], HEADS, -1)
        return summed + jnp.einsum(
            "qhk,khd->qhd", prob_low, values_part, preferred_element_type=jnp.float32
        ).reshape(summed.shape)

    def query_grad_block(summed, pieces, first_row):
        key_pos, key_doc = key_place(first_row, pieces[0].shape[0])
        unused_probs, score_grad = pair_terms(
            queries,
            attended_grad,
            log_total,
            row_delta,
            query_pos,
            query_doc,
            pieces[0],
            pieces[1],
            key_pos,
            key_doc,
        )
        keys_part = pieces[0].reshape(pieces[0].shape[0], HEADS, -1)
        return summed + jnp.einsum(
            "qhk,khd->qhd", score_grad, keys_part, preferred_element_type=jnp.float32
        ).reshape(summed.shape)

    def key_grad_block(carried, pieces, first_row):
        amount = pieces[0].shape[0]
        part_pos, part_doc = key_place(first_row, amount)
        part_log = lax.dynamic_slice_in_dim(all_log, first_row, amount, 0)
        part_delta = lax.dynamic_slice_in_dim(all_delta, first_row, amount, 0)
        prob_low, score_grad = pair_terms(
            pieces[0],
            pieces[1],
            part_log,
            part_delta,
            part_pos,
            part_doc,
            key_rows,
            value_rows,
            query_pos,
            query_doc,
        )
        grad_keys = carried[0] + jnp.einsum(
            "qhk,qhd->khd",
            score_grad,
            pieces[0].reshape(amount, HEADS, -1),
            preferred_element_type=jnp.float32,
        ).reshape(tok_dev, -1)
        grad_values = carried[1] + jnp.einsum(
            "qhk,qhd->khd",
            prob_low,
            pieces[1].reshape(amount, HEADS, -1),
            preferred_element_type=jnp.float32,
        ).reshape(tok_dev, -1)
        return (grad_keys, grad_values)

    zero_stats = (
        jnp.full((tok_dev, HEADS), FLOOR, jnp.float32),
        jnp.zeros((tok_dev, HEADS), jnp.float32),
    )
    zero_rows = jnp.zeros((tok_dev, att_width), jnp.float32)
    running_max, running_sum = in_blocks(
        stat_block, zero_stats, (lax.all_gather(key_rows, "ctx", axis=0, tiled=True),)
    )
    log_total = running_max + jnp.log(running_sum)
    attended = in_blocks(
        output_block,
        zero_rows,
        (
            lax.all_gather(key_rows, "ctx", axis=0, tiled=True),
            lax.all_gather(value_rows, "ctx", axis=0, tiled=True),
        ),
    )
    attended_low = attended.astype(jnp.bfloat16)
    resid = x_float + jnp.dot(attended_low, full_out, preferred_element_type=jnp.float32)
    inv_mlp = lax.rsqrt(jnp.mean(resid * resid, axis=1, keepdims=True) + EPS)
    normed_mlp = (resid * inv_mlp * mlp_gain_f).astype(jnp.bfloat16)
    up_proj = jnp.dot(normed_mlp, full_up, preferred_element_type=jnp.float32)
    act_low = jax.nn.silu(up_proj).astype(jnp.bfloat16)
    result = resid + jnp.dot(act_low, full_down, preferred_element_type=jnp.float32)
    cot_float = dealt_dy.astype(jnp.float32)
    grad_down = jnp.dot(act_low.T, dealt_dy, preferred_element_type=jnp.float32)
    act_grad = jnp.dot(dealt_dy, full_down.T, preferred_element_type=jnp.float32)
    sigma = jax.nn.sigmoid(up_proj)
    up_grad = (act_grad * sigma * (1.0 + up_proj * (1.0 - sigma))).astype(jnp.bfloat16)
    grad_up = jnp.dot(normed_mlp.T, up_grad, preferred_element_type=jnp.float32)
    norm_mlp_grad = jnp.dot(up_grad, full_up.T, preferred_element_type=jnp.float32)
    grad_mlp_gain = jnp.sum(norm_mlp_grad * resid * inv_mlp, axis=0)
    scaled_mlp = norm_mlp_grad * mlp_gain_f
    resid_grad = cot_float + inv_mlp * (
        scaled_mlp - resid * inv_mlp * inv_mlp * jnp.mean(scaled_mlp * resid, axis=1, keepdims=True)
    )
    branch_grad = resid_grad.astype(jnp.bfloat16)
    grad_out = jnp.dot(attended_low.T, branch_grad, preferred_element_type=jnp.float32)
    attended_grad = jnp.dot(branch_grad, full_out.T, preferred_element_type=jnp.float32).astype(
        jnp.bfloat16
    )
    row_delta = jnp.sum(
        (attended_grad.astype(jnp.float32) * attended).reshape(tok_dev, HEADS, -1), axis=2
    )
    query_grads = in_blocks(
        query_grad_block,
        zero_rows,
        (
            lax.all_gather(key_rows, "ctx", axis=0, tiled=True),
            lax.all_gather(value_rows, "ctx", axis=0, tiled=True),
        ),
    )
    all_log, all_delta = (
        lax.all_gather(log_total, "ctx", axis=0, tiled=True),
        lax.all_gather(row_delta, "ctx", axis=0, tiled=True),
    )
    key_grad_f, value_grad_f = in_blocks(
        key_grad_block,
        (zero_rows, zero_rows),
        (
            lax.all_gather(queries, "ctx", axis=0, tiled=True),
            lax.all_gather(attended_grad, "ctx", axis=0, tiled=True),
        ),
    )
    scale_terms = jnp.sum((query_grads * raw_query).reshape(tok_dev, -1, head_dim), axis=(0, 1))
    grad_scale = scale_terms * base_scale * jax.nn.sigmoid(scale_float)
    proj_grad = jnp.concatenate(
        [
            (query_grads * multiplier).astype(jnp.bfloat16),
            key_grad_f.astype(jnp.bfloat16),
            value_grad_f.astype(jnp.bfloat16),
        ],
        axis=1,
    )
    grad_qkv = jnp.dot(normed_attn.T, proj_grad, preferred_element_type=jnp.float32)
    norm_attn_grad = jnp.dot(proj_grad, full_qkv.T, preferred_element_type=jnp.float32)
    grad_attn_gain = jnp.sum(norm_attn_grad * x_float * inv_attn, axis=0)
    scaled_attn = norm_attn_grad * attn_gain_f
    input_grad = resid_grad + inv_attn * (
        scaled_attn
        - x_float * inv_attn * inv_attn * jnp.mean(scaled_attn * x_float, axis=1, keepdims=True)
    )
    owned = (
        lax.psum_scatter(grad_qkv, "fsdp", scatter_dimension=0, tiled=True),
        lax.psum_scatter(grad_out, "fsdp", scatter_dimension=0, tiled=True),
        lax.psum_scatter(grad_up, "fsdp", scatter_dimension=0, tiled=True),
        lax.psum_scatter(grad_down, "fsdp", scatter_dimension=0, tiled=True),
        lax.psum_scatter(grad_attn_gain, "fsdp", scatter_dimension=0, tiled=True),
        lax.psum_scatter(grad_mlp_gain, "fsdp", scatter_dimension=0, tiled=True),
        lax.psum_scatter(grad_scale, "fsdp", scatter_dimension=0, tiled=True),
    )
    summed_grads = lax.psum(
        (owned[0], owned[1], owned[2], owned[3], owned[4], owned[5], owned[6]), "ctx"
    )
    back_out, back_grad = (
        lax.all_to_all(result[arrived_slot], "ctx", split_axis=0, concat_axis=0, tiled=True),
        lax.all_to_all(input_grad[arrived_slot], "ctx", split_axis=0, concat_axis=0, tiled=True),
    )
    return (
        back_out[my_slots][None],
        back_grad[my_slots][None],
        summed_grads[0],
        summed_grads[1],
        summed_grads[2],
        summed_grads[3],
        summed_grads[4],
        summed_grads[5],
        summed_grads[6],
    )


HUB_WAYS = {k: ((2, 0), (2, 1)) for k in range(1, 8)}
HUB_WAYS[1] += ((1, 0),)
HUB_WAYS[2] += ((0, 1),)
HUB_WAYS[4] += ((0, 0), (0, 1), (1, 0), (1, 1))
HUB_WAYS[6] += ((0, 0), (0, 1))

SPLIT = (False, True, False)
WEIGHT_STEPS = ((2, 2, 1), (4, 2, 0), (6, 3, 1))


def attend_kernel(
    ends_ref,
    x_ref,
    w_ref,
    aux_ref,
    pos_ref,
    out_w_ref,
    up_w_ref,
    down_w_ref,
    dy_ref,
    att_ref,
    normed_out,
    qkv_out,
    lse_ref,
    out_ref,
    auxsum_ref,
    place_ref,
    w_out,
    result_ref,
    resid_grad_ref,
    branch_ref,
    up_grad_ref,
    act_ref,
    normed_mlp_ref,
    grad_ref,
    x_mine,
    w_mine,
    dy_mine,
    x_all,
    normed_ref,
    qkv_ref,
    w_all,
    w_own,
    w_small,
    weights,
    aux_all,
    pos_all,
    v_turned,
    key_pos,
    att_send,
    x_send_sem,
    x_recv_sem,
    w_send_sem,
    w_recv_sem,
    aux_send_sem,
    aux_recv_sem,
    pos_sem,
    att_send_sem,
    att_recv_sem,
    m_send_sem,
    m_recv_sem,
    local_sem,
    save_sem,
    shard_sem,
):
    w_load = pltpu.make_async_copy(w_ref, w_mine, local_sem.at[0])
    w_load.start()
    x_load = pltpu.make_async_copy(x_ref, x_mine, local_sem.at[2])
    dy_load = pltpu.make_async_copy(dy_ref, dy_mine, local_sem.at[4])
    at = Place()
    meet_plane(at)
    c, f = at.c, at.f
    hub = at.core == at.half

    aux_own = pltpu.make_async_copy(aux_ref, aux_all.at[f], local_sem.at[1])
    aux_own.start()
    x_own = pltpu.make_async_copy(x_ref, x_all.at[c], local_sem.at[3])

    halves = (pl.ds(0, 128), pl.ds(128, 128))

    def x_far(part):
        return pltpu.make_async_remote_copy(
            src_ref=x_ref.at[halves[part]],
            dst_ref=x_all.at[c, halves[part]],
            send_sem=x_send_sem.at[0, 0, part],
            recv_sem=x_recv_sem.at[c, part],
            device_id=dev(flip(c, 4), f),
            device_id_type=MESH,
        )

    @pl.when(hub)
    def _():
        x_own.start()
        for part in range(2):
            for k, where in enumerate((dev(flip(c, 1), f), dev(flip(c, 2), f), dev(c, at.twin))):
                send(
                    x_ref.at[halves[part]],
                    x_all.at[c, halves[part]],
                    x_send_sem.at[0, k, part],
                    x_recv_sem.at[c, part],
                    where,
                )

    @pl.when(jnp.logical_not(hub))
    def _():
        x_far(0).start()
        x_far(1).start()

    w_copies, aux_copies = [], []
    for k in (2, 1, 3):
        aux_copies.append(
            send(
                aux_ref,
                aux_all.at[f],
                aux_send_sem.at[k],
                aux_recv_sem.at[f],
                dev(c, (f + k) % 4),
            )
        )

    pos = pos_ref[...]
    start = jnp.zeros_like(pos)
    end = 0
    for k in range(4):
        end = end + ends_ref[0, k]
        start = jnp.where(pos >= end, end, start)
    pos_all[at.core, 0:1, :] = pos.astype(F32)
    pos_all[at.core, 1:2, :] = start.astype(F32)
    pos_all[at.core, 2:8, :] = jnp.zeros((6, 2048), F32)
    pos_copy = send(
        pos_all.at[at.core], pos_all.at[at.core], pos_sem.at[0], pos_sem.at[1], dev(c, at.twin)
    )

    row = lax.broadcasted_iota(jnp.int32, (1280, 512), 0)
    column = lax.broadcasted_iota(jnp.int32, (1280, 512), 1)
    first = (c % 4) * 320
    w_load.wait()
    for k in range(2):
        some = jnp.zeros((320, 512), F32)
        for j in range(3):
            pick = (row - first - k * 160 == column - j * 160) & (column // 160 == j)
            pick = jnp.where(pick, 1.0, 0.0).astype(BF)
            some += jnp.dot(w_mine[:, j * 1280 : (j + 1) * 1280], pick, preferred_element_type=F32)
        w_own[k] = some.astype(BF)
    mine_rows = span(f * 320, 320, 320)
    for k in (2, 3, 1):
        to = (f + k) % 4
        w_copies.append(
            send(
                w_own.at[to % 2],
                w_small.at[mine_rows],
                w_send_sem.at[k],
                w_recv_sem.at[f],
                dev(c, to),
            )
        )
    w_small[mine_rows, :] = w_own[at.core]
    x_load.start()
    dy_load.start()


    shards = (out_w_ref, up_w_ref, down_w_ref)
    xbit = c % 2
    other = (f + 2) % 4

    def part(m, owner, x):
        return weights.at[m, span(owner * 320 + x * 160, 160, 160)]

    def weight_copy(m, way):
        if way == 0:
            src, dst, to = shards[m], weights.at[m, mine_rows], dev(c, at.twin)
        elif way == 1 and not SPLIT[m]:
            src, dst, to = shards[m], weights.at[m, mine_rows], dev(c, other)
        elif way == 3 and not SPLIT[m]:
            src = dst = weights.at[m, span(other * 320, 320, 320)]
            to = dev(c, at.twin)
        elif way == 1:
            src = shards[m].at[span(xbit * 160, 160, 160)]
            dst, to = part(m, f, xbit), dev(c, other)
        else:
            x = (xbit, xbit, 1 - xbit)[way - 2]
            src = dst = part(m, other, x)
            to = (dev(flip(c, 1), f), dev(c, at.twin), dev(c, at.twin))[way - 2]
        return pltpu.make_async_remote_copy(
            src_ref=src,
            dst_ref=dst,
            send_sem=m_send_sem.at[m, way],
            recv_sem=m_recv_sem.at[m, way],
            device_id=to,
            device_id_type=MESH,
        )

    def shard_copy(m):
        return pltpu.make_async_copy(shards[m], weights.at[m, mine_rows], shard_sem.at[m])

    def weight_first(m):
        weight_copy(m, 0).start()
        weight_copy(m, 1).start()
        shard_copy(m).start()

    def weight_second(m):
        weight_copy(m, 1).wait_recv()
        if SPLIT[m]:
            weight_copy(m, 2).start()
        weight_copy(m, 3).start()

    def weight_third(m):
        if SPLIT[m]:
            weight_copy(m, 2).wait_recv()
            weight_copy(m, 4).start()

    def weight_last(m):
        shard_copy(m).wait()
        for way in (0, 3, 4) if SPLIT[m] else (0, 3):
            weight_copy(m, way).wait_recv()


    aux_own.wait()
    for k in (1, 2, 3):
        await_recv(aux_all.at[0], aux_recv_sem.at[(f + k) % 4])
    aux = jnp.zeros((16, 1280), F32)
    scale = jnp.zeros((16, LANES), F32)
    row = lax.broadcasted_iota(jnp.int32, (384, 1280), 0)
    column = lax.broadcasted_iota(jnp.int32, (384, 1280), 1)
    for k in range(4):
        put = jnp.where((column == row + k * 320) & (row < 320), 1.0, 0.0).astype(BF)
        aux = aux + jnp.dot(aux_all[k], put, preferred_element_type=F32)
        put = (column[:LANES, :LANES] == row[:LANES, :LANES] + k * 20) & (row[:LANES, :LANES] < 20)
        put = jnp.where(put, 1.0, 0.0).astype(BF)
        scale = scale + jnp.dot(aux_all[k, :, :LANES], put, preferred_element_type=F32)
    auxsum_ref[...] = aux
    auxsum_ref[2:3, :LANES] = scale[2:3]
    gain = aux[0:1, :]
    mlp_gain = aux[1:2, :]
    scale = scale[2:3]
    real = lax.broadcasted_iota(jnp.int32, (1, LANES), 1) < 80
    mult = jnp.where(
        real, LOG2E / math.sqrt(80) * (jnp.maximum(scale, 0.0) + jnp.log1p(jnp.exp(-jnp.abs(scale)))), 0.0
    )
    one = jnp.ones_like(mult)
    mults = jnp.concatenate([mult, mult, one, one, one, one], axis=1)

    await_recv(pos_all.at[0], pos_sem.at[1])
    place_ref[...] = pos_all[at.half]
    for k in range(8):
        block = place_ref[0:1, k * 256 : (k + 1) * 256]
        key_pos[k * 256 : (k + 1) * 256, :] = jnp.transpose(
            jnp.broadcast_to(block, (LANES, 256))
        )

    def arrive(step, carry):
        k = step + jnp.where(step == 3, 1, 0) - jnp.where(step == 4, 1, 0)
        slot = flip(c, k)
        for part in range(2):
            piece = x_all.at[slot, halves[part]]
            if part == 0:

                @pl.when(jnp.logical_and(hub, k == 0))
                def _():
                    x_own.wait()

            @pl.when(jnp.logical_not(jnp.logical_and(hub, k == 0)))
            def _(part=part, piece=piece):
                await_recv(piece, x_recv_sem.at[slot, part])

            def onward(way, where, part=part, piece=piece):
                send(
                    piece, piece, x_send_sem.at[k, way, part], x_recv_sem.at[slot, part], where
                )

            for way, where in enumerate((dev(flip(c, 1), f), dev(flip(c, 2), f), dev(c, at.twin))):
                due = False
                for when in HUB_WAYS:
                    if (way, part) in HUB_WAYS[when]:
                        due = jnp.logical_or(due, k == when)

                @pl.when(jnp.logical_and(hub, due))
                def _(way=way, where=where, onward=onward):
                    onward(way, where)

        @pl.when(step == 3)
        def _():
            weight_first(0)

        @pl.when(step == 5)
        def _():
            weight_first(1)


        xf = x_all[slot].astype(F32)
        inv = lax.rsqrt(jnp.mean(xf * xf, axis=1, keepdims=True) + EPS)
        rows = span(slot * 256, 256, 256)
        normed_ref[rows, :] = (xf * inv * gain).astype(BF)
        pltpu.make_async_copy(
            normed_ref.at[rows], normed_out.at[rows], save_sem.at[slot, 0]
        ).start()
        return carry

    def project(step, carry):
        slot = flip(c, step)
        rows = span(slot * 256, 256, 256)
        proj = jnp.dot(normed_ref[rows, :], w_all[...], preferred_element_type=F32)
        qkv_ref[rows, :] = (proj * mults).astype(BF)
        pltpu.make_async_copy(qkv_ref.at[rows], qkv_out.at[rows], save_sem.at[slot, 1]).start()
        return carry

    lax.fori_loop(0, 7, arrive, 0)
    for k in (1, 2, 3):
        await_recv(w_small.at[pl.ds(0, 320)], w_recv_sem.at[(f + k) % 4])
    weight_first(2)
    row = lax.broadcasted_iota(jnp.int32, (512, 768), 0)
    column = lax.broadcasted_iota(jnp.int32, (512, 768), 1)
    spread = (row == column // LANES * 80 + column % LANES) & (column % LANES < 80)
    spread = jnp.where(spread, 1.0, 0.0).astype(BF)
    w_all[...] = jnp.dot(w_small[...], spread, preferred_element_type=F32).astype(BF)
    w_save = pltpu.make_async_copy(w_all, w_out, local_sem.at[5])
    w_save.start()
    lax.fori_loop(0, 5, project, 0)
    lax.fori_loop(7, 8, arrive, 0)
    lax.fori_loop(5, 8, project, 0)

    for h in range(2):
        v_turned[h] = jnp.transpose(qkv_ref[:, (4 + h) * LANES : (5 + h) * LANES])

    att_own = pltpu.make_async_copy(
        att_send.at[c], att_ref.at[span(at.group * 160, 160, 160)], local_sem.at[3]
    )

    def att_copy(block):
        return pltpu.make_async_remote_copy(
            src_ref=att_send.at[block],
            dst_ref=att_ref.at[span(at.group * 160, 160, 160)],
            send_sem=att_send_sem.at[block],
            recv_sem=att_recv_sem.at[at.group],
            device_id=dev(block, at.pack),
            device_id_type=MESH,
        )

    mine = at.core == at.half

    def attend(step, carry):
        block = flip(c, 7 - step)
        lanes = span(block * 256, 256, 256)
        high = place_ref[0:1, lanes]
        least = place_ref[1:2, lanes]
        for h in range(2):
            query = qkv_ref[lanes, h * LANES : (h + 1) * LANES]
            scores, top = [], None
            for part in range(2):
                rows = slice(part * 1024, (part + 1) * 1024)
                kp = key_pos[rows, :]
                kp = jnp.concatenate([kp, kp], axis=1)
                keys = qkv_ref[rows, (2 + h) * LANES : (3 + h) * LANES]
                s = lax.dot_general(
                    keys, query, (((1,), (1,)), ((), ())), preferred_element_type=F32
                )
                s = jnp.where((kp >= least) & (kp <= high), s, FLOOR)
                scores.append(s)
                most = jnp.max(s, axis=0, keepdims=True)
                top = most if top is None else jnp.maximum(top, most)
            total = jnp.zeros((1, 256), F32)
            o = jnp.zeros((LANES, 256), F32)
            for part in range(2):
                p = jnp.exp(scores[part] - top)
                total += jnp.sum(p, axis=0, keepdims=True)
                values = v_turned[h, :, part * 1024 : (part + 1) * 1024]
                o += jnp.dot(values, p.astype(BF), preferred_element_type=F32)
            o = o[:80] / total
            lse_ref[h : h + 1, lanes] = top + jnp.log(total)
            out_ref[h * 80 : (h + 1) * 80, lanes] = o.astype(BF)
            att_send[block, h * 80 : (h + 1) * 80, :] = o.astype(BF)

        @pl.when(jnp.logical_and(mine, step == 7))
        def _():
            att_own.start()

        @pl.when(jnp.logical_not(jnp.logical_and(mine, step == 7)))
        def _():
            att_copy(block).start()

        for when, todo, m in WEIGHT_STEPS:

            @pl.when(step == when)
            def _(todo=todo, m=m):
                (weight_second if todo == 2 else weight_third)(m)

        return carry

    lax.fori_loop(0, 8, attend, 0)
    weight_second(2)
    lse_ref[2:8, :] = jnp.zeros((6, 2048), F32)

    def land(block, carry):
        @pl.when(jnp.logical_not(jnp.logical_and(mine, block == at.group)))
        def _():
            await_recv(att_ref.at[pl.ds(0, 160)], att_recv_sem.at[block])

        return carry

    @pl.when(mine)
    def _():
        att_own.wait()

    weight_last(0)
    lax.fori_loop(0, 8, land, 0)

    def across(left, right):
        return lax.dot_general(
            left, right, (((1,), (1,)), ((), ())), preferred_element_type=F32
        )

    x_load.wait()
    dy_load.wait()
    xf = x_mine[...].astype(F32)
    resid = xf + jnp.dot(jnp.transpose(att_ref[...]), weights[0], preferred_element_type=F32)
    inv = lax.rsqrt(jnp.mean(resid * resid, axis=1, keepdims=True) + EPS)
    normed_mlp = (resid * inv * mlp_gain).astype(BF)
    normed_mlp_ref[...] = jnp.transpose(normed_mlp)
    weight_last(1)
    up = jnp.dot(normed_mlp, weights[1], preferred_element_type=F32)
    sigma = 1.0 / (1.0 + jnp.exp(-up))
    act = (up * sigma).astype(BF)
    act_ref[...] = jnp.transpose(act)
    slope = sigma * (1.0 + up * (1.0 - sigma))
    weight_last(2)
    dy = dy_mine[...]
    up_grad = (across(dy, weights[2]) * slope).astype(BF)
    up_grad_ref[...] = up_grad
    scaled = across(up_grad, weights[1]) * mlp_gain
    resid_grad = dy.astype(F32) + inv * (
        scaled - resid * inv * inv * jnp.mean(scaled * resid, axis=1, keepdims=True)
    )
    resid_grad_ref[...] = resid_grad
    branch = resid_grad.astype(BF)
    branch_ref[...] = branch
    grad_ref[...] = across(weights[0], branch).astype(BF)
    result_ref[...] = resid + jnp.dot(act, weights[2], preferred_element_type=F32)

    w_save.wait()
    for k in range(8):
        rows = pl.ds(k * 256, 256)
        pltpu.make_async_copy(normed_ref.at[rows], normed_out.at[rows], save_sem.at[k, 0]).wait()
        pltpu.make_async_copy(qkv_ref.at[rows], qkv_out.at[rows], save_sem.at[k, 1]).wait()
    for copy in w_copies + aux_copies:
        copy.wait_send()
    pos_copy.wait_send()
    for m in range(3):
        for way in range(5) if SPLIT[m] else (0, 1, 3):
            weight_copy(m, way).wait_send()

    @pl.when(hub)
    def _():
        for k in range(8):
            for way, part in HUB_WAYS.get(k, ((0, 0), (0, 1), (1, 0), (1, 1), (2, 0), (2, 1))):
                await_recv(x_mine.at[halves[part]], x_send_sem.at[k, way, part])

    @pl.when(jnp.logical_not(hub))
    def _():
        x_far(0).wait_send()
        x_far(1).wait_send()

    def finish(block, carry):
        @pl.when(jnp.logical_not(jnp.logical_and(mine, block == c)))
        def _():
            att_copy(block).wait_send()

        return carry

    lax.fori_loop(0, 8, finish, 0)


def forward(*args):
    shape = jax.ShapeDtypeStruct
    dma = pltpu.SemaphoreType.DMA
    return pl.pallas_call(
        attend_kernel,
        name="forward",
        out_shape=(
            shape((1280, 256), BF),
            shape((2048, 1280), BF),
            shape((2048, 768), BF),
            shape((8, 2048), F32),
            shape((160, 2048), BF),
            shape((16, 1280), F32),
            shape((8, 2048), F32),
            shape((1280, 768), BF),
            shape((256, 1280), F32),
            shape((256, 1280), F32),
            shape((256, 1280), BF),
            shape((256, 1280), BF),
            shape((1280, 256), BF),
            shape((1280, 256), BF),
            shape((1280, 256), BF),
        ),
        in_specs=[pl.BlockSpec(memory_space=pltpu.SMEM)] + [ANY_SPEC] * 2 + [VMEM_SPEC] * 2 + [ANY_SPEC] * 4,
        out_specs=(VMEM_SPEC,) + (ANY_SPEC,) * 2 + (VMEM_SPEC,) * 4 + (ANY_SPEC,) + (VMEM_SPEC,) * 7,
        scratch_shapes=[
            pltpu.VMEM((256, 1280), BF),
            pltpu.VMEM((320, 3840), BF),
            pltpu.VMEM((256, 1280), BF),
            pltpu.VMEM((8, 256, 1280), BF),
            pltpu.VMEM((2048, 1280), BF),
            pltpu.VMEM((2048, 768), BF),
            pltpu.VMEM((1280, 768), BF),
            pltpu.VMEM((2, 320, 512), BF),
            pltpu.VMEM((1280, 512), BF),
            pltpu.VMEM((3, 1280, 1280), BF),
            pltpu.VMEM((4, 16, 384), BF),
            pltpu.VMEM((2, 8, 2048), F32),
            pltpu.VMEM((2, 128, 2048), BF),
            pltpu.VMEM((2048, LANES), F32),
            pltpu.VMEM((8, 160, 256), BF),
            dma((8, 3, 2)),
            dma((8, 2)),
            dma((4,)),
            dma((4,)),
            dma((4,)),
            dma((4,)),
            dma((2,)),
            dma((8,)),
            dma((8,)),
            dma((3, 5)),
            dma((3, 5)),
            dma((6,)),
            dma((8, 2)),
            dma((3,)),
        ],
        compiler_params=pltpu.CompilerParams(
            collective_id=0, has_side_effects=True, vmem_limit_bytes=VMEM_LIMIT
        ),
        cost_estimate=pl.CostEstimate(
            flops=20_000_000_000, bytes_accessed=40_000_000, transcendentals=8_400_000
        ),
    )(*args)


def add_into(target, source, rows, step):
    def one(k, carry):
        part = span(k * step, step, step)
        target[part, :] = (target[part, :].astype(F32) + source[part, :].astype(F32)).astype(BF)
        return carry

    lax.fori_loop(0, rows // step, one, 0)


def add_into(target, source, rows, step):
    def one(k, carry):
        part = span(k * step, step, step)
        target[part, :] = (target[part, :].astype(F32) + source[part, :].astype(F32)).astype(BF)
        return carry

    lax.fori_loop(0, rows // step, one, 0)


SUM_WAYS = ("xzyh", "xyzh", "zxyh")
SPREAD_WAYS = ("zhx", "hzx", "hxz")
HEAD_WAYS = "hzx"

PLAN = (
    "mt0", "mt1", "mt2", "prep", "m00", "m02", "take", "L00", "L01", "L02", "L03", "L04",
    "L05", "L06", "L07", "E0", "qs0", "m10", "m01", "L10", "L11", "L12", "L13", "L14", "L15",
    "qa0", "m12", "L16", "L17", "E1", "v0", "qs1", "nt0", "v1", "q00", "nt1", "nt2", "v2",
    "nt3", "na0", "m11", "na1", "v3", "qa1", "na2", "q10", "na3", "m20", "m22", "v4", "v5",
    "q01", "m21", "q20", "m30", "m32", "q11", "g00", "m31", "g02", "nb0", "nb1", "g10", "qc0",
    "g01", "g12", "q21", "qw0", "g22", "g11", "g20", "qc1", "nc_f", "nc_n", "qw1", "g21",
    "mw0", "mw2", "mw1", "nfin", "turn",
)

KEY_PARTS = 2
KEY_ROWS = 2048 // KEY_PARTS


def backward_kernel(
    grad_ref,
    att_hbm,
    branch_hbm,
    normed_mlp_hbm,
    up_grad_hbm,
    act_hbm,
    dy_hbm,
    qkv_hbm,
    lse_ref,
    out_hbm,
    place_ref,
    normed_hbm,
    w_hbm,
    mult_ref,
    x_hbm,
    resid_grad_hbm,
    gain_ref,
    first_out,
    second_out,
    third_out,
    slice_out,
    input_grad_ref,
    scale_ref,
    att_ref,
    branch_ref,
    normed_mlp_ref,
    up_grad_ref,
    act_ref,
    dy_ref,
    qkv_ref,
    out_ref,
    w_ref,
    x_ref,
    resid_grad_ref,
    grad_all,
    key_pos,
    k_turned,
    delta,
    key_sum,
    value_sum,
    turned,
    normed_part,
    n_core,
    n_x,
    n_z,
    n_last,
    sums,
    core_in,
    taken,
    slices,
    s1,
    s2,
    gathered,
    strip,
    scale_in,
    g_send_sem,
    g_recv_sem,
    local_sem,
    m_send,
    m_recv,
    q_send,
    q_recv,
    nc_send,
    nc_recv,
    n_send,
    n_recv,
    v_send,
    v_recv,
    load_sem,
):
    loads = {
        name: pltpu.make_async_copy(src, dst, load_sem.at[k])
        for k, (name, src, dst) in enumerate(
            (
                ("act", act_hbm, act_ref),
                ("dy", dy_hbm, dy_ref),
                ("normed", normed_mlp_hbm, normed_mlp_ref),
                ("up", up_grad_hbm, up_grad_ref),
                ("att", att_hbm, att_ref),
                ("branch", branch_hbm, branch_ref),
                ("qkv", qkv_hbm, qkv_ref),
                ("out", out_hbm, out_ref),
                ("w", w_hbm, w_ref),
                ("x", x_hbm, x_ref),
                ("resid", resid_grad_hbm, resid_grad_ref),
            )
        )
    }
    for load in loads.values():
        load.start()
    at = Place()
    meet_plane(at)
    c, f, core, half = at.c, at.f, at.core, at.half
    mine = core == half
    row = f // 2
    xbit, zbit = c % 2, (c // 2) % 2
    twin, across = dev(c, at.twin), dev(c, at.across)
    xpeer, zpeer, hpeer = dev(flip(c, 1), f), dev(flip(c, 2), f), dev(flip(c, 4), f)

    def remote(src, dst, send_sem, recv_sem, where):
        return pltpu.make_async_remote_copy(
            src_ref=src,
            dst_ref=dst,
            send_sem=send_sem,
            recv_sem=recv_sem,
            device_id=where,
            device_id_type=MESH,
        )

    def grad_copy(group, h):
        return remote(
            grad_ref.at[span(group * 160 + h * 80, 80, 80)],
            grad_all.at[h, pl.ds(0, 80), span(c * 256, 256, 256)],
            g_send_sem.at[group, h],
            g_recv_sem.at[c, h],
            dev(core * 4 + group // 2, at.plane + group % 2),
        )

    def grad_own(h):
        return pltpu.make_async_copy(
            grad_ref.at[span(at.group * 160 + h * 80, 80, 80)],
            grad_all.at[h, pl.ds(0, 80), span(c * 256, 256, 256)],
            local_sem.at[h],
        )

    def give(k, carry):
        group = flip(at.group, k)

        @pl.when(jnp.logical_and(mine, k == 0))
        def _():
            grad_own(0).start()
            grad_own(1).start()

        @pl.when(jnp.logical_not(jnp.logical_and(mine, k == 0)))
        def _():
            grad_copy(group, 0).start()
            grad_copy(group, 1).start()

        return carry

    lax.fori_loop(0, 8, give, 0)

    bits = {"y": row, "x": xbit, "z": zbit, "h": half}
    peers = {"y": across, "x": xpeer, "z": zpeer, "h": hpeer}
    results = (first_out, second_out, third_out)

    def finer(m):
        return "z" if SUM_WAYS[m].index("x") < SUM_WAYS[m].index("z") else "x"

    def cut(ref, way, bit):
        if way == "y":
            return (bit,)
        lead = (slice(None),) * (len(ref.shape) - 2)
        if way == "h":
            return lead + (slice(None), span(bit * 640, 640, 640))
        rows = ref.shape[-2] // 2
        return lead + (span(bit * rows, rows, rows),)

    def main_copy(stage, m):
        if stage < 0:
            y = stage + 2
            src, dst, to = sums.at[pl.ds((m * 2 + y) * 320, 320)], core_in.at[m, y], twin
        elif stage < 4:
            way = SUM_WAYS[m][stage]
            ref = core_in.at[m] if stage == 0 else taken[m][stage - 1]
            src, dst, to = ref.at[cut(ref, way, 1 - bits[way])], taken[m][stage], peers[way]
        else:
            way = SPREAD_WAYS[m][stage - 4]
            known = SPREAD_WAYS[m][: stage - 4]
            low = finer(m)
            high = "x" if low == "z" else "z"
            if high in known:
                rows = pl.ds(0, 320)
            elif low in known:
                rows = span(bits[high] * 160, 160, 160)
            else:
                rows = span(bits[high] * 160 + bits[low] * 80, 80, 80)
            lanes = pl.ds(0, 1280) if "h" in known else span(half * 640, 640, 640)
            src = dst = results[m].at[rows, lanes]
            to = peers[way]
        return remote(src, dst, m_send.at[stage + 2, m], m_recv.at[stage + 2, m], to)

    def added(ref, other, spot):
        for k in range(2) if len(ref.shape) == 3 else (None,):
            here = () if k is None else (k,)
            there = spot if k is None else (k,) + spot[1:]
            ref[here] = (ref[here].astype(F32) + other[there].astype(F32)).astype(BF)

    def main(stage, m):
        if stage == 0:
            for y in range(2):
                main_copy(y - 2, m).wait_recv()
                total = core_in[m, y].astype(F32) + weight_rows(m, 2 * y + core)
                core_in[m, y] = total.astype(BF)
        elif stage < 5:
            main_copy(stage - 1, m).wait_recv()
            way = SUM_WAYS[m][stage - 1]
            ref = core_in.at[m] if stage == 1 else taken[m][stage - 2]
            spot = cut(ref, way, bits[way])
            if stage < 4:
                added(taken[m][stage - 1], ref, spot)
            else:
                low = finer(m)
                high = "x" if low == "z" else "z"
                rows = span(bits[high] * 160 + bits[low] * 80, 80, 80)
                results[m][rows, span(half * 640, 640, 640)] = (
                    taken[m][3][...].astype(F32) + ref[spot].astype(F32)
                ).astype(BF)
        else:
            main_copy(stage - 1, m).wait_recv()
        if stage < 7:
            main_copy(stage, m).start()

    lefts = (act_ref, normed_mlp_ref, att_ref)
    rights = (dy_ref, up_grad_ref, branch_ref)

    def weight_rows(m, quarter):
        rows = span(quarter * 320, 320, 320)
        return jnp.dot(lefts[m][rows, :], rights[m][...], preferred_element_type=F32)

    def main_first(m):
        for name in (("act", "dy"), ("normed", "up"), ("att", "branch"))[m]:
            loads[name].wait()
        for y in range(2):
            part = weight_rows(m, 2 * y + 1 - core)
            sums[(m * 2 + y) * 320 : (m * 2 + y + 1) * 320, :] = part.astype(BF)
            main_copy(y - 2, m).start()

    def prepare():
        loads["qkv"].wait()
        for h in range(2):
            grad_all[h, 80:, :] = jnp.zeros((48, 2048), BF)
            k_turned[h] = jnp.transpose(qkv_ref[:, (2 + h) * LANES : (3 + h) * LANES])
        for k in range(8):
            block = place_ref[0:1, k * 256 : (k + 1) * 256]
            key_pos[k * 256 : (k + 1) * 256, :] = jnp.transpose(
                jnp.broadcast_to(block, (LANES, 256))
            )
        scale_ref[...] = jnp.zeros((8, LANES), F32)

    def take(k, carry):
        block = flip(c, k)

        @pl.when(jnp.logical_and(mine, k == 0))
        def _():
            grad_own(0).wait()
            grad_own(1).wait()

        @pl.when(jnp.logical_not(jnp.logical_and(mine, k == 0)))
        def _():
            for h in range(2):
                await_recv(
                    grad_all.at[h, pl.ds(0, 80), pl.ds(0, 256)], g_recv_sem.at[block, h]
                )

        return carry

    def take_all():
        loads["out"].wait()
        lax.fori_loop(0, 8, take, 0)
        for h in range(2):
            delta[h : h + 1, :] = jnp.sum(
                grad_all[h, :80, :].astype(F32) * out_ref[h * 80 : (h + 1) * 80, :].astype(F32),
                axis=0,
                keepdims=True,
            )

    def head_copy(stage, h):
        if stage == 0:
            src, dst, to = slices.at[h, :, span((1 - row) * 640, 640, 640)], s1.at[h], across
        elif stage == 1:
            src, dst, to = s1.at[h, span(128 - half * 128, 128, 128)], s2.at[h], hpeer
        elif stage < 5:
            way = HEAD_WAYS[stage - 2]
            known = HEAD_WAYS[: stage - 2]
            where = (core,) + tuple(slice(None) if d in known else bits[d] for d in "xz") + (h,)
            rows = slice(None) if "h" in known else span(half * 128, 128, 128)
            src = dst = gathered.at[where + (rows,)]
            to = peers[way]
        else:
            src = dst = gathered.at[core, :, :, h]
            to = twin
        return remote(src, dst, q_send.at[stage, h], q_recv.at[stage, h], to)

    def head(stage, h):
        if stage > 0:
            head_copy(stage - 1, h).wait_recv()
        if stage == 1:
            add_into(s1.at[h], slices.at[h, :, span(row * 640, 640, 640)], 256, 128)
        if stage == 2:
            own = span(half * 128, 128, 128)
            gathered[core, xbit, zbit, h, own, :] = (
                s2[h].astype(F32) + s1[h, own, :].astype(F32)
            ).astype(BF)
        if stage < 6:
            head_copy(stage, h).start()

    def normed_load(part):
        return pltpu.make_async_copy(
            normed_hbm.at[:, pl.ds(part * 256, 256)], normed_part.at[part % 2], local_sem.at[2 + part % 2]
        )

    def attend_head(h, hooks):
        key_sum[...] = jnp.zeros((2048, LANES), F32)
        value_sum[...] = jnp.zeros((2048, LANES), F32)

        def block_grad(block, carry):
            lanes = span(block * 256, 256, 256)
            high = place_ref[0:1, lanes]
            least = place_ref[1:2, lanes]
            query = qkv_ref[lanes, h * LANES : (h + 1) * LANES]
            grad_t = grad_all[h, :, lanes]
            q_grad = jnp.zeros((LANES, 256), F32)
            for part in range(KEY_PARTS):
                some = slice(part * KEY_ROWS, (part + 1) * KEY_ROWS)
                kp = key_pos[some, :]
                kp = jnp.concatenate([kp, kp], axis=1)
                keys = qkv_ref[some, (2 + h) * LANES : (3 + h) * LANES]
                values = qkv_ref[some, (4 + h) * LANES : (5 + h) * LANES]
                s = lax.dot_general(
                    keys, query, (((1,), (1,)), ((), ())), preferred_element_type=F32
                )
                visible = (kp >= least) & (kp <= high)
                p = jnp.exp(jnp.where(visible, s - lse_ref[h : h + 1, lanes], FLOOR))
                gp = jnp.dot(values, grad_t, preferred_element_type=F32)
                gs = (p * (gp - delta[h : h + 1, lanes])).astype(BF)
                value_sum[some, :] += lax.dot_general(
                    p.astype(BF), grad_t, (((1,), (1,)), ((), ())), preferred_element_type=F32
                )
                key_sum[some, :] += jnp.dot(gs, query, preferred_element_type=F32)
                q_grad += jnp.dot(k_turned[h, :, some], gs, preferred_element_type=F32)
            scale_ref[0:1, :] += jnp.sum(
                jnp.transpose(q_grad) * query.astype(F32), axis=0, keepdims=True
            )
            turned[h * LANES : (h + 1) * LANES, lanes] = (q_grad * mult_ref[:, 0:1]).astype(BF)
            for step, todo in hooks.items():

                @pl.when(block == step)
                def _(todo=todo):
                    for one in todo:
                        one()

            return carry

        lax.fori_loop(0, 8, block_grad, 0)

    def attend_end(h):
        for j, total in ((1, key_sum), (2, value_sum)):
            low = jnp.transpose(total[...]).astype(BF)
            turned[(2 * j + h) * LANES : (2 * j + h + 1) * LANES, :] = low

    def head_first(h):
        slices[h, 240:, :] = jnp.zeros((16, 1280), BF)
        for part in range(5):
            normed_load(part).wait()
            if part + 1 < 5:
                normed_load(part + 1).start()
            for j in range(3):
                first = (2 * j + h) * LANES
                slices[h, j * 80 : (j + 1) * 80, part * 256 : (part + 1) * 256] = jnp.dot(
                    turned[first : first + 80, :],
                    normed_part[part % 2],
                    preferred_element_type=F32,
                ).astype(BF)
        if h == 0:
            normed_load(0).start()
        head(0, h)

    def norm_bits(k):
        return (1 - xbit, 1 - xbit, xbit, xbit)[k], (1 - zbit, zbit, 1 - zbit, zbit)[k]

    def norm_spot(k, hh):
        slot = 2 * k + hh
        return sums.at[pl.ds(slot // 5 * 640, 640), pl.ds(slot % 5 * 256, 256)]

    def norm_copy(stage, k, hh=0):
        if stage == 0:
            return remote(
                norm_spot(k, hh), n_core.at[k, hh], nc_send.at[k, hh], nc_recv.at[k, hh], twin
            )
        took = k
        if stage == 1:
            ends = n_core.at[k], n_x.at[k], xpeer
        elif stage == 2:
            ends = n_core.at[2, (1 - half, half)[k]], n_z.at[k], zpeer
        else:
            to = dev(flip(c, 4), at.pack) if k == 0 else dev(c, at.twin)
            took = (core, 2)[k]
            ends = n_core.at[3, (1 - half, half)[k]], n_last.at[core], to
        return remote(ends[0], ends[1], n_send.at[stage, k], n_recv.at[stage, took], ends[2])

    def norm_part(k, hh, which):
        xs, zs = norm_bits(k)
        lanes = span((hh * 4 + zs * 2 + xs) * 256, 256, 256)
        rows = span(which * 640, 640, 640)
        return jnp.dot(w_ref[rows, :], turned[:, lanes], preferred_element_type=F32)

    def norm_first(k):
        if k == 0:
            loads["w"].wait()
            for m in range(3):
                for stage in range(2):
                    main_copy(stage - 2, m).wait_send()
        for hh in range(2):
            norm_spot(k, hh)[...] = norm_part(k, hh, 1 - core).astype(BF)
            norm_copy(0, k, hh).start()

    def norm_core(k):
        for hh in range(2):
            norm_copy(0, k, hh).wait_recv()
            n_core[k, hh] = (n_core[k, hh].astype(F32) + norm_part(k, hh, core)).astype(BF)
        if k < 2:
            norm_copy(1, k).start()

    def scale_copy(stage):
        where = (twin, across, xpeer, zpeer, hpeer)[stage]
        return remote(scale_ref, scale_in.at[stage], v_send.at[stage], v_recv.at[stage], where)

    def tiny(stage):
        if stage > 0:
            scale_copy(stage - 1).wait()
            scale_ref[...] += scale_in[stage - 1]
        if stage < 5:
            scale_copy(stage).start()

    def norm_x(k):
        norm_copy(1, k).wait_recv()
        for hh in range(2):
            add_into(n_core.at[2 + k, hh], n_x.at[k, hh], 640, 80)
        if k == 0:
            norm_copy(2, 0).start()
            norm_copy(2, 1).start()

    def norm_far():
        norm_copy(2, 0).wait_recv()
        add_into(n_core.at[3, 1 - half], n_z.at[0], 640, 80)
        norm_copy(3, 0).start()

    def norm_near():
        norm_copy(2, 1).wait_recv()
        add_into(n_core.at[3, half], n_z.at[1], 640, 80)

        @pl.when(jnp.logical_not(mine))
        def _():
            norm_copy(3, 1).start()

    def norm_last():
        loads["x"].wait()
        loads["resid"].wait()
        @pl.when(mine)
        def _():
            n_last[core] = n_core[3, half]
            await_recv(n_last.at[0], n_recv.at[3, 2])

        @pl.when(jnp.logical_not(mine))
        def _():
            await_recv(n_last.at[0], n_recv.at[3, 0])
            await_recv(n_last.at[1], n_recv.at[3, 1])

        xf = x_ref[...].astype(F32)
        inv = lax.rsqrt(jnp.mean(xf * xf, axis=1, keepdims=True) + EPS)
        scaled = jnp.concatenate(
            [jnp.transpose(n_last[k].astype(F32)) for k in range(2)], axis=1
        ) * gain_ref[0:1, :]
        input_grad_ref[...] = resid_grad_ref[...] + inv * (
            scaled - xf * inv * inv * jnp.mean(scaled * xf, axis=1, keepdims=True)
        )

    def turn_all():
        for k in range(4):
            for hh in range(2):
                norm_copy(0, k, hh).wait_send()
        for core_k in range(2):
            for m4 in range(4):
                group = 2 * m4 + core_k
                for h in range(2):
                    for j in range(3):
                        start = j * 1280 + (group * 2 + h) * 80
                        sums[
                            start % 1920 : start % 1920 + 80, start // 1920 * 640 : start // 1920 * 640 + 640
                        ] = gathered[core_k, m4 % 2, m4 // 2, h, j * 80 : (j + 1) * 80, :]

        for part in range(2):

            def turn(k, carry, part=part):
                strip[...] = jnp.transpose(sums[span(k * LANES, LANES, LANES), part * 640 : part * 640 + 640])
                slice_out[:, span(part * 1920 + k * LANES, LANES, LANES)] = strip[span(core * 320, 320, 320), :]
                return carry

            lax.fori_loop(0, 15, turn, 0)


    tasks = {"prep": prepare, "take": take_all, "nb0": lambda: norm_x(0), "nb1": lambda: norm_x(1)}
    tasks |= {"nc_f": norm_far, "nc_n": norm_near, "nfin": norm_last, "turn": turn_all}
    for m in range(3):
        tasks[f"mt{m}"] = functools.partial(main_first, m)
        for stage in range(4):
            tasks[f"m{stage}{m}"] = functools.partial(main, stage, m)
        for stage in range(3):
            tasks[f"g{stage}{m}"] = functools.partial(main, 4 + stage, m)
        tasks[f"mw{m}"] = functools.partial(main, 7, m)
    for h in range(2):
        tasks[f"E{h}"] = functools.partial(attend_end, h)
        tasks[f"qs{h}"] = functools.partial(head_first, h)
        for stage, name in enumerate(("qa", "q0", "q1", "q2", "qc", "qw")):
            tasks[f"{name}{h}"] = functools.partial(head, 1 + stage, h)
    for k in range(4):
        tasks[f"nt{k}"] = functools.partial(norm_first, k)
        tasks[f"na{k}"] = functools.partial(norm_core, k)
    for stage in range(6):
        tasks[f"v{stage}"] = functools.partial(tiny, stage)

    normed_load(0).start()
    spot = 0
    while spot < len(PLAN):
        name = PLAN[spot]
        if name[0] != "L":
            tasks[name]()
            spot += 1
            continue
        h, step, hooks = int(name[1]), -1, {}
        while step < 7 or PLAN[spot][0] == "L":
            if PLAN[spot][0] == "L":
                step = int(PLAN[spot][2])
                if step == 7:
                    spot += 1
                    break
            else:
                hooks.setdefault(step, []).append(tasks[PLAN[spot]])
            spot += 1
        attend_head(h, hooks)

    def sent(block, carry):
        own_in = jnp.logical_and(mine, block == at.group)

        @pl.when(jnp.logical_not(own_in))
        def _():
            for h in range(2):
                grad_copy(block, h).wait_send()

        return carry

    lax.fori_loop(0, 8, sent, 0)
    for m in range(3):
        for stage in range(7):
            main_copy(stage, m).wait_send()
    for h in range(2):
        for stage in range(6):
            head_copy(stage, h).wait_send()
    for k in range(2):
        norm_copy(1, k).wait_send()
        norm_copy(2, k).wait_send()
    norm_copy(3, 0).wait_send()

    @pl.when(jnp.logical_not(mine))
    def _():
        norm_copy(3, 1).wait_send()


def sum_slots():
    slots = []
    for ways in SUM_WAYS:
        shape, own = [2, 320, 1280], []
        for way in ways:
            if way == "y":
                shape = shape[1:]
            else:
                shape[-1 if way == "h" else -2] //= 2
            own.append(pltpu.VMEM(tuple(shape), BF))
        slots.append(own)
    return slots


def backward(*args):
    shape = jax.ShapeDtypeStruct
    dma = pltpu.SemaphoreType.DMA
    specs = [ANY_SPEC] * 17
    for k in (8, 10, 13, 16):
        specs[k] = VMEM_SPEC
    return pl.pallas_call(
        backward_kernel,
        name="backward",
        out_shape=(
            shape((320, 1280), BF),
            shape((320, 1280), BF),
            shape((320, 1280), BF),
            shape((320, 3840), BF),
            shape((256, 1280), F32),
            shape((8, LANES), F32),
        ),
        in_specs=specs,
        out_specs=(VMEM_SPEC,) * 6,
        scratch_shapes=[
            pltpu.VMEM((1280, 256), BF),
            pltpu.VMEM((256, 1280), BF),
            pltpu.VMEM((1280, 256), BF),
            pltpu.VMEM((256, 1280), BF),
            pltpu.VMEM((1280, 256), BF),
            pltpu.VMEM((256, 1280), BF),
            pltpu.VMEM((2048, 768), BF),
            pltpu.VMEM((160, 2048), BF),
            pltpu.VMEM((1280, 768), BF),
            pltpu.VMEM((256, 1280), BF),
            pltpu.VMEM((256, 1280), F32),
            pltpu.VMEM((2, 128, 2048), BF),
            pltpu.VMEM((2048, LANES), F32),
            pltpu.VMEM((2, 128, 2048), BF),
            pltpu.VMEM((8, 2048), F32),
            pltpu.VMEM((2048, LANES), F32),
            pltpu.VMEM((2048, LANES), F32),
            pltpu.VMEM((768, 2048), BF),
            pltpu.VMEM((2, 2048, 256), BF),
            pltpu.VMEM((4, 2, 640, 256), BF),
            pltpu.VMEM((2, 2, 640, 256), BF),
            pltpu.VMEM((2, 640, 256), BF),
            pltpu.VMEM((2, 640, 256), BF),
            pltpu.VMEM((1920, 1280), BF),
            pltpu.VMEM((3, 2, 320, 1280), BF),
            sum_slots(),
            pltpu.VMEM((2, 256, 1280), BF),
            pltpu.VMEM((2, 256, 640), BF),
            pltpu.VMEM((2, 128, 640), BF),
            pltpu.VMEM((2, 2, 2, 2, 256, 640), BF),
            pltpu.VMEM((640, LANES), BF),
            pltpu.VMEM((5, 8, LANES), F32),
            dma((8, 2)),
            dma((8, 2)),
            dma((4,)),
            dma((9, 3)),
            dma((9, 3)),
            dma((6, 2)),
            dma((6, 2)),
            dma((4, 2)),
            dma((4, 2)),
            dma((4, 4)),
            dma((4, 4)),
            dma((5,)),
            dma((5,)),
            dma((11,)),
        ],
        compiler_params=pltpu.CompilerParams(
            collective_id=1, has_side_effects=True, vmem_limit_bytes=VMEM_LIMIT
        ),
        cost_estimate=pl.CostEstimate(
            flops=30_000_000_000, bytes_accessed=60_000_000, transcendentals=8_400_000
        ),
    )(*args)


def fast_body(
    tokens,
    lengths,
    position,
    qkv_weight,
    out_weight,
    up_weight,
    down_weight,
    attn_gain,
    mlp_gain,
    query_scale,
    cotangent,
):
    f = lax.axis_index("fsdp")
    x, dy = tokens[0], cotangent[0]
    small = [jnp.pad(a, (0, 384 - a.shape[0])) for a in (attn_gain, mlp_gain, query_scale)]
    small = jnp.stack(small + [jnp.zeros((384,), BF)] * 13)
    (
        att_t, normed, qkv, lse, out, auxsum, place, w_heads,
        result, resid_grad, branch_grad, up_grad, act_t, normed_mlp_t, grad_t,
    ) = forward(
        lengths, x, qkv_weight, small, position, out_weight, up_weight, down_weight, dy
    )
    scale_float = auxsum[2, :80]
    base_scale = LOG2E / math.sqrt(80)
    soft = jax.nn.softplus(scale_float)
    mult = jnp.broadcast_to(jnp.pad(base_scale * soft, (0, 48))[:, None], (LANES, LANES))
    g_down, g_up, g_out, g_qkv, input_grad, scale_sum = backward(
        grad_t,
        att_t,
        branch_grad,
        normed_mlp_t,
        up_grad,
        act_t,
        dy,
        qkv,
        lse,
        out,
        place,
        normed,
        w_heads,
        mult,
        x,
        resid_grad,
        auxsum,
    )
    g_down, g_up, g_out = (g.astype(F32) for g in (g_down, g_up, g_out))
    g_qkv = g_qkv.astype(F32)
    grad_attn_gain = jnp.sum(qkv_weight.astype(F32) * g_qkv, axis=1) / attn_gain.astype(F32)
    grad_mlp_gain = jnp.sum(up_weight.astype(F32) * g_up, axis=1) / mlp_gain.astype(F32)
    grad_scale = scale_sum[0, :80] / soft * jax.nn.sigmoid(scale_float)
    return (
        result[None],
        input_grad[None],
        g_qkv,
        g_out,
        g_up,
        g_down,
        grad_attn_gain,
        grad_mlp_gain,
        lax.dynamic_slice_in_dim(grad_scale, f * 20, 20),
    )


def solution(mesh):
    placed = (
        P("fsdp", "ctx", None),
        P("fsdp", None),
        P("fsdp", None),
        P("fsdp", None),
        P("fsdp", None),
        P("fsdp", None),
        P("fsdp", None),
        P("fsdp"),
        P("fsdp"),
        P("fsdp"),
        P("fsdp", "ctx", None),
    )
    fits = mesh.shape["ctx"] == 8 and mesh.shape["fsdp"] == 4
    return jax.shard_map(
        fast_body if fits else body,
        mesh=mesh,
        in_specs=placed,
        out_specs=(
            P("fsdp", "ctx", None),
            P("fsdp", "ctx", None),
            P("fsdp", None),
            P("fsdp", None),
            P("fsdp", None),
            P("fsdp", None),
            P("fsdp"),
            P("fsdp"),
            P("fsdp"),
        ),
        check_vma=False,
    )
```

```python
import functools
import math

import jax
import jax.numpy as jnp
from jax import lax
from jax.experimental import pallas as pl
from jax.experimental.pallas import tpu as pltpu
from jax.sharding import PartitionSpec as P

HEADS = 16


EPS = 1e-06
FLOOR = -1e30
LOG2E = 1.442695041

MESH = pl.DeviceIdType.MESH
LANES = 128
BF = jnp.bfloat16
F32 = jnp.float32
VMEM_SPEC = pl.BlockSpec(memory_space=pltpu.VMEM)
ANY_SPEC = pl.BlockSpec(memory_space=pl.ANY)
VMEM_LIMIT = 60 << 20


def flip(number, mask):
    total = 0
    for bit in (1, 2, 4):
        left = (number // bit) % 2
        right = (mask // bit) % 2
        total = total + bit * (left + right - 2 * left * right)
    return total


class Place:
    def __init__(self):
        self.c = lax.axis_index("ctx")
        self.f = lax.axis_index("fsdp")
        self.core = self.f % 2
        self.plane = self.f - self.core
        self.half = self.c // 4
        self.pack = self.plane + self.half
        self.group = (self.c % 4) * 2 + self.core
        self.twin = self.plane + 1 - self.core
        self.across = (self.f + 2) % 4


def dev(ctx, fsdp):
    return {"ctx": ctx, "fsdp": fsdp}


def send(src, dst, send_sem, recv_sem, device):
    copy = pltpu.make_async_remote_copy(
        src_ref=src,
        dst_ref=dst,
        send_sem=send_sem,
        recv_sem=recv_sem,
        device_id=device,
        device_id_type=MESH,
    )
    copy.start()
    return copy


def await_recv(ref, sem):
    pltpu.make_async_copy(ref, ref, sem).wait()


def meet_plane(at):
    barrier = pltpu.get_barrier_semaphore()

    def greet(k, carry):
        pl.semaphore_signal(
            barrier,
            1,
            device_id=dev((at.c + k // 2) % 8, at.plane + (at.core + k) % 2),
            device_id_type=MESH,
        )
        return carry

    lax.fori_loop(1, 16, greet, 0)
    for k in range(2):
        pl.semaphore_signal(
            barrier, 1, device_id=dev(at.c, (at.plane + 2) % 4 + k), device_id_type=MESH
        )
    pl.semaphore_wait(barrier, 17)


def span(start, size, unit):
    return pl.ds(pl.multiple_of(start, unit), size)


def doc_index(places, seq_ends):
    return jnp.sum((places[:, None] >= seq_ends[None, :]).astype(jnp.int32), axis=1)


def spread_position(gathered_index, tok_dev, cycle_size):
    return gathered_index % tok_dev * cycle_size + gathered_index // tok_dev


def pair_scores(left_rows, right_rows):
    return jnp.einsum(
        "qhd,khd->qhk",
        left_rows.reshape(left_rows.shape[0], HEADS, -1),
        right_rows.reshape(right_rows.shape[0], HEADS, -1),
        preferred_element_type=jnp.float32,
    )


def pair_mask(query_pos, query_doc, key_pos, key_doc):
    return ((query_doc[:, None] == key_doc[None, :]) & (key_pos[None, :] <= query_pos[:, None]))[
        :, None, :
    ]


def in_blocks(advance, carried, pieces):
    total_rows = pieces[0].shape[0]
    block_rows = math.gcd(total_rows, 1024)
    block_count = total_rows // block_rows
    split = tuple((p.reshape((block_count, block_rows) + p.shape[1:]) for p in pieces))

    def inner(running, entry):
        return (advance(running, entry[1], entry[0] * block_rows), None)

    result, unused = lax.scan(inner, carried, (jnp.arange(block_count, dtype=jnp.int32), split))
    return result


def pair_terms(
    query_part,
    grad_part,
    log_part,
    delta_part,
    query_pos,
    query_doc,
    key_part,
    value_part,
    key_pos,
    key_doc,
):
    visible = pair_mask(query_pos, query_doc, key_pos, key_doc)
    prob_float = jnp.where(
        visible, jnp.exp(pair_scores(query_part, key_part) - log_part[:, :, None]), 0.0
    )
    grad_probs = pair_scores(grad_part, value_part)
    score_grad = (prob_float * (grad_probs - delta_part[:, :, None])).astype(jnp.bfloat16)
    return (prob_float.astype(jnp.bfloat16), score_grad)


def body(
    tokens,
    lengths,
    position,
    qkv_weight,
    out_weight,
    up_weight,
    down_weight,
    attn_gain,
    mlp_gain,
    query_scale,
    cotangent,
):
    cycle_size = lax.axis_size("ctx")
    my_index = lax.axis_index("ctx")
    tok_dev = tokens.shape[1]
    share_rows = tok_dev // cycle_size
    seq_ends = jnp.cumsum(lengths[0])
    place_row = position[0]
    residue = (place_row % cycle_size).reshape(cycle_size, tok_dev)
    landing = place_row // cycle_size
    matches = (
        residue[:, :, None] == jnp.arange(cycle_size, dtype=jnp.int32)[None, None, :]
    ).astype(jnp.int32)
    ranked = jnp.sum(jnp.cumsum(matches, axis=1) * matches, axis=2) - 1
    buffer_slot = residue * share_rows + ranked
    my_slots = lax.dynamic_index_in_dim(buffer_slot, my_index, 0, keepdims=False)
    local_rows = jnp.arange(tok_dev, dtype=jnp.int32)
    outgoing = jnp.zeros((tok_dev,), jnp.int32).at[my_slots].set(local_rows)
    flat_slot = (jnp.arange(cycle_size, dtype=jnp.int32)[:, None] * tok_dev + buffer_slot).reshape(
        -1
    )
    landing_table = (
        jnp.zeros((cycle_size * tok_dev,), jnp.int32)
        .at[flat_slot]
        .set(landing)
        .reshape(cycle_size, cycle_size, share_rows)
    )
    arrived_slot = lax.dynamic_index_in_dim(landing_table, my_index, 1, keepdims=False).reshape(-1)
    arrived_order = jnp.zeros((tok_dev,), jnp.int32).at[arrived_slot].set(local_rows)
    moved_x, moved_dy = (
        lax.all_to_all(tokens[0][outgoing], "ctx", split_axis=0, concat_axis=0, tiled=True),
        lax.all_to_all(cotangent[0][outgoing], "ctx", split_axis=0, concat_axis=0, tiled=True),
    )
    dealt_x = moved_x[arrived_order]
    dealt_dy = moved_dy[arrived_order]
    query_pos = local_rows * cycle_size + my_index
    query_doc = doc_index(query_pos, seq_ends)
    full_qkv, full_out, full_up, full_down, attn_gain_full, mlp_gain_full, scale_full = (
        lax.all_gather(qkv_weight, "fsdp", axis=0, tiled=True),
        lax.all_gather(out_weight, "fsdp", axis=0, tiled=True),
        lax.all_gather(up_weight, "fsdp", axis=0, tiled=True),
        lax.all_gather(down_weight, "fsdp", axis=0, tiled=True),
        lax.all_gather(attn_gain, "fsdp", axis=0, tiled=True),
        lax.all_gather(mlp_gain, "fsdp", axis=0, tiled=True),
        lax.all_gather(query_scale, "fsdp", axis=0, tiled=True),
    )
    attn_gain_f = attn_gain_full.astype(jnp.float32)
    mlp_gain_f = mlp_gain_full.astype(jnp.float32)
    scale_float = scale_full.astype(jnp.float32)
    x_float = dealt_x.astype(jnp.float32)
    inv_attn = lax.rsqrt(jnp.mean(x_float * x_float, axis=1, keepdims=True) + EPS)
    normed_attn = (x_float * inv_attn * attn_gain_f).astype(jnp.bfloat16)
    projected = jnp.dot(normed_attn, full_qkv, preferred_element_type=jnp.float32)
    att_width = projected.shape[1] // 3
    head_dim = scale_full.shape[0]
    base_scale = LOG2E / math.sqrt(head_dim)
    multiplier = jnp.tile(base_scale * jax.nn.softplus(scale_float), att_width // head_dim)
    raw_query = projected[:, :att_width]
    queries = (raw_query * multiplier).astype(jnp.bfloat16)
    key_rows = projected[:, att_width : 2 * att_width].astype(jnp.bfloat16)
    value_rows = projected[:, 2 * att_width :].astype(jnp.bfloat16)

    def key_place(first_row, amount):
        gathered_index = first_row + jnp.arange(amount, dtype=jnp.int32)
        key_pos = spread_position(gathered_index, tok_dev, cycle_size)
        return (key_pos, doc_index(key_pos, seq_ends))

    def stat_block(carried, pieces, first_row):
        running_max, running_sum = carried
        key_pos, key_doc = key_place(first_row, pieces[0].shape[0])
        visible = pair_mask(query_pos, query_doc, key_pos, key_doc)
        logits = jnp.where(visible, pair_scores(queries, pieces[0]), FLOOR)
        new_max = jnp.maximum(running_max, jnp.max(logits, axis=2))
        added = jnp.sum(jnp.where(visible, jnp.exp(logits - new_max[:, :, None]), 0.0), axis=2)
        return (new_max, running_sum * jnp.exp(running_max - new_max) + added)

    def output_block(summed, pieces, first_row):
        key_pos, key_doc = key_place(first_row, pieces[0].shape[0])
        visible = pair_mask(query_pos, query_doc, key_pos, key_doc)
        prob_low = jnp.where(
            visible, jnp.exp(pair_scores(queries, pieces[0]) - log_total[:, :, None]), 0.0
        ).astype(jnp.bfloat16)
        values_part = pieces[1].reshape(pieces[1].shape[0], HEADS, -1)
        return summed + jnp.einsum(
            "qhk,khd->qhd", prob_low, values_part, preferred_element_type=jnp.float32
        ).reshape(summed.shape)

    def query_grad_block(summed, pieces, first_row):
        key_pos, key_doc = key_place(first_row, pieces[0].shape[0])
        unused_probs, score_grad = pair_terms(
            queries,
            attended_grad,
            log_total,
            row_delta,
            query_pos,
            query_doc,
            pieces[0],
            pieces[1],
            key_pos,
            key_doc,
        )
        keys_part = pieces[0].reshape(pieces[0].shape[0], HEADS, -1)
        return summed + jnp.einsum(
            "qhk,khd->qhd", score_grad, keys_part, preferred_element_type=jnp.float32
        ).reshape(summed.shape)

    def key_grad_block(carried, pieces, first_row):
        amount = pieces[0].shape[0]
        part_pos, part_doc = key_place(first_row, amount)
        part_log = lax.dynamic_slice_in_dim(all_log, first_row, amount, 0)
        part_delta = lax.dynamic_slice_in_dim(all_delta, first_row, amount, 0)
        prob_low, score_grad = pair_terms(
            pieces[0],
            pieces[1],
            part_log,
            part_delta,
            part_pos,
            part_doc,
            key_rows,
            value_rows,
            query_pos,
            query_doc,
        )
        grad_keys = carried[0] + jnp.einsum(
            "qhk,qhd->khd",
            score_grad,
            pieces[0].reshape(amount, HEADS, -1),
            preferred_element_type=jnp.float32,
        ).reshape(tok_dev, -1)
        grad_values = carried[1] + jnp.einsum(
            "qhk,qhd->khd",
            prob_low,
            pieces[1].reshape(amount, HEADS, -1),
            preferred_element_type=jnp.float32,
        ).reshape(tok_dev, -1)
        return (grad_keys, grad_values)

    zero_stats = (
        jnp.full((tok_dev, HEADS), FLOOR, jnp.float32),
        jnp.zeros((tok_dev, HEADS), jnp.float32),
    )
    zero_rows = jnp.zeros((tok_dev, att_width), jnp.float32)
    running_max, running_sum = in_blocks(
        stat_block, zero_stats, (lax.all_gather(key_rows, "ctx", axis=0, tiled=True),)
    )
    log_total = running_max + jnp.log(running_sum)
    attended = in_blocks(
        output_block,
        zero_rows,
        (
            lax.all_gather(key_rows, "ctx", axis=0, tiled=True),
            lax.all_gather(value_rows, "ctx", axis=0, tiled=True),
        ),
    )
    attended_low = attended.astype(jnp.bfloat16)
    resid = x_float + jnp.dot(attended_low, full_out, preferred_element_type=jnp.float32)
    inv_mlp = lax.rsqrt(jnp.mean(resid * resid, axis=1, keepdims=True) + EPS)
    normed_mlp = (resid * inv_mlp * mlp_gain_f).astype(jnp.bfloat16)
    up_proj = jnp.dot(normed_mlp, full_up, preferred_element_type=jnp.float32)
    act_low = jax.nn.silu(up_proj).astype(jnp.bfloat16)
    result = resid + jnp.dot(act_low, full_down, preferred_element_type=jnp.float32)
    cot_float = dealt_dy.astype(jnp.float32)
    grad_down = jnp.dot(act_low.T, dealt_dy, preferred_element_type=jnp.float32)
    act_grad = jnp.dot(dealt_dy, full_down.T, preferred_element_type=jnp.float32)
    sigma = jax.nn.sigmoid(up_proj)
    up_grad = (act_grad * sigma * (1.0 + up_proj * (1.0 - sigma))).astype(jnp.bfloat16)
    grad_up = jnp.dot(normed_mlp.T, up_grad, preferred_element_type=jnp.float32)
    norm_mlp_grad = jnp.dot(up_grad, full_up.T, preferred_element_type=jnp.float32)
    grad_mlp_gain = jnp.sum(norm_mlp_grad * resid * inv_mlp, axis=0)
    scaled_mlp = norm_mlp_grad * mlp_gain_f
    resid_grad = cot_float + inv_mlp * (
        scaled_mlp - resid * inv_mlp * inv_mlp * jnp.mean(scaled_mlp * resid, axis=1, keepdims=True)
    )
    branch_grad = resid_grad.astype(jnp.bfloat16)
    grad_out = jnp.dot(attended_low.T, branch_grad, preferred_element_type=jnp.float32)
    attended_grad = jnp.dot(branch_grad, full_out.T, preferred_element_type=jnp.float32).astype(
        jnp.bfloat16
    )
    row_delta = jnp.sum(
        (attended_grad.astype(jnp.float32) * attended).reshape(tok_dev, HEADS, -1), axis=2
    )
    query_grads = in_blocks(
        query_grad_block,
        zero_rows,
        (
            lax.all_gather(key_rows, "ctx", axis=0, tiled=True),
            lax.all_gather(value_rows, "ctx", axis=0, tiled=True),
        ),
    )
    all_log, all_delta = (
        lax.all_gather(log_total, "ctx", axis=0, tiled=True),
        lax.all_gather(row_delta, "ctx", axis=0, tiled=True),
    )
    key_grad_f, value_grad_f = in_blocks(
        key_grad_block,
        (zero_rows, zero_rows),
        (
            lax.all_gather(queries, "ctx", axis=0, tiled=True),
            lax.all_gather(attended_grad, "ctx", axis=0, tiled=True),
        ),
    )
    scale_terms = jnp.sum((query_grads * raw_query).reshape(tok_dev, -1, head_dim), axis=(0, 1))
    grad_scale = scale_terms * base_scale * jax.nn.sigmoid(scale_float)
    proj_grad = jnp.concatenate(
        [
            (query_grads * multiplier).astype(jnp.bfloat16),
            key_grad_f.astype(jnp.bfloat16),
            value_grad_f.astype(jnp.bfloat16),
        ],
        axis=1,
    )
    grad_qkv = jnp.dot(normed_attn.T, proj_grad, preferred_element_type=jnp.float32)
    norm_attn_grad = jnp.dot(proj_grad, full_qkv.T, preferred_element_type=jnp.float32)
    grad_attn_gain = jnp.sum(norm_attn_grad * x_float * inv_attn, axis=0)
    scaled_attn = norm_attn_grad * attn_gain_f
    input_grad = resid_grad + inv_attn * (
        scaled_attn
        - x_float * inv_attn * inv_attn * jnp.mean(scaled_attn * x_float, axis=1, keepdims=True)
    )
    owned = (
        lax.psum_scatter(grad_qkv, "fsdp", scatter_dimension=0, tiled=True),
        lax.psum_scatter(grad_out, "fsdp", scatter_dimension=0, tiled=True),
        lax.psum_scatter(grad_up, "fsdp", scatter_dimension=0, tiled=True),
        lax.psum_scatter(grad_down, "fsdp", scatter_dimension=0, tiled=True),
        lax.psum_scatter(grad_attn_gain, "fsdp", scatter_dimension=0, tiled=True),
        lax.psum_scatter(grad_mlp_gain, "fsdp", scatter_dimension=0, tiled=True),
        lax.psum_scatter(grad_scale, "fsdp", scatter_dimension=0, tiled=True),
    )
    summed_grads = lax.psum(
        (owned[0], owned[1], owned[2], owned[3], owned[4], owned[5], owned[6]), "ctx"
    )
    back_out, back_grad = (
        lax.all_to_all(result[arrived_slot], "ctx", split_axis=0, concat_axis=0, tiled=True),
        lax.all_to_all(input_grad[arrived_slot], "ctx", split_axis=0, concat_axis=0, tiled=True),
    )
    return (
        back_out[my_slots][None],
        back_grad[my_slots][None],
        summed_grads[0],
        summed_grads[1],
        summed_grads[2],
        summed_grads[3],
        summed_grads[4],
        summed_grads[5],
        summed_grads[6],
    )


HUB_WAYS = {k: ((2, 0), (2, 1)) for k in range(1, 8)}
HUB_WAYS[1] += ((1, 0),)
HUB_WAYS[2] += ((0, 1),)
HUB_WAYS[4] += ((0, 0), (0, 1), (1, 0), (1, 1))
HUB_WAYS[6] += ((0, 0), (0, 1))

SPLIT = (False, True, False)
WEIGHT_STEPS = ((2, 2, 1), (4, 2, 0), (6, 3, 1))


def attend_kernel(
    ends_ref,
    x_ref,
    w_ref,
    aux_ref,
    pos_ref,
    out_w_ref,
    up_w_ref,
    down_w_ref,
    dy_ref,
    att_ref,
    normed_out,
    qkv_out,
    lse_ref,
    out_ref,
    auxsum_ref,
    place_ref,
    w_out,
    result_ref,
    resid_grad_ref,
    branch_ref,
    up_grad_ref,
    act_ref,
    normed_mlp_ref,
    grad_ref,
    x_mine,
    w_mine,
    dy_mine,
    x_all,
    normed_ref,
    qkv_ref,
    w_all,
    w_own,
    w_small,
    weights,
    aux_all,
    pos_all,
    v_turned,
    key_pos,
    att_send,
    x_send_sem,
    x_recv_sem,
    w_send_sem,
    w_recv_sem,
    aux_send_sem,
    aux_recv_sem,
    pos_sem,
    att_send_sem,
    att_recv_sem,
    m_send_sem,
    m_recv_sem,
    local_sem,
    save_sem,
    shard_sem,
):
    w_load = pltpu.make_async_copy(w_ref, w_mine, local_sem.at[0])
    w_load.start()
    x_load = pltpu.make_async_copy(x_ref, x_mine, local_sem.at[2])
    dy_load = pltpu.make_async_copy(dy_ref, dy_mine, local_sem.at[4])
    at = Place()
    meet_plane(at)
    c, f = at.c, at.f
    hub = at.core == at.half

    aux_own = pltpu.make_async_copy(aux_ref, aux_all.at[f], local_sem.at[1])
    aux_own.start()
    x_own = pltpu.make_async_copy(x_ref, x_all.at[c], local_sem.at[3])

    halves = (pl.ds(0, 128), pl.ds(128, 128))

    def x_far(part):
        return pltpu.make_async_remote_copy(
            src_ref=x_ref.at[halves[part]],
            dst_ref=x_all.at[c, halves[part]],
            send_sem=x_send_sem.at[0, 0, part],
            recv_sem=x_recv_sem.at[c, part],
            device_id=dev(flip(c, 4), f),
            device_id_type=MESH,
        )

    @pl.when(hub)
    def _():
        x_own.start()
        for part in range(2):
            for k, where in enumerate((dev(flip(c, 1), f), dev(flip(c, 2), f), dev(c, at.twin))):
                send(
                    x_ref.at[halves[part]],
                    x_all.at[c, halves[part]],
                    x_send_sem.at[0, k, part],
                    x_recv_sem.at[c, part],
                    where,
                )

    @pl.when(jnp.logical_not(hub))
    def _():
        x_far(0).start()
        x_far(1).start()

    w_copies, aux_copies = [], []
    for k in (2, 1, 3):
        aux_copies.append(
            send(
                aux_ref,
                aux_all.at[f],
                aux_send_sem.at[k],
                aux_recv_sem.at[f],
                dev(c, (f + k) % 4),
            )
        )

    pos = pos_ref[...]
    start = jnp.zeros_like(pos)
    end = 0
    for k in range(4):
        end = end + ends_ref[0, k]
        start = jnp.where(pos >= end, end, start)
    pos_all[at.core, 0:1, :] = pos.astype(F32)
    pos_all[at.core, 1:2, :] = start.astype(F32)
    pos_all[at.core, 2:8, :] = jnp.zeros((6, 2048), F32)
    pos_copy = send(
        pos_all.at[at.core], pos_all.at[at.core], pos_sem.at[0], pos_sem.at[1], dev(c, at.twin)
    )

    row = lax.broadcasted_iota(jnp.int32, (1280, 512), 0)
    column = lax.broadcasted_iota(jnp.int32, (1280, 512), 1)
    first = (c % 4) * 320
    w_load.wait()
    for k in range(2):
        some = jnp.zeros((320, 512), F32)
        for j in range(3):
            pick = (row - first - k * 160 == column - j * 160) & (column // 160 == j)
            pick = jnp.where(pick, 1.0, 0.0).astype(BF)
            some += jnp.dot(w_mine[:, j * 1280 : (j + 1) * 1280], pick, preferred_element_type=F32)
        w_own[k] = some.astype(BF)
    mine_rows = span(f * 320, 320, 320)
    for k in (2, 3, 1):
        to = (f + k) % 4
        w_copies.append(
            send(
                w_own.at[to % 2],
                w_small.at[mine_rows],
                w_send_sem.at[k],
                w_recv_sem.at[f],
                dev(c, to),
            )
        )
    w_small[mine_rows, :] = w_own[at.core]
    x_load.start()
    dy_load.start()


    shards = (out_w_ref, up_w_ref, down_w_ref)
    xbit = c % 2
    other = (f + 2) % 4

    def part(m, owner, x):
        return weights.at[m, span(owner * 320 + x * 160, 160, 160)]

    def weight_copy(m, way):
        if way == 0:
            src, dst, to = shards[m], weights.at[m, mine_rows], dev(c, at.twin)
        elif way == 1 and not SPLIT[m]:
            src, dst, to = shards[m], weights.at[m, mine_rows], dev(c, other)
        elif way == 3 and not SPLIT[m]:
            src = dst = weights.at[m, span(other * 320, 320, 320)]
            to = dev(c, at.twin)
        elif way == 1:
            src = shards[m].at[span(xbit * 160, 160, 160)]
            dst, to = part(m, f, xbit), dev(c, other)
        else:
            x = (xbit, xbit, 1 - xbit)[way - 2]
            src = dst = part(m, other, x)
            to = (dev(flip(c, 1), f), dev(c, at.twin), dev(c, at.twin))[way - 2]
        return pltpu.make_async_remote_copy(
            src_ref=src,
            dst_ref=dst,
            send_sem=m_send_sem.at[m, way],
            recv_sem=m_recv_sem.at[m, way],
            device_id=to,
            device_id_type=MESH,
        )

    def shard_copy(m):
        return pltpu.make_async_copy(shards[m], weights.at[m, mine_rows], shard_sem.at[m])

    def weight_first(m):
        weight_copy(m, 0).start()
        weight_copy(m, 1).start()
        shard_copy(m).start()

    def weight_second(m):
        weight_copy(m, 1).wait_recv()
        if SPLIT[m]:
            weight_copy(m, 2).start()
        weight_copy(m, 3).start()

    def weight_third(m):
        if SPLIT[m]:
            weight_copy(m, 2).wait_recv()
            weight_copy(m, 4).start()

    def weight_last(m):
        shard_copy(m).wait()
        for way in (0, 3, 4) if SPLIT[m] else (0, 3):
            weight_copy(m, way).wait_recv()


    aux_own.wait()
    for k in (1, 2, 3):
        await_recv(aux_all.at[0], aux_recv_sem.at[(f + k) % 4])
    aux = jnp.zeros((16, 1280), F32)
    scale = jnp.zeros((16, LANES), F32)
    row = lax.broadcasted_iota(jnp.int32, (384, 1280), 0)
    column = lax.broadcasted_iota(jnp.int32, (384, 1280), 1)
    for k in range(4):
        put = jnp.where((column == row + k * 320) & (row < 320), 1.0, 0.0).astype(BF)
        aux = aux + jnp.dot(aux_all[k], put, preferred_element_type=F32)
        put = (column[:LANES, :LANES] == row[:LANES, :LANES] + k * 20) & (row[:LANES, :LANES] < 20)
        put = jnp.where(put, 1.0, 0.0).astype(BF)
        scale = scale + jnp.dot(aux_all[k, :, :LANES], put, preferred_element_type=F32)
    auxsum_ref[...] = aux
    auxsum_ref[2:3, :LANES] = scale[2:3]
    gain = aux[0:1, :]
    mlp_gain = aux[1:2, :]
    scale = scale[2:3]
    real = lax.broadcasted_iota(jnp.int32, (1, LANES), 1) < 80
    mult = jnp.where(
        real, LOG2E / math.sqrt(80) * (jnp.maximum(scale, 0.0) + jnp.log1p(jnp.exp(-jnp.abs(scale)))), 0.0
    )
    one = jnp.ones_like(mult)
    mults = jnp.concatenate([mult, mult, one, one, one, one], axis=1)

    await_recv(pos_all.at[0], pos_sem.at[1])
    place_ref[...] = pos_all[at.half]
    for k in range(8):
        block = place_ref[0:1, k * 256 : (k + 1) * 256]
        key_pos[k * 256 : (k + 1) * 256, :] = jnp.transpose(
            jnp.broadcast_to(block, (LANES, 256))
        )

    def arrive(step, carry):
        k = step + jnp.where(step == 3, 1, 0) - jnp.where(step == 4, 1, 0)
        slot = flip(c, k)
        for part in range(2):
            piece = x_all.at[slot, halves[part]]
            if part == 0:

                @pl.when(jnp.logical_and(hub, k == 0))
                def _():
                    x_own.wait()

            @pl.when(jnp.logical_not(jnp.logical_and(hub, k == 0)))
            def _(part=part, piece=piece):
                await_recv(piece, x_recv_sem.at[slot, part])

            def onward(way, where, part=part, piece=piece):
                send(
                    piece, piece, x_send_sem.at[k, way, part], x_recv_sem.at[slot, part], where
                )

            for way, where in enumerate((dev(flip(c, 1), f), dev(flip(c, 2), f), dev(c, at.twin))):
                due = False
                for when in HUB_WAYS:
                    if (way, part) in HUB_WAYS[when]:
                        due = jnp.logical_or(due, k == when)

                @pl.when(jnp.logical_and(hub, due))
                def _(way=way, where=where, onward=onward):
                    onward(way, where)

        @pl.when(step == 3)
        def _():
            weight_first(0)

        @pl.when(step == 5)
        def _():
            weight_first(1)


        xf = x_all[slot].astype(F32)
        inv = lax.rsqrt(jnp.mean(xf * xf, axis=1, keepdims=True) + EPS)
        rows = span(slot * 256, 256, 256)
        normed_ref[rows, :] = (xf * inv * gain).astype(BF)
        pltpu.make_async_copy(
            normed_ref.at[rows], normed_out.at[rows], save_sem.at[slot, 0]
        ).start()
        return carry

    def project(step, carry):
        slot = flip(c, step)
        rows = span(slot * 256, 256, 256)
        proj = jnp.dot(normed_ref[rows, :], w_all[...], preferred_element_type=F32)
        qkv_ref[rows, :] = (proj * mults).astype(BF)
        pltpu.make_async_copy(qkv_ref.at[rows], qkv_out.at[rows], save_sem.at[slot, 1]).start()
        return carry

    lax.fori_loop(0, 7, arrive, 0)
    for k in (1, 2, 3):
        await_recv(w_small.at[pl.ds(0, 320)], w_recv_sem.at[(f + k) % 4])
    weight_first(2)
    row = lax.broadcasted_iota(jnp.int32, (512, 768), 0)
    column = lax.broadcasted_iota(jnp.int32, (512, 768), 1)
    spread = (row == column // LANES * 80 + column % LANES) & (column % LANES < 80)
    spread = jnp.where(spread, 1.0, 0.0).astype(BF)
    w_all[...] = jnp.dot(w_small[...], spread, preferred_element_type=F32).astype(BF)
    w_save = pltpu.make_async_copy(w_all, w_out, local_sem.at[5])
    w_save.start()
    lax.fori_loop(0, 5, project, 0)
    lax.fori_loop(7, 8, arrive, 0)
    lax.fori_loop(5, 8, project, 0)

    for h in range(2):
        v_turned[h] = jnp.transpose(qkv_ref[:, (4 + h) * LANES : (5 + h) * LANES])

    att_own = pltpu.make_async_copy(
        att_send.at[c], att_ref.at[span(at.group * 160, 160, 160)], local_sem.at[3]
    )

    def att_copy(block):
        return pltpu.make_async_remote_copy(
            src_ref=att_send.at[block],
            dst_ref=att_ref.at[span(at.group * 160, 160, 160)],
            send_sem=att_send_sem.at[block],
            recv_sem=att_recv_sem.at[at.group],
            device_id=dev(block, at.pack),
            device_id_type=MESH,
        )

    mine = at.core == at.half

    def attend(step, carry):
        block = flip(c, 7 - step)
        lanes = span(block * 256, 256, 256)
        high = place_ref[0:1, lanes]
        least = place_ref[1:2, lanes]
        for h in range(2):
            query = qkv_ref[lanes, h * LANES : (h + 1) * LANES]
            scores, top = [], None
            for part in range(2):
                rows = slice(part * 1024, (part + 1) * 1024)
                kp = key_pos[rows, :]
                kp = jnp.concatenate([kp, kp], axis=1)
                keys = qkv_ref[rows, (2 + h) * LANES : (3 + h) * LANES]
                s = lax.dot_general(
                    keys, query, (((1,), (1,)), ((), ())), preferred_element_type=F32
                )
                s = jnp.where((kp >= least) & (kp <= high), s, FLOOR)
                scores.append(s)
                most = jnp.max(s, axis=0, keepdims=True)
                top = most if top is None else jnp.maximum(top, most)
            total = jnp.zeros((1, 256), F32)
            o = jnp.zeros((LANES, 256), F32)
            for part in range(2):
                p = jnp.exp(scores[part] - top)
                total += jnp.sum(p, axis=0, keepdims=True)
                values = v_turned[h, :, part * 1024 : (part + 1) * 1024]
                o += jnp.dot(values, p.astype(BF), preferred_element_type=F32)
            o = o[:80] / total
            lse_ref[h : h + 1, lanes] = top + jnp.log(total)
            out_ref[h * 80 : (h + 1) * 80, lanes] = o.astype(BF)
            att_send[block, h * 80 : (h + 1) * 80, :] = o.astype(BF)

        @pl.when(jnp.logical_and(mine, step == 7))
        def _():
            att_own.start()

        @pl.when(jnp.logical_not(jnp.logical_and(mine, step == 7)))
        def _():
            att_copy(block).start()

        for when, todo, m in WEIGHT_STEPS:

            @pl.when(step == when)
            def _(todo=todo, m=m):
                (weight_second if todo == 2 else weight_third)(m)

        return carry

    lax.fori_loop(0, 8, attend, 0)
    weight_second(2)
    lse_ref[2:8, :] = jnp.zeros((6, 2048), F32)

    def land(block, carry):
        @pl.when(jnp.logical_not(jnp.logical_and(mine, block == at.group)))
        def _():
            await_recv(att_ref.at[pl.ds(0, 160)], att_recv_sem.at[block])

        return carry

    @pl.when(mine)
    def _():
        att_own.wait()

    weight_last(0)
    lax.fori_loop(0, 8, land, 0)

    def across(left, right):
        return lax.dot_general(
            left, right, (((1,), (1,)), ((), ())), preferred_element_type=F32
        )

    x_load.wait()
    dy_load.wait()
    xf = x_mine[...].astype(F32)
    resid = xf + jnp.dot(jnp.transpose(att_ref[...]), weights[0], preferred_element_type=F32)
    inv = lax.rsqrt(jnp.mean(resid * resid, axis=1, keepdims=True) + EPS)
    normed_mlp = (resid * inv * mlp_gain).astype(BF)
    normed_mlp_ref[...] = jnp.transpose(normed_mlp)
    weight_last(1)
    up = jnp.dot(normed_mlp, weights[1], preferred_element_type=F32)
    sigma = 1.0 / (1.0 + jnp.exp(-up))
    act = (up * sigma).astype(BF)
    act_ref[...] = jnp.transpose(act)
    slope = sigma * (1.0 + up * (1.0 - sigma))
    weight_last(2)
    dy = dy_mine[...]
    up_grad = (across(dy, weights[2]) * slope).astype(BF)
    up_grad_ref[...] = up_grad
    scaled = across(up_grad, weights[1]) * mlp_gain
    resid_grad = dy.astype(F32) + inv * (
        scaled - resid * inv * inv * jnp.mean(scaled * resid, axis=1, keepdims=True)
    )
    resid_grad_ref[...] = resid_grad
    branch = resid_grad.astype(BF)
    branch_ref[...] = branch
    grad_ref[...] = across(weights[0], branch).astype(BF)
    result_ref[...] = resid + jnp.dot(act, weights[2], preferred_element_type=F32)

    w_save.wait()
    for k in range(8):
        rows = pl.ds(k * 256, 256)
        pltpu.make_async_copy(normed_ref.at[rows], normed_out.at[rows], save_sem.at[k, 0]).wait()
        pltpu.make_async_copy(qkv_ref.at[rows], qkv_out.at[rows], save_sem.at[k, 1]).wait()
    for copy in w_copies + aux_copies:
        copy.wait_send()
    pos_copy.wait_send()
    for m in range(3):
        for way in range(5) if SPLIT[m] else (0, 1, 3):
            weight_copy(m, way).wait_send()

    @pl.when(hub)
    def _():
        for k in range(8):
            for way, part in HUB_WAYS.get(k, ((0, 0), (0, 1), (1, 0), (1, 1), (2, 0), (2, 1))):
                await_recv(x_mine.at[halves[part]], x_send_sem.at[k, way, part])

    @pl.when(jnp.logical_not(hub))
    def _():
        x_far(0).wait_send()
        x_far(1).wait_send()

    def finish(block, carry):
        @pl.when(jnp.logical_not(jnp.logical_and(mine, block == c)))
        def _():
            att_copy(block).wait_send()

        return carry

    lax.fori_loop(0, 8, finish, 0)


def forward(*args):
    shape = jax.ShapeDtypeStruct
    dma = pltpu.SemaphoreType.DMA
    return pl.pallas_call(
        attend_kernel,
        name="forward",
        out_shape=(
            shape((1280, 256), BF),
            shape((2048, 1280), BF),
            shape((2048, 768), BF),
            shape((8, 2048), F32),
            shape((160, 2048), BF),
            shape((16, 1280), F32),
            shape((8, 2048), F32),
            shape((1280, 768), BF),
            shape((256, 1280), F32),
            shape((256, 1280), F32),
            shape((256, 1280), BF),
            shape((256, 1280), BF),
            shape((1280, 256), BF),
            shape((1280, 256), BF),
            shape((1280, 256), BF),
        ),
        in_specs=[pl.BlockSpec(memory_space=pltpu.SMEM)] + [ANY_SPEC] * 2 + [VMEM_SPEC] * 2 + [ANY_SPEC] * 4,
        out_specs=(VMEM_SPEC,) + (ANY_SPEC,) * 2 + (VMEM_SPEC,) * 4 + (ANY_SPEC,) + (VMEM_SPEC,) * 7,
        scratch_shapes=[
            pltpu.VMEM((256, 1280), BF),
            pltpu.VMEM((320, 3840), BF),
            pltpu.VMEM((256, 1280), BF),
            pltpu.VMEM((8, 256, 1280), BF),
            pltpu.VMEM((2048, 1280), BF),
            pltpu.VMEM((2048, 768), BF),
            pltpu.VMEM((1280, 768), BF),
            pltpu.VMEM((2, 320, 512), BF),
            pltpu.VMEM((1280, 512), BF),
            pltpu.VMEM((3, 1280, 1280), BF),
            pltpu.VMEM((4, 16, 384), BF),
            pltpu.VMEM((2, 8, 2048), F32),
            pltpu.VMEM((2, 128, 2048), BF),
            pltpu.VMEM((2048, LANES), F32),
            pltpu.VMEM((8, 160, 256), BF),
            dma((8, 3, 2)),
            dma((8, 2)),
            dma((4,)),
            dma((4,)),
            dma((4,)),
            dma((4,)),
            dma((2,)),
            dma((8,)),
            dma((8,)),
            dma((3, 5)),
            dma((3, 5)),
            dma((6,)),
            dma((8, 2)),
            dma((3,)),
        ],
        compiler_params=pltpu.CompilerParams(
            collective_id=0, has_side_effects=True, vmem_limit_bytes=VMEM_LIMIT
        ),
        cost_estimate=pl.CostEstimate(
            flops=20_000_000_000, bytes_accessed=40_000_000, transcendentals=8_400_000
        ),
    )(*args)


def add_into(target, source, rows, step):
    def one(k, carry):
        part = span(k * step, step, step)
        target[part, :] = (target[part, :].astype(F32) + source[part, :].astype(F32)).astype(BF)
        return carry

    lax.fori_loop(0, rows // step, one, 0)


SUM_WAYS = ("yxzh", "zyxh", "zxyh")
SPREAD_WAYS = ("zhx", "hxz", "hxz")
HEAD_WAYS = "hzx"

PLAN = (
    "prep", "mt0", "m00", "mt2", "m02", "mt1", "take", "L00", "L01", "L02", "L03", "L04",
    "m01", "L05", "L06", "L07", "E0", "qs0", "L10", "L11", "L12", "L13", "L14", "L15", "L16",
    "qa0", "m10", "L17", "m12", "E1", "v0", "qs1", "nt0", "nt1", "nt2", "q00", "v1", "nt3",
    "v2", "v3", "na0", "v4", "na1", "na2", "qa1", "na3", "v5", "m11", "q10", "m20", "q01",
    "m22", "m21", "m32", "m30", "q11", "q20", "g02", "g00", "m31", "g12", "nb0", "g10", "g01",
    "nb1", "q21", "g22", "g11", "g20", "nc_f", "nc_n", "g21", "qc0", "qw0", "mw2", "qc1",
    "mw0", "nfin", "qw1", "mw1", "turn",
)

KEY_PARTS = 2
KEY_ROWS = 2048 // KEY_PARTS


def backward_kernel(
    grad_ref,
    att_hbm,
    branch_hbm,
    normed_mlp_hbm,
    up_grad_hbm,
    act_hbm,
    dy_hbm,
    qkv_hbm,
    lse_ref,
    out_hbm,
    place_ref,
    normed_hbm,
    w_hbm,
    mult_ref,
    x_hbm,
    resid_grad_hbm,
    gain_ref,
    first_out,
    second_out,
    third_out,
    slice_out,
    input_grad_out,
    scale_ref,
    first_ref,
    second_ref,
    third_ref,
    slice_ref,
    input_ref,
    att_ref,
    branch_ref,
    normed_mlp_ref,
    up_grad_ref,
    act_ref,
    dy_ref,
    qkv_ref,
    out_ref,
    w_ref,
    x_ref,
    resid_grad_ref,
    grad_all,
    key_pos,
    k_turned,
    delta,
    key_sum,
    value_sum,
    turned,
    normed_part,
    n_core,
    n_x,
    n_z,
    n_last,
    sums,
    core_in,
    taken,
    slices,
    s1,
    s2,
    gathered,
    scale_in,
    g_send_sem,
    g_recv_sem,
    local_sem,
    m_send,
    m_recv,
    q_send,
    q_recv,
    nc_send,
    nc_recv,
    n_send,
    n_recv,
    v_send,
    v_recv,
    load_sem,
    save_sem,
):
    loads = {
        name: pltpu.make_async_copy(src, dst, load_sem.at[k])
        for k, (name, src, dst) in enumerate(
            (
                ("act", act_hbm, act_ref),
                ("dy", dy_hbm, dy_ref),
                ("normed", normed_mlp_hbm, normed_mlp_ref),
                ("up", up_grad_hbm, up_grad_ref),
                ("att", att_hbm, att_ref),
                ("branch", branch_hbm, branch_ref),
                ("qkv", qkv_hbm, qkv_ref),
                ("out", out_hbm, out_ref),
                ("w", w_hbm, w_ref),
                ("x", x_hbm, x_ref),
                ("resid", resid_grad_hbm, resid_grad_ref),
            )
        )
    }
    for load in loads.values():
        load.start()
    at = Place()
    meet_plane(at)
    c, f, core, half = at.c, at.f, at.core, at.half
    mine = core == half
    row = f // 2
    xbit, zbit = c % 2, (c // 2) % 2
    twin, across = dev(c, at.twin), dev(c, at.across)
    xpeer, zpeer, hpeer = dev(flip(c, 1), f), dev(flip(c, 2), f), dev(flip(c, 4), f)

    def remote(src, dst, send_sem, recv_sem, where):
        return pltpu.make_async_remote_copy(
            src_ref=src,
            dst_ref=dst,
            send_sem=send_sem,
            recv_sem=recv_sem,
            device_id=where,
            device_id_type=MESH,
        )

    def grad_copy(group, h):
        return remote(
            grad_ref.at[span(group * 160 + h * 80, 80, 80)],
            grad_all.at[h, pl.ds(0, 80), span(c * 256, 256, 256)],
            g_send_sem.at[group, h],
            g_recv_sem.at[c, h],
            dev(core * 4 + group // 2, at.plane + group % 2),
        )

    def grad_own(h):
        return pltpu.make_async_copy(
            grad_ref.at[span(at.group * 160 + h * 80, 80, 80)],
            grad_all.at[h, pl.ds(0, 80), span(c * 256, 256, 256)],
            local_sem.at[h],
        )

    def give(k, carry):
        group = flip(at.group, k)

        @pl.when(jnp.logical_and(mine, k == 0))
        def _():
            grad_own(0).start()
            grad_own(1).start()

        @pl.when(jnp.logical_not(jnp.logical_and(mine, k == 0)))
        def _():
            grad_copy(group, 0).start()
            grad_copy(group, 1).start()

        return carry

    lax.fori_loop(0, 8, give, 0)

    bits = {"y": row, "x": xbit, "z": zbit, "h": half}
    peers = {"y": across, "x": xpeer, "z": zpeer, "h": hpeer}
    results = (first_ref, second_ref, third_ref)

    def finer(m):
        return "z" if SUM_WAYS[m].index("x") < SUM_WAYS[m].index("z") else "x"

    def cut(ref, way, bit):
        if way == "y":
            return (bit,)
        lead = (slice(None),) * (len(ref.shape) - 2)
        if way == "h":
            return lead + (slice(None), span(bit * 640, 640, 640))
        rows = ref.shape[-2] // 2
        return lead + (span(bit * rows, rows, rows),)

    def main_copy(stage, m):
        if stage < 0:
            y = stage + 2
            src, dst, to = sums.at[pl.ds((m * 2 + y) * 320, 320)], core_in.at[m, y], twin
        elif stage < 4:
            way = SUM_WAYS[m][stage]
            ref = core_in.at[m] if stage == 0 else taken[m][stage - 1]
            src, dst, to = ref.at[cut(ref, way, 1 - bits[way])], taken[m][stage], peers[way]
        else:
            way = SPREAD_WAYS[m][stage - 4]
            known = SPREAD_WAYS[m][: stage - 4]
            low = finer(m)
            high = "x" if low == "z" else "z"
            if high in known:
                rows = pl.ds(0, 320)
            elif low in known:
                rows = span(bits[high] * 160, 160, 160)
            else:
                rows = span(bits[high] * 160 + bits[low] * 80, 80, 80)
            lanes = pl.ds(0, 1280) if "h" in known else span(half * 640, 640, 640)
            src = dst = results[m].at[rows, lanes]
            to = peers[way]
        return remote(src, dst, m_send.at[stage + 2, m], m_recv.at[stage + 2, m], to)

    def added(ref, other, spot):
        for k in range(2) if len(ref.shape) == 3 else (None,):
            here = () if k is None else (k,)
            there = spot if k is None else (k,) + spot[1:]
            ref[here] = (ref[here].astype(F32) + other[there].astype(F32)).astype(BF)

    def main(stage, m):
        if stage == 0:
            for y in range(2):
                main_copy(y - 2, m).wait_recv()
                total = core_in[m, y].astype(F32) + weight_rows(m, 2 * y + core)
                core_in[m, y] = total.astype(BF)
        elif stage < 5:
            main_copy(stage - 1, m).wait_recv()
            way = SUM_WAYS[m][stage - 1]
            ref = core_in.at[m] if stage == 1 else taken[m][stage - 2]
            spot = cut(ref, way, bits[way])
            if stage < 4:
                added(taken[m][stage - 1], ref, spot)
            else:
                low = finer(m)
                high = "x" if low == "z" else "z"
                rows = span(bits[high] * 160 + bits[low] * 80, 80, 80)
                results[m][rows, span(half * 640, 640, 640)] = (
                    taken[m][3][...].astype(F32) + ref[spot].astype(F32)
                ).astype(BF)
        else:
            main_copy(stage - 1, m).wait_recv()
        if stage < 7:
            main_copy(stage, m).start()
        else:
            save(m).start()

    lefts = (act_ref, normed_mlp_ref, att_ref)
    rights = (dy_ref, up_grad_ref, branch_ref)

    def weight_rows(m, quarter):
        rows = span(quarter * 320, 320, 320)
        return jnp.dot(lefts[m][rows, :], rights[m][...], preferred_element_type=F32)

    def main_first(m):
        for name in (("act", "dy"), ("normed", "up"), ("att", "branch"))[m]:
            loads[name].wait()
        for y in range(2):
            part = weight_rows(m, 2 * y + 1 - core)
            sums[(m * 2 + y) * 320 : (m * 2 + y + 1) * 320, :] = part.astype(BF)
            main_copy(y - 2, m).start()

    def prepare():
        loads["qkv"].wait()
        for h in range(2):
            grad_all[h, 80:, :] = jnp.zeros((48, 2048), BF)
            k_turned[h] = jnp.transpose(qkv_ref[:, (2 + h) * LANES : (3 + h) * LANES])
        for k in range(8):
            block = place_ref[0:1, k * 256 : (k + 1) * 256]
            key_pos[k * 256 : (k + 1) * 256, :] = jnp.transpose(
                jnp.broadcast_to(block, (LANES, 256))
            )
        scale_ref[...] = jnp.zeros((8, LANES), F32)

    def take(k, carry):
        block = flip(c, k)

        @pl.when(jnp.logical_and(mine, k == 0))
        def _():
            grad_own(0).wait()
            grad_own(1).wait()

        @pl.when(jnp.logical_not(jnp.logical_and(mine, k == 0)))
        def _():
            for h in range(2):
                await_recv(
                    grad_all.at[h, pl.ds(0, 80), pl.ds(0, 256)], g_recv_sem.at[block, h]
                )

        return carry

    def take_all():
        loads["out"].wait()
        lax.fori_loop(0, 8, take, 0)
        for h in range(2):
            delta[h : h + 1, :] = jnp.sum(
                grad_all[h, :80, :].astype(F32) * out_ref[h * 80 : (h + 1) * 80, :].astype(F32),
                axis=0,
                keepdims=True,
            )

    def head_copy(stage, h):
        if stage == 0:
            src, dst, to = slices.at[h, :, span((1 - row) * 640, 640, 640)], s1.at[h], across
        elif stage == 1:
            src, dst, to = s1.at[h, span(128 - half * 128, 128, 128)], s2.at[h], hpeer
        elif stage < 5:
            way = HEAD_WAYS[stage - 2]
            known = HEAD_WAYS[: stage - 2]
            where = (core,) + tuple(slice(None) if d in known else bits[d] for d in "xz") + (h,)
            rows = slice(None) if "h" in known else span(half * 128, 128, 128)
            src = dst = gathered.at[where + (rows,)]
            to = peers[way]
        else:
            src = dst = gathered.at[core, :, :, h]
            to = twin
        return remote(src, dst, q_send.at[stage, h], q_recv.at[stage, h], to)

    def head(stage, h):
        if stage > 0:
            head_copy(stage - 1, h).wait_recv()
        if stage == 1:
            add_into(s1.at[h], slices.at[h, :, span(row * 640, 640, 640)], 256, 128)
        if stage == 2:
            own = span(half * 128, 128, 128)
            gathered[core, xbit, zbit, h, own, :] = (
                s2[h].astype(F32) + s1[h, own, :].astype(F32)
            ).astype(BF)
        if stage < 6:
            head_copy(stage, h).start()
        else:
            head_flat(h)

    def normed_load(part):
        return pltpu.make_async_copy(
            normed_hbm.at[:, pl.ds(part * 256, 256)], normed_part.at[part % 2], local_sem.at[2 + part % 2]
        )

    def attend_head(h, hooks):
        key_sum[...] = jnp.zeros((2048, LANES), F32)
        value_sum[...] = jnp.zeros((2048, LANES), F32)

        def block_grad(block, carry):
            lanes = span(block * 256, 256, 256)
            high = place_ref[0:1, lanes]
            least = place_ref[1:2, lanes]
            query = qkv_ref[lanes, h * LANES : (h + 1) * LANES]
            grad_t = grad_all[h, :, lanes]
            q_grad = jnp.zeros((LANES, 256), F32)
            for part in range(KEY_PARTS):
                some = slice(part * KEY_ROWS, (part + 1) * KEY_ROWS)
                kp = key_pos[some, :]
                kp = jnp.concatenate([kp, kp], axis=1)
                keys = qkv_ref[some, (2 + h) * LANES : (3 + h) * LANES]
                values = qkv_ref[some, (4 + h) * LANES : (5 + h) * LANES]
                s = lax.dot_general(
                    keys, query, (((1,), (1,)), ((), ())), preferred_element_type=F32
                )
                visible = (kp >= least) & (kp <= high)
                p = jnp.exp(jnp.where(visible, s - lse_ref[h : h + 1, lanes], FLOOR))
                gp = jnp.dot(values, grad_t, preferred_element_type=F32)
                gs = (p * (gp - delta[h : h + 1, lanes])).astype(BF)
                value_sum[some, :] += lax.dot_general(
                    p.astype(BF), grad_t, (((1,), (1,)), ((), ())), preferred_element_type=F32
                )
                key_sum[some, :] += jnp.dot(gs, query, preferred_element_type=F32)
                q_grad += jnp.dot(k_turned[h, :, some], gs, preferred_element_type=F32)
            scale_ref[0:1, :] += jnp.sum(
                jnp.transpose(q_grad) * query.astype(F32), axis=0, keepdims=True
            )
            turned[h * LANES : (h + 1) * LANES, lanes] = (q_grad * mult_ref[:, 0:1]).astype(BF)
            for step, todo in hooks.items():

                @pl.when(block == step)
                def _(todo=todo):
                    for one in todo:
                        one()

            return carry

        lax.fori_loop(0, 8, block_grad, 0)

    def attend_end(h):
        for j, total in ((1, key_sum), (2, value_sum)):
            low = jnp.transpose(total[...]).astype(BF)
            turned[(2 * j + h) * LANES : (2 * j + h + 1) * LANES, :] = low

    def head_first(h):
        slices[h, 240:, :] = jnp.zeros((16, 1280), BF)
        for part in range(5):
            normed_load(part).wait()
            if part + 1 < 5:
                normed_load(part + 1).start()
            for j in range(3):
                first = (2 * j + h) * LANES
                slices[h, j * 80 : (j + 1) * 80, part * 256 : (part + 1) * 256] = jnp.dot(
                    turned[first : first + 80, :],
                    normed_part[part % 2],
                    preferred_element_type=F32,
                ).astype(BF)
        if h == 0:
            normed_load(0).start()
        head(0, h)

    def norm_bits(k):
        return (1 - xbit, 1 - xbit, xbit, xbit)[k], (1 - zbit, zbit, 1 - zbit, zbit)[k]

    def norm_spot(k, hh):
        slot = 2 * k + hh
        return sums.at[pl.ds(slot // 5 * 640, 640), pl.ds(slot % 5 * 256, 256)]

    def norm_copy(stage, k, hh=0):
        if stage == 0:
            return remote(
                norm_spot(k, hh), n_core.at[k, hh], nc_send.at[k, hh], nc_recv.at[k, hh], twin
            )
        took = k
        if stage == 1:
            ends = n_core.at[k], n_x.at[k], xpeer
        elif stage == 2:
            ends = n_core.at[2, (1 - half, half)[k]], n_z.at[k], zpeer
        else:
            to = dev(flip(c, 4), at.pack) if k == 0 else dev(c, at.twin)
            took = (core, 2)[k]
            ends = n_core.at[3, (1 - half, half)[k]], n_last.at[core], to
        return remote(ends[0], ends[1], n_send.at[stage, k], n_recv.at[stage, took], ends[2])

    def norm_part(k, hh, which):
        xs, zs = norm_bits(k)
        lanes = span((hh * 4 + zs * 2 + xs) * 256, 256, 256)
        rows = span(which * 640, 640, 640)
        return jnp.dot(w_ref[rows, :], turned[:, lanes], preferred_element_type=F32)

    def norm_first(k):
        if k == 0:
            loads["w"].wait()
            for m in range(3):
                for stage in range(2):
                    main_copy(stage - 2, m).wait_send()
        for hh in range(2):
            norm_spot(k, hh)[...] = norm_part(k, hh, 1 - core).astype(BF)
            norm_copy(0, k, hh).start()

    def norm_core(k):
        for hh in range(2):
            norm_copy(0, k, hh).wait_recv()
            n_core[k, hh] = (n_core[k, hh].astype(F32) + norm_part(k, hh, core)).astype(BF)
        if k < 2:
            norm_copy(1, k).start()

    def scale_copy(stage):
        where = (twin, across, xpeer, zpeer, hpeer)[stage]
        return remote(scale_ref, scale_in.at[stage], v_send.at[stage], v_recv.at[stage], where)

    def tiny(stage):
        if stage > 0:
            scale_copy(stage - 1).wait()
            scale_ref[...] += scale_in[stage - 1]
        if stage < 5:
            scale_copy(stage).start()

    def norm_x(k):
        norm_copy(1, k).wait_recv()
        for hh in range(2):
            add_into(n_core.at[2 + k, hh], n_x.at[k, hh], 640, 80)
        if k == 0:
            norm_copy(2, 0).start()
            norm_copy(2, 1).start()

    def norm_far():
        norm_copy(2, 0).wait_recv()
        add_into(n_core.at[3, 1 - half], n_z.at[0], 640, 80)
        norm_copy(3, 0).start()

    def norm_near():
        norm_copy(2, 1).wait_recv()
        add_into(n_core.at[3, half], n_z.at[1], 640, 80)

        @pl.when(jnp.logical_not(mine))
        def _():
            norm_copy(3, 1).start()

    def norm_last():
        loads["x"].wait()
        loads["resid"].wait()
        @pl.when(mine)
        def _():
            n_last[core] = n_core[3, half]
            await_recv(n_last.at[0], n_recv.at[3, 2])

        @pl.when(jnp.logical_not(mine))
        def _():
            await_recv(n_last.at[0], n_recv.at[3, 0])
            await_recv(n_last.at[1], n_recv.at[3, 1])

        xf = x_ref[...].astype(F32)
        inv = lax.rsqrt(jnp.mean(xf * xf, axis=1, keepdims=True) + EPS)
        scaled = jnp.concatenate(
            [jnp.transpose(n_last[k].astype(F32)) for k in range(2)], axis=1
        ) * gain_ref[0:1, :]
        input_ref[...] = resid_grad_ref[...] + inv * (
            scaled - xf * inv * inv * jnp.mean(scaled * xf, axis=1, keepdims=True)
        )
        save(3).start()

    def head_flat(h):
        if h == 0:
            for k in range(4):
                for hh in range(2):
                    norm_copy(0, k, hh).wait_send()
        for core_k in range(2):
            for m4 in range(4):
                for j in range(3):
                    start = j * 1280 + (4 * m4 + 2 * core_k + h) * 80
                    first = start // 1920 * 640
                    sums[start % 1920 : start % 1920 + 80, first : first + 640] = gathered[
                        core_k, m4 % 2, m4 // 2, h, j * 80 : (j + 1) * 80, :
                    ]

    def save(k):
        src, dst = (
            (first_ref, first_out),
            (second_ref, second_out),
            (third_ref, third_out),
            (input_ref, input_grad_out),
            (slice_ref.at[:, pl.ds(0, 1920)], slice_out.at[:, pl.ds(0, 1920)]),
            (slice_ref.at[:, pl.ds(1920, 1920)], slice_out.at[:, pl.ds(1920, 1920)]),
        )[k]
        return pltpu.make_async_copy(src, dst, save_sem.at[k])

    def turn_all():
        for part in range(2):

            def turn(k, carry, part=part):
                rows = span(k * 384, 384, 384)
                lanes = span(part * 1920 + k * 384, 384, 384)

                @pl.when(core == 0)
                def _():
                    strip = jnp.transpose(sums[rows, part * 640 : part * 640 + 384])
                    slice_ref[:, lanes] = strip[:320]

                @pl.when(core == 1)
                def _():
                    strip = jnp.transpose(sums[rows, part * 640 + 256 : part * 640 + 640])
                    slice_ref[:, lanes] = strip[64:]

                return carry

            lax.fori_loop(0, 5, turn, 0)
            save(4 + part).start()

    tasks = {"prep": prepare, "take": take_all, "nb0": lambda: norm_x(0), "nb1": lambda: norm_x(1)}
    tasks |= {"nc_f": norm_far, "nc_n": norm_near, "nfin": norm_last, "turn": turn_all}
    for m in range(3):
        tasks[f"mt{m}"] = functools.partial(main_first, m)
        for stage in range(4):
            tasks[f"m{stage}{m}"] = functools.partial(main, stage, m)
        for stage in range(3):
            tasks[f"g{stage}{m}"] = functools.partial(main, 4 + stage, m)
        tasks[f"mw{m}"] = functools.partial(main, 7, m)
    for h in range(2):
        tasks[f"E{h}"] = functools.partial(attend_end, h)
        tasks[f"qs{h}"] = functools.partial(head_first, h)
        for stage, name in enumerate(("qa", "q0", "q1", "q2", "qc", "qw")):
            tasks[f"{name}{h}"] = functools.partial(head, 1 + stage, h)
    for k in range(4):
        tasks[f"nt{k}"] = functools.partial(norm_first, k)
        tasks[f"na{k}"] = functools.partial(norm_core, k)
    for stage in range(6):
        tasks[f"v{stage}"] = functools.partial(tiny, stage)

    normed_load(0).start()
    spot = 0
    while spot < len(PLAN):
        name = PLAN[spot]
        if name[0] != "L":
            tasks[name]()
            spot += 1
            continue
        h, step, hooks = int(name[1]), -1, {}
        while step < 7 or PLAN[spot][0] == "L":
            if PLAN[spot][0] == "L":
                step = int(PLAN[spot][2])
                if step == 7:
                    spot += 1
                    break
            else:
                hooks.setdefault(step, []).append(tasks[PLAN[spot]])
            spot += 1
        attend_head(h, hooks)

    for k in range(6):
        save(k).wait()
    def sent(block, carry):
        own_in = jnp.logical_and(mine, block == at.group)

        @pl.when(jnp.logical_not(own_in))
        def _():
            for h in range(2):
                grad_copy(block, h).wait_send()

        return carry

    lax.fori_loop(0, 8, sent, 0)
    for m in range(3):
        for stage in range(7):
            main_copy(stage, m).wait_send()
    for h in range(2):
        for stage in range(6):
            head_copy(stage, h).wait_send()
    for k in range(2):
        norm_copy(1, k).wait_send()
        norm_copy(2, k).wait_send()
    norm_copy(3, 0).wait_send()

    @pl.when(jnp.logical_not(mine))
    def _():
        norm_copy(3, 1).wait_send()


def sum_slots():
    slots = []
    for ways in SUM_WAYS:
        shape, own = [2, 320, 1280], []
        for way in ways:
            if way == "y":
                shape = shape[1:]
            else:
                shape[-1 if way == "h" else -2] //= 2
            own.append(pltpu.VMEM(tuple(shape), BF))
        slots.append(own)
    return slots


def backward(*args):
    shape = jax.ShapeDtypeStruct
    dma = pltpu.SemaphoreType.DMA
    specs = [ANY_SPEC] * 17
    for k in (8, 10, 13, 16):
        specs[k] = VMEM_SPEC
    return pl.pallas_call(
        backward_kernel,
        name="backward",
        out_shape=(
            shape((320, 1280), BF),
            shape((320, 1280), BF),
            shape((320, 1280), BF),
            shape((320, 3840), BF),
            shape((256, 1280), F32),
            shape((8, LANES), F32),
        ),
        in_specs=specs,
        out_specs=(ANY_SPEC,) * 5 + (VMEM_SPEC,),
        scratch_shapes=[
            pltpu.VMEM((320, 1280), BF),
            pltpu.VMEM((320, 1280), BF),
            pltpu.VMEM((320, 1280), BF),
            pltpu.VMEM((320, 3840), BF),
            pltpu.VMEM((256, 1280), F32),
            pltpu.VMEM((1280, 256), BF),
            pltpu.VMEM((256, 1280), BF),
            pltpu.VMEM((1280, 256), BF),
            pltpu.VMEM((256, 1280), BF),
            pltpu.VMEM((1280, 256), BF),
            pltpu.VMEM((256, 1280), BF),
            pltpu.VMEM((2048, 768), BF),
            pltpu.VMEM((160, 2048), BF),
            pltpu.VMEM((1280, 768), BF),
            pltpu.VMEM((256, 1280), BF),
            pltpu.VMEM((256, 1280), F32),
            pltpu.VMEM((2, 128, 2048), BF),
            pltpu.VMEM((2048, LANES), F32),
            pltpu.VMEM((2, 128, 2048), BF),
            pltpu.VMEM((8, 2048), F32),
            pltpu.VMEM((2048, LANES), F32),
            pltpu.VMEM((2048, LANES), F32),
            pltpu.VMEM((768, 2048), BF),
            pltpu.VMEM((2, 2048, 256), BF),
            pltpu.VMEM((4, 2, 640, 256), BF),
            pltpu.VMEM((2, 2, 640, 256), BF),
            pltpu.VMEM((2, 640, 256), BF),
            pltpu.VMEM((2, 640, 256), BF),
            pltpu.VMEM((1920, 1280), BF),
            pltpu.VMEM((3, 2, 320, 1280), BF),
            sum_slots(),
            pltpu.VMEM((2, 256, 1280), BF),
            pltpu.VMEM((2, 256, 640), BF),
            pltpu.VMEM((2, 128, 640), BF),
            pltpu.VMEM((2, 2, 2, 2, 256, 640), BF),
            pltpu.VMEM((5, 8, LANES), F32),
            dma((8, 2)),
            dma((8, 2)),
            dma((4,)),
            dma((9, 3)),
            dma((9, 3)),
            dma((6, 2)),
            dma((6, 2)),
            dma((4, 2)),
            dma((4, 2)),
            dma((4, 4)),
            dma((4, 4)),
            dma((5,)),
            dma((5,)),
            dma((11,)),
            dma((6,)),
        ],
        compiler_params=pltpu.CompilerParams(
            collective_id=1, has_side_effects=True, vmem_limit_bytes=VMEM_LIMIT
        ),
        cost_estimate=pl.CostEstimate(
            flops=30_000_000_000, bytes_accessed=60_000_000, transcendentals=8_400_000
        ),
    )(*args)


def fast_body(
    tokens,
    lengths,
    position,
    qkv_weight,
    out_weight,
    up_weight,
    down_weight,
    attn_gain,
    mlp_gain,
    query_scale,
    cotangent,
):
    f = lax.axis_index("fsdp")
    x, dy = tokens[0], cotangent[0]
    small = [jnp.pad(a, (0, 384 - a.shape[0])) for a in (attn_gain, mlp_gain, query_scale)]
    small = jnp.stack(small + [jnp.zeros((384,), BF)] * 13)
    (
        att_t, normed, qkv, lse, out, auxsum, place, w_heads,
        result, resid_grad, branch_grad, up_grad, act_t, normed_mlp_t, grad_t,
    ) = forward(
        lengths, x, qkv_weight, small, position, out_weight, up_weight, down_weight, dy
    )
    scale_float = auxsum[2, :80]
    base_scale = LOG2E / math.sqrt(80)
    soft = jax.nn.softplus(scale_float)
    mult = jnp.broadcast_to(jnp.pad(base_scale * soft, (0, 48))[:, None], (LANES, LANES))
    g_down, g_up, g_out, g_qkv, input_grad, scale_sum = backward(
        grad_t,
        att_t,
        branch_grad,
        normed_mlp_t,
        up_grad,
        act_t,
        dy,
        qkv,
        lse,
        out,
        place,
        normed,
        w_heads,
        mult,
        x,
        resid_grad,
        auxsum,
    )
    g_down, g_up, g_out = (g.astype(F32) for g in (g_down, g_up, g_out))
    g_qkv = g_qkv.astype(F32)
    grad_attn_gain = jnp.sum(qkv_weight.astype(F32) * g_qkv, axis=1) / attn_gain.astype(F32)
    grad_mlp_gain = jnp.sum(up_weight.astype(F32) * g_up, axis=1) / mlp_gain.astype(F32)
    grad_scale = scale_sum[0, :80] / soft * jax.nn.sigmoid(scale_float)
    return (
        result[None],
        input_grad[None],
        g_qkv,
        g_out,
        g_up,
        g_down,
        grad_attn_gain,
        grad_mlp_gain,
        lax.dynamic_slice_in_dim(grad_scale, f * 20, 20),
    )


def solution(mesh):
    placed = (
        P("fsdp", "ctx", None),
        P("fsdp", None),
        P("fsdp", None),
        P("fsdp", None),
        P("fsdp", None),
        P("fsdp", None),
        P("fsdp", None),
        P("fsdp"),
        P("fsdp"),
        P("fsdp"),
        P("fsdp", "ctx", None),
    )
    fits = mesh.shape["ctx"] == 8 and mesh.shape["fsdp"] == 4
    return jax.shard_map(
        fast_body if fits else body,
        mesh=mesh,
        in_specs=placed,
        out_specs=(
            P("fsdp", "ctx", None),
            P("fsdp", "ctx", None),
            P("fsdp", None),
            P("fsdp", None),
            P("fsdp", None),
            P("fsdp", None),
            P("fsdp"),
            P("fsdp"),
            P("fsdp"),
        ),
        check_vma=False,
    )
```

```python
import functools
import math

import jax
import jax.numpy as jnp
from jax import lax
from jax.experimental import pallas as pl
from jax.experimental.pallas import tpu as pltpu
from jax.sharding import PartitionSpec as P

HEADS = 16


EPS = 1e-06
FLOOR = -1e30
LOG2E = 1.442695041

MESH = pl.DeviceIdType.MESH
LANES = 128
BF = jnp.bfloat16
F32 = jnp.float32
VMEM_SPEC = pl.BlockSpec(memory_space=pltpu.VMEM)
ANY_SPEC = pl.BlockSpec(memory_space=pl.ANY)
VMEM_LIMIT = 60 << 20


def flip(number, mask):
    total = 0
    for bit in (1, 2, 4):
        left = (number // bit) % 2
        right = (mask // bit) % 2
        total = total + bit * (left + right - 2 * left * right)
    return total


class Place:
    def __init__(self):
        self.c = lax.axis_index("ctx")
        self.f = lax.axis_index("fsdp")
        self.core = self.f % 2
        self.plane = self.f - self.core
        self.half = self.c // 4
        self.pack = self.plane + self.half
        self.group = (self.c % 4) * 2 + self.core
        self.twin = self.plane + 1 - self.core
        self.across = (self.f + 2) % 4


def dev(ctx, fsdp):
    return {"ctx": ctx, "fsdp": fsdp}


def send(src, dst, send_sem, recv_sem, device):
    copy = pltpu.make_async_remote_copy(
        src_ref=src,
        dst_ref=dst,
        send_sem=send_sem,
        recv_sem=recv_sem,
        device_id=device,
        device_id_type=MESH,
    )
    copy.start()
    return copy


def await_recv(ref, sem):
    pltpu.make_async_copy(ref, ref, sem).wait()


def meet_plane(at):
    barrier = pltpu.get_barrier_semaphore()

    def greet(k, carry):
        pl.semaphore_signal(
            barrier,
            1,
            device_id=dev((at.c + k // 2) % 8, at.plane + (at.core + k) % 2),
            device_id_type=MESH,
        )
        return carry

    lax.fori_loop(1, 16, greet, 0)
    for k in range(2):
        pl.semaphore_signal(
            barrier, 1, device_id=dev(at.c, (at.plane + 2) % 4 + k), device_id_type=MESH
        )
    pl.semaphore_wait(barrier, 17)


def span(start, size, unit):
    return pl.ds(pl.multiple_of(start, unit), size)


def doc_index(places, seq_ends):
    return jnp.sum((places[:, None] >= seq_ends[None, :]).astype(jnp.int32), axis=1)


def spread_position(gathered_index, tok_dev, cycle_size):
    return gathered_index % tok_dev * cycle_size + gathered_index // tok_dev


def pair_scores(left_rows, right_rows):
    return jnp.einsum(
        "qhd,khd->qhk",
        left_rows.reshape(left_rows.shape[0], HEADS, -1),
        right_rows.reshape(right_rows.shape[0], HEADS, -1),
        preferred_element_type=jnp.float32,
    )


def pair_mask(query_pos, query_doc, key_pos, key_doc):
    return ((query_doc[:, None] == key_doc[None, :]) & (key_pos[None, :] <= query_pos[:, None]))[
        :, None, :
    ]


def in_blocks(advance, carried, pieces):
    total_rows = pieces[0].shape[0]
    block_rows = math.gcd(total_rows, 1024)
    block_count = total_rows // block_rows
    split = tuple((p.reshape((block_count, block_rows) + p.shape[1:]) for p in pieces))

    def inner(running, entry):
        return (advance(running, entry[1], entry[0] * block_rows), None)

    result, unused = lax.scan(inner, carried, (jnp.arange(block_count, dtype=jnp.int32), split))
    return result


def pair_terms(
    query_part,
    grad_part,
    log_part,
    delta_part,
    query_pos,
    query_doc,
    key_part,
    value_part,
    key_pos,
    key_doc,
):
    visible = pair_mask(query_pos, query_doc, key_pos, key_doc)
    prob_float = jnp.where(
        visible, jnp.exp(pair_scores(query_part, key_part) - log_part[:, :, None]), 0.0
    )
    grad_probs = pair_scores(grad_part, value_part)
    score_grad = (prob_float * (grad_probs - delta_part[:, :, None])).astype(jnp.bfloat16)
    return (prob_float.astype(jnp.bfloat16), score_grad)


def body(
    tokens,
    lengths,
    position,
    qkv_weight,
    out_weight,
    up_weight,
    down_weight,
    attn_gain,
    mlp_gain,
    query_scale,
    cotangent,
):
    cycle_size = lax.axis_size("ctx")
    my_index = lax.axis_index("ctx")
    tok_dev = tokens.shape[1]
    share_rows = tok_dev // cycle_size
    seq_ends = jnp.cumsum(lengths[0])
    place_row = position[0]
    residue = (place_row % cycle_size).reshape(cycle_size, tok_dev)
    landing = place_row // cycle_size
    matches = (
        residue[:, :, None] == jnp.arange(cycle_size, dtype=jnp.int32)[None, None, :]
    ).astype(jnp.int32)
    ranked = jnp.sum(jnp.cumsum(matches, axis=1) * matches, axis=2) - 1
    buffer_slot = residue * share_rows + ranked
    my_slots = lax.dynamic_index_in_dim(buffer_slot, my_index, 0, keepdims=False)
    local_rows = jnp.arange(tok_dev, dtype=jnp.int32)
    outgoing = jnp.zeros((tok_dev,), jnp.int32).at[my_slots].set(local_rows)
    flat_slot = (jnp.arange(cycle_size, dtype=jnp.int32)[:, None] * tok_dev + buffer_slot).reshape(
        -1
    )
    landing_table = (
        jnp.zeros((cycle_size * tok_dev,), jnp.int32)
        .at[flat_slot]
        .set(landing)
        .reshape(cycle_size, cycle_size, share_rows)
    )
    arrived_slot = lax.dynamic_index_in_dim(landing_table, my_index, 1, keepdims=False).reshape(-1)
    arrived_order = jnp.zeros((tok_dev,), jnp.int32).at[arrived_slot].set(local_rows)
    moved_x, moved_dy = (
        lax.all_to_all(tokens[0][outgoing], "ctx", split_axis=0, concat_axis=0, tiled=True),
        lax.all_to_all(cotangent[0][outgoing], "ctx", split_axis=0, concat_axis=0, tiled=True),
    )
    dealt_x = moved_x[arrived_order]
    dealt_dy = moved_dy[arrived_order]
    query_pos = local_rows * cycle_size + my_index
    query_doc = doc_index(query_pos, seq_ends)
    full_qkv, full_out, full_up, full_down, attn_gain_full, mlp_gain_full, scale_full = (
        lax.all_gather(qkv_weight, "fsdp", axis=0, tiled=True),
        lax.all_gather(out_weight, "fsdp", axis=0, tiled=True),
        lax.all_gather(up_weight, "fsdp", axis=0, tiled=True),
        lax.all_gather(down_weight, "fsdp", axis=0, tiled=True),
        lax.all_gather(attn_gain, "fsdp", axis=0, tiled=True),
        lax.all_gather(mlp_gain, "fsdp", axis=0, tiled=True),
        lax.all_gather(query_scale, "fsdp", axis=0, tiled=True),
    )
    attn_gain_f = attn_gain_full.astype(jnp.float32)
    mlp_gain_f = mlp_gain_full.astype(jnp.float32)
    scale_float = scale_full.astype(jnp.float32)
    x_float = dealt_x.astype(jnp.float32)
    inv_attn = lax.rsqrt(jnp.mean(x_float * x_float, axis=1, keepdims=True) + EPS)
    normed_attn = (x_float * inv_attn * attn_gain_f).astype(jnp.bfloat16)
    projected = jnp.dot(normed_attn, full_qkv, preferred_element_type=jnp.float32)
    att_width = projected.shape[1] // 3
    head_dim = scale_full.shape[0]
    base_scale = LOG2E / math.sqrt(head_dim)
    multiplier = jnp.tile(base_scale * jax.nn.softplus(scale_float), att_width // head_dim)
    raw_query = projected[:, :att_width]
    queries = (raw_query * multiplier).astype(jnp.bfloat16)
    key_rows = projected[:, att_width : 2 * att_width].astype(jnp.bfloat16)
    value_rows = projected[:, 2 * att_width :].astype(jnp.bfloat16)

    def key_place(first_row, amount):
        gathered_index = first_row + jnp.arange(amount, dtype=jnp.int32)
        key_pos = spread_position(gathered_index, tok_dev, cycle_size)
        return (key_pos, doc_index(key_pos, seq_ends))

    def stat_block(carried, pieces, first_row):
        running_max, running_sum = carried
        key_pos, key_doc = key_place(first_row, pieces[0].shape[0])
        visible = pair_mask(query_pos, query_doc, key_pos, key_doc)
        logits = jnp.where(visible, pair_scores(queries, pieces[0]), FLOOR)
        new_max = jnp.maximum(running_max, jnp.max(logits, axis=2))
        added = jnp.sum(jnp.where(visible, jnp.exp(logits - new_max[:, :, None]), 0.0), axis=2)
        return (new_max, running_sum * jnp.exp(running_max - new_max) + added)

    def output_block(summed, pieces, first_row):
        key_pos, key_doc = key_place(first_row, pieces[0].shape[0])
        visible = pair_mask(query_pos, query_doc, key_pos, key_doc)
        prob_low = jnp.where(
            visible, jnp.exp(pair_scores(queries, pieces[0]) - log_total[:, :, None]), 0.0
        ).astype(jnp.bfloat16)
        values_part = pieces[1].reshape(pieces[1].shape[0], HEADS, -1)
        return summed + jnp.einsum(
            "qhk,khd->qhd", prob_low, values_part, preferred_element_type=jnp.float32
        ).reshape(summed.shape)

    def query_grad_block(summed, pieces, first_row):
        key_pos, key_doc = key_place(first_row, pieces[0].shape[0])
        unused_probs, score_grad = pair_terms(
            queries,
            attended_grad,
            log_total,
            row_delta,
            query_pos,
            query_doc,
            pieces[0],
            pieces[1],
            key_pos,
            key_doc,
        )
        keys_part = pieces[0].reshape(pieces[0].shape[0], HEADS, -1)
        return summed + jnp.einsum(
            "qhk,khd->qhd", score_grad, keys_part, preferred_element_type=jnp.float32
        ).reshape(summed.shape)

    def key_grad_block(carried, pieces, first_row):
        amount = pieces[0].shape[0]
        part_pos, part_doc = key_place(first_row, amount)
        part_log = lax.dynamic_slice_in_dim(all_log, first_row, amount, 0)
        part_delta = lax.dynamic_slice_in_dim(all_delta, first_row, amount, 0)
        prob_low, score_grad = pair_terms(
            pieces[0],
            pieces[1],
            part_log,
            part_delta,
            part_pos,
            part_doc,
            key_rows,
            value_rows,
            query_pos,
            query_doc,
        )
        grad_keys = carried[0] + jnp.einsum(
            "qhk,qhd->khd",
            score_grad,
            pieces[0].reshape(amount, HEADS, -1),
            preferred_element_type=jnp.float32,
        ).reshape(tok_dev, -1)
        grad_values = carried[1] + jnp.einsum(
            "qhk,qhd->khd",
            prob_low,
            pieces[1].reshape(amount, HEADS, -1),
            preferred_element_type=jnp.float32,
        ).reshape(tok_dev, -1)
        return (grad_keys, grad_values)

    zero_stats = (
        jnp.full((tok_dev, HEADS), FLOOR, jnp.float32),
        jnp.zeros((tok_dev, HEADS), jnp.float32),
    )
    zero_rows = jnp.zeros((tok_dev, att_width), jnp.float32)
    running_max, running_sum = in_blocks(
        stat_block, zero_stats, (lax.all_gather(key_rows, "ctx", axis=0, tiled=True),)
    )
    log_total = running_max + jnp.log(running_sum)
    attended = in_blocks(
        output_block,
        zero_rows,
        (
            lax.all_gather(key_rows, "ctx", axis=0, tiled=True),
            lax.all_gather(value_rows, "ctx", axis=0, tiled=True),
        ),
    )
    attended_low = attended.astype(jnp.bfloat16)
    resid = x_float + jnp.dot(attended_low, full_out, preferred_element_type=jnp.float32)
    inv_mlp = lax.rsqrt(jnp.mean(resid * resid, axis=1, keepdims=True) + EPS)
    normed_mlp = (resid * inv_mlp * mlp_gain_f).astype(jnp.bfloat16)
    up_proj = jnp.dot(normed_mlp, full_up, preferred_element_type=jnp.float32)
    act_low = jax.nn.silu(up_proj).astype(jnp.bfloat16)
    result = resid + jnp.dot(act_low, full_down, preferred_element_type=jnp.float32)
    cot_float = dealt_dy.astype(jnp.float32)
    grad_down = jnp.dot(act_low.T, dealt_dy, preferred_element_type=jnp.float32)
    act_grad = jnp.dot(dealt_dy, full_down.T, preferred_element_type=jnp.float32)
    sigma = jax.nn.sigmoid(up_proj)
    up_grad = (act_grad * sigma * (1.0 + up_proj * (1.0 - sigma))).astype(jnp.bfloat16)
    grad_up = jnp.dot(normed_mlp.T, up_grad, preferred_element_type=jnp.float32)
    norm_mlp_grad = jnp.dot(up_grad, full_up.T, preferred_element_type=jnp.float32)
    grad_mlp_gain = jnp.sum(norm_mlp_grad * resid * inv_mlp, axis=0)
    scaled_mlp = norm_mlp_grad * mlp_gain_f
    resid_grad = cot_float + inv_mlp * (
        scaled_mlp - resid * inv_mlp * inv_mlp * jnp.mean(scaled_mlp * resid, axis=1, keepdims=True)
    )
    branch_grad = resid_grad.astype(jnp.bfloat16)
    grad_out = jnp.dot(attended_low.T, branch_grad, preferred_element_type=jnp.float32)
    attended_grad = jnp.dot(branch_grad, full_out.T, preferred_element_type=jnp.float32).astype(
        jnp.bfloat16
    )
    row_delta = jnp.sum(
        (attended_grad.astype(jnp.float32) * attended).reshape(tok_dev, HEADS, -1), axis=2
    )
    query_grads = in_blocks(
        query_grad_block,
        zero_rows,
        (
            lax.all_gather(key_rows, "ctx", axis=0, tiled=True),
            lax.all_gather(value_rows, "ctx", axis=0, tiled=True),
        ),
    )
    all_log, all_delta = (
        lax.all_gather(log_total, "ctx", axis=0, tiled=True),
        lax.all_gather(row_delta, "ctx", axis=0, tiled=True),
    )
    key_grad_f, value_grad_f = in_blocks(
        key_grad_block,
        (zero_rows, zero_rows),
        (
            lax.all_gather(queries, "ctx", axis=0, tiled=True),
            lax.all_gather(attended_grad, "ctx", axis=0, tiled=True),
        ),
    )
    scale_terms = jnp.sum((query_grads * raw_query).reshape(tok_dev, -1, head_dim), axis=(0, 1))
    grad_scale = scale_terms * base_scale * jax.nn.sigmoid(scale_float)
    proj_grad = jnp.concatenate(
        [
            (query_grads * multiplier).astype(jnp.bfloat16),
            key_grad_f.astype(jnp.bfloat16),
            value_grad_f.astype(jnp.bfloat16),
        ],
        axis=1,
    )
    grad_qkv = jnp.dot(normed_attn.T, proj_grad, preferred_element_type=jnp.float32)
    norm_attn_grad = jnp.dot(proj_grad, full_qkv.T, preferred_element_type=jnp.float32)
    grad_attn_gain = jnp.sum(norm_attn_grad * x_float * inv_attn, axis=0)
    scaled_attn = norm_attn_grad * attn_gain_f
    input_grad = resid_grad + inv_attn * (
        scaled_attn
        - x_float * inv_attn * inv_attn * jnp.mean(scaled_attn * x_float, axis=1, keepdims=True)
    )
    owned = (
        lax.psum_scatter(grad_qkv, "fsdp", scatter_dimension=0, tiled=True),
        lax.psum_scatter(grad_out, "fsdp", scatter_dimension=0, tiled=True),
        lax.psum_scatter(grad_up, "fsdp", scatter_dimension=0, tiled=True),
        lax.psum_scatter(grad_down, "fsdp", scatter_dimension=0, tiled=True),
        lax.psum_scatter(grad_attn_gain, "fsdp", scatter_dimension=0, tiled=True),
        lax.psum_scatter(grad_mlp_gain, "fsdp", scatter_dimension=0, tiled=True),
        lax.psum_scatter(grad_scale, "fsdp", scatter_dimension=0, tiled=True),
    )
    summed_grads = lax.psum(
        (owned[0], owned[1], owned[2], owned[3], owned[4], owned[5], owned[6]), "ctx"
    )
    back_out, back_grad = (
        lax.all_to_all(result[arrived_slot], "ctx", split_axis=0, concat_axis=0, tiled=True),
        lax.all_to_all(input_grad[arrived_slot], "ctx", split_axis=0, concat_axis=0, tiled=True),
    )
    return (
        back_out[my_slots][None],
        back_grad[my_slots][None],
        summed_grads[0],
        summed_grads[1],
        summed_grads[2],
        summed_grads[3],
        summed_grads[4],
        summed_grads[5],
        summed_grads[6],
    )


HUB_WAYS = {k: ((2, 0), (2, 1)) for k in range(1, 8)}
HUB_WAYS[1] += ((1, 0),)
HUB_WAYS[2] += ((0, 1),)
HUB_WAYS[4] += ((0, 0), (0, 1), (1, 0), (1, 1))
HUB_WAYS[6] += ((0, 0), (0, 1))

SPLIT = (False, True, False)
WEIGHT_STEPS = ((2, 2, 1), (4, 2, 0), (6, 3, 1))


def attend_kernel(
    ends_ref,
    x_ref,
    w_ref,
    aux_ref,
    pos_ref,
    out_w_ref,
    up_w_ref,
    down_w_ref,
    dy_ref,
    att_ref,
    normed_out,
    qkv_out,
    lse_ref,
    out_ref,
    auxsum_ref,
    place_ref,
    w_out,
    result_ref,
    resid_grad_ref,
    branch_ref,
    up_grad_ref,
    act_ref,
    normed_mlp_ref,
    grad_ref,
    mult_ref,
    x_mine,
    w_mine,
    dy_mine,
    x_all,
    normed_ref,
    qkv_ref,
    w_all,
    w_own,
    w_small,
    weights,
    aux_all,
    pos_all,
    v_turned,
    key_pos,
    att_send,
    x_send_sem,
    x_recv_sem,
    w_send_sem,
    w_recv_sem,
    aux_send_sem,
    aux_recv_sem,
    pos_sem,
    att_send_sem,
    att_recv_sem,
    m_send_sem,
    m_recv_sem,
    local_sem,
    save_sem,
    shard_sem,
):
    w_load = pltpu.make_async_copy(w_ref, w_mine, local_sem.at[0])
    w_load.start()
    x_load = pltpu.make_async_copy(x_ref, x_mine, local_sem.at[2])
    dy_load = pltpu.make_async_copy(dy_ref, dy_mine, local_sem.at[4])
    at = Place()
    meet_plane(at)
    c, f = at.c, at.f
    hub = at.core == at.half

    aux_own = pltpu.make_async_copy(aux_ref, aux_all.at[f], local_sem.at[1])
    aux_own.start()
    x_own = pltpu.make_async_copy(x_ref, x_all.at[c], local_sem.at[3])

    halves = (pl.ds(0, 128), pl.ds(128, 128))

    def x_far(part):
        return pltpu.make_async_remote_copy(
            src_ref=x_ref.at[halves[part]],
            dst_ref=x_all.at[c, halves[part]],
            send_sem=x_send_sem.at[0, 0, part],
            recv_sem=x_recv_sem.at[c, part],
            device_id=dev(flip(c, 4), f),
            device_id_type=MESH,
        )

    @pl.when(hub)
    def _():
        x_own.start()
        for part in range(2):
            for k, where in enumerate((dev(flip(c, 1), f), dev(flip(c, 2), f), dev(c, at.twin))):
                send(
                    x_ref.at[halves[part]],
                    x_all.at[c, halves[part]],
                    x_send_sem.at[0, k, part],
                    x_recv_sem.at[c, part],
                    where,
                )

    @pl.when(jnp.logical_not(hub))
    def _():
        x_far(0).start()
        x_far(1).start()

    w_copies, aux_copies = [], []
    for k in (2, 1, 3):
        aux_copies.append(
            send(
                aux_ref,
                aux_all.at[f],
                aux_send_sem.at[k],
                aux_recv_sem.at[f],
                dev(c, (f + k) % 4),
            )
        )

    pos = pos_ref[...]
    start = jnp.zeros_like(pos)
    end = 0
    for k in range(4):
        end = end + ends_ref[0, k]
        start = jnp.where(pos >= end, end, start)
    pos_all[at.core, 0:1, :] = pos.astype(F32)
    pos_all[at.core, 1:2, :] = start.astype(F32)
    pos_all[at.core, 2:8, :] = jnp.zeros((6, 2048), F32)
    pos_copy = send(
        pos_all.at[at.core], pos_all.at[at.core], pos_sem.at[0], pos_sem.at[1], dev(c, at.twin)
    )

    row = lax.broadcasted_iota(jnp.int32, (1280, 512), 0)
    column = lax.broadcasted_iota(jnp.int32, (1280, 512), 1)
    first = (c % 4) * 320
    w_load.wait()
    for k in range(2):
        some = jnp.zeros((320, 512), F32)
        for j in range(3):
            pick = (row - first - k * 160 == column - j * 160) & (column // 160 == j)
            pick = jnp.where(pick, 1.0, 0.0).astype(BF)
            some += jnp.dot(w_mine[:, j * 1280 : (j + 1) * 1280], pick, preferred_element_type=F32)
        w_own[k] = some.astype(BF)
    mine_rows = span(f * 320, 320, 320)
    for k in (2, 3, 1):
        to = (f + k) % 4
        w_copies.append(
            send(
                w_own.at[to % 2],
                w_small.at[mine_rows],
                w_send_sem.at[k],
                w_recv_sem.at[f],
                dev(c, to),
            )
        )
    w_small[mine_rows, :] = w_own[at.core]
    x_load.start()
    dy_load.start()


    shards = (out_w_ref, up_w_ref, down_w_ref)
    xbit = c % 2
    other = (f + 2) % 4

    def part(m, owner, x):
        return weights.at[m, span(owner * 320 + x * 160, 160, 160)]

    def weight_copy(m, way):
        if way == 0:
            src, dst, to = shards[m], weights.at[m, mine_rows], dev(c, at.twin)
        elif way == 1 and not SPLIT[m]:
            src, dst, to = shards[m], weights.at[m, mine_rows], dev(c, other)
        elif way == 3 and not SPLIT[m]:
            src = dst = weights.at[m, span(other * 320, 320, 320)]
            to = dev(c, at.twin)
        elif way == 1:
            src = shards[m].at[span(xbit * 160, 160, 160)]
            dst, to = part(m, f, xbit), dev(c, other)
        else:
            x = (xbit, xbit, 1 - xbit)[way - 2]
            src = dst = part(m, other, x)
            to = (dev(flip(c, 1), f), dev(c, at.twin), dev(c, at.twin))[way - 2]
        return pltpu.make_async_remote_copy(
            src_ref=src,
            dst_ref=dst,
            send_sem=m_send_sem.at[m, way],
            recv_sem=m_recv_sem.at[m, way],
            device_id=to,
            device_id_type=MESH,
        )

    def shard_copy(m):
        return pltpu.make_async_copy(shards[m], weights.at[m, mine_rows], shard_sem.at[m])

    def weight_first(m):
        weight_copy(m, 0).start()
        weight_copy(m, 1).start()
        shard_copy(m).start()

    def weight_second(m):
        weight_copy(m, 1).wait_recv()
        if SPLIT[m]:
            weight_copy(m, 2).start()
        weight_copy(m, 3).start()

    def weight_third(m):
        if SPLIT[m]:
            weight_copy(m, 2).wait_recv()
            weight_copy(m, 4).start()

    def weight_last(m):
        shard_copy(m).wait()
        for way in (0, 3, 4) if SPLIT[m] else (0, 3):
            weight_copy(m, way).wait_recv()


    aux_own.wait()
    for k in (1, 2, 3):
        await_recv(aux_all.at[0], aux_recv_sem.at[(f + k) % 4])
    aux = jnp.zeros((16, 1280), F32)
    scale = jnp.zeros((16, LANES), F32)
    row = lax.broadcasted_iota(jnp.int32, (384, 1280), 0)
    column = lax.broadcasted_iota(jnp.int32, (384, 1280), 1)
    for k in range(4):
        put = jnp.where((column == row + k * 320) & (row < 320), 1.0, 0.0).astype(BF)
        aux = aux + jnp.dot(aux_all[k], put, preferred_element_type=F32)
        put = (column[:LANES, :LANES] == row[:LANES, :LANES] + k * 20) & (row[:LANES, :LANES] < 20)
        put = jnp.where(put, 1.0, 0.0).astype(BF)
        scale = scale + jnp.dot(aux_all[k, :, :LANES], put, preferred_element_type=F32)
    auxsum_ref[...] = aux
    auxsum_ref[2:3, :LANES] = scale[2:3]
    gain = aux[0:1, :]
    mlp_gain = aux[1:2, :]
    scale = scale[2:3]
    real = lax.broadcasted_iota(jnp.int32, (1, LANES), 1) < 80
    mult = jnp.where(
        real, LOG2E / math.sqrt(80) * (jnp.maximum(scale, 0.0) + jnp.log1p(jnp.exp(-jnp.abs(scale)))), 0.0
    )
    mult_ref[...] = jnp.transpose(jnp.broadcast_to(mult, (LANES, LANES)))
    one = jnp.ones_like(mult)
    mults = jnp.concatenate([mult, mult, one, one, one, one], axis=1)

    await_recv(pos_all.at[0], pos_sem.at[1])
    place_ref[...] = pos_all[at.half]
    for k in range(8):
        block = place_ref[0:1, k * 256 : (k + 1) * 256]
        key_pos[k * 256 : (k + 1) * 256, :] = jnp.transpose(
            jnp.broadcast_to(block, (LANES, 256))
        )

    def arrive(step, carry):
        k = step + jnp.where(step == 3, 1, 0) - jnp.where(step == 4, 1, 0)
        slot = flip(c, k)
        for part in range(2):
            piece = x_all.at[slot, halves[part]]
            if part == 0:

                @pl.when(jnp.logical_and(hub, k == 0))
                def _():
                    x_own.wait()

            @pl.when(jnp.logical_not(jnp.logical_and(hub, k == 0)))
            def _(part=part, piece=piece):
                await_recv(piece, x_recv_sem.at[slot, part])

            def onward(way, where, part=part, piece=piece):
                send(
                    piece, piece, x_send_sem.at[k, way, part], x_recv_sem.at[slot, part], where
                )

            for way, where in enumerate((dev(flip(c, 1), f), dev(flip(c, 2), f), dev(c, at.twin))):
                due = False
                for when in HUB_WAYS:
                    if (way, part) in HUB_WAYS[when]:
                        due = jnp.logical_or(due, k == when)

                @pl.when(jnp.logical_and(hub, due))
                def _(way=way, where=where, onward=onward):
                    onward(way, where)

        @pl.when(step == 3)
        def _():
            weight_first(0)

        @pl.when(step == 5)
        def _():
            weight_first(1)


        xf = x_all[slot].astype(F32)
        inv = lax.rsqrt(jnp.mean(xf * xf, axis=1, keepdims=True) + EPS)
        rows = span(slot * 256, 256, 256)
        normed_ref[rows, :] = (xf * inv * gain).astype(BF)
        pltpu.make_async_copy(
            normed_ref.at[rows], normed_out.at[rows], save_sem.at[slot, 0]
        ).start()
        return carry

    def project(step, carry):
        slot = flip(c, step)
        rows = span(slot * 256, 256, 256)
        proj = jnp.dot(normed_ref[rows, :], w_all[...], preferred_element_type=F32)
        qkv_ref[rows, :] = (proj * mults).astype(BF)
        pltpu.make_async_copy(qkv_ref.at[rows], qkv_out.at[rows], save_sem.at[slot, 1]).start()
        return carry

    lax.fori_loop(0, 7, arrive, 0)
    for k in (1, 2, 3):
        await_recv(w_small.at[pl.ds(0, 320)], w_recv_sem.at[(f + k) % 4])
    weight_first(2)
    row = lax.broadcasted_iota(jnp.int32, (512, 768), 0)
    column = lax.broadcasted_iota(jnp.int32, (512, 768), 1)
    spread = (row == column // LANES * 80 + column % LANES) & (column % LANES < 80)
    spread = jnp.where(spread, 1.0, 0.0).astype(BF)
    w_all[...] = jnp.dot(w_small[...], spread, preferred_element_type=F32).astype(BF)
    w_save = pltpu.make_async_copy(w_all, w_out, local_sem.at[5])
    w_save.start()
    lax.fori_loop(0, 5, project, 0)
    lax.fori_loop(7, 8, arrive, 0)
    lax.fori_loop(5, 8, project, 0)

    for h in range(2):
        v_turned[h] = jnp.transpose(qkv_ref[:, (4 + h) * LANES : (5 + h) * LANES])

    att_own = pltpu.make_async_copy(
        att_send.at[c], att_ref.at[span(at.group * 160, 160, 160)], local_sem.at[3]
    )

    def att_copy(block):
        return pltpu.make_async_remote_copy(
            src_ref=att_send.at[block],
            dst_ref=att_ref.at[span(at.group * 160, 160, 160)],
            send_sem=att_send_sem.at[block],
            recv_sem=att_recv_sem.at[at.group],
            device_id=dev(block, at.pack),
            device_id_type=MESH,
        )

    mine = at.core == at.half

    def attend(step, carry):
        block = flip(c, 7 - step)
        lanes = span(block * 256, 256, 256)
        high = place_ref[0:1, lanes]
        least = place_ref[1:2, lanes]
        for h in range(2):
            query = qkv_ref[lanes, h * LANES : (h + 1) * LANES]
            scores, top = [], None
            for part in range(2):
                rows = slice(part * 1024, (part + 1) * 1024)
                kp = key_pos[rows, :]
                kp = jnp.concatenate([kp, kp], axis=1)
                keys = qkv_ref[rows, (2 + h) * LANES : (3 + h) * LANES]
                s = lax.dot_general(
                    keys, query, (((1,), (1,)), ((), ())), preferred_element_type=F32
                )
                s = jnp.where((kp >= least) & (kp <= high), s, FLOOR)
                scores.append(s)
                most = jnp.max(s, axis=0, keepdims=True)
                top = most if top is None else jnp.maximum(top, most)
            total = jnp.zeros((1, 256), F32)
            o = jnp.zeros((LANES, 256), F32)
            for part in range(2):
                p = jnp.exp(scores[part] - top)
                total += jnp.sum(p, axis=0, keepdims=True)
                values = v_turned[h, :, part * 1024 : (part + 1) * 1024]
                o += jnp.dot(values, p.astype(BF), preferred_element_type=F32)
            o = o[:80] / total
            lse_ref[h : h + 1, lanes] = top + jnp.log(total)
            out_ref[h * 80 : (h + 1) * 80, lanes] = o.astype(BF)
            att_send[block, h * 80 : (h + 1) * 80, :] = o.astype(BF)

        @pl.when(jnp.logical_and(mine, step == 7))
        def _():
            att_own.start()

        @pl.when(jnp.logical_not(jnp.logical_and(mine, step == 7)))
        def _():
            att_copy(block).start()

        for when, todo, m in WEIGHT_STEPS:

            @pl.when(step == when)
            def _(todo=todo, m=m):
                (weight_second if todo == 2 else weight_third)(m)

        return carry

    lax.fori_loop(0, 8, attend, 0)
    weight_second(2)
    lse_ref[2:8, :] = jnp.zeros((6, 2048), F32)

    def land(block, carry):
        @pl.when(jnp.logical_not(jnp.logical_and(mine, block == at.group)))
        def _():
            await_recv(att_ref.at[pl.ds(0, 160)], att_recv_sem.at[block])

        return carry

    @pl.when(mine)
    def _():
        att_own.wait()

    weight_last(0)
    lax.fori_loop(0, 8, land, 0)

    def across(left, right):
        return lax.dot_general(
            left, right, (((1,), (1,)), ((), ())), preferred_element_type=F32
        )

    x_load.wait()
    dy_load.wait()
    xf = x_mine[...].astype(F32)
    resid = xf + jnp.dot(jnp.transpose(att_ref[...]), weights[0], preferred_element_type=F32)
    inv = lax.rsqrt(jnp.mean(resid * resid, axis=1, keepdims=True) + EPS)
    normed_mlp = (resid * inv * mlp_gain).astype(BF)
    normed_mlp_ref[...] = jnp.transpose(normed_mlp)
    weight_last(1)
    up = jnp.dot(normed_mlp, weights[1], preferred_element_type=F32)
    sigma = 1.0 / (1.0 + jnp.exp(-up))
    act = (up * sigma).astype(BF)
    act_ref[...] = jnp.transpose(act)
    slope = sigma * (1.0 + up * (1.0 - sigma))
    weight_last(2)
    dy = dy_mine[...]
    up_grad = (across(dy, weights[2]) * slope).astype(BF)
    up_grad_ref[...] = up_grad
    scaled = across(up_grad, weights[1]) * mlp_gain
    resid_grad = dy.astype(F32) + inv * (
        scaled - resid * inv * inv * jnp.mean(scaled * resid, axis=1, keepdims=True)
    )
    resid_grad_ref[...] = resid_grad
    branch = resid_grad.astype(BF)
    branch_ref[...] = branch
    grad_ref[...] = across(weights[0], branch).astype(BF)
    result_ref[...] = resid + jnp.dot(act, weights[2], preferred_element_type=F32)

    w_save.wait()
    for k in range(8):
        rows = pl.ds(k * 256, 256)
        pltpu.make_async_copy(normed_ref.at[rows], normed_out.at[rows], save_sem.at[k, 0]).wait()
        pltpu.make_async_copy(qkv_ref.at[rows], qkv_out.at[rows], save_sem.at[k, 1]).wait()
    for copy in w_copies + aux_copies:
        copy.wait_send()
    pos_copy.wait_send()
    for m in range(3):
        for way in range(5) if SPLIT[m] else (0, 1, 3):
            weight_copy(m, way).wait_send()

    @pl.when(hub)
    def _():
        for k in range(8):
            for way, part in HUB_WAYS.get(k, ((0, 0), (0, 1), (1, 0), (1, 1), (2, 0), (2, 1))):
                await_recv(x_mine.at[halves[part]], x_send_sem.at[k, way, part])

    @pl.when(jnp.logical_not(hub))
    def _():
        x_far(0).wait_send()
        x_far(1).wait_send()

    def finish(block, carry):
        @pl.when(jnp.logical_not(jnp.logical_and(mine, block == c)))
        def _():
            att_copy(block).wait_send()

        return carry

    lax.fori_loop(0, 8, finish, 0)


def forward(*args):
    shape = jax.ShapeDtypeStruct
    dma = pltpu.SemaphoreType.DMA
    return pl.pallas_call(
        attend_kernel,
        name="forward",
        out_shape=(
            shape((1280, 256), BF),
            shape((2048, 1280), BF),
            shape((2048, 768), BF),
            shape((8, 2048), F32),
            shape((160, 2048), BF),
            shape((16, 1280), F32),
            shape((8, 2048), F32),
            shape((1280, 768), BF),
            shape((256, 1280), F32),
            shape((256, 1280), F32),
            shape((256, 1280), BF),
            shape((256, 1280), BF),
            shape((1280, 256), BF),
            shape((1280, 256), BF),
            shape((1280, 256), BF),
            shape((LANES, LANES), F32),
        ),
        in_specs=[pl.BlockSpec(memory_space=pltpu.SMEM)] + [ANY_SPEC] * 2 + [VMEM_SPEC] * 2 + [ANY_SPEC] * 4,
        out_specs=(VMEM_SPEC,) + (ANY_SPEC,) * 2 + (VMEM_SPEC,) * 4 + (ANY_SPEC,) + (VMEM_SPEC,) * 8,
        scratch_shapes=[
            pltpu.VMEM((256, 1280), BF),
            pltpu.VMEM((320, 3840), BF),
            pltpu.VMEM((256, 1280), BF),
            pltpu.VMEM((8, 256, 1280), BF),
            pltpu.VMEM((2048, 1280), BF),
            pltpu.VMEM((2048, 768), BF),
            pltpu.VMEM((1280, 768), BF),
            pltpu.VMEM((2, 320, 512), BF),
            pltpu.VMEM((1280, 512), BF),
            pltpu.VMEM((3, 1280, 1280), BF),
            pltpu.VMEM((4, 16, 384), BF),
            pltpu.VMEM((2, 8, 2048), F32),
            pltpu.VMEM((2, 128, 2048), BF),
            pltpu.VMEM((2048, LANES), F32),
            pltpu.VMEM((8, 160, 256), BF),
            dma((8, 3, 2)),
            dma((8, 2)),
            dma((4,)),
            dma((4,)),
            dma((4,)),
            dma((4,)),
            dma((2,)),
            dma((8,)),
            dma((8,)),
            dma((3, 5)),
            dma((3, 5)),
            dma((6,)),
            dma((8, 2)),
            dma((3,)),
        ],
        compiler_params=pltpu.CompilerParams(
            collective_id=0, has_side_effects=True, vmem_limit_bytes=VMEM_LIMIT
        ),
        cost_estimate=pl.CostEstimate(
            flops=20_000_000_000, bytes_accessed=40_000_000, transcendentals=8_400_000
        ),
    )(*args)


def add_into(target, source, rows, step):
    def one(k, carry):
        part = span(k * step, step, step)
        target[part, :] = (target[part, :].astype(F32) + source[part, :].astype(F32)).astype(BF)
        return carry

    lax.fori_loop(0, rows // step, one, 0)


SUM_WAYS = ("yxzh", "zyxh", "zxyh")
SPREAD_WAYS = ("zhx", "hxz", "hxz")
HEAD_WAYS = "hzx"

PLAN = (
    "prep", "mt0", "m00", "mt2", "m02", "mt1", "take", "L00", "L01", "L02", "L03", "L04",
    "m01", "L05", "L06", "L07", "E0", "qs0", "L10", "L11", "L12", "L13", "L14", "L15", "L16",
    "qa0", "m10", "L17", "m12", "E1", "v0", "qs1", "nt0", "nt1", "nt2", "q00", "v1", "nt3",
    "v2", "v3", "na0", "v4", "na1", "na2", "qa1", "na3", "v5", "m11", "q10", "m20", "q01",
    "m22", "m21", "m32", "m30", "q11", "q20", "g02", "g00", "m31", "g12", "nb0", "g10", "g01",
    "nb1", "q21", "g22", "g11", "g20", "nc_f", "nc_n", "g21", "qc0", "qw0", "mw2", "qc1",
    "mw0", "nfin", "qw1", "mw1", "turn",
)

KEY_PARTS = 2
KEY_ROWS = 2048 // KEY_PARTS


def backward_kernel(
    grad_ref,
    att_hbm,
    branch_hbm,
    normed_mlp_hbm,
    up_grad_hbm,
    act_hbm,
    dy_hbm,
    qkv_hbm,
    lse_ref,
    out_hbm,
    place_ref,
    normed_hbm,
    w_hbm,
    mult_ref,
    x_hbm,
    resid_grad_hbm,
    gain_ref,
    first_out,
    second_out,
    third_out,
    slice_out,
    input_grad_out,
    scale_ref,
    first_ref,
    second_ref,
    third_ref,
    slice_ref,
    input_ref,
    att_ref,
    branch_ref,
    normed_mlp_ref,
    up_grad_ref,
    act_ref,
    dy_ref,
    qkv_ref,
    out_ref,
    w_ref,
    x_ref,
    resid_grad_ref,
    grad_all,
    key_pos,
    k_turned,
    delta,
    key_sum,
    value_sum,
    turned,
    normed_part,
    n_core,
    n_x,
    n_z,
    n_last,
    sums,
    core_in,
    taken,
    slices,
    s1,
    s2,
    gathered,
    scale_in,
    g_send_sem,
    g_recv_sem,
    local_sem,
    m_send,
    m_recv,
    q_send,
    q_recv,
    nc_send,
    nc_recv,
    n_send,
    n_recv,
    v_send,
    v_recv,
    load_sem,
    save_sem,
):
    loads = {
        name: pltpu.make_async_copy(src, dst, load_sem.at[k])
        for k, (name, src, dst) in enumerate(
            (
                ("act", act_hbm, act_ref),
                ("dy", dy_hbm, dy_ref),
                ("normed", normed_mlp_hbm, normed_mlp_ref),
                ("up", up_grad_hbm, up_grad_ref),
                ("att", att_hbm, att_ref),
                ("branch", branch_hbm, branch_ref),
                ("qkv", qkv_hbm, qkv_ref),
                ("out", out_hbm, out_ref),
                ("w", w_hbm, w_ref),
                ("x", x_hbm, x_ref),
                ("resid", resid_grad_hbm, resid_grad_ref),
            )
        )
    }
    for load in loads.values():
        load.start()
    at = Place()
    meet_plane(at)
    c, f, core, half = at.c, at.f, at.core, at.half
    mine = core == half
    row = f // 2
    xbit, zbit = c % 2, (c // 2) % 2
    twin, across = dev(c, at.twin), dev(c, at.across)
    xpeer, zpeer, hpeer = dev(flip(c, 1), f), dev(flip(c, 2), f), dev(flip(c, 4), f)

    def remote(src, dst, send_sem, recv_sem, where):
        return pltpu.make_async_remote_copy(
            src_ref=src,
            dst_ref=dst,
            send_sem=send_sem,
            recv_sem=recv_sem,
            device_id=where,
            device_id_type=MESH,
        )

    def grad_copy(group, h):
        return remote(
            grad_ref.at[span(group * 160 + h * 80, 80, 80)],
            grad_all.at[h, pl.ds(0, 80), span(c * 256, 256, 256)],
            g_send_sem.at[group, h],
            g_recv_sem.at[c, h],
            dev(core * 4 + group // 2, at.plane + group % 2),
        )

    def grad_own(h):
        return pltpu.make_async_copy(
            grad_ref.at[span(at.group * 160 + h * 80, 80, 80)],
            grad_all.at[h, pl.ds(0, 80), span(c * 256, 256, 256)],
            local_sem.at[h],
        )

    def give(k, carry):
        group = flip(at.group, k)

        @pl.when(jnp.logical_and(mine, k == 0))
        def _():
            grad_own(0).start()
            grad_own(1).start()

        @pl.when(jnp.logical_not(jnp.logical_and(mine, k == 0)))
        def _():
            grad_copy(group, 0).start()
            grad_copy(group, 1).start()

        return carry

    lax.fori_loop(0, 8, give, 0)

    bits = {"y": row, "x": xbit, "z": zbit, "h": half}
    peers = {"y": across, "x": xpeer, "z": zpeer, "h": hpeer}
    results = (first_ref, second_ref, third_ref)

    def finer(m):
        return "z" if SUM_WAYS[m].index("x") < SUM_WAYS[m].index("z") else "x"

    def cut(ref, way, bit):
        if way == "y":
            return (bit,)
        lead = (slice(None),) * (len(ref.shape) - 2)
        if way == "h":
            return lead + (slice(None), span(bit * 640, 640, 640))
        rows = ref.shape[-2] // 2
        return lead + (span(bit * rows, rows, rows),)

    def main_copy(stage, m):
        if stage < 0:
            y = stage + 2
            src, dst, to = sums.at[pl.ds((m * 2 + y) * 320, 320)], core_in.at[m, y], twin
        elif stage < 4:
            way = SUM_WAYS[m][stage]
            ref = core_in.at[m] if stage == 0 else taken[m][stage - 1]
            src, dst, to = ref.at[cut(ref, way, 1 - bits[way])], taken[m][stage], peers[way]
        else:
            way = SPREAD_WAYS[m][stage - 4]
            known = SPREAD_WAYS[m][: stage - 4]
            low = finer(m)
            high = "x" if low == "z" else "z"
            if high in known:
                rows = pl.ds(0, 320)
            elif low in known:
                rows = span(bits[high] * 160, 160, 160)
            else:
                rows = span(bits[high] * 160 + bits[low] * 80, 80, 80)
            lanes = pl.ds(0, 1280) if "h" in known else span(half * 640, 640, 640)
            src = dst = results[m].at[rows, lanes]
            to = peers[way]
        return remote(src, dst, m_send.at[stage + 2, m], m_recv.at[stage + 2, m], to)

    def added(ref, other, spot):
        for k in range(2) if len(ref.shape) == 3 else (None,):
            here = () if k is None else (k,)
            there = spot if k is None else (k,) + spot[1:]
            ref[here] = (ref[here].astype(F32) + other[there].astype(F32)).astype(BF)

    def main(stage, m):
        if stage == 0:
            for y in range(2):
                main_copy(y - 2, m).wait_recv()
                total = core_in[m, y].astype(F32) + weight_rows(m, 2 * y + core)
                core_in[m, y] = total.astype(BF)
        elif stage < 5:
            main_copy(stage - 1, m).wait_recv()
            way = SUM_WAYS[m][stage - 1]
            ref = core_in.at[m] if stage == 1 else taken[m][stage - 2]
            spot = cut(ref, way, bits[way])
            if stage < 4:
                added(taken[m][stage - 1], ref, spot)
            else:
                low = finer(m)
                high = "x" if low == "z" else "z"
                rows = span(bits[high] * 160 + bits[low] * 80, 80, 80)
                results[m][rows, span(half * 640, 640, 640)] = (
                    taken[m][3][...].astype(F32) + ref[spot].astype(F32)
                ).astype(BF)
        else:
            main_copy(stage - 1, m).wait_recv()
        if stage < 7:
            main_copy(stage, m).start()
        else:
            save(m).start()

    lefts = (act_ref, normed_mlp_ref, att_ref)
    rights = (dy_ref, up_grad_ref, branch_ref)

    def weight_rows(m, quarter):
        rows = span(quarter * 320, 320, 320)
        return jnp.dot(lefts[m][rows, :], rights[m][...], preferred_element_type=F32)

    def main_first(m):
        for name in (("act", "dy"), ("normed", "up"), ("att", "branch"))[m]:
            loads[name].wait()
        for y in range(2):
            part = weight_rows(m, 2 * y + 1 - core)
            sums[(m * 2 + y) * 320 : (m * 2 + y + 1) * 320, :] = part.astype(BF)
            main_copy(y - 2, m).start()

    def prepare():
        loads["qkv"].wait()
        for h in range(2):
            grad_all[h, 80:, :] = jnp.zeros((48, 2048), BF)
            k_turned[h] = jnp.transpose(qkv_ref[:, (2 + h) * LANES : (3 + h) * LANES])
        for k in range(8):
            block = place_ref[0:1, k * 256 : (k + 1) * 256]
            key_pos[k * 256 : (k + 1) * 256, :] = jnp.transpose(
                jnp.broadcast_to(block, (LANES, 256))
            )
        scale_ref[...] = jnp.zeros((8, LANES), F32)

    def take(k, carry):
        block = flip(c, k)

        @pl.when(jnp.logical_and(mine, k == 0))
        def _():
            grad_own(0).wait()
            grad_own(1).wait()

        @pl.when(jnp.logical_not(jnp.logical_and(mine, k == 0)))
        def _():
            for h in range(2):
                await_recv(
                    grad_all.at[h, pl.ds(0, 80), pl.ds(0, 256)], g_recv_sem.at[block, h]
                )

        return carry

    def take_all():
        loads["out"].wait()
        lax.fori_loop(0, 8, take, 0)
        for h in range(2):
            delta[h : h + 1, :] = jnp.sum(
                grad_all[h, :80, :].astype(F32) * out_ref[h * 80 : (h + 1) * 80, :].astype(F32),
                axis=0,
                keepdims=True,
            )

    def head_copy(stage, h):
        if stage == 0:
            src, dst, to = slices.at[h, :, span((1 - row) * 640, 640, 640)], s1.at[h], across
        elif stage == 1:
            src, dst, to = s1.at[h, span(128 - half * 128, 128, 128)], s2.at[h], hpeer
        elif stage < 5:
            way = HEAD_WAYS[stage - 2]
            known = HEAD_WAYS[: stage - 2]
            where = (core,) + tuple(slice(None) if d in known else bits[d] for d in "xz") + (h,)
            rows = slice(None) if "h" in known else span(half * 128, 128, 128)
            src = dst = gathered.at[where + (rows,)]
            to = peers[way]
        else:
            src = dst = gathered.at[core, :, :, h]
            to = twin
        return remote(src, dst, q_send.at[stage, h], q_recv.at[stage, h], to)

    def head(stage, h):
        if stage > 0:
            head_copy(stage - 1, h).wait_recv()
        if stage == 1:
            add_into(s1.at[h], slices.at[h, :, span(row * 640, 640, 640)], 256, 128)
        if stage == 2:
            own = span(half * 128, 128, 128)
            gathered[core, xbit, zbit, h, own, :] = (
                s2[h].astype(F32) + s1[h, own, :].astype(F32)
            ).astype(BF)
        if stage < 6:
            head_copy(stage, h).start()
        else:
            head_flat(h)

    def normed_load(part):
        return pltpu.make_async_copy(
            normed_hbm.at[:, pl.ds(part * 256, 256)], normed_part.at[part % 2], local_sem.at[2 + part % 2]
        )

    def attend_head(h, hooks):
        key_sum[...] = jnp.zeros((2048, LANES), F32)
        value_sum[...] = jnp.zeros((2048, LANES), F32)

        def block_grad(block, carry):
            lanes = span(block * 256, 256, 256)
            high = place_ref[0:1, lanes]
            least = place_ref[1:2, lanes]
            query = qkv_ref[lanes, h * LANES : (h + 1) * LANES]
            grad_t = grad_all[h, :, lanes]
            q_grad = jnp.zeros((LANES, 256), F32)
            for part in range(KEY_PARTS):
                some = slice(part * KEY_ROWS, (part + 1) * KEY_ROWS)
                kp = key_pos[some, :]
                kp = jnp.concatenate([kp, kp], axis=1)
                keys = qkv_ref[some, (2 + h) * LANES : (3 + h) * LANES]
                values = qkv_ref[some, (4 + h) * LANES : (5 + h) * LANES]
                s = lax.dot_general(
                    keys, query, (((1,), (1,)), ((), ())), preferred_element_type=F32
                )
                visible = (kp >= least) & (kp <= high)
                p = jnp.exp(jnp.where(visible, s - lse_ref[h : h + 1, lanes], FLOOR))
                gp = jnp.dot(values, grad_t, preferred_element_type=F32)
                gs = (p * (gp - delta[h : h + 1, lanes])).astype(BF)
                value_sum[some, :] += lax.dot_general(
                    p.astype(BF), grad_t, (((1,), (1,)), ((), ())), preferred_element_type=F32
                )
                key_sum[some, :] += jnp.dot(gs, query, preferred_element_type=F32)
                q_grad += jnp.dot(k_turned[h, :, some], gs, preferred_element_type=F32)
            scale_ref[0:1, :] += jnp.sum(
                jnp.transpose(q_grad) * query.astype(F32), axis=0, keepdims=True
            )
            turned[h * LANES : (h + 1) * LANES, lanes] = (q_grad * mult_ref[:, 0:1]).astype(BF)
            for step, todo in hooks.items():

                @pl.when(block == step)
                def _(todo=todo):
                    for one in todo:
                        one()

            return carry

        lax.fori_loop(0, 8, block_grad, 0)

    def attend_end(h):
        for j, total in ((1, key_sum), (2, value_sum)):
            low = jnp.transpose(total[...]).astype(BF)
            turned[(2 * j + h) * LANES : (2 * j + h + 1) * LANES, :] = low

    def head_first(h):
        slices[h, 240:, :] = jnp.zeros((16, 1280), BF)
        for part in range(5):
            normed_load(part).wait()
            if part + 1 < 5:
                normed_load(part + 1).start()
            for j in range(3):
                first = (2 * j + h) * LANES
                slices[h, j * 80 : (j + 1) * 80, part * 256 : (part + 1) * 256] = jnp.dot(
                    turned[first : first + 80, :],
                    normed_part[part % 2],
                    preferred_element_type=F32,
                ).astype(BF)
        if h == 0:
            normed_load(0).start()
        head(0, h)

    def norm_bits(k):
        return (1 - xbit, 1 - xbit, xbit, xbit)[k], (1 - zbit, zbit, 1 - zbit, zbit)[k]

    def norm_spot(k, hh):
        slot = 2 * k + hh
        return sums.at[pl.ds(slot // 5 * 640, 640), pl.ds(slot % 5 * 256, 256)]

    def norm_copy(stage, k, hh=0):
        if stage == 0:
            return remote(
                norm_spot(k, hh), n_core.at[k, hh], nc_send.at[k, hh], nc_recv.at[k, hh], twin
            )
        took = k
        if stage == 1:
            ends = n_core.at[k], n_x.at[k], xpeer
        elif stage == 2:
            ends = n_core.at[2, (1 - half, half)[k]], n_z.at[k], zpeer
        else:
            to = dev(flip(c, 4), at.pack) if k == 0 else dev(c, at.twin)
            took = (core, 2)[k]
            ends = n_core.at[3, (1 - half, half)[k]], n_last.at[core], to
        return remote(ends[0], ends[1], n_send.at[stage, k], n_recv.at[stage, took], ends[2])

    def norm_part(k, hh, which):
        xs, zs = norm_bits(k)
        lanes = span((hh * 4 + zs * 2 + xs) * 256, 256, 256)
        rows = span(which * 640, 640, 640)
        return jnp.dot(w_ref[rows, :], turned[:, lanes], preferred_element_type=F32)

    def norm_first(k):
        if k == 0:
            loads["w"].wait()
            for m in range(3):
                for stage in range(2):
                    main_copy(stage - 2, m).wait_send()
        for hh in range(2):
            norm_spot(k, hh)[...] = norm_part(k, hh, 1 - core).astype(BF)
            norm_copy(0, k, hh).start()

    def norm_core(k):
        for hh in range(2):
            norm_copy(0, k, hh).wait_recv()
            n_core[k, hh] = (n_core[k, hh].astype(F32) + norm_part(k, hh, core)).astype(BF)
        if k < 2:
            norm_copy(1, k).start()

    def scale_copy(stage):
        where = (twin, across, xpeer, zpeer, hpeer)[stage]
        return remote(scale_ref, scale_in.at[stage], v_send.at[stage], v_recv.at[stage], where)

    def tiny(stage):
        if stage > 0:
            scale_copy(stage - 1).wait()
            scale_ref[...] += scale_in[stage - 1]
        if stage < 5:
            scale_copy(stage).start()
        else:
            given = gain_ref[2:3, :LANES]
            soft = jnp.maximum(given, 0.0) + jnp.log1p(jnp.exp(-jnp.abs(given)))
            scale_ref[0:1, :] = scale_ref[0:1, :] / (soft * (1.0 + jnp.exp(-given)))

    def norm_x(k):
        norm_copy(1, k).wait_recv()
        for hh in range(2):
            add_into(n_core.at[2 + k, hh], n_x.at[k, hh], 640, 80)
        if k == 0:
            norm_copy(2, 0).start()
            norm_copy(2, 1).start()

    def norm_far():
        norm_copy(2, 0).wait_recv()
        add_into(n_core.at[3, 1 - half], n_z.at[0], 640, 80)
        norm_copy(3, 0).start()

    def norm_near():
        norm_copy(2, 1).wait_recv()
        add_into(n_core.at[3, half], n_z.at[1], 640, 80)

        @pl.when(jnp.logical_not(mine))
        def _():
            norm_copy(3, 1).start()

    def norm_last():
        loads["x"].wait()
        loads["resid"].wait()
        @pl.when(mine)
        def _():
            n_last[core] = n_core[3, half]
            await_recv(n_last.at[0], n_recv.at[3, 2])

        @pl.when(jnp.logical_not(mine))
        def _():
            await_recv(n_last.at[0], n_recv.at[3, 0])
            await_recv(n_last.at[1], n_recv.at[3, 1])

        xf = x_ref[...].astype(F32)
        inv = lax.rsqrt(jnp.mean(xf * xf, axis=1, keepdims=True) + EPS)
        scaled = jnp.concatenate(
            [jnp.transpose(n_last[k].astype(F32)) for k in range(2)], axis=1
        ) * gain_ref[0:1, :]
        input_ref[...] = resid_grad_ref[...] + inv * (
            scaled - xf * inv * inv * jnp.mean(scaled * xf, axis=1, keepdims=True)
        )
        save(3).start()

    def head_flat(h):
        if h == 0:
            for k in range(4):
                for hh in range(2):
                    norm_copy(0, k, hh).wait_send()
        for core_k in range(2):
            for m4 in range(4):
                for j in range(3):
                    start = j * 1280 + (4 * m4 + 2 * core_k + h) * 80
                    first = start // 1920 * 640
                    sums[start % 1920 : start % 1920 + 80, first : first + 640] = gathered[
                        core_k, m4 % 2, m4 // 2, h, j * 80 : (j + 1) * 80, :
                    ]

    def save(k):
        src, dst = (
            (first_ref, first_out),
            (second_ref, second_out),
            (third_ref, third_out),
            (input_ref, input_grad_out),
            (slice_ref.at[:, pl.ds(0, 1920)], slice_out.at[:, pl.ds(0, 1920)]),
            (slice_ref.at[:, pl.ds(1920, 1920)], slice_out.at[:, pl.ds(1920, 1920)]),
        )[k]
        return pltpu.make_async_copy(src, dst, save_sem.at[k])

    def turn_all():
        for part in range(2):

            def turn(k, carry, part=part):
                rows = span(k * 384, 384, 384)
                lanes = span(part * 1920 + k * 384, 384, 384)

                @pl.when(core == 0)
                def _():
                    strip = jnp.transpose(sums[rows, part * 640 : part * 640 + 384])
                    slice_ref[:, lanes] = strip[:320]

                @pl.when(core == 1)
                def _():
                    strip = jnp.transpose(sums[rows, part * 640 + 256 : part * 640 + 640])
                    slice_ref[:, lanes] = strip[64:]

                return carry

            lax.fori_loop(0, 5, turn, 0)
            save(4 + part).start()

    tasks = {"prep": prepare, "take": take_all, "nb0": lambda: norm_x(0), "nb1": lambda: norm_x(1)}
    tasks |= {"nc_f": norm_far, "nc_n": norm_near, "nfin": norm_last, "turn": turn_all}
    for m in range(3):
        tasks[f"mt{m}"] = functools.partial(main_first, m)
        for stage in range(4):
            tasks[f"m{stage}{m}"] = functools.partial(main, stage, m)
        for stage in range(3):
            tasks[f"g{stage}{m}"] = functools.partial(main, 4 + stage, m)
        tasks[f"mw{m}"] = functools.partial(main, 7, m)
    for h in range(2):
        tasks[f"E{h}"] = functools.partial(attend_end, h)
        tasks[f"qs{h}"] = functools.partial(head_first, h)
        for stage, name in enumerate(("qa", "q0", "q1", "q2", "qc", "qw")):
            tasks[f"{name}{h}"] = functools.partial(head, 1 + stage, h)
    for k in range(4):
        tasks[f"nt{k}"] = functools.partial(norm_first, k)
        tasks[f"na{k}"] = functools.partial(norm_core, k)
    for stage in range(6):
        tasks[f"v{stage}"] = functools.partial(tiny, stage)

    normed_load(0).start()
    spot = 0
    while spot < len(PLAN):
        name = PLAN[spot]
        if name[0] != "L":
            tasks[name]()
            spot += 1
            continue
        h, step, hooks = int(name[1]), -1, {}
        while step < 7 or PLAN[spot][0] == "L":
            if PLAN[spot][0] == "L":
                step = int(PLAN[spot][2])
                if step == 7:
                    spot += 1
                    break
            else:
                hooks.setdefault(step, []).append(tasks[PLAN[spot]])
            spot += 1
        attend_head(h, hooks)

    for k in range(6):
        save(k).wait()
    def sent(block, carry):
        own_in = jnp.logical_and(mine, block == at.group)

        @pl.when(jnp.logical_not(own_in))
        def _():
            for h in range(2):
                grad_copy(block, h).wait_send()

        return carry

    lax.fori_loop(0, 8, sent, 0)
    for m in range(3):
        for stage in range(7):
            main_copy(stage, m).wait_send()
    for h in range(2):
        for stage in range(6):
            head_copy(stage, h).wait_send()
    for k in range(2):
        norm_copy(1, k).wait_send()
        norm_copy(2, k).wait_send()
    norm_copy(3, 0).wait_send()

    @pl.when(jnp.logical_not(mine))
    def _():
        norm_copy(3, 1).wait_send()


def sum_slots():
    slots = []
    for ways in SUM_WAYS:
        shape, own = [2, 320, 1280], []
        for way in ways:
            if way == "y":
                shape = shape[1:]
            else:
                shape[-1 if way == "h" else -2] //= 2
            own.append(pltpu.VMEM(tuple(shape), BF))
        slots.append(own)
    return slots


def backward(*args):
    shape = jax.ShapeDtypeStruct
    dma = pltpu.SemaphoreType.DMA
    specs = [ANY_SPEC] * 17
    for k in (8, 10, 13, 16):
        specs[k] = VMEM_SPEC
    return pl.pallas_call(
        backward_kernel,
        name="backward",
        out_shape=(
            shape((320, 1280), BF),
            shape((320, 1280), BF),
            shape((320, 1280), BF),
            shape((320, 3840), BF),
            shape((256, 1280), F32),
            shape((8, LANES), F32),
        ),
        in_specs=specs,
        out_specs=(ANY_SPEC,) * 5 + (VMEM_SPEC,),
        scratch_shapes=[
            pltpu.VMEM((320, 1280), BF),
            pltpu.VMEM((320, 1280), BF),
            pltpu.VMEM((320, 1280), BF),
            pltpu.VMEM((320, 3840), BF),
            pltpu.VMEM((256, 1280), F32),
            pltpu.VMEM((1280, 256), BF),
            pltpu.VMEM((256, 1280), BF),
            pltpu.VMEM((1280, 256), BF),
            pltpu.VMEM((256, 1280), BF),
            pltpu.VMEM((1280, 256), BF),
            pltpu.VMEM((256, 1280), BF),
            pltpu.VMEM((2048, 768), BF),
            pltpu.VMEM((160, 2048), BF),
            pltpu.VMEM((1280, 768), BF),
            pltpu.VMEM((256, 1280), BF),
            pltpu.VMEM((256, 1280), F32),
            pltpu.VMEM((2, 128, 2048), BF),
            pltpu.VMEM((2048, LANES), F32),
            pltpu.VMEM((2, 128, 2048), BF),
            pltpu.VMEM((8, 2048), F32),
            pltpu.VMEM((2048, LANES), F32),
            pltpu.VMEM((2048, LANES), F32),
            pltpu.VMEM((768, 2048), BF),
            pltpu.VMEM((2, 2048, 256), BF),
            pltpu.VMEM((4, 2, 640, 256), BF),
            pltpu.VMEM((2, 2, 640, 256), BF),
            pltpu.VMEM((2, 640, 256), BF),
            pltpu.VMEM((2, 640, 256), BF),
            pltpu.VMEM((1920, 1280), BF),
            pltpu.VMEM((3, 2, 320, 1280), BF),
            sum_slots(),
            pltpu.VMEM((2, 256, 1280), BF),
            pltpu.VMEM((2, 256, 640), BF),
            pltpu.VMEM((2, 128, 640), BF),
            pltpu.VMEM((2, 2, 2, 2, 256, 640), BF),
            pltpu.VMEM((5, 8, LANES), F32),
            dma((8, 2)),
            dma((8, 2)),
            dma((4,)),
            dma((9, 3)),
            dma((9, 3)),
            dma((6, 2)),
            dma((6, 2)),
            dma((4, 2)),
            dma((4, 2)),
            dma((4, 4)),
            dma((4, 4)),
            dma((5,)),
            dma((5,)),
            dma((11,)),
            dma((6,)),
        ],
        compiler_params=pltpu.CompilerParams(
            collective_id=1, has_side_effects=True, vmem_limit_bytes=VMEM_LIMIT
        ),
        cost_estimate=pl.CostEstimate(
            flops=30_000_000_000, bytes_accessed=60_000_000, transcendentals=8_400_000
        ),
    )(*args)


def widen_kernel(*refs):
    total = []
    for k in range(4):
        value = refs[k][...].astype(F32)
        refs[6 + k][...] = value
        if k in (0, 2):
            total.append(jnp.sum(value * refs[4 + k // 2][...].astype(F32), axis=1, keepdims=True))
    lane = lax.broadcasted_iota(jnp.int32, refs[10].shape, 1)
    refs[10][...] = jnp.where(lane == 0, total[0], total[1])


def widen(*args):
    rows = 160
    shape = jax.ShapeDtypeStruct
    specs = [pl.BlockSpec((rows, a.shape[1]), lambda k: (k, 0)) for a in args]
    return pl.pallas_call(
        widen_kernel,
        name="widen",
        grid=(args[0].shape[0] // rows,),
        out_shape=tuple(shape(a.shape, F32) for a in args[:4]) + (shape((320, LANES), F32),),
        in_specs=specs,
        out_specs=tuple(specs[:4]) + (pl.BlockSpec((rows, LANES), lambda k: (k, 0)),),
        compiler_params=pltpu.CompilerParams(vmem_limit_bytes=VMEM_LIMIT),
    )(*args)


def fast_body(
    tokens,
    lengths,
    position,
    qkv_weight,
    out_weight,
    up_weight,
    down_weight,
    attn_gain,
    mlp_gain,
    query_scale,
    cotangent,
):
    f = lax.axis_index("fsdp")
    x, dy = tokens[0], cotangent[0]
    small = jnp.zeros((16, 384), BF)
    for k, own in enumerate((attn_gain, mlp_gain, query_scale)):
        small = lax.dynamic_update_slice(small, own[None], (k, 0))
    (
        att_t, normed, qkv, lse, out, auxsum, place, w_heads,
        result, resid_grad, branch_grad, up_grad, act_t, normed_mlp_t, grad_t, mult,
    ) = forward(
        lengths, x, qkv_weight, small, position, out_weight, up_weight, down_weight, dy
    )
    g_down, g_up, g_out, g_qkv, input_grad, scale_sum = backward(
        grad_t,
        att_t,
        branch_grad,
        normed_mlp_t,
        up_grad,
        act_t,
        dy,
        qkv,
        lse,
        out,
        place,
        normed,
        w_heads,
        mult,
        x,
        resid_grad,
        auxsum,
    )
    g_qkv, g_out, g_up, g_down, sums = widen(g_qkv, g_out, g_up, g_down, qkv_weight, up_weight)
    grad_attn_gain = sums[:, 0] / attn_gain.astype(F32)
    grad_mlp_gain = sums[:, 1] / mlp_gain.astype(F32)
    return (
        result[None],
        input_grad[None],
        g_qkv,
        g_out,
        g_up,
        g_down,
        grad_attn_gain,
        grad_mlp_gain,
        lax.dynamic_slice_in_dim(scale_sum[0, :80], f * 20, 20),
    )


def solution(mesh):
    placed = (
        P("fsdp", "ctx", None),
        P("fsdp", None),
        P("fsdp", None),
        P("fsdp", None),
        P("fsdp", None),
        P("fsdp", None),
        P("fsdp", None),
        P("fsdp"),
        P("fsdp"),
        P("fsdp"),
        P("fsdp", "ctx", None),
    )
    fits = mesh.shape["ctx"] == 8 and mesh.shape["fsdp"] == 4
    return jax.shard_map(
        fast_body if fits else body,
        mesh=mesh,
        in_specs=placed,
        out_specs=(
            P("fsdp", "ctx", None),
            P("fsdp", "ctx", None),
            P("fsdp", None),
            P("fsdp", None),
            P("fsdp", None),
            P("fsdp", None),
            P("fsdp"),
            P("fsdp"),
            P("fsdp"),
        ),
        check_vma=False,
    )
```

```python
import functools
import math

import jax
import jax.numpy as jnp
from jax import lax
from jax.experimental import pallas as pl
from jax.experimental.pallas import tpu as pltpu
from jax.sharding import PartitionSpec as P

HEADS = 16


EPS = 1e-06
FLOOR = -1e30
LOG2E = 1.442695041

MESH = pl.DeviceIdType.MESH
LANES = 128
BF = jnp.bfloat16
F32 = jnp.float32
VMEM_SPEC = pl.BlockSpec(memory_space=pltpu.VMEM)
ANY_SPEC = pl.BlockSpec(memory_space=pl.ANY)
VMEM_LIMIT = 60 << 20


def flip(number, mask):
    total = 0
    for bit in (1, 2, 4):
        left = (number // bit) % 2
        right = (mask // bit) % 2
        total = total + bit * (left + right - 2 * left * right)
    return total


class Place:
    def __init__(self):
        self.c = lax.axis_index("ctx")
        self.f = lax.axis_index("fsdp")
        self.core = self.f % 2
        self.plane = self.f - self.core
        self.half = self.c // 4
        self.pack = self.plane + self.half
        self.group = (self.c % 4) * 2 + self.core
        self.twin = self.plane + 1 - self.core
        self.across = (self.f + 2) % 4


def dev(ctx, fsdp):
    return {"ctx": ctx, "fsdp": fsdp}


def send(src, dst, send_sem, recv_sem, device):
    copy = pltpu.make_async_remote_copy(
        src_ref=src,
        dst_ref=dst,
        send_sem=send_sem,
        recv_sem=recv_sem,
        device_id=device,
        device_id_type=MESH,
    )
    copy.start()
    return copy


def await_recv(ref, sem):
    pltpu.make_async_copy(ref, ref, sem).wait()


def meet_plane(at):
    barrier = pltpu.get_barrier_semaphore()

    def greet(k, carry):
        pl.semaphore_signal(
            barrier,
            1,
            device_id=dev((at.c + k // 2) % 8, at.plane + (at.core + k) % 2),
            device_id_type=MESH,
        )
        return carry

    lax.fori_loop(1, 16, greet, 0)
    for k in range(2):
        pl.semaphore_signal(
            barrier, 1, device_id=dev(at.c, (at.plane + 2) % 4 + k), device_id_type=MESH
        )
    pl.semaphore_wait(barrier, 17)


def span(start, size, unit):
    return pl.ds(pl.multiple_of(start, unit), size)


def doc_index(places, seq_ends):
    return jnp.sum((places[:, None] >= seq_ends[None, :]).astype(jnp.int32), axis=1)


def spread_position(gathered_index, tok_dev, cycle_size):
    return gathered_index % tok_dev * cycle_size + gathered_index // tok_dev


def pair_scores(left_rows, right_rows):
    return jnp.einsum(
        "qhd,khd->qhk",
        left_rows.reshape(left_rows.shape[0], HEADS, -1),
        right_rows.reshape(right_rows.shape[0], HEADS, -1),
        preferred_element_type=jnp.float32,
    )


def pair_mask(query_pos, query_doc, key_pos, key_doc):
    return ((query_doc[:, None] == key_doc[None, :]) & (key_pos[None, :] <= query_pos[:, None]))[
        :, None, :
    ]


def in_blocks(advance, carried, pieces):
    total_rows = pieces[0].shape[0]
    block_rows = math.gcd(total_rows, 1024)
    block_count = total_rows // block_rows
    split = tuple((p.reshape((block_count, block_rows) + p.shape[1:]) for p in pieces))

    def inner(running, entry):
        return (advance(running, entry[1], entry[0] * block_rows), None)

    result, unused = lax.scan(inner, carried, (jnp.arange(block_count, dtype=jnp.int32), split))
    return result


def pair_terms(
    query_part,
    grad_part,
    log_part,
    delta_part,
    query_pos,
    query_doc,
    key_part,
    value_part,
    key_pos,
    key_doc,
):
    visible = pair_mask(query_pos, query_doc, key_pos, key_doc)
    prob_float = jnp.where(
        visible, jnp.exp(pair_scores(query_part, key_part) - log_part[:, :, None]), 0.0
    )
    grad_probs = pair_scores(grad_part, value_part)
    score_grad = (prob_float * (grad_probs - delta_part[:, :, None])).astype(jnp.bfloat16)
    return (prob_float.astype(jnp.bfloat16), score_grad)


def body(
    tokens,
    lengths,
    position,
    qkv_weight,
    out_weight,
    up_weight,
    down_weight,
    attn_gain,
    mlp_gain,
    query_scale,
    cotangent,
):
    cycle_size = lax.axis_size("ctx")
    my_index = lax.axis_index("ctx")
    tok_dev = tokens.shape[1]
    share_rows = tok_dev // cycle_size
    seq_ends = jnp.cumsum(lengths[0])
    place_row = position[0]
    residue = (place_row % cycle_size).reshape(cycle_size, tok_dev)
    landing = place_row // cycle_size
    matches = (
        residue[:, :, None] == jnp.arange(cycle_size, dtype=jnp.int32)[None, None, :]
    ).astype(jnp.int32)
    ranked = jnp.sum(jnp.cumsum(matches, axis=1) * matches, axis=2) - 1
    buffer_slot = residue * share_rows + ranked
    my_slots = lax.dynamic_index_in_dim(buffer_slot, my_index, 0, keepdims=False)
    local_rows = jnp.arange(tok_dev, dtype=jnp.int32)
    outgoing = jnp.zeros((tok_dev,), jnp.int32).at[my_slots].set(local_rows)
    flat_slot = (jnp.arange(cycle_size, dtype=jnp.int32)[:, None] * tok_dev + buffer_slot).reshape(
        -1
    )
    landing_table = (
        jnp.zeros((cycle_size * tok_dev,), jnp.int32)
        .at[flat_slot]
        .set(landing)
        .reshape(cycle_size, cycle_size, share_rows)
    )
    arrived_slot = lax.dynamic_index_in_dim(landing_table, my_index, 1, keepdims=False).reshape(-1)
    arrived_order = jnp.zeros((tok_dev,), jnp.int32).at[arrived_slot].set(local_rows)
    moved_x, moved_dy = (
        lax.all_to_all(tokens[0][outgoing], "ctx", split_axis=0, concat_axis=0, tiled=True),
        lax.all_to_all(cotangent[0][outgoing], "ctx", split_axis=0, concat_axis=0, tiled=True),
    )
    dealt_x = moved_x[arrived_order]
    dealt_dy = moved_dy[arrived_order]
    query_pos = local_rows * cycle_size + my_index
    query_doc = doc_index(query_pos, seq_ends)
    full_qkv, full_out, full_up, full_down, attn_gain_full, mlp_gain_full, scale_full = (
        lax.all_gather(qkv_weight, "fsdp", axis=0, tiled=True),
        lax.all_gather(out_weight, "fsdp", axis=0, tiled=True),
        lax.all_gather(up_weight, "fsdp", axis=0, tiled=True),
        lax.all_gather(down_weight, "fsdp", axis=0, tiled=True),
        lax.all_gather(attn_gain, "fsdp", axis=0, tiled=True),
        lax.all_gather(mlp_gain, "fsdp", axis=0, tiled=True),
        lax.all_gather(query_scale, "fsdp", axis=0, tiled=True),
    )
    attn_gain_f = attn_gain_full.astype(jnp.float32)
    mlp_gain_f = mlp_gain_full.astype(jnp.float32)
    scale_float = scale_full.astype(jnp.float32)
    x_float = dealt_x.astype(jnp.float32)
    inv_attn = lax.rsqrt(jnp.mean(x_float * x_float, axis=1, keepdims=True) + EPS)
    normed_attn = (x_float * inv_attn * attn_gain_f).astype(jnp.bfloat16)
    projected = jnp.dot(normed_attn, full_qkv, preferred_element_type=jnp.float32)
    att_width = projected.shape[1] // 3
    head_dim = scale_full.shape[0]
    base_scale = LOG2E / math.sqrt(head_dim)
    multiplier = jnp.tile(base_scale * jax.nn.softplus(scale_float), att_width // head_dim)
    raw_query = projected[:, :att_width]
    queries = (raw_query * multiplier).astype(jnp.bfloat16)
    key_rows = projected[:, att_width : 2 * att_width].astype(jnp.bfloat16)
    value_rows = projected[:, 2 * att_width :].astype(jnp.bfloat16)

    def key_place(first_row, amount):
        gathered_index = first_row + jnp.arange(amount, dtype=jnp.int32)
        key_pos = spread_position(gathered_index, tok_dev, cycle_size)
        return (key_pos, doc_index(key_pos, seq_ends))

    def stat_block(carried, pieces, first_row):
        running_max, running_sum = carried
        key_pos, key_doc = key_place(first_row, pieces[0].shape[0])
        visible = pair_mask(query_pos, query_doc, key_pos, key_doc)
        logits = jnp.where(visible, pair_scores(queries, pieces[0]), FLOOR)
        new_max = jnp.maximum(running_max, jnp.max(logits, axis=2))
        added = jnp.sum(jnp.where(visible, jnp.exp(logits - new_max[:, :, None]), 0.0), axis=2)
        return (new_max, running_sum * jnp.exp(running_max - new_max) + added)

    def output_block(summed, pieces, first_row):
        key_pos, key_doc = key_place(first_row, pieces[0].shape[0])
        visible = pair_mask(query_pos, query_doc, key_pos, key_doc)
        prob_low = jnp.where(
            visible, jnp.exp(pair_scores(queries, pieces[0]) - log_total[:, :, None]), 0.0
        ).astype(jnp.bfloat16)
        values_part = pieces[1].reshape(pieces[1].shape[0], HEADS, -1)
        return summed + jnp.einsum(
            "qhk,khd->qhd", prob_low, values_part, preferred_element_type=jnp.float32
        ).reshape(summed.shape)

    def query_grad_block(summed, pieces, first_row):
        key_pos, key_doc = key_place(first_row, pieces[0].shape[0])
        unused_probs, score_grad = pair_terms(
            queries,
            attended_grad,
            log_total,
            row_delta,
            query_pos,
            query_doc,
            pieces[0],
            pieces[1],
            key_pos,
            key_doc,
        )
        keys_part = pieces[0].reshape(pieces[0].shape[0], HEADS, -1)
        return summed + jnp.einsum(
            "qhk,khd->qhd", score_grad, keys_part, preferred_element_type=jnp.float32
        ).reshape(summed.shape)

    def key_grad_block(carried, pieces, first_row):
        amount = pieces[0].shape[0]
        part_pos, part_doc = key_place(first_row, amount)
        part_log = lax.dynamic_slice_in_dim(all_log, first_row, amount, 0)
        part_delta = lax.dynamic_slice_in_dim(all_delta, first_row, amount, 0)
        prob_low, score_grad = pair_terms(
            pieces[0],
            pieces[1],
            part_log,
            part_delta,
            part_pos,
            part_doc,
            key_rows,
            value_rows,
            query_pos,
            query_doc,
        )
        grad_keys = carried[0] + jnp.einsum(
            "qhk,qhd->khd",
            score_grad,
            pieces[0].reshape(amount, HEADS, -1),
            preferred_element_type=jnp.float32,
        ).reshape(tok_dev, -1)
        grad_values = carried[1] + jnp.einsum(
            "qhk,qhd->khd",
            prob_low,
            pieces[1].reshape(amount, HEADS, -1),
            preferred_element_type=jnp.float32,
        ).reshape(tok_dev, -1)
        return (grad_keys, grad_values)

    zero_stats = (
        jnp.full((tok_dev, HEADS), FLOOR, jnp.float32),
        jnp.zeros((tok_dev, HEADS), jnp.float32),
    )
    zero_rows = jnp.zeros((tok_dev, att_width), jnp.float32)
    running_max, running_sum = in_blocks(
        stat_block, zero_stats, (lax.all_gather(key_rows, "ctx", axis=0, tiled=True),)
    )
    log_total = running_max + jnp.log(running_sum)
    attended = in_blocks(
        output_block,
        zero_rows,
        (
            lax.all_gather(key_rows, "ctx", axis=0, tiled=True),
            lax.all_gather(value_rows, "ctx", axis=0, tiled=True),
        ),
    )
    attended_low = attended.astype(jnp.bfloat16)
    resid = x_float + jnp.dot(attended_low, full_out, preferred_element_type=jnp.float32)
    inv_mlp = lax.rsqrt(jnp.mean(resid * resid, axis=1, keepdims=True) + EPS)
    normed_mlp = (resid * inv_mlp * mlp_gain_f).astype(jnp.bfloat16)
    up_proj = jnp.dot(normed_mlp, full_up, preferred_element_type=jnp.float32)
    act_low = jax.nn.silu(up_proj).astype(jnp.bfloat16)
    result = resid + jnp.dot(act_low, full_down, preferred_element_type=jnp.float32)
    cot_float = dealt_dy.astype(jnp.float32)
    grad_down = jnp.dot(act_low.T, dealt_dy, preferred_element_type=jnp.float32)
    act_grad = jnp.dot(dealt_dy, full_down.T, preferred_element_type=jnp.float32)
    sigma = jax.nn.sigmoid(up_proj)
    up_grad = (act_grad * sigma * (1.0 + up_proj * (1.0 - sigma))).astype(jnp.bfloat16)
    grad_up = jnp.dot(normed_mlp.T, up_grad, preferred_element_type=jnp.float32)
    norm_mlp_grad = jnp.dot(up_grad, full_up.T, preferred_element_type=jnp.float32)
    grad_mlp_gain = jnp.sum(norm_mlp_grad * resid * inv_mlp, axis=0)
    scaled_mlp = norm_mlp_grad * mlp_gain_f
    resid_grad = cot_float + inv_mlp * (
        scaled_mlp - resid * inv_mlp * inv_mlp * jnp.mean(scaled_mlp * resid, axis=1, keepdims=True)
    )
    branch_grad = resid_grad.astype(jnp.bfloat16)
    grad_out = jnp.dot(attended_low.T, branch_grad, preferred_element_type=jnp.float32)
    attended_grad = jnp.dot(branch_grad, full_out.T, preferred_element_type=jnp.float32).astype(
        jnp.bfloat16
    )
    row_delta = jnp.sum(
        (attended_grad.astype(jnp.float32) * attended).reshape(tok_dev, HEADS, -1), axis=2
    )
    query_grads = in_blocks(
        query_grad_block,
        zero_rows,
        (
            lax.all_gather(key_rows, "ctx", axis=0, tiled=True),
            lax.all_gather(value_rows, "ctx", axis=0, tiled=True),
        ),
    )
    all_log, all_delta = (
        lax.all_gather(log_total, "ctx", axis=0, tiled=True),
        lax.all_gather(row_delta, "ctx", axis=0, tiled=True),
    )
    key_grad_f, value_grad_f = in_blocks(
        key_grad_block,
        (zero_rows, zero_rows),
        (
            lax.all_gather(queries, "ctx", axis=0, tiled=True),
            lax.all_gather(attended_grad, "ctx", axis=0, tiled=True),
        ),
    )
    scale_terms = jnp.sum((query_grads * raw_query).reshape(tok_dev, -1, head_dim), axis=(0, 1))
    grad_scale = scale_terms * base_scale * jax.nn.sigmoid(scale_float)
    proj_grad = jnp.concatenate(
        [
            (query_grads * multiplier).astype(jnp.bfloat16),
            key_grad_f.astype(jnp.bfloat16),
            value_grad_f.astype(jnp.bfloat16),
        ],
        axis=1,
    )
    grad_qkv = jnp.dot(normed_attn.T, proj_grad, preferred_element_type=jnp.float32)
    norm_attn_grad = jnp.dot(proj_grad, full_qkv.T, preferred_element_type=jnp.float32)
    grad_attn_gain = jnp.sum(norm_attn_grad * x_float * inv_attn, axis=0)
    scaled_attn = norm_attn_grad * attn_gain_f
    input_grad = resid_grad + inv_attn * (
        scaled_attn
        - x_float * inv_attn * inv_attn * jnp.mean(scaled_attn * x_float, axis=1, keepdims=True)
    )
    owned = (
        lax.psum_scatter(grad_qkv, "fsdp", scatter_dimension=0, tiled=True),
        lax.psum_scatter(grad_out, "fsdp", scatter_dimension=0, tiled=True),
        lax.psum_scatter(grad_up, "fsdp", scatter_dimension=0, tiled=True),
        lax.psum_scatter(grad_down, "fsdp", scatter_dimension=0, tiled=True),
        lax.psum_scatter(grad_attn_gain, "fsdp", scatter_dimension=0, tiled=True),
        lax.psum_scatter(grad_mlp_gain, "fsdp", scatter_dimension=0, tiled=True),
        lax.psum_scatter(grad_scale, "fsdp", scatter_dimension=0, tiled=True),
    )
    summed_grads = lax.psum(
        (owned[0], owned[1], owned[2], owned[3], owned[4], owned[5], owned[6]), "ctx"
    )
    back_out, back_grad = (
        lax.all_to_all(result[arrived_slot], "ctx", split_axis=0, concat_axis=0, tiled=True),
        lax.all_to_all(input_grad[arrived_slot], "ctx", split_axis=0, concat_axis=0, tiled=True),
    )
    return (
        back_out[my_slots][None],
        back_grad[my_slots][None],
        summed_grads[0],
        summed_grads[1],
        summed_grads[2],
        summed_grads[3],
        summed_grads[4],
        summed_grads[5],
        summed_grads[6],
    )


HUB_WAYS = {k: ((2, 0), (2, 1)) for k in range(1, 8)}
HUB_WAYS[1] += ((1, 0),)
HUB_WAYS[2] += ((0, 1),)
HUB_WAYS[4] += ((0, 0), (0, 1), (1, 0), (1, 1))
HUB_WAYS[6] += ((0, 0), (0, 1))

SPLIT = (False, True, False)
WEIGHT_STEPS = ((2, 2, 1), (4, 2, 0), (6, 3, 1))


def attend_kernel(
    ends_ref,
    x_ref,
    w_ref,
    aux_ref,
    pos_ref,
    out_w_ref,
    up_w_ref,
    down_w_ref,
    dy_ref,
    att_save,
    normed_out,
    qkv_out,
    lse_ref,
    out_save,
    auxsum_ref,
    place_ref,
    w_out,
    result_ref,
    resid_grad_save,
    branch_save,
    up_grad_save,
    act_save,
    normed_mlp_save,
    grad_ref,
    mult_ref,
    x_mine,
    w_mine,
    dy_mine,
    x_all,
    normed_ref,
    qkv_ref,
    w_all,
    w_own,
    w_small,
    weights,
    aux_all,
    pos_all,
    v_turned,
    key_pos,
    att_send,
    x_send_sem,
    x_recv_sem,
    w_send_sem,
    w_recv_sem,
    aux_send_sem,
    aux_recv_sem,
    pos_sem,
    att_send_sem,
    att_recv_sem,
    m_send_sem,
    m_recv_sem,
    local_sem,
    save_sem,
    shard_sem,
    att_ref,
    out_ref,
    resid_grad_ref,
    branch_ref,
    up_grad_ref,
    act_ref,
    normed_mlp_ref,
    early_sem,
):
    early = {
        name: pltpu.make_async_copy(src, dst, early_sem.at[k])
        for k, (name, src, dst) in enumerate(
            (
                ("att", att_ref, att_save),
                ("out", out_ref, out_save),
                ("resid_grad", resid_grad_ref, resid_grad_save),
                ("branch", branch_ref, branch_save),
                ("up_grad", up_grad_ref, up_grad_save),
                ("act", act_ref, act_save),
                ("normed_mlp", normed_mlp_ref, normed_mlp_save),
            )
        )
    }
    w_load = pltpu.make_async_copy(w_ref, w_mine, local_sem.at[0])
    w_load.start()
    x_load = pltpu.make_async_copy(x_ref, x_mine, local_sem.at[2])
    dy_load = pltpu.make_async_copy(dy_ref, dy_mine, local_sem.at[4])
    at = Place()
    meet_plane(at)
    c, f = at.c, at.f
    hub = at.core == at.half

    aux_own = pltpu.make_async_copy(aux_ref, aux_all.at[f], local_sem.at[1])
    aux_own.start()
    x_own = pltpu.make_async_copy(x_ref, x_all.at[c], local_sem.at[3])

    halves = (pl.ds(0, 128), pl.ds(128, 128))

    def x_far(part):
        return pltpu.make_async_remote_copy(
            src_ref=x_ref.at[halves[part]],
            dst_ref=x_all.at[c, halves[part]],
            send_sem=x_send_sem.at[0, 0, part],
            recv_sem=x_recv_sem.at[c, part],
            device_id=dev(flip(c, 4), f),
            device_id_type=MESH,
        )

    @pl.when(hub)
    def _():
        x_own.start()
        for part in range(2):
            for k, where in enumerate((dev(flip(c, 1), f), dev(flip(c, 2), f), dev(c, at.twin))):
                send(
                    x_ref.at[halves[part]],
                    x_all.at[c, halves[part]],
                    x_send_sem.at[0, k, part],
                    x_recv_sem.at[c, part],
                    where,
                )

    @pl.when(jnp.logical_not(hub))
    def _():
        x_far(0).start()
        x_far(1).start()

    w_copies, aux_copies = [], []
    for k in (2, 1, 3):
        aux_copies.append(
            send(
                aux_ref,
                aux_all.at[f],
                aux_send_sem.at[k],
                aux_recv_sem.at[f],
                dev(c, (f + k) % 4),
            )
        )

    pos = pos_ref[...]
    start = jnp.zeros_like(pos)
    end = 0
    for k in range(4):
        end = end + ends_ref[0, k]
        start = jnp.where(pos >= end, end, start)
    pos_all[at.core, 0:1, :] = pos.astype(F32)
    pos_all[at.core, 1:2, :] = start.astype(F32)
    pos_all[at.core, 2:8, :] = jnp.zeros((6, 2048), F32)
    pos_copy = send(
        pos_all.at[at.core], pos_all.at[at.core], pos_sem.at[0], pos_sem.at[1], dev(c, at.twin)
    )

    row = lax.broadcasted_iota(jnp.int32, (1280, 512), 0)
    column = lax.broadcasted_iota(jnp.int32, (1280, 512), 1)
    first = (c % 4) * 320
    w_load.wait()
    for k in range(2):
        some = jnp.zeros((320, 512), F32)
        for j in range(3):
            pick = (row - first - k * 160 == column - j * 160) & (column // 160 == j)
            pick = jnp.where(pick, 1.0, 0.0).astype(BF)
            some += jnp.dot(w_mine[:, j * 1280 : (j + 1) * 1280], pick, preferred_element_type=F32)
        w_own[k] = some.astype(BF)
    mine_rows = span(f * 320, 320, 320)
    for k in (2, 3, 1):
        to = (f + k) % 4
        w_copies.append(
            send(
                w_own.at[to % 2],
                w_small.at[mine_rows],
                w_send_sem.at[k],
                w_recv_sem.at[f],
                dev(c, to),
            )
        )
    w_small[mine_rows, :] = w_own[at.core]
    x_load.start()
    dy_load.start()


    shards = (out_w_ref, up_w_ref, down_w_ref)
    xbit = c % 2
    other = (f + 2) % 4

    def part(m, owner, x):
        return weights.at[m, span(owner * 320 + x * 160, 160, 160)]

    def weight_copy(m, way):
        if way == 0:
            src, dst, to = shards[m], weights.at[m, mine_rows], dev(c, at.twin)
        elif way == 1 and not SPLIT[m]:
            src, dst, to = shards[m], weights.at[m, mine_rows], dev(c, other)
        elif way == 3 and not SPLIT[m]:
            src = dst = weights.at[m, span(other * 320, 320, 320)]
            to = dev(c, at.twin)
        elif way == 1:
            src = shards[m].at[span(xbit * 160, 160, 160)]
            dst, to = part(m, f, xbit), dev(c, other)
        else:
            x = (xbit, xbit, 1 - xbit)[way - 2]
            src = dst = part(m, other, x)
            to = (dev(flip(c, 1), f), dev(c, at.twin), dev(c, at.twin))[way - 2]
        return pltpu.make_async_remote_copy(
            src_ref=src,
            dst_ref=dst,
            send_sem=m_send_sem.at[m, way],
            recv_sem=m_recv_sem.at[m, way],
            device_id=to,
            device_id_type=MESH,
        )

    def shard_copy(m):
        return pltpu.make_async_copy(shards[m], weights.at[m, mine_rows], shard_sem.at[m])

    def weight_first(m):
        weight_copy(m, 0).start()
        weight_copy(m, 1).start()
        shard_copy(m).start()

    def weight_second(m):
        weight_copy(m, 1).wait_recv()
        if SPLIT[m]:
            weight_copy(m, 2).start()
        weight_copy(m, 3).start()

    def weight_third(m):
        if SPLIT[m]:
            weight_copy(m, 2).wait_recv()
            weight_copy(m, 4).start()

    def weight_last(m):
        shard_copy(m).wait()
        for way in (0, 3, 4) if SPLIT[m] else (0, 3):
            weight_copy(m, way).wait_recv()


    aux_own.wait()
    for k in (1, 2, 3):
        await_recv(aux_all.at[0], aux_recv_sem.at[(f + k) % 4])
    aux = jnp.zeros((16, 1280), F32)
    scale = jnp.zeros((16, LANES), F32)
    row = lax.broadcasted_iota(jnp.int32, (384, 1280), 0)
    column = lax.broadcasted_iota(jnp.int32, (384, 1280), 1)
    for k in range(4):
        put = jnp.where((column == row + k * 320) & (row < 320), 1.0, 0.0).astype(BF)
        aux = aux + jnp.dot(aux_all[k], put, preferred_element_type=F32)
        put = (column[:LANES, :LANES] == row[:LANES, :LANES] + k * 20) & (row[:LANES, :LANES] < 20)
        put = jnp.where(put, 1.0, 0.0).astype(BF)
        scale = scale + jnp.dot(aux_all[k, :, :LANES], put, preferred_element_type=F32)
    auxsum_ref[...] = aux
    auxsum_ref[2:3, :LANES] = scale[2:3]
    gain = aux[0:1, :]
    mlp_gain = aux[1:2, :]
    scale = scale[2:3]
    real = lax.broadcasted_iota(jnp.int32, (1, LANES), 1) < 80
    mult = jnp.where(
        real, LOG2E / math.sqrt(80) * (jnp.maximum(scale, 0.0) + jnp.log1p(jnp.exp(-jnp.abs(scale)))), 0.0
    )
    mult_ref[...] = jnp.transpose(jnp.broadcast_to(mult, (LANES, LANES)))
    one = jnp.ones_like(mult)
    mults = jnp.concatenate([mult, mult, one, one, one, one], axis=1)

    await_recv(pos_all.at[0], pos_sem.at[1])
    place_ref[...] = pos_all[at.half]
    for k in range(8):
        block = place_ref[0:1, k * 256 : (k + 1) * 256]
        key_pos[k * 256 : (k + 1) * 256, :] = jnp.transpose(
            jnp.broadcast_to(block, (LANES, 256))
        )

    def arrive(step, carry):
        k = step + jnp.where(step == 3, 1, 0) - jnp.where(step == 4, 1, 0)
        slot = flip(c, k)
        for part in range(2):
            piece = x_all.at[slot, halves[part]]
            if part == 0:

                @pl.when(jnp.logical_and(hub, k == 0))
                def _():
                    x_own.wait()

            @pl.when(jnp.logical_not(jnp.logical_and(hub, k == 0)))
            def _(part=part, piece=piece):
                await_recv(piece, x_recv_sem.at[slot, part])

            def onward(way, where, part=part, piece=piece):
                send(
                    piece, piece, x_send_sem.at[k, way, part], x_recv_sem.at[slot, part], where
                )

            for way, where in enumerate((dev(flip(c, 1), f), dev(flip(c, 2), f), dev(c, at.twin))):
                due = False
                for when in HUB_WAYS:
                    if (way, part) in HUB_WAYS[when]:
                        due = jnp.logical_or(due, k == when)

                @pl.when(jnp.logical_and(hub, due))
                def _(way=way, where=where, onward=onward):
                    onward(way, where)

        @pl.when(step == 2)
        def _():
            weight_first(0)

        @pl.when(step == 4)
        def _():
            weight_first(1)


        xf = x_all[slot].astype(F32)
        inv = lax.rsqrt(jnp.mean(xf * xf, axis=1, keepdims=True) + EPS)
        rows = span(slot * 256, 256, 256)
        normed_ref[rows, :] = (xf * inv * gain).astype(BF)
        pltpu.make_async_copy(
            normed_ref.at[rows], normed_out.at[rows], save_sem.at[slot, 0]
        ).start()
        return carry

    def project(step, carry):
        slot = flip(c, step)
        rows = span(slot * 256, 256, 256)
        proj = jnp.dot(normed_ref[rows, :], w_all[...], preferred_element_type=F32)
        qkv_ref[rows, :] = (proj * mults).astype(BF)
        pltpu.make_async_copy(qkv_ref.at[rows], qkv_out.at[rows], save_sem.at[slot, 1]).start()
        return carry

    lax.fori_loop(0, 7, arrive, 0)
    for k in (1, 2, 3):
        await_recv(w_small.at[pl.ds(0, 320)], w_recv_sem.at[(f + k) % 4])
    weight_first(2)
    row = lax.broadcasted_iota(jnp.int32, (512, 768), 0)
    column = lax.broadcasted_iota(jnp.int32, (512, 768), 1)
    spread = (row == column // LANES * 80 + column % LANES) & (column % LANES < 80)
    spread = jnp.where(spread, 1.0, 0.0).astype(BF)
    w_all[...] = jnp.dot(w_small[...], spread, preferred_element_type=F32).astype(BF)
    w_save = pltpu.make_async_copy(w_all, w_out, local_sem.at[5])
    w_save.start()
    lax.fori_loop(0, 5, project, 0)
    lax.fori_loop(7, 8, arrive, 0)
    lax.fori_loop(5, 8, project, 0)

    for h in range(2):
        v_turned[h] = jnp.transpose(qkv_ref[:, (4 + h) * LANES : (5 + h) * LANES])

    att_own = pltpu.make_async_copy(
        att_send.at[c], att_ref.at[span(at.group * 160, 160, 160)], local_sem.at[3]
    )

    def att_copy(block):
        return pltpu.make_async_remote_copy(
            src_ref=att_send.at[block],
            dst_ref=att_ref.at[span(at.group * 160, 160, 160)],
            send_sem=att_send_sem.at[block],
            recv_sem=att_recv_sem.at[at.group],
            device_id=dev(block, at.pack),
            device_id_type=MESH,
        )

    mine = at.core == at.half

    def attend(step, carry):
        block = flip(c, 7 - step)
        lanes = span(block * 256, 256, 256)
        high = place_ref[0:1, lanes]
        least = place_ref[1:2, lanes]
        for h in range(2):
            query = qkv_ref[lanes, h * LANES : (h + 1) * LANES]
            scores, top = [], None
            for part in range(2):
                rows = slice(part * 1024, (part + 1) * 1024)
                kp = key_pos[rows, :]
                kp = jnp.concatenate([kp, kp], axis=1)
                keys = qkv_ref[rows, (2 + h) * LANES : (3 + h) * LANES]
                s = lax.dot_general(
                    keys, query, (((1,), (1,)), ((), ())), preferred_element_type=F32
                )
                s = jnp.where((kp >= least) & (kp <= high), s, FLOOR)
                scores.append(s)
                most = jnp.max(s, axis=0, keepdims=True)
                top = most if top is None else jnp.maximum(top, most)
            total = jnp.zeros((1, 256), F32)
            o = jnp.zeros((LANES, 256), F32)
            for part in range(2):
                p = jnp.exp(scores[part] - top)
                total += jnp.sum(p, axis=0, keepdims=True)
                values = v_turned[h, :, part * 1024 : (part + 1) * 1024]
                o += jnp.dot(values, p.astype(BF), preferred_element_type=F32)
            o = o[:80] / total
            lse_ref[h : h + 1, lanes] = top + jnp.log(total)
            out_ref[h * 80 : (h + 1) * 80, lanes] = o.astype(BF)
            att_send[block, h * 80 : (h + 1) * 80, :] = o.astype(BF)

        @pl.when(jnp.logical_and(mine, step == 7))
        def _():
            att_own.start()

        @pl.when(jnp.logical_not(jnp.logical_and(mine, step == 7)))
        def _():
            att_copy(block).start()

        for when, todo, m in WEIGHT_STEPS:

            @pl.when(step == when)
            def _(todo=todo, m=m):
                (weight_second if todo == 2 else weight_third)(m)

        return carry

    lax.fori_loop(0, 8, attend, 0)
    weight_second(2)
    early["out"].start()
    lse_ref[2:8, :] = jnp.zeros((6, 2048), F32)

    def land(block, carry):
        @pl.when(jnp.logical_not(jnp.logical_and(mine, block == at.group)))
        def _():
            await_recv(att_ref.at[pl.ds(0, 160)], att_recv_sem.at[block])

        return carry

    @pl.when(mine)
    def _():
        att_own.wait()

    weight_last(0)
    lax.fori_loop(0, 8, land, 0)
    early["att"].start()

    def across(left, right):
        return lax.dot_general(
            left, right, (((1,), (1,)), ((), ())), preferred_element_type=F32
        )

    x_load.wait()
    dy_load.wait()
    xf = x_mine[...].astype(F32)
    resid = xf + jnp.dot(jnp.transpose(att_ref[...]), weights[0], preferred_element_type=F32)
    inv = lax.rsqrt(jnp.mean(resid * resid, axis=1, keepdims=True) + EPS)
    normed_mlp = (resid * inv * mlp_gain).astype(BF)
    normed_mlp_ref[...] = jnp.transpose(normed_mlp)
    early["normed_mlp"].start()
    weight_last(1)
    up = jnp.dot(normed_mlp, weights[1], preferred_element_type=F32)
    sigma = 1.0 / (1.0 + jnp.exp(-up))
    act = (up * sigma).astype(BF)
    act_ref[...] = jnp.transpose(act)
    early["act"].start()
    slope = sigma * (1.0 + up * (1.0 - sigma))
    weight_last(2)
    dy = dy_mine[...]
    up_grad = (across(dy, weights[2]) * slope).astype(BF)
    up_grad_ref[...] = up_grad
    early["up_grad"].start()
    scaled = across(up_grad, weights[1]) * mlp_gain
    resid_grad = dy.astype(F32) + inv * (
        scaled - resid * inv * inv * jnp.mean(scaled * resid, axis=1, keepdims=True)
    )
    resid_grad_ref[...] = resid_grad
    early["resid_grad"].start()
    branch = resid_grad.astype(BF)
    branch_ref[...] = branch
    early["branch"].start()
    grad_ref[...] = across(weights[0], branch).astype(BF)
    result_ref[...] = resid + jnp.dot(act, weights[2], preferred_element_type=F32)

    w_save.wait()
    for copy in early.values():
        copy.wait()
    for k in range(8):
        rows = pl.ds(k * 256, 256)
        pltpu.make_async_copy(normed_ref.at[rows], normed_out.at[rows], save_sem.at[k, 0]).wait()
        pltpu.make_async_copy(qkv_ref.at[rows], qkv_out.at[rows], save_sem.at[k, 1]).wait()
    for copy in w_copies + aux_copies:
        copy.wait_send()
    pos_copy.wait_send()
    for m in range(3):
        for way in range(5) if SPLIT[m] else (0, 1, 3):
            weight_copy(m, way).wait_send()

    @pl.when(hub)
    def _():
        for k in range(8):
            for way, part in HUB_WAYS.get(k, ((0, 0), (0, 1), (1, 0), (1, 1), (2, 0), (2, 1))):
                await_recv(x_mine.at[halves[part]], x_send_sem.at[k, way, part])

    @pl.when(jnp.logical_not(hub))
    def _():
        x_far(0).wait_send()
        x_far(1).wait_send()

    def finish(block, carry):
        @pl.when(jnp.logical_not(jnp.logical_and(mine, block == c)))
        def _():
            att_copy(block).wait_send()

        return carry

    lax.fori_loop(0, 8, finish, 0)


def forward(*args):
    shape = jax.ShapeDtypeStruct
    dma = pltpu.SemaphoreType.DMA
    return pl.pallas_call(
        attend_kernel,
        name="forward",
        out_shape=(
            shape((1280, 256), BF),
            shape((2048, 1280), BF),
            shape((2048, 768), BF),
            shape((8, 2048), F32),
            shape((160, 2048), BF),
            shape((16, 1280), F32),
            shape((8, 2048), F32),
            shape((1280, 768), BF),
            shape((256, 1280), F32),
            shape((256, 1280), F32),
            shape((256, 1280), BF),
            shape((256, 1280), BF),
            shape((1280, 256), BF),
            shape((1280, 256), BF),
            shape((1280, 256), BF),
            shape((LANES, LANES), F32),
        ),
        in_specs=[pl.BlockSpec(memory_space=pltpu.SMEM)] + [ANY_SPEC] * 2 + [VMEM_SPEC] * 2 + [ANY_SPEC] * 4,
        out_specs=(ANY_SPEC,) * 3
        + (VMEM_SPEC, ANY_SPEC, VMEM_SPEC, VMEM_SPEC, ANY_SPEC, VMEM_SPEC)
        + (ANY_SPEC,) * 5
        + (VMEM_SPEC,) * 2,
        scratch_shapes=[
            pltpu.VMEM((256, 1280), BF),
            pltpu.VMEM((320, 3840), BF),
            pltpu.VMEM((256, 1280), BF),
            pltpu.VMEM((8, 256, 1280), BF),
            pltpu.VMEM((2048, 1280), BF),
            pltpu.VMEM((2048, 768), BF),
            pltpu.VMEM((1280, 768), BF),
            pltpu.VMEM((2, 320, 512), BF),
            pltpu.VMEM((1280, 512), BF),
            pltpu.VMEM((3, 1280, 1280), BF),
            pltpu.VMEM((4, 16, 384), BF),
            pltpu.VMEM((2, 8, 2048), F32),
            pltpu.VMEM((2, 128, 2048), BF),
            pltpu.VMEM((2048, LANES), F32),
            pltpu.VMEM((8, 160, 256), BF),
            dma((8, 3, 2)),
            dma((8, 2)),
            dma((4,)),
            dma((4,)),
            dma((4,)),
            dma((4,)),
            dma((2,)),
            dma((8,)),
            dma((8,)),
            dma((3, 5)),
            dma((3, 5)),
            dma((6,)),
            dma((8, 2)),
            dma((3,)),
            pltpu.VMEM((1280, 256), BF),
            pltpu.VMEM((160, 2048), BF),
            pltpu.VMEM((256, 1280), F32),
            pltpu.VMEM((256, 1280), BF),
            pltpu.VMEM((256, 1280), BF),
            pltpu.VMEM((1280, 256), BF),
            pltpu.VMEM((1280, 256), BF),
            dma((7,)),
        ],
        compiler_params=pltpu.CompilerParams(
            collective_id=0, has_side_effects=True, vmem_limit_bytes=VMEM_LIMIT
        ),
        cost_estimate=pl.CostEstimate(
            flops=20_000_000_000, bytes_accessed=40_000_000, transcendentals=8_400_000
        ),
    )(*args)


def add_into(target, source, rows, step):
    def one(k, carry):
        part = span(k * step, step, step)
        target[part, :] = (target[part, :].astype(F32) + source[part, :].astype(F32)).astype(BF)
        return carry

    lax.fori_loop(0, rows // step, one, 0)


SUM_WAYS = ("yxzh", "zyxh", "zxyh")
SPREAD_WAYS = ("zhx", "hxz", "hxz")
HEAD_WAYS = "hzx"

PLAN = (
    "prep", "mt0", "m00", "mt2", "m02", "mt1", "take", "L00", "L01", "L02", "L03", "L04",
    "m01", "L05", "L06", "L07", "E0", "qs0", "L10", "L11", "L12", "L13", "L14", "L15", "L16",
    "qa0", "m10", "L17", "m12", "E1", "v0", "qs1", "nt0", "nt1", "nt2", "q00", "v1", "nt3",
    "v2", "v3", "na0", "v4", "na1", "na2", "qa1", "na3", "v5", "m11", "q10", "m20", "q01",
    "m22", "m21", "m32", "m30", "q11", "q20", "g02", "g00", "m31", "g12", "nb0", "g10", "g01",
    "nb1", "q21", "g22", "g11", "g20", "nc_f", "nc_n", "g21", "qc0", "qw0", "mw2", "qc1",
    "mw0", "nfin", "qw1", "mw1", "turn",
)

KEY_PARTS = 2
KEY_ROWS = 2048 // KEY_PARTS


def backward_kernel(
    grad_ref,
    att_hbm,
    branch_hbm,
    normed_mlp_hbm,
    up_grad_hbm,
    act_hbm,
    dy_hbm,
    qkv_hbm,
    lse_ref,
    out_hbm,
    place_ref,
    normed_hbm,
    w_hbm,
    mult_ref,
    x_hbm,
    resid_grad_hbm,
    gain_ref,
    first_out,
    second_out,
    third_out,
    slice_out,
    input_grad_out,
    scale_ref,
    first_ref,
    second_ref,
    third_ref,
    slice_ref,
    input_ref,
    att_ref,
    branch_ref,
    normed_mlp_ref,
    up_grad_ref,
    act_ref,
    dy_ref,
    qkv_ref,
    out_ref,
    w_ref,
    x_ref,
    resid_grad_ref,
    grad_all,
    key_pos,
    k_turned,
    delta,
    key_sum,
    value_sum,
    turned,
    normed_part,
    n_core,
    n_x,
    n_z,
    n_last,
    sums,
    core_in,
    taken,
    slices,
    s1,
    s2,
    gathered,
    scale_in,
    g_send_sem,
    g_recv_sem,
    local_sem,
    m_send,
    m_recv,
    q_send,
    q_recv,
    nc_send,
    nc_recv,
    n_send,
    n_recv,
    v_send,
    v_recv,
    load_sem,
    save_sem,
):
    loads = {
        name: pltpu.make_async_copy(src, dst, load_sem.at[k])
        for k, (name, src, dst) in enumerate(
            (
                ("act", act_hbm, act_ref),
                ("dy", dy_hbm, dy_ref),
                ("normed", normed_mlp_hbm, normed_mlp_ref),
                ("up", up_grad_hbm, up_grad_ref),
                ("att", att_hbm, att_ref),
                ("branch", branch_hbm, branch_ref),
                ("qkv", qkv_hbm, qkv_ref),
                ("out", out_hbm, out_ref),
                ("w", w_hbm, w_ref),
                ("x", x_hbm, x_ref),
                ("resid", resid_grad_hbm, resid_grad_ref),
            )
        )
    }
    for load in loads.values():
        load.start()
    at = Place()
    meet_plane(at)
    c, f, core, half = at.c, at.f, at.core, at.half
    mine = core == half
    row = f // 2
    xbit, zbit = c % 2, (c // 2) % 2
    twin, across = dev(c, at.twin), dev(c, at.across)
    xpeer, zpeer, hpeer = dev(flip(c, 1), f), dev(flip(c, 2), f), dev(flip(c, 4), f)

    def remote(src, dst, send_sem, recv_sem, where):
        return pltpu.make_async_remote_copy(
            src_ref=src,
            dst_ref=dst,
            send_sem=send_sem,
            recv_sem=recv_sem,
            device_id=where,
            device_id_type=MESH,
        )

    def grad_copy(group, h):
        return remote(
            grad_ref.at[span(group * 160 + h * 80, 80, 80)],
            grad_all.at[h, pl.ds(0, 80), span(c * 256, 256, 256)],
            g_send_sem.at[group, h],
            g_recv_sem.at[c, h],
            dev(core * 4 + group // 2, at.plane + group % 2),
        )

    def grad_own(h):
        return pltpu.make_async_copy(
            grad_ref.at[span(at.group * 160 + h * 80, 80, 80)],
            grad_all.at[h, pl.ds(0, 80), span(c * 256, 256, 256)],
            local_sem.at[h],
        )

    def give(k, carry):
        group = flip(at.group, k)

        @pl.when(jnp.logical_and(mine, k == 0))
        def _():
            grad_own(0).start()
            grad_own(1).start()

        @pl.when(jnp.logical_not(jnp.logical_and(mine, k == 0)))
        def _():
            grad_copy(group, 0).start()
            grad_copy(group, 1).start()

        return carry

    lax.fori_loop(0, 8, give, 0)

    bits = {"y": row, "x": xbit, "z": zbit, "h": half}
    peers = {"y": across, "x": xpeer, "z": zpeer, "h": hpeer}
    results = (first_ref, second_ref, third_ref)

    def finer(m):
        return "z" if SUM_WAYS[m].index("x") < SUM_WAYS[m].index("z") else "x"

    def cut(ref, way, bit):
        if way == "y":
            return (bit,)
        lead = (slice(None),) * (len(ref.shape) - 2)
        if way == "h":
            return lead + (slice(None), span(bit * 640, 640, 640))
        rows = ref.shape[-2] // 2
        return lead + (span(bit * rows, rows, rows),)

    def main_copy(stage, m):
        if stage < 0:
            y = stage + 2
            src, dst, to = sums.at[pl.ds((m * 2 + y) * 320, 320)], core_in.at[m, y], twin
        elif stage < 4:
            way = SUM_WAYS[m][stage]
            ref = core_in.at[m] if stage == 0 else taken[m][stage - 1]
            src, dst, to = ref.at[cut(ref, way, 1 - bits[way])], taken[m][stage], peers[way]
        else:
            way = SPREAD_WAYS[m][stage - 4]
            known = SPREAD_WAYS[m][: stage - 4]
            low = finer(m)
            high = "x" if low == "z" else "z"
            if high in known:
                rows = pl.ds(0, 320)
            elif low in known:
                rows = span(bits[high] * 160, 160, 160)
            else:
                rows = span(bits[high] * 160 + bits[low] * 80, 80, 80)
            lanes = pl.ds(0, 1280) if "h" in known else span(half * 640, 640, 640)
            src = dst = results[m].at[rows, lanes]
            to = peers[way]
        return remote(src, dst, m_send.at[stage + 2, m], m_recv.at[stage + 2, m], to)

    def added(ref, other, spot):
        for k in range(2) if len(ref.shape) == 3 else (None,):
            here = () if k is None else (k,)
            there = spot if k is None else (k,) + spot[1:]
            ref[here] = (ref[here].astype(F32) + other[there].astype(F32)).astype(BF)

    def main(stage, m):
        if stage == 0:
            for y in range(2):
                main_copy(y - 2, m).wait_recv()
                total = core_in[m, y].astype(F32) + weight_rows(m, 2 * y + core)
                core_in[m, y] = total.astype(BF)
        elif stage < 5:
            main_copy(stage - 1, m).wait_recv()
            way = SUM_WAYS[m][stage - 1]
            ref = core_in.at[m] if stage == 1 else taken[m][stage - 2]
            spot = cut(ref, way, bits[way])
            if stage < 4:
                added(taken[m][stage - 1], ref, spot)
            else:
                low = finer(m)
                high = "x" if low == "z" else "z"
                rows = span(bits[high] * 160 + bits[low] * 80, 80, 80)
                results[m][rows, span(half * 640, 640, 640)] = (
                    taken[m][3][...].astype(F32) + ref[spot].astype(F32)
                ).astype(BF)
        else:
            main_copy(stage - 1, m).wait_recv()
        if stage < 7:
            main_copy(stage, m).start()
        else:
            save(m).start()

    lefts = (act_ref, normed_mlp_ref, att_ref)
    rights = (dy_ref, up_grad_ref, branch_ref)

    def weight_rows(m, quarter):
        rows = span(quarter * 320, 320, 320)
        return jnp.dot(lefts[m][rows, :], rights[m][...], preferred_element_type=F32)

    def main_first(m):
        for name in (("act", "dy"), ("normed", "up"), ("att", "branch"))[m]:
            loads[name].wait()
        for y in range(2):
            part = weight_rows(m, 2 * y + 1 - core)
            sums[(m * 2 + y) * 320 : (m * 2 + y + 1) * 320, :] = part.astype(BF)
            main_copy(y - 2, m).start()

    def prepare():
        loads["qkv"].wait()
        for h in range(2):
            grad_all[h, 80:, :] = jnp.zeros((48, 2048), BF)
            k_turned[h] = jnp.transpose(qkv_ref[:, (2 + h) * LANES : (3 + h) * LANES])
        for k in range(8):
            block = place_ref[0:1, k * 256 : (k + 1) * 256]
            key_pos[k * 256 : (k + 1) * 256, :] = jnp.transpose(
                jnp.broadcast_to(block, (LANES, 256))
            )
        scale_ref[...] = jnp.zeros((8, LANES), F32)

    def take(k, carry):
        block = flip(c, k)

        @pl.when(jnp.logical_and(mine, k == 0))
        def _():
            grad_own(0).wait()
            grad_own(1).wait()

        @pl.when(jnp.logical_not(jnp.logical_and(mine, k == 0)))
        def _():
            for h in range(2):
                await_recv(
                    grad_all.at[h, pl.ds(0, 80), pl.ds(0, 256)], g_recv_sem.at[block, h]
                )

        return carry

    def take_all():
        loads["out"].wait()
        lax.fori_loop(0, 8, take, 0)
        for h in range(2):
            delta[h : h + 1, :] = jnp.sum(
                grad_all[h, :80, :].astype(F32) * out_ref[h * 80 : (h + 1) * 80, :].astype(F32),
                axis=0,
                keepdims=True,
            )

    def head_copy(stage, h):
        if stage == 0:
            rows = pl.ds(0, 240)
            src, to = slices.at[h, rows, span((1 - row) * 640, 640, 640)], across
            dst = s1.at[h, rows]
        elif stage == 1:
            src, dst, to = s1.at[h, span(128 - half * 128, 128, 128)], s2.at[h], hpeer
        elif stage < 5:
            way = HEAD_WAYS[stage - 2]
            known = HEAD_WAYS[: stage - 2]
            where = (core,) + tuple(slice(None) if d in known else bits[d] for d in "xz") + (h,)
            rows = pl.ds(0, 240) if "h" in known else span(half * 128, 128, 128)
            src = dst = gathered.at[where + (rows,)]
            to = peers[way]
        else:
            src = dst = gathered.at[core, :, :, h, pl.ds(0, 240)]
            to = twin
        return remote(src, dst, q_send.at[stage, h], q_recv.at[stage, h], to)

    def head(stage, h):
        if stage > 0:
            head_copy(stage - 1, h).wait_recv()
        if stage == 1:
            add_into(s1.at[h], slices.at[h, :, span(row * 640, 640, 640)], 256, 128)
        if stage == 2:
            own = span(half * 128, 128, 128)
            gathered[core, xbit, zbit, h, own, :] = (
                s2[h].astype(F32) + s1[h, own, :].astype(F32)
            ).astype(BF)
        if stage < 6:
            head_copy(stage, h).start()
        else:
            head_flat(h)

    def normed_load(part):
        return pltpu.make_async_copy(
            normed_hbm.at[:, pl.ds(part * 256, 256)], normed_part.at[part % 2], local_sem.at[2 + part % 2]
        )

    def attend_head(h, hooks):
        key_sum[...] = jnp.zeros((2048, LANES), F32)
        value_sum[...] = jnp.zeros((2048, LANES), F32)

        def block_grad(block, carry):
            lanes = span(block * 256, 256, 256)
            high = place_ref[0:1, lanes]
            least = place_ref[1:2, lanes]
            query = qkv_ref[lanes, h * LANES : (h + 1) * LANES]
            grad_t = grad_all[h, :, lanes]
            q_grad = jnp.zeros((LANES, 256), F32)
            for part in range(KEY_PARTS):
                some = slice(part * KEY_ROWS, (part + 1) * KEY_ROWS)
                kp = key_pos[some, :]
                kp = jnp.concatenate([kp, kp], axis=1)
                keys = qkv_ref[some, (2 + h) * LANES : (3 + h) * LANES]
                values = qkv_ref[some, (4 + h) * LANES : (5 + h) * LANES]
                s = lax.dot_general(
                    keys, query, (((1,), (1,)), ((), ())), preferred_element_type=F32
                )
                visible = (kp >= least) & (kp <= high)
                p = jnp.exp(jnp.where(visible, s - lse_ref[h : h + 1, lanes], FLOOR))
                gp = jnp.dot(values, grad_t, preferred_element_type=F32)
                gs = (p * (gp - delta[h : h + 1, lanes])).astype(BF)
                value_sum[some, :] += lax.dot_general(
                    p.astype(BF), grad_t, (((1,), (1,)), ((), ())), preferred_element_type=F32
                )
                key_sum[some, :] += jnp.dot(gs, query, preferred_element_type=F32)
                q_grad += jnp.dot(k_turned[h, :, some], gs, preferred_element_type=F32)
            scale_ref[0:1, :] += jnp.sum(
                jnp.transpose(q_grad) * query.astype(F32), axis=0, keepdims=True
            )
            turned[h * LANES : (h + 1) * LANES, lanes] = (q_grad * mult_ref[:, 0:1]).astype(BF)
            for step, todo in hooks.items():

                @pl.when(block == step)
                def _(todo=todo):
                    for one in todo:
                        one()

            return carry

        lax.fori_loop(0, 8, block_grad, 0)

    def attend_end(h):
        for j, total in ((1, key_sum), (2, value_sum)):
            low = jnp.transpose(total[...]).astype(BF)
            turned[(2 * j + h) * LANES : (2 * j + h + 1) * LANES, :] = low

    def head_first(h):
        slices[h, 240:, :] = jnp.zeros((16, 1280), BF)
        s1[h, 240:, :] = jnp.zeros((16, 640), BF)
        for part in range(5):
            normed_load(part).wait()
            if part + 1 < 5:
                normed_load(part + 1).start()
            for j in range(3):
                first = (2 * j + h) * LANES
                slices[h, j * 80 : (j + 1) * 80, part * 256 : (part + 1) * 256] = jnp.dot(
                    turned[first : first + 80, :],
                    normed_part[part % 2],
                    preferred_element_type=F32,
                ).astype(BF)
        if h == 0:
            normed_load(0).start()
        head(0, h)

    def norm_bits(k):
        return (1 - xbit, 1 - xbit, xbit, xbit)[k], (1 - zbit, zbit, 1 - zbit, zbit)[k]

    def norm_spot(k, hh):
        slot = 2 * k + hh
        return sums.at[pl.ds(slot // 5 * 640, 640), pl.ds(slot % 5 * 256, 256)]

    def norm_copy(stage, k, hh=0):
        if stage == 0:
            return remote(
                norm_spot(k, hh), n_core.at[k, hh], nc_send.at[k, hh], nc_recv.at[k, hh], twin
            )
        took = k
        if stage == 1:
            ends = n_core.at[k], n_x.at[k], xpeer
        elif stage == 2:
            ends = n_core.at[2, (1 - half, half)[k]], n_z.at[k], zpeer
        else:
            to = dev(flip(c, 4), at.pack) if k == 0 else dev(c, at.twin)
            took = (core, 2)[k]
            ends = n_core.at[3, (1 - half, half)[k]], n_last.at[core], to
        return remote(ends[0], ends[1], n_send.at[stage, k], n_recv.at[stage, took], ends[2])

    def norm_part(k, hh, which):
        xs, zs = norm_bits(k)
        lanes = span((hh * 4 + zs * 2 + xs) * 256, 256, 256)
        rows = span(which * 640, 640, 640)
        return jnp.dot(w_ref[rows, :], turned[:, lanes], preferred_element_type=F32)

    def norm_first(k):
        if k == 0:
            loads["w"].wait()
            for m in range(3):
                for stage in range(2):
                    main_copy(stage - 2, m).wait_send()
        for hh in range(2):
            norm_spot(k, hh)[...] = norm_part(k, hh, 1 - core).astype(BF)
            norm_copy(0, k, hh).start()

    def norm_core(k):
        for hh in range(2):
            norm_copy(0, k, hh).wait_recv()
            n_core[k, hh] = (n_core[k, hh].astype(F32) + norm_part(k, hh, core)).astype(BF)
        if k < 2:
            norm_copy(1, k).start()

    def scale_copy(stage):
        where = (twin, across, xpeer, zpeer, hpeer)[stage]
        return remote(scale_ref, scale_in.at[stage], v_send.at[stage], v_recv.at[stage], where)

    def tiny(stage):
        if stage > 0:
            scale_copy(stage - 1).wait()
            scale_ref[...] += scale_in[stage - 1]
        if stage < 5:
            scale_copy(stage).start()
        else:
            given = gain_ref[2:3, :LANES]
            soft = jnp.maximum(given, 0.0) + jnp.log1p(jnp.exp(-jnp.abs(given)))
            scale_ref[0:1, :] = scale_ref[0:1, :] / (soft * (1.0 + jnp.exp(-given)))

    def norm_x(k):
        norm_copy(1, k).wait_recv()
        for hh in range(2):
            add_into(n_core.at[2 + k, hh], n_x.at[k, hh], 640, 80)
        if k == 0:
            norm_copy(2, 0).start()
            norm_copy(2, 1).start()

    def norm_far():
        norm_copy(2, 0).wait_recv()
        add_into(n_core.at[3, 1 - half], n_z.at[0], 640, 80)
        norm_copy(3, 0).start()

    def norm_near():
        norm_copy(2, 1).wait_recv()
        add_into(n_core.at[3, half], n_z.at[1], 640, 80)

        @pl.when(jnp.logical_not(mine))
        def _():
            norm_copy(3, 1).start()

    def norm_last():
        loads["x"].wait()
        loads["resid"].wait()
        @pl.when(mine)
        def _():
            n_last[core] = n_core[3, half]
            await_recv(n_last.at[0], n_recv.at[3, 2])

        @pl.when(jnp.logical_not(mine))
        def _():
            await_recv(n_last.at[0], n_recv.at[3, 0])
            await_recv(n_last.at[1], n_recv.at[3, 1])

        xf = x_ref[...].astype(F32)
        inv = lax.rsqrt(jnp.mean(xf * xf, axis=1, keepdims=True) + EPS)
        scaled = jnp.concatenate(
            [jnp.transpose(n_last[k].astype(F32)) for k in range(2)], axis=1
        ) * gain_ref[0:1, :]
        input_ref[...] = resid_grad_ref[...] + inv * (
            scaled - xf * inv * inv * jnp.mean(scaled * xf, axis=1, keepdims=True)
        )
        save(3).start()

    def head_flat(h):
        if h == 0:
            for k in range(4):
                for hh in range(2):
                    norm_copy(0, k, hh).wait_send()
        for core_k in range(2):
            for m4 in range(4):
                for j in range(3):
                    start = j * 1280 + (4 * m4 + 2 * core_k + h) * 80
                    first = start // 1920 * 640
                    sums[start % 1920 : start % 1920 + 80, first : first + 640] = gathered[
                        core_k, m4 % 2, m4 // 2, h, j * 80 : (j + 1) * 80, :
                    ]

    def save(k):
        src, dst = (
            (first_ref, first_out),
            (second_ref, second_out),
            (third_ref, third_out),
            (input_ref, input_grad_out),
            (slice_ref.at[:, pl.ds(0, 1920)], slice_out.at[:, pl.ds(0, 1920)]),
            (slice_ref.at[:, pl.ds(1920, 1920)], slice_out.at[:, pl.ds(1920, 1920)]),
        )[k]
        return pltpu.make_async_copy(src, dst, save_sem.at[k])

    def turn_all():
        for part in range(2):

            def turn(k, carry, part=part):
                rows = span(k * 384, 384, 384)
                lanes = span(part * 1920 + k * 384, 384, 384)

                @pl.when(core == 0)
                def _():
                    strip = jnp.transpose(sums[rows, part * 640 : part * 640 + 384])
                    slice_ref[:, lanes] = strip[:320]

                @pl.when(core == 1)
                def _():
                    strip = jnp.transpose(sums[rows, part * 640 + 256 : part * 640 + 640])
                    slice_ref[:, lanes] = strip[64:]

                return carry

            lax.fori_loop(0, 5, turn, 0)
            save(4 + part).start()

    tasks = {"prep": prepare, "take": take_all, "nb0": lambda: norm_x(0), "nb1": lambda: norm_x(1)}
    tasks |= {"nc_f": norm_far, "nc_n": norm_near, "nfin": norm_last, "turn": turn_all}
    for m in range(3):
        tasks[f"mt{m}"] = functools.partial(main_first, m)
        for stage in range(4):
            tasks[f"m{stage}{m}"] = functools.partial(main, stage, m)
        for stage in range(3):
            tasks[f"g{stage}{m}"] = functools.partial(main, 4 + stage, m)
        tasks[f"mw{m}"] = functools.partial(main, 7, m)
    for h in range(2):
        tasks[f"E{h}"] = functools.partial(attend_end, h)
        tasks[f"qs{h}"] = functools.partial(head_first, h)
        for stage, name in enumerate(("qa", "q0", "q1", "q2", "qc", "qw")):
            tasks[f"{name}{h}"] = functools.partial(head, 1 + stage, h)
    for k in range(4):
        tasks[f"nt{k}"] = functools.partial(norm_first, k)
        tasks[f"na{k}"] = functools.partial(norm_core, k)
    for stage in range(6):
        tasks[f"v{stage}"] = functools.partial(tiny, stage)

    normed_load(0).start()
    spot = 0
    while spot < len(PLAN):
        name = PLAN[spot]
        if name[0] != "L":
            tasks[name]()
            spot += 1
            continue
        h, step, hooks = int(name[1]), -1, {}
        while step < 7 or PLAN[spot][0] == "L":
            if PLAN[spot][0] == "L":
                step = int(PLAN[spot][2])
                if step == 7:
                    spot += 1
                    break
            else:
                hooks.setdefault(step, []).append(tasks[PLAN[spot]])
            spot += 1
        attend_head(h, hooks)

    for k in range(6):
        save(k).wait()
    def sent(block, carry):
        own_in = jnp.logical_and(mine, block == at.group)

        @pl.when(jnp.logical_not(own_in))
        def _():
            for h in range(2):
                grad_copy(block, h).wait_send()

        return carry

    lax.fori_loop(0, 8, sent, 0)
    for m in range(3):
        for stage in range(7):
            main_copy(stage, m).wait_send()
    for h in range(2):
        for stage in range(6):
            head_copy(stage, h).wait_send()
    for k in range(2):
        norm_copy(1, k).wait_send()
        norm_copy(2, k).wait_send()
    norm_copy(3, 0).wait_send()

    @pl.when(jnp.logical_not(mine))
    def _():
        norm_copy(3, 1).wait_send()


def sum_slots():
    slots = []
    for ways in SUM_WAYS:
        shape, own = [2, 320, 1280], []
        for way in ways:
            if way == "y":
                shape = shape[1:]
            else:
                shape[-1 if way == "h" else -2] //= 2
            own.append(pltpu.VMEM(tuple(shape), BF))
        slots.append(own)
    return slots


def backward(*args):
    shape = jax.ShapeDtypeStruct
    dma = pltpu.SemaphoreType.DMA
    specs = [ANY_SPEC] * 17
    for k in (8, 10, 13, 16):
        specs[k] = VMEM_SPEC
    return pl.pallas_call(
        backward_kernel,
        name="backward",
        out_shape=(
            shape((320, 1280), BF),
            shape((320, 1280), BF),
            shape((320, 1280), BF),
            shape((320, 3840), BF),
            shape((256, 1280), F32),
            shape((8, LANES), F32),
        ),
        in_specs=specs,
        out_specs=(ANY_SPEC,) * 5 + (VMEM_SPEC,),
        scratch_shapes=[
            pltpu.VMEM((320, 1280), BF),
            pltpu.VMEM((320, 1280), BF),
            pltpu.VMEM((320, 1280), BF),
            pltpu.VMEM((320, 3840), BF),
            pltpu.VMEM((256, 1280), F32),
            pltpu.VMEM((1280, 256), BF),
            pltpu.VMEM((256, 1280), BF),
            pltpu.VMEM((1280, 256), BF),
            pltpu.VMEM((256, 1280), BF),
            pltpu.VMEM((1280, 256), BF),
            pltpu.VMEM((256, 1280), BF),
            pltpu.VMEM((2048, 768), BF),
            pltpu.VMEM((160, 2048), BF),
            pltpu.VMEM((1280, 768), BF),
            pltpu.VMEM((256, 1280), BF),
            pltpu.VMEM((256, 1280), F32),
            pltpu.VMEM((2, 128, 2048), BF),
            pltpu.VMEM((2048, LANES), F32),
            pltpu.VMEM((2, 128, 2048), BF),
            pltpu.VMEM((8, 2048), F32),
            pltpu.VMEM((2048, LANES), F32),
            pltpu.VMEM((2048, LANES), F32),
            pltpu.VMEM((768, 2048), BF),
            pltpu.VMEM((2, 2048, 256), BF),
            pltpu.VMEM((4, 2, 640, 256), BF),
            pltpu.VMEM((2, 2, 640, 256), BF),
            pltpu.VMEM((2, 640, 256), BF),
            pltpu.VMEM((2, 640, 256), BF),
            pltpu.VMEM((1920, 1280), BF),
            pltpu.VMEM((3, 2, 320, 1280), BF),
            sum_slots(),
            pltpu.VMEM((2, 256, 1280), BF),
            pltpu.VMEM((2, 256, 640), BF),
            pltpu.VMEM((2, 128, 640), BF),
            pltpu.VMEM((2, 2, 2, 2, 256, 640), BF),
            pltpu.VMEM((5, 8, LANES), F32),
            dma((8, 2)),
            dma((8, 2)),
            dma((4,)),
            dma((9, 3)),
            dma((9, 3)),
            dma((6, 2)),
            dma((6, 2)),
            dma((4, 2)),
            dma((4, 2)),
            dma((4, 4)),
            dma((4, 4)),
            dma((5,)),
            dma((5,)),
            dma((11,)),
            dma((6,)),
        ],
        compiler_params=pltpu.CompilerParams(
            collective_id=1, has_side_effects=True, vmem_limit_bytes=VMEM_LIMIT
        ),
        cost_estimate=pl.CostEstimate(
            flops=30_000_000_000, bytes_accessed=60_000_000, transcendentals=8_400_000
        ),
    )(*args)


def widen_kernel(*refs):
    total = []
    for k in range(4):
        value = refs[k][...].astype(F32)
        refs[6 + k][...] = value
        if k in (0, 2):
            total.append(jnp.sum(value * refs[4 + k // 2][...].astype(F32), axis=1, keepdims=True))
    lane = lax.broadcasted_iota(jnp.int32, refs[10].shape, 1)
    refs[10][...] = jnp.where(lane == 0, total[0], total[1])


def widen(*args):
    rows = 160
    shape = jax.ShapeDtypeStruct
    specs = [pl.BlockSpec((rows, a.shape[1]), lambda k: (k, 0)) for a in args]
    return pl.pallas_call(
        widen_kernel,
        name="widen",
        grid=(args[0].shape[0] // rows,),
        out_shape=tuple(shape(a.shape, F32) for a in args[:4]) + (shape((320, LANES), F32),),
        in_specs=specs,
        out_specs=tuple(specs[:4]) + (pl.BlockSpec((rows, LANES), lambda k: (k, 0)),),
        compiler_params=pltpu.CompilerParams(vmem_limit_bytes=VMEM_LIMIT),
    )(*args)


def fast_body(
    tokens,
    lengths,
    position,
    qkv_weight,
    out_weight,
    up_weight,
    down_weight,
    attn_gain,
    mlp_gain,
    query_scale,
    cotangent,
):
    f = lax.axis_index("fsdp")
    x, dy = tokens[0], cotangent[0]
    small = jnp.zeros((16, 384), BF)
    for k, own in enumerate((attn_gain, mlp_gain, query_scale)):
        small = lax.dynamic_update_slice(small, own[None], (k, 0))
    (
        att_t, normed, qkv, lse, out, auxsum, place, w_heads,
        result, resid_grad, branch_grad, up_grad, act_t, normed_mlp_t, grad_t, mult,
    ) = forward(
        lengths, x, qkv_weight, small, position, out_weight, up_weight, down_weight, dy
    )
    g_down, g_up, g_out, g_qkv, input_grad, scale_sum = backward(
        grad_t,
        att_t,
        branch_grad,
        normed_mlp_t,
        up_grad,
        act_t,
        dy,
        qkv,
        lse,
        out,
        place,
        normed,
        w_heads,
        mult,
        x,
        resid_grad,
        auxsum,
    )
    g_qkv, g_out, g_up, g_down, sums = widen(g_qkv, g_out, g_up, g_down, qkv_weight, up_weight)
    grad_attn_gain = sums[:, 0] / attn_gain.astype(F32)
    grad_mlp_gain = sums[:, 1] / mlp_gain.astype(F32)
    return (
        result[None],
        input_grad[None],
        g_qkv,
        g_out,
        g_up,
        g_down,
        grad_attn_gain,
        grad_mlp_gain,
        lax.dynamic_slice_in_dim(scale_sum[0, :80], f * 20, 20),
    )


def solution(mesh):
    placed = (
        P("fsdp", "ctx", None),
        P("fsdp", None),
        P("fsdp", None),
        P("fsdp", None),
        P("fsdp", None),
        P("fsdp", None),
        P("fsdp", None),
        P("fsdp"),
        P("fsdp"),
        P("fsdp"),
        P("fsdp", "ctx", None),
    )
    fits = mesh.shape["ctx"] == 8 and mesh.shape["fsdp"] == 4
    return jax.shard_map(
        fast_body if fits else body,
        mesh=mesh,
        in_specs=placed,
        out_specs=(
            P("fsdp", "ctx", None),
            P("fsdp", "ctx", None),
            P("fsdp", None),
            P("fsdp", None),
            P("fsdp", None),
            P("fsdp", None),
            P("fsdp"),
            P("fsdp"),
            P("fsdp"),
        ),
        check_vma=False,
    )
```

```python
import functools
import math

import jax
import jax.numpy as jnp
from jax import lax
from jax.experimental import pallas as pl
from jax.experimental.pallas import tpu as pltpu
from jax.sharding import PartitionSpec as P

HEADS = 16


EPS = 1e-06
FLOOR = -1e30
LOG2E = 1.442695041

MESH = pl.DeviceIdType.MESH
LANES = 128
BF = jnp.bfloat16
F32 = jnp.float32
VMEM_SPEC = pl.BlockSpec(memory_space=pltpu.VMEM)
ANY_SPEC = pl.BlockSpec(memory_space=pl.ANY)
VMEM_LIMIT = 60 << 20


def flip(number, mask):
    total = 0
    for bit in (1, 2, 4):
        left = (number // bit) % 2
        right = (mask // bit) % 2
        total = total + bit * (left + right - 2 * left * right)
    return total


class Place:
    def __init__(self):
        self.c = lax.axis_index("ctx")
        self.f = lax.axis_index("fsdp")
        self.core = self.f % 2
        self.plane = self.f - self.core
        self.half = self.c // 4
        self.pack = self.plane + self.half
        self.group = (self.c % 4) * 2 + self.core
        self.twin = self.plane + 1 - self.core
        self.across = (self.f + 2) % 4


def dev(ctx, fsdp):
    return {"ctx": ctx, "fsdp": fsdp}


def send(src, dst, send_sem, recv_sem, device):
    copy = pltpu.make_async_remote_copy(
        src_ref=src,
        dst_ref=dst,
        send_sem=send_sem,
        recv_sem=recv_sem,
        device_id=device,
        device_id_type=MESH,
    )
    copy.start()
    return copy


def await_recv(ref, sem):
    pltpu.make_async_copy(ref, ref, sem).wait()


def meet_plane(at):
    barrier = pltpu.get_barrier_semaphore()

    def greet(k, carry):
        pl.semaphore_signal(
            barrier,
            1,
            device_id=dev((at.c + k // 2) % 8, at.plane + (at.core + k) % 2),
            device_id_type=MESH,
        )
        return carry

    lax.fori_loop(1, 16, greet, 0)
    for k in range(2):
        pl.semaphore_signal(
            barrier, 1, device_id=dev(at.c, (at.plane + 2) % 4 + k), device_id_type=MESH
        )
    pl.semaphore_wait(barrier, 17)


def span(start, size, unit):
    return pl.ds(pl.multiple_of(start, unit), size)


def doc_index(places, seq_ends):
    return jnp.sum((places[:, None] >= seq_ends[None, :]).astype(jnp.int32), axis=1)


def spread_position(gathered_index, tok_dev, cycle_size):
    return gathered_index % tok_dev * cycle_size + gathered_index // tok_dev


def pair_scores(left_rows, right_rows):
    return jnp.einsum(
        "qhd,khd->qhk",
        left_rows.reshape(left_rows.shape[0], HEADS, -1),
        right_rows.reshape(right_rows.shape[0], HEADS, -1),
        preferred_element_type=jnp.float32,
    )


def pair_mask(query_pos, query_doc, key_pos, key_doc):
    return ((query_doc[:, None] == key_doc[None, :]) & (key_pos[None, :] <= query_pos[:, None]))[
        :, None, :
    ]


def in_blocks(advance, carried, pieces):
    total_rows = pieces[0].shape[0]
    block_rows = math.gcd(total_rows, 1024)
    block_count = total_rows // block_rows
    split = tuple((p.reshape((block_count, block_rows) + p.shape[1:]) for p in pieces))

    def inner(running, entry):
        return (advance(running, entry[1], entry[0] * block_rows), None)

    result, unused = lax.scan(inner, carried, (jnp.arange(block_count, dtype=jnp.int32), split))
    return result


def pair_terms(
    query_part,
    grad_part,
    log_part,
    delta_part,
    query_pos,
    query_doc,
    key_part,
    value_part,
    key_pos,
    key_doc,
):
    visible = pair_mask(query_pos, query_doc, key_pos, key_doc)
    prob_float = jnp.where(
        visible, jnp.exp(pair_scores(query_part, key_part) - log_part[:, :, None]), 0.0
    )
    grad_probs = pair_scores(grad_part, value_part)
    score_grad = (prob_float * (grad_probs - delta_part[:, :, None])).astype(jnp.bfloat16)
    return (prob_float.astype(jnp.bfloat16), score_grad)


def body(
    tokens,
    lengths,
    position,
    qkv_weight,
    out_weight,
    up_weight,
    down_weight,
    attn_gain,
    mlp_gain,
    query_scale,
    cotangent,
):
    cycle_size = lax.axis_size("ctx")
    my_index = lax.axis_index("ctx")
    tok_dev = tokens.shape[1]
    share_rows = tok_dev // cycle_size
    seq_ends = jnp.cumsum(lengths[0])
    place_row = position[0]
    residue = (place_row % cycle_size).reshape(cycle_size, tok_dev)
    landing = place_row // cycle_size
    matches = (
        residue[:, :, None] == jnp.arange(cycle_size, dtype=jnp.int32)[None, None, :]
    ).astype(jnp.int32)
    ranked = jnp.sum(jnp.cumsum(matches, axis=1) * matches, axis=2) - 1
    buffer_slot = residue * share_rows + ranked
    my_slots = lax.dynamic_index_in_dim(buffer_slot, my_index, 0, keepdims=False)
    local_rows = jnp.arange(tok_dev, dtype=jnp.int32)
    outgoing = jnp.zeros((tok_dev,), jnp.int32).at[my_slots].set(local_rows)
    flat_slot = (jnp.arange(cycle_size, dtype=jnp.int32)[:, None] * tok_dev + buffer_slot).reshape(
        -1
    )
    landing_table = (
        jnp.zeros((cycle_size * tok_dev,), jnp.int32)
        .at[flat_slot]
        .set(landing)
        .reshape(cycle_size, cycle_size, share_rows)
    )
    arrived_slot = lax.dynamic_index_in_dim(landing_table, my_index, 1, keepdims=False).reshape(-1)
    arrived_order = jnp.zeros((tok_dev,), jnp.int32).at[arrived_slot].set(local_rows)
    moved_x, moved_dy = (
        lax.all_to_all(tokens[0][outgoing], "ctx", split_axis=0, concat_axis=0, tiled=True),
        lax.all_to_all(cotangent[0][outgoing], "ctx", split_axis=0, concat_axis=0, tiled=True),
    )
    dealt_x = moved_x[arrived_order]
    dealt_dy = moved_dy[arrived_order]
    query_pos = local_rows * cycle_size + my_index
    query_doc = doc_index(query_pos, seq_ends)
    full_qkv, full_out, full_up, full_down, attn_gain_full, mlp_gain_full, scale_full = (
        lax.all_gather(qkv_weight, "fsdp", axis=0, tiled=True),
        lax.all_gather(out_weight, "fsdp", axis=0, tiled=True),
        lax.all_gather(up_weight, "fsdp", axis=0, tiled=True),
        lax.all_gather(down_weight, "fsdp", axis=0, tiled=True),
        lax.all_gather(attn_gain, "fsdp", axis=0, tiled=True),
        lax.all_gather(mlp_gain, "fsdp", axis=0, tiled=True),
        lax.all_gather(query_scale, "fsdp", axis=0, tiled=True),
    )
    attn_gain_f = attn_gain_full.astype(jnp.float32)
    mlp_gain_f = mlp_gain_full.astype(jnp.float32)
    scale_float = scale_full.astype(jnp.float32)
    x_float = dealt_x.astype(jnp.float32)
    inv_attn = lax.rsqrt(jnp.mean(x_float * x_float, axis=1, keepdims=True) + EPS)
    normed_attn = (x_float * inv_attn * attn_gain_f).astype(jnp.bfloat16)
    projected = jnp.dot(normed_attn, full_qkv, preferred_element_type=jnp.float32)
    att_width = projected.shape[1] // 3
    head_dim = scale_full.shape[0]
    base_scale = LOG2E / math.sqrt(head_dim)
    multiplier = jnp.tile(base_scale * jax.nn.softplus(scale_float), att_width // head_dim)
    raw_query = projected[:, :att_width]
    queries = (raw_query * multiplier).astype(jnp.bfloat16)
    key_rows = projected[:, att_width : 2 * att_width].astype(jnp.bfloat16)
    value_rows = projected[:, 2 * att_width :].astype(jnp.bfloat16)

    def key_place(first_row, amount):
        gathered_index = first_row + jnp.arange(amount, dtype=jnp.int32)
        key_pos = spread_position(gathered_index, tok_dev, cycle_size)
        return (key_pos, doc_index(key_pos, seq_ends))

    def stat_block(carried, pieces, first_row):
        running_max, running_sum = carried
        key_pos, key_doc = key_place(first_row, pieces[0].shape[0])
        visible = pair_mask(query_pos, query_doc, key_pos, key_doc)
        logits = jnp.where(visible, pair_scores(queries, pieces[0]), FLOOR)
        new_max = jnp.maximum(running_max, jnp.max(logits, axis=2))
        added = jnp.sum(jnp.where(visible, jnp.exp(logits - new_max[:, :, None]), 0.0), axis=2)
        return (new_max, running_sum * jnp.exp(running_max - new_max) + added)

    def output_block(summed, pieces, first_row):
        key_pos, key_doc = key_place(first_row, pieces[0].shape[0])
        visible = pair_mask(query_pos, query_doc, key_pos, key_doc)
        prob_low = jnp.where(
            visible, jnp.exp(pair_scores(queries, pieces[0]) - log_total[:, :, None]), 0.0
        ).astype(jnp.bfloat16)
        values_part = pieces[1].reshape(pieces[1].shape[0], HEADS, -1)
        return summed + jnp.einsum(
            "qhk,khd->qhd", prob_low, values_part, preferred_element_type=jnp.float32
        ).reshape(summed.shape)

    def query_grad_block(summed, pieces, first_row):
        key_pos, key_doc = key_place(first_row, pieces[0].shape[0])
        unused_probs, score_grad = pair_terms(
            queries,
            attended_grad,
            log_total,
            row_delta,
            query_pos,
            query_doc,
            pieces[0],
            pieces[1],
            key_pos,
            key_doc,
        )
        keys_part = pieces[0].reshape(pieces[0].shape[0], HEADS, -1)
        return summed + jnp.einsum(
            "qhk,khd->qhd", score_grad, keys_part, preferred_element_type=jnp.float32
        ).reshape(summed.shape)

    def key_grad_block(carried, pieces, first_row):
        amount = pieces[0].shape[0]
        part_pos, part_doc = key_place(first_row, amount)
        part_log = lax.dynamic_slice_in_dim(all_log, first_row, amount, 0)
        part_delta = lax.dynamic_slice_in_dim(all_delta, first_row, amount, 0)
        prob_low, score_grad = pair_terms(
            pieces[0],
            pieces[1],
            part_log,
            part_delta,
            part_pos,
            part_doc,
            key_rows,
            value_rows,
            query_pos,
            query_doc,
        )
        grad_keys = carried[0] + jnp.einsum(
            "qhk,qhd->khd",
            score_grad,
            pieces[0].reshape(amount, HEADS, -1),
            preferred_element_type=jnp.float32,
        ).reshape(tok_dev, -1)
        grad_values = carried[1] + jnp.einsum(
            "qhk,qhd->khd",
            prob_low,
            pieces[1].reshape(amount, HEADS, -1),
            preferred_element_type=jnp.float32,
        ).reshape(tok_dev, -1)
        return (grad_keys, grad_values)

    zero_stats = (
        jnp.full((tok_dev, HEADS), FLOOR, jnp.float32),
        jnp.zeros((tok_dev, HEADS), jnp.float32),
    )
    zero_rows = jnp.zeros((tok_dev, att_width), jnp.float32)
    running_max, running_sum = in_blocks(
        stat_block, zero_stats, (lax.all_gather(key_rows, "ctx", axis=0, tiled=True),)
    )
    log_total = running_max + jnp.log(running_sum)
    attended = in_blocks(
        output_block,
        zero_rows,
        (
            lax.all_gather(key_rows, "ctx", axis=0, tiled=True),
            lax.all_gather(value_rows, "ctx", axis=0, tiled=True),
        ),
    )
    attended_low = attended.astype(jnp.bfloat16)
    resid = x_float + jnp.dot(attended_low, full_out, preferred_element_type=jnp.float32)
    inv_mlp = lax.rsqrt(jnp.mean(resid * resid, axis=1, keepdims=True) + EPS)
    normed_mlp = (resid * inv_mlp * mlp_gain_f).astype(jnp.bfloat16)
    up_proj = jnp.dot(normed_mlp, full_up, preferred_element_type=jnp.float32)
    act_low = jax.nn.silu(up_proj).astype(jnp.bfloat16)
    result = resid + jnp.dot(act_low, full_down, preferred_element_type=jnp.float32)
    cot_float = dealt_dy.astype(jnp.float32)
    grad_down = jnp.dot(act_low.T, dealt_dy, preferred_element_type=jnp.float32)
    act_grad = jnp.dot(dealt_dy, full_down.T, preferred_element_type=jnp.float32)
    sigma = jax.nn.sigmoid(up_proj)
    up_grad = (act_grad * sigma * (1.0 + up_proj * (1.0 - sigma))).astype(jnp.bfloat16)
    grad_up = jnp.dot(normed_mlp.T, up_grad, preferred_element_type=jnp.float32)
    norm_mlp_grad = jnp.dot(up_grad, full_up.T, preferred_element_type=jnp.float32)
    grad_mlp_gain = jnp.sum(norm_mlp_grad * resid * inv_mlp, axis=0)
    scaled_mlp = norm_mlp_grad * mlp_gain_f
    resid_grad = cot_float + inv_mlp * (
        scaled_mlp - resid * inv_mlp * inv_mlp * jnp.mean(scaled_mlp * resid, axis=1, keepdims=True)
    )
    branch_grad = resid_grad.astype(jnp.bfloat16)
    grad_out = jnp.dot(attended_low.T, branch_grad, preferred_element_type=jnp.float32)
    attended_grad = jnp.dot(branch_grad, full_out.T, preferred_element_type=jnp.float32).astype(
        jnp.bfloat16
    )
    row_delta = jnp.sum(
        (attended_grad.astype(jnp.float32) * attended).reshape(tok_dev, HEADS, -1), axis=2
    )
    query_grads = in_blocks(
        query_grad_block,
        zero_rows,
        (
            lax.all_gather(key_rows, "ctx", axis=0, tiled=True),
            lax.all_gather(value_rows, "ctx", axis=0, tiled=True),
        ),
    )
    all_log, all_delta = (
        lax.all_gather(log_total, "ctx", axis=0, tiled=True),
        lax.all_gather(row_delta, "ctx", axis=0, tiled=True),
    )
    key_grad_f, value_grad_f = in_blocks(
        key_grad_block,
        (zero_rows, zero_rows),
        (
            lax.all_gather(queries, "ctx", axis=0, tiled=True),
            lax.all_gather(attended_grad, "ctx", axis=0, tiled=True),
        ),
    )
    scale_terms = jnp.sum((query_grads * raw_query).reshape(tok_dev, -1, head_dim), axis=(0, 1))
    grad_scale = scale_terms * base_scale * jax.nn.sigmoid(scale_float)
    proj_grad = jnp.concatenate(
        [
            (query_grads * multiplier).astype(jnp.bfloat16),
            key_grad_f.astype(jnp.bfloat16),
            value_grad_f.astype(jnp.bfloat16),
        ],
        axis=1,
    )
    grad_qkv = jnp.dot(normed_attn.T, proj_grad, preferred_element_type=jnp.float32)
    norm_attn_grad = jnp.dot(proj_grad, full_qkv.T, preferred_element_type=jnp.float32)
    grad_attn_gain = jnp.sum(norm_attn_grad * x_float * inv_attn, axis=0)
    scaled_attn = norm_attn_grad * attn_gain_f
    input_grad = resid_grad + inv_attn * (
        scaled_attn
        - x_float * inv_attn * inv_attn * jnp.mean(scaled_attn * x_float, axis=1, keepdims=True)
    )
    owned = (
        lax.psum_scatter(grad_qkv, "fsdp", scatter_dimension=0, tiled=True),
        lax.psum_scatter(grad_out, "fsdp", scatter_dimension=0, tiled=True),
        lax.psum_scatter(grad_up, "fsdp", scatter_dimension=0, tiled=True),
        lax.psum_scatter(grad_down, "fsdp", scatter_dimension=0, tiled=True),
        lax.psum_scatter(grad_attn_gain, "fsdp", scatter_dimension=0, tiled=True),
        lax.psum_scatter(grad_mlp_gain, "fsdp", scatter_dimension=0, tiled=True),
        lax.psum_scatter(grad_scale, "fsdp", scatter_dimension=0, tiled=True),
    )
    summed_grads = lax.psum(
        (owned[0], owned[1], owned[2], owned[3], owned[4], owned[5], owned[6]), "ctx"
    )
    back_out, back_grad = (
        lax.all_to_all(result[arrived_slot], "ctx", split_axis=0, concat_axis=0, tiled=True),
        lax.all_to_all(input_grad[arrived_slot], "ctx", split_axis=0, concat_axis=0, tiled=True),
    )
    return (
        back_out[my_slots][None],
        back_grad[my_slots][None],
        summed_grads[0],
        summed_grads[1],
        summed_grads[2],
        summed_grads[3],
        summed_grads[4],
        summed_grads[5],
        summed_grads[6],
    )


HUB_WAYS = {k: ((2, 0), (2, 1)) for k in range(1, 8)}
HUB_WAYS[1] += ((1, 0),)
HUB_WAYS[2] += ((0, 1),)
HUB_WAYS[4] += ((0, 0), (0, 1), (1, 0), (1, 1))
HUB_WAYS[6] += ((0, 0), (0, 1))

SPLIT = (False, True, False)
WEIGHT_STEPS = ((2, 2, 1), (4, 2, 0), (6, 3, 1))


def attend_kernel(
    ends_ref,
    x_ref,
    w_ref,
    aux_ref,
    pos_ref,
    out_w_ref,
    up_w_ref,
    down_w_ref,
    dy_ref,
    att_save,
    normed_out,
    qkv_out,
    lse_ref,
    out_save,
    auxsum_ref,
    place_ref,
    w_out,
    result_ref,
    resid_grad_save,
    branch_save,
    up_grad_save,
    act_save,
    normed_mlp_save,
    grad_ref,
    mult_ref,
    x_mine,
    w_mine,
    dy_mine,
    x_all,
    normed_ref,
    qkv_ref,
    w_all,
    w_own,
    w_small,
    weights,
    aux_all,
    pos_all,
    v_turned,
    key_pos,
    att_send,
    x_send_sem,
    x_recv_sem,
    w_send_sem,
    w_recv_sem,
    aux_send_sem,
    aux_recv_sem,
    pos_sem,
    att_send_sem,
    att_recv_sem,
    m_send_sem,
    m_recv_sem,
    local_sem,
    save_sem,
    shard_sem,
    att_ref,
    out_ref,
    resid_grad_ref,
    branch_ref,
    up_grad_ref,
    act_ref,
    normed_mlp_ref,
    early_sem,
):
    early = {
        name: pltpu.make_async_copy(src, dst, early_sem.at[k])
        for k, (name, src, dst) in enumerate(
            (
                ("att", att_ref, att_save),
                ("out", out_ref, out_save),
                ("resid_grad", resid_grad_ref, resid_grad_save),
                ("branch", branch_ref, branch_save),
                ("up_grad", up_grad_ref, up_grad_save),
                ("act", act_ref, act_save),
                ("normed_mlp", normed_mlp_ref, normed_mlp_save),
            )
        )
    }
    w_load = pltpu.make_async_copy(w_ref, w_mine, local_sem.at[0])
    w_load.start()
    x_load = pltpu.make_async_copy(x_ref, x_mine, local_sem.at[2])
    dy_load = pltpu.make_async_copy(dy_ref, dy_mine, local_sem.at[4])
    at = Place()
    meet_plane(at)
    c, f = at.c, at.f
    hub = at.core == at.half

    aux_own = pltpu.make_async_copy(aux_ref, aux_all.at[f], local_sem.at[1])
    aux_own.start()
    x_own = pltpu.make_async_copy(x_ref, x_all.at[c], local_sem.at[3])

    halves = (pl.ds(0, 128), pl.ds(128, 128))

    def x_far(part):
        return pltpu.make_async_remote_copy(
            src_ref=x_ref.at[halves[part]],
            dst_ref=x_all.at[c, halves[part]],
            send_sem=x_send_sem.at[0, 0, part],
            recv_sem=x_recv_sem.at[c, part],
            device_id=dev(flip(c, 4), f),
            device_id_type=MESH,
        )

    @pl.when(hub)
    def _():
        x_own.start()
        for part in range(2):
            for k, where in enumerate((dev(flip(c, 1), f), dev(flip(c, 2), f), dev(c, at.twin))):
                send(
                    x_ref.at[halves[part]],
                    x_all.at[c, halves[part]],
                    x_send_sem.at[0, k, part],
                    x_recv_sem.at[c, part],
                    where,
                )

    @pl.when(jnp.logical_not(hub))
    def _():
        x_far(0).start()
        x_far(1).start()

    w_copies, aux_copies = [], []
    for k in (2, 1, 3):
        aux_copies.append(
            send(
                aux_ref,
                aux_all.at[f],
                aux_send_sem.at[k],
                aux_recv_sem.at[f],
                dev(c, (f + k) % 4),
            )
        )

    pos = pos_ref[...]
    start = jnp.zeros_like(pos)
    end = 0
    for k in range(4):
        end = end + ends_ref[0, k]
        start = jnp.where(pos >= end, end, start)
    pos_all[at.core, 0:1, :] = pos.astype(F32)
    pos_all[at.core, 1:2, :] = start.astype(F32)
    pos_all[at.core, 2:8, :] = jnp.zeros((6, 2048), F32)
    pos_copy = send(
        pos_all.at[at.core], pos_all.at[at.core], pos_sem.at[0], pos_sem.at[1], dev(c, at.twin)
    )

    row = lax.broadcasted_iota(jnp.int32, (1280, 512), 0)
    column = lax.broadcasted_iota(jnp.int32, (1280, 512), 1)
    first = (c % 4) * 320
    w_load.wait()
    for k in range(2):
        some = jnp.zeros((320, 512), F32)
        for j in range(3):
            pick = (row - first - k * 160 == column - j * 160) & (column // 160 == j)
            pick = jnp.where(pick, 1.0, 0.0).astype(BF)
            some += jnp.dot(w_mine[:, j * 1280 : (j + 1) * 1280], pick, preferred_element_type=F32)
        w_own[k] = some.astype(BF)
    mine_rows = span(f * 320, 320, 320)
    for k in (2, 3, 1):
        to = (f + k) % 4
        w_copies.append(
            send(
                w_own.at[to % 2],
                w_small.at[mine_rows],
                w_send_sem.at[k],
                w_recv_sem.at[f],
                dev(c, to),
            )
        )
    w_small[mine_rows, :] = w_own[at.core]
    x_load.start()
    dy_load.start()


    shards = (out_w_ref, up_w_ref, down_w_ref)
    xbit = c % 2
    other = (f + 2) % 4

    def part(m, owner, x):
        return weights.at[m, span(owner * 320 + x * 160, 160, 160)]

    def weight_copy(m, way):
        if way == 0:
            src, dst, to = shards[m], weights.at[m, mine_rows], dev(c, at.twin)
        elif way == 1 and not SPLIT[m]:
            src, dst, to = shards[m], weights.at[m, mine_rows], dev(c, other)
        elif way == 3 and not SPLIT[m]:
            src = dst = weights.at[m, span(other * 320, 320, 320)]
            to = dev(c, at.twin)
        elif way == 1:
            src = shards[m].at[span(xbit * 160, 160, 160)]
            dst, to = part(m, f, xbit), dev(c, other)
        else:
            x = (xbit, xbit, 1 - xbit)[way - 2]
            src = dst = part(m, other, x)
            to = (dev(flip(c, 1), f), dev(c, at.twin), dev(c, at.twin))[way - 2]
        return pltpu.make_async_remote_copy(
            src_ref=src,
            dst_ref=dst,
            send_sem=m_send_sem.at[m, way],
            recv_sem=m_recv_sem.at[m, way],
            device_id=to,
            device_id_type=MESH,
        )

    def shard_copy(m):
        return pltpu.make_async_copy(shards[m], weights.at[m, mine_rows], shard_sem.at[m])

    def weight_first(m):
        weight_copy(m, 0).start()
        weight_copy(m, 1).start()
        shard_copy(m).start()

    def weight_second(m):
        weight_copy(m, 1).wait_recv()
        if SPLIT[m]:
            weight_copy(m, 2).start()
        weight_copy(m, 3).start()

    def weight_third(m):
        if SPLIT[m]:
            weight_copy(m, 2).wait_recv()
            weight_copy(m, 4).start()

    def weight_last(m):
        shard_copy(m).wait()
        for way in (0, 3, 4) if SPLIT[m] else (0, 3):
            weight_copy(m, way).wait_recv()


    aux_own.wait()
    for k in (1, 2, 3):
        await_recv(aux_all.at[0], aux_recv_sem.at[(f + k) % 4])
    aux = jnp.zeros((16, 1280), F32)
    scale = jnp.zeros((16, LANES), F32)
    row = lax.broadcasted_iota(jnp.int32, (384, 1280), 0)
    column = lax.broadcasted_iota(jnp.int32, (384, 1280), 1)
    for k in range(4):
        put = jnp.where((column == row + k * 320) & (row < 320), 1.0, 0.0).astype(BF)
        aux = aux + jnp.dot(aux_all[k], put, preferred_element_type=F32)
        put = (column[:LANES, :LANES] == row[:LANES, :LANES] + k * 20) & (row[:LANES, :LANES] < 20)
        put = jnp.where(put, 1.0, 0.0).astype(BF)
        scale = scale + jnp.dot(aux_all[k, :, :LANES], put, preferred_element_type=F32)
    auxsum_ref[...] = aux
    auxsum_ref[2:3, :LANES] = scale[2:3]
    gain = aux[0:1, :]
    mlp_gain = aux[1:2, :]
    scale = scale[2:3]
    real = lax.broadcasted_iota(jnp.int32, (1, LANES), 1) < 80
    mult = jnp.where(
        real, LOG2E / math.sqrt(80) * (jnp.maximum(scale, 0.0) + jnp.log1p(jnp.exp(-jnp.abs(scale)))), 0.0
    )
    mult_ref[...] = jnp.transpose(jnp.broadcast_to(mult, (LANES, LANES)))
    one = jnp.ones_like(mult)
    mults = jnp.concatenate([mult, mult, one, one, one, one], axis=1)

    await_recv(pos_all.at[0], pos_sem.at[1])
    place_ref[...] = pos_all[at.half]
    for k in range(8):
        block = place_ref[0:1, k * 256 : (k + 1) * 256]
        key_pos[k * 256 : (k + 1) * 256, :] = jnp.transpose(
            jnp.broadcast_to(block, (LANES, 256))
        )

    def arrive(step, carry):
        k = step + jnp.where(step == 3, 1, 0) - jnp.where(step == 4, 1, 0)
        slot = flip(c, k)
        for part in range(2):
            piece = x_all.at[slot, halves[part]]
            if part == 0:

                @pl.when(jnp.logical_and(hub, k == 0))
                def _():
                    x_own.wait()

            @pl.when(jnp.logical_not(jnp.logical_and(hub, k == 0)))
            def _(part=part, piece=piece):
                await_recv(piece, x_recv_sem.at[slot, part])

            def onward(way, where, part=part, piece=piece):
                send(
                    piece, piece, x_send_sem.at[k, way, part], x_recv_sem.at[slot, part], where
                )

            for way, where in enumerate((dev(flip(c, 1), f), dev(flip(c, 2), f), dev(c, at.twin))):
                due = False
                for when in HUB_WAYS:
                    if (way, part) in HUB_WAYS[when]:
                        due = jnp.logical_or(due, k == when)

                @pl.when(jnp.logical_and(hub, due))
                def _(way=way, where=where, onward=onward):
                    onward(way, where)

        @pl.when(step == 2)
        def _():
            weight_first(0)

        @pl.when(step == 4)
        def _():
            weight_first(1)


        xf = x_all[slot].astype(F32)
        inv = lax.rsqrt(jnp.mean(xf * xf, axis=1, keepdims=True) + EPS)
        rows = span(slot * 256, 256, 256)
        normed_ref[rows, :] = (xf * inv * gain).astype(BF)
        pltpu.make_async_copy(
            normed_ref.at[rows], normed_out.at[rows], save_sem.at[slot, 0]
        ).start()
        return carry

    def project(step, carry):
        slot = flip(c, step)
        rows = span(slot * 256, 256, 256)
        proj = jnp.dot(normed_ref[rows, :], w_all[...], preferred_element_type=F32)
        qkv_ref[rows, :] = (proj * mults).astype(BF)
        pltpu.make_async_copy(qkv_ref.at[rows], qkv_out.at[rows], save_sem.at[slot, 1]).start()
        return carry

    lax.fori_loop(0, 7, arrive, 0)
    for k in (1, 2, 3):
        await_recv(w_small.at[pl.ds(0, 320)], w_recv_sem.at[(f + k) % 4])
    weight_first(2)
    row = lax.broadcasted_iota(jnp.int32, (512, 768), 0)
    column = lax.broadcasted_iota(jnp.int32, (512, 768), 1)
    spread = (row == column // LANES * 80 + column % LANES) & (column % LANES < 80)
    spread = jnp.where(spread, 1.0, 0.0).astype(BF)
    w_all[...] = jnp.dot(w_small[...], spread, preferred_element_type=F32).astype(BF)
    w_save = pltpu.make_async_copy(w_all, w_out, local_sem.at[5])
    w_save.start()
    lax.fori_loop(0, 5, project, 0)
    lax.fori_loop(7, 8, arrive, 0)
    lax.fori_loop(5, 8, project, 0)

    for h in range(2):
        v_turned[h] = jnp.transpose(qkv_ref[:, (4 + h) * LANES : (5 + h) * LANES])

    att_own = pltpu.make_async_copy(
        att_send.at[c], att_ref.at[span(at.group * 160, 160, 160)], local_sem.at[3]
    )

    def att_copy(block):
        return pltpu.make_async_remote_copy(
            src_ref=att_send.at[block],
            dst_ref=att_ref.at[span(at.group * 160, 160, 160)],
            send_sem=att_send_sem.at[block],
            recv_sem=att_recv_sem.at[at.group],
            device_id=dev(block, at.pack),
            device_id_type=MESH,
        )

    mine = at.core == at.half

    def attend(step, carry):
        block = flip(c, 7 - step)
        lanes = span(block * 256, 256, 256)
        high = place_ref[0:1, lanes]
        least = place_ref[1:2, lanes]
        for h in range(2):
            query = qkv_ref[lanes, h * LANES : (h + 1) * LANES]
            scores, top = [], None
            for part in range(2):
                rows = slice(part * 1024, (part + 1) * 1024)
                kp = key_pos[rows, :]
                kp = jnp.concatenate([kp, kp], axis=1)
                keys = qkv_ref[rows, (2 + h) * LANES : (3 + h) * LANES]
                s = lax.dot_general(
                    keys, query, (((1,), (1,)), ((), ())), preferred_element_type=F32
                )
                s = jnp.where((kp >= least) & (kp <= high), s, FLOOR)
                scores.append(s)
                most = jnp.max(s, axis=0, keepdims=True)
                top = most if top is None else jnp.maximum(top, most)
            total = jnp.zeros((1, 256), F32)
            o = jnp.zeros((LANES, 256), F32)
            for part in range(2):
                p = jnp.exp(scores[part] - top)
                total += jnp.sum(p, axis=0, keepdims=True)
                values = v_turned[h, :, part * 1024 : (part + 1) * 1024]
                o += jnp.dot(values, p.astype(BF), preferred_element_type=F32)
            o = o[:80] / total
            lse_ref[h : h + 1, lanes] = top + jnp.log(total)
            out_ref[h * 80 : (h + 1) * 80, lanes] = o.astype(BF)
            att_send[block, h * 80 : (h + 1) * 80, :] = o.astype(BF)

        @pl.when(jnp.logical_and(mine, step == 7))
        def _():
            att_own.start()

        @pl.when(jnp.logical_not(jnp.logical_and(mine, step == 7)))
        def _():
            att_copy(block).start()

        for when, todo, m in WEIGHT_STEPS:

            @pl.when(step == when)
            def _(todo=todo, m=m):
                (weight_second if todo == 2 else weight_third)(m)

        return carry

    lax.fori_loop(0, 8, attend, 0)
    weight_second(2)
    early["out"].start()
    lse_ref[2:8, :] = jnp.zeros((6, 2048), F32)

    def land(block, carry):
        @pl.when(jnp.logical_not(jnp.logical_and(mine, block == at.group)))
        def _():
            await_recv(att_ref.at[pl.ds(0, 160)], att_recv_sem.at[block])

        return carry

    @pl.when(mine)
    def _():
        att_own.wait()

    weight_last(0)
    lax.fori_loop(0, 8, land, 0)
    early["att"].start()

    def across(left, right):
        return lax.dot_general(
            left, right, (((1,), (1,)), ((), ())), preferred_element_type=F32
        )

    x_load.wait()
    dy_load.wait()
    xf = x_mine[...].astype(F32)
    resid = xf + jnp.dot(jnp.transpose(att_ref[...]), weights[0], preferred_element_type=F32)
    inv = lax.rsqrt(jnp.mean(resid * resid, axis=1, keepdims=True) + EPS)
    normed_mlp = (resid * inv * mlp_gain).astype(BF)
    normed_mlp_ref[...] = jnp.transpose(normed_mlp)
    early["normed_mlp"].start()
    weight_last(1)
    up = jnp.dot(normed_mlp, weights[1], preferred_element_type=F32)
    sigma = 1.0 / (1.0 + jnp.exp(-up))
    act = (up * sigma).astype(BF)
    act_ref[...] = jnp.transpose(act)
    early["act"].start()
    slope = sigma * (1.0 + up * (1.0 - sigma))
    weight_last(2)
    dy = dy_mine[...]
    up_grad = (across(dy, weights[2]) * slope).astype(BF)
    up_grad_ref[...] = up_grad
    early["up_grad"].start()
    scaled = across(up_grad, weights[1]) * mlp_gain
    resid_grad = dy.astype(F32) + inv * (
        scaled - resid * inv * inv * jnp.mean(scaled * resid, axis=1, keepdims=True)
    )
    resid_grad_ref[...] = resid_grad
    early["resid_grad"].start()
    branch = resid_grad.astype(BF)
    branch_ref[...] = branch
    early["branch"].start()
    grad_ref[...] = across(weights[0], branch).astype(BF)
    result_ref[...] = resid + jnp.dot(act, weights[2], preferred_element_type=F32)

    w_save.wait()
    for copy in early.values():
        copy.wait()
    for k in range(8):
        rows = pl.ds(k * 256, 256)
        pltpu.make_async_copy(normed_ref.at[rows], normed_out.at[rows], save_sem.at[k, 0]).wait()
        pltpu.make_async_copy(qkv_ref.at[rows], qkv_out.at[rows], save_sem.at[k, 1]).wait()
    for copy in w_copies + aux_copies:
        copy.wait_send()
    pos_copy.wait_send()
    for m in range(3):
        for way in range(5) if SPLIT[m] else (0, 1, 3):
            weight_copy(m, way).wait_send()

    @pl.when(hub)
    def _():
        for k in range(8):
            for way, part in HUB_WAYS.get(k, ((0, 0), (0, 1), (1, 0), (1, 1), (2, 0), (2, 1))):
                await_recv(x_mine.at[halves[part]], x_send_sem.at[k, way, part])

    @pl.when(jnp.logical_not(hub))
    def _():
        x_far(0).wait_send()
        x_far(1).wait_send()

    def finish(block, carry):
        @pl.when(jnp.logical_not(jnp.logical_and(mine, block == c)))
        def _():
            att_copy(block).wait_send()

        return carry

    lax.fori_loop(0, 8, finish, 0)


def forward(*args):
    shape = jax.ShapeDtypeStruct
    dma = pltpu.SemaphoreType.DMA
    return pl.pallas_call(
        attend_kernel,
        name="forward",
        out_shape=(
            shape((1280, 256), BF),
            shape((2048, 1280), BF),
            shape((2048, 768), BF),
            shape((8, 2048), F32),
            shape((160, 2048), BF),
            shape((16, 1280), F32),
            shape((8, 2048), F32),
            shape((1280, 768), BF),
            shape((256, 1280), F32),
            shape((256, 1280), F32),
            shape((256, 1280), BF),
            shape((256, 1280), BF),
            shape((1280, 256), BF),
            shape((1280, 256), BF),
            shape((1280, 256), BF),
            shape((LANES, LANES), F32),
        ),
        in_specs=[pl.BlockSpec(memory_space=pltpu.SMEM)] + [ANY_SPEC] * 2 + [VMEM_SPEC] * 2 + [ANY_SPEC] * 4,
        out_specs=(ANY_SPEC,) * 3
        + (VMEM_SPEC, ANY_SPEC, VMEM_SPEC, VMEM_SPEC, ANY_SPEC, VMEM_SPEC)
        + (ANY_SPEC,) * 5
        + (VMEM_SPEC,) * 2,
        scratch_shapes=[
            pltpu.VMEM((256, 1280), BF),
            pltpu.VMEM((320, 3840), BF),
            pltpu.VMEM((256, 1280), BF),
            pltpu.VMEM((8, 256, 1280), BF),
            pltpu.VMEM((2048, 1280), BF),
            pltpu.VMEM((2048, 768), BF),
            pltpu.VMEM((1280, 768), BF),
            pltpu.VMEM((2, 320, 512), BF),
            pltpu.VMEM((1280, 512), BF),
            pltpu.VMEM((3, 1280, 1280), BF),
            pltpu.VMEM((4, 16, 384), BF),
            pltpu.VMEM((2, 8, 2048), F32),
            pltpu.VMEM((2, 128, 2048), BF),
            pltpu.VMEM((2048, LANES), F32),
            pltpu.VMEM((8, 160, 256), BF),
            dma((8, 3, 2)),
            dma((8, 2)),
            dma((4,)),
            dma((4,)),
            dma((4,)),
            dma((4,)),
            dma((2,)),
            dma((8,)),
            dma((8,)),
            dma((3, 5)),
            dma((3, 5)),
            dma((6,)),
            dma((8, 2)),
            dma((3,)),
            pltpu.VMEM((1280, 256), BF),
            pltpu.VMEM((160, 2048), BF),
            pltpu.VMEM((256, 1280), F32),
            pltpu.VMEM((256, 1280), BF),
            pltpu.VMEM((256, 1280), BF),
            pltpu.VMEM((1280, 256), BF),
            pltpu.VMEM((1280, 256), BF),
            dma((7,)),
        ],
        compiler_params=pltpu.CompilerParams(
            collective_id=0, has_side_effects=True, vmem_limit_bytes=VMEM_LIMIT
        ),
        cost_estimate=pl.CostEstimate(
            flops=20_000_000_000, bytes_accessed=40_000_000, transcendentals=8_400_000
        ),
    )(*args)


def add_into(target, source, rows, step):
    def one(k, carry):
        part = span(k * step, step, step)
        target[part, :] = (target[part, :].astype(F32) + source[part, :].astype(F32)).astype(BF)
        return carry

    lax.fori_loop(0, rows // step, one, 0)


SUM_WAYS = ("yxzh", "zyxh", "zxyh")
SPREAD_WAYS = ("hzx", "hxz", "hxz")
HEAD_WAYS = "hzx"

PLAN = (
    "prep", "mt0", "m00", "mt2", "m02", "mt1", "take", "L00", "L01", "L02", "L03", "L04",
    "m01", "L05", "L06", "L07", "E0", "qs0", "L10", "L11", "L12", "L13", "L14", "L15", "L16",
    "qa0", "m10", "L17", "m12", "E1", "v0", "qs1", "nt0", "nt1", "nt2", "q00", "v1", "nt3",
    "v2", "v3", "na0", "v4", "na1", "na2", "qa1", "na3", "v5", "m11", "q10", "m20", "q01",
    "m22", "m21", "m32", "m30", "q11", "q20", "g02", "g00", "m31", "g12", "nb0", "g10", "g01",
    "nb1", "q21", "g22", "g11", "g20", "nc_f", "nc_n", "g21", "qc0", "qw0", "mw2", "qc1",
    "mw0", "nfin", "qw1", "mw1", "turn",
)

KEY_PARTS = 2
KEY_ROWS = 2048 // KEY_PARTS


def backward_kernel(
    grad_ref,
    att_hbm,
    branch_hbm,
    normed_mlp_hbm,
    up_grad_hbm,
    act_hbm,
    dy_hbm,
    qkv_hbm,
    lse_ref,
    out_hbm,
    place_ref,
    normed_hbm,
    w_hbm,
    mult_ref,
    x_hbm,
    resid_grad_hbm,
    gain_ref,
    first_out,
    second_out,
    third_out,
    slice_out,
    input_grad_out,
    scale_ref,
    first_ref,
    second_ref,
    third_ref,
    slice_ref,
    input_ref,
    att_ref,
    branch_ref,
    normed_mlp_ref,
    up_grad_ref,
    act_ref,
    dy_ref,
    qkv_ref,
    out_ref,
    w_ref,
    x_ref,
    resid_grad_ref,
    grad_all,
    key_pos,
    k_turned,
    delta,
    key_sum,
    value_sum,
    turned,
    normed_part,
    n_core,
    n_x,
    n_z,
    n_last,
    sums,
    core_in,
    taken,
    slices,
    s1,
    s2,
    gathered,
    scale_in,
    g_send_sem,
    g_recv_sem,
    local_sem,
    m_send,
    m_recv,
    q_send,
    q_recv,
    nc_send,
    nc_recv,
    n_send,
    n_recv,
    v_send,
    v_recv,
    load_sem,
    save_sem,
):
    loads = {
        name: pltpu.make_async_copy(src, dst, load_sem.at[k])
        for k, (name, src, dst) in enumerate(
            (
                ("act", act_hbm, act_ref),
                ("dy", dy_hbm, dy_ref),
                ("normed", normed_mlp_hbm, normed_mlp_ref),
                ("up", up_grad_hbm, up_grad_ref),
                ("att", att_hbm, att_ref),
                ("branch", branch_hbm, branch_ref),
                ("qkv", qkv_hbm, qkv_ref),
                ("out", out_hbm, out_ref),
                ("w", w_hbm, w_ref),
                ("x", x_hbm, x_ref),
                ("resid", resid_grad_hbm, resid_grad_ref),
            )
        )
    }
    for load in loads.values():
        load.start()
    at = Place()
    meet_plane(at)
    c, f, core, half = at.c, at.f, at.core, at.half
    mine = core == half
    row = f // 2
    xbit, zbit = c % 2, (c // 2) % 2
    twin, across = dev(c, at.twin), dev(c, at.across)
    xpeer, zpeer, hpeer = dev(flip(c, 1), f), dev(flip(c, 2), f), dev(flip(c, 4), f)

    def remote(src, dst, send_sem, recv_sem, where):
        return pltpu.make_async_remote_copy(
            src_ref=src,
            dst_ref=dst,
            send_sem=send_sem,
            recv_sem=recv_sem,
            device_id=where,
            device_id_type=MESH,
        )

    def grad_copy(group, h):
        return remote(
            grad_ref.at[span(group * 160 + h * 80, 80, 80)],
            grad_all.at[h, pl.ds(0, 80), span(c * 256, 256, 256)],
            g_send_sem.at[group, h],
            g_recv_sem.at[c, h],
            dev(core * 4 + group // 2, at.plane + group % 2),
        )

    def grad_own(h):
        return pltpu.make_async_copy(
            grad_ref.at[span(at.group * 160 + h * 80, 80, 80)],
            grad_all.at[h, pl.ds(0, 80), span(c * 256, 256, 256)],
            local_sem.at[h],
        )

    def give(k, carry):
        group = flip(at.group, k)

        @pl.when(jnp.logical_and(mine, k == 0))
        def _():
            grad_own(0).start()
            grad_own(1).start()

        @pl.when(jnp.logical_not(jnp.logical_and(mine, k == 0)))
        def _():
            grad_copy(group, 0).start()
            grad_copy(group, 1).start()

        return carry

    lax.fori_loop(0, 8, give, 0)

    bits = {"y": row, "x": xbit, "z": zbit, "h": half}
    peers = {"y": across, "x": xpeer, "z": zpeer, "h": hpeer}
    results = (first_ref, second_ref, third_ref)

    def finer(m):
        return "z" if SUM_WAYS[m].index("x") < SUM_WAYS[m].index("z") else "x"

    def cut(ref, way, bit):
        if way == "y":
            return (bit,)
        lead = (slice(None),) * (len(ref.shape) - 2)
        if way == "h":
            return lead + (slice(None), span(bit * 640, 640, 640))
        rows = ref.shape[-2] // 2
        return lead + (span(bit * rows, rows, rows),)

    def main_copy(stage, m):
        if stage < 0:
            y = stage + 2
            src, dst, to = sums.at[pl.ds((m * 2 + y) * 320, 320)], core_in.at[m, y], twin
        elif stage < 4:
            way = SUM_WAYS[m][stage]
            ref = core_in.at[m] if stage == 0 else taken[m][stage - 1]
            src, dst, to = ref.at[cut(ref, way, 1 - bits[way])], taken[m][stage], peers[way]
        else:
            way = SPREAD_WAYS[m][stage - 4]
            known = SPREAD_WAYS[m][: stage - 4]
            low = finer(m)
            high = "x" if low == "z" else "z"
            if high in known:
                rows = pl.ds(0, 320)
            elif low in known:
                rows = span(bits[high] * 160, 160, 160)
            else:
                rows = span(bits[high] * 160 + bits[low] * 80, 80, 80)
            lanes = pl.ds(0, 1280) if "h" in known else span(half * 640, 640, 640)
            src = dst = results[m].at[rows, lanes]
            to = peers[way]
        return remote(src, dst, m_send.at[stage + 2, m], m_recv.at[stage + 2, m], to)

    def added(ref, other, spot):
        for k in range(2) if len(ref.shape) == 3 else (None,):
            here = () if k is None else (k,)
            there = spot if k is None else (k,) + spot[1:]
            ref[here] = (ref[here].astype(F32) + other[there].astype(F32)).astype(BF)

    def main(stage, m):
        if stage == 0:
            for y in range(2):
                main_copy(y - 2, m).wait_recv()
                total = core_in[m, y].astype(F32) + weight_rows(m, 2 * y + core)
                core_in[m, y] = total.astype(BF)
        elif stage < 5:
            main_copy(stage - 1, m).wait_recv()
            way = SUM_WAYS[m][stage - 1]
            ref = core_in.at[m] if stage == 1 else taken[m][stage - 2]
            spot = cut(ref, way, bits[way])
            if stage < 4:
                added(taken[m][stage - 1], ref, spot)
            else:
                low = finer(m)
                high = "x" if low == "z" else "z"
                rows = span(bits[high] * 160 + bits[low] * 80, 80, 80)
                results[m][rows, span(half * 640, 640, 640)] = (
                    taken[m][3][...].astype(F32) + ref[spot].astype(F32)
                ).astype(BF)
        else:
            main_copy(stage - 1, m).wait_recv()
        if stage < 7:
            main_copy(stage, m).start()
        else:
            save(m).start()

    lefts = (act_ref, normed_mlp_ref, att_ref)
    rights = (dy_ref, up_grad_ref, branch_ref)

    def weight_rows(m, quarter):
        rows = span(quarter * 320, 320, 320)
        return jnp.dot(lefts[m][rows, :], rights[m][...], preferred_element_type=F32)

    def main_first(m):
        for name in (("act", "dy"), ("normed", "up"), ("att", "branch"))[m]:
            loads[name].wait()
        for y in range(2):
            part = weight_rows(m, 2 * y + 1 - core)
            sums[(m * 2 + y) * 320 : (m * 2 + y + 1) * 320, :] = part.astype(BF)
            main_copy(y - 2, m).start()

    def prepare():
        loads["qkv"].wait()
        for h in range(2):
            grad_all[h, 80:, :] = jnp.zeros((48, 2048), BF)
            k_turned[h] = jnp.transpose(qkv_ref[:, (2 + h) * LANES : (3 + h) * LANES])
        for k in range(8):
            block = place_ref[0:1, k * 256 : (k + 1) * 256]
            key_pos[k * 256 : (k + 1) * 256, :] = jnp.transpose(
                jnp.broadcast_to(block, (LANES, 256))
            )
        scale_ref[...] = jnp.zeros((8, LANES), F32)

    def take(k, carry):
        block = flip(c, k)

        @pl.when(jnp.logical_and(mine, k == 0))
        def _():
            grad_own(0).wait()
            grad_own(1).wait()

        @pl.when(jnp.logical_not(jnp.logical_and(mine, k == 0)))
        def _():
            for h in range(2):
                await_recv(
                    grad_all.at[h, pl.ds(0, 80), pl.ds(0, 256)], g_recv_sem.at[block, h]
                )

        return carry

    def take_all():
        loads["out"].wait()
        lax.fori_loop(0, 8, take, 0)
        for h in range(2):
            delta[h : h + 1, :] = jnp.sum(
                grad_all[h, :80, :].astype(F32) * out_ref[h * 80 : (h + 1) * 80, :].astype(F32),
                axis=0,
                keepdims=True,
            )

    def head_copy(stage, h):
        if stage == 0:
            rows = pl.ds(0, 240)
            src, to = slices.at[h, rows, span((1 - row) * 640, 640, 640)], across
            dst = s1.at[h, rows]
        elif stage == 1:
            src, dst, to = s1.at[h, span(128 - half * 128, 128, 128)], s2.at[h], hpeer
        elif stage < 5:
            way = HEAD_WAYS[stage - 2]
            known = HEAD_WAYS[: stage - 2]
            where = (core,) + tuple(slice(None) if d in known else bits[d] for d in "xz") + (h,)
            rows = pl.ds(0, 240) if "h" in known else span(half * 128, 128, 128)
            src = dst = gathered.at[where + (rows,)]
            to = peers[way]
        else:
            src = dst = gathered.at[core, :, :, h, pl.ds(0, 240)]
            to = twin
        return remote(src, dst, q_send.at[stage, h], q_recv.at[stage, h], to)

    def head(stage, h):
        if stage > 0:
            head_copy(stage - 1, h).wait_recv()
        if stage == 1:
            add_into(s1.at[h], slices.at[h, :, span(row * 640, 640, 640)], 256, 128)
        if stage == 2:
            own = span(half * 128, 128, 128)
            gathered[core, xbit, zbit, h, own, :] = (
                s2[h].astype(F32) + s1[h, own, :].astype(F32)
            ).astype(BF)
        if stage < 6:
            head_copy(stage, h).start()
        else:
            head_flat(h)

    def normed_load(part):
        return pltpu.make_async_copy(
            normed_hbm.at[:, pl.ds(part * 256, 256)], normed_part.at[part % 2], local_sem.at[2 + part % 2]
        )

    def attend_head(h, hooks):
        key_sum[...] = jnp.zeros((2048, LANES), F32)
        value_sum[...] = jnp.zeros((2048, LANES), F32)

        def block_grad(block, carry):
            lanes = span(block * 256, 256, 256)
            high = place_ref[0:1, lanes]
            least = place_ref[1:2, lanes]
            query = qkv_ref[lanes, h * LANES : (h + 1) * LANES]
            grad_t = grad_all[h, :, lanes]
            q_grad = jnp.zeros((LANES, 256), F32)
            for part in range(KEY_PARTS):
                some = slice(part * KEY_ROWS, (part + 1) * KEY_ROWS)
                kp = key_pos[some, :]
                kp = jnp.concatenate([kp, kp], axis=1)
                keys = qkv_ref[some, (2 + h) * LANES : (3 + h) * LANES]
                values = qkv_ref[some, (4 + h) * LANES : (5 + h) * LANES]
                s = lax.dot_general(
                    keys, query, (((1,), (1,)), ((), ())), preferred_element_type=F32
                )
                visible = (kp >= least) & (kp <= high)
                p = jnp.exp(jnp.where(visible, s - lse_ref[h : h + 1, lanes], FLOOR))
                gp = jnp.dot(values, grad_t, preferred_element_type=F32)
                gs = (p * (gp - delta[h : h + 1, lanes])).astype(BF)
                value_sum[some, :] += lax.dot_general(
                    p.astype(BF), grad_t, (((1,), (1,)), ((), ())), preferred_element_type=F32
                )
                key_sum[some, :] += jnp.dot(gs, query, preferred_element_type=F32)
                q_grad += jnp.dot(k_turned[h, :, some], gs, preferred_element_type=F32)
            scale_ref[0:1, :] += jnp.sum(
                jnp.transpose(q_grad) * query.astype(F32), axis=0, keepdims=True
            )
            turned[h * LANES : (h + 1) * LANES, lanes] = (q_grad * mult_ref[:, 0:1]).astype(BF)
            for step, todo in hooks.items():

                @pl.when(block == step)
                def _(todo=todo):
                    for one in todo:
                        one()

            return carry

        lax.fori_loop(0, 8, block_grad, 0)

    def attend_end(h):
        for j, total in ((1, key_sum), (2, value_sum)):
            low = jnp.transpose(total[...]).astype(BF)
            turned[(2 * j + h) * LANES : (2 * j + h + 1) * LANES, :] = low

    def head_first(h):
        slices[h, 240:, :] = jnp.zeros((16, 1280), BF)
        s1[h, 240:, :] = jnp.zeros((16, 640), BF)
        for part in range(5):
            normed_load(part).wait()
            if part + 1 < 5:
                normed_load(part + 1).start()
            for j in range(3):
                first = (2 * j + h) * LANES
                slices[h, j * 80 : (j + 1) * 80, part * 256 : (part + 1) * 256] = jnp.dot(
                    turned[first : first + 80, :],
                    normed_part[part % 2],
                    preferred_element_type=F32,
                ).astype(BF)
        if h == 0:
            normed_load(0).start()
        head(0, h)

    def norm_bits(k):
        return (1 - xbit, 1 - xbit, xbit, xbit)[k], (1 - zbit, zbit, 1 - zbit, zbit)[k]

    def norm_spot(k, hh):
        slot = 2 * k + hh
        return sums.at[pl.ds(slot // 5 * 640, 640), pl.ds(slot % 5 * 256, 256)]

    def norm_copy(stage, k, hh=0):
        if stage == 0:
            return remote(
                norm_spot(k, hh), n_core.at[k, hh], nc_send.at[k, hh], nc_recv.at[k, hh], twin
            )
        took = k
        if stage == 1:
            ends = n_core.at[k], n_x.at[k], xpeer
        elif stage == 2:
            ends = n_core.at[2, (1 - half, half)[k]], n_z.at[k], zpeer
        else:
            to = dev(flip(c, 4), at.pack) if k == 0 else dev(c, at.twin)
            took = (core, 2)[k]
            ends = n_core.at[3, (1 - half, half)[k]], n_last.at[core], to
        return remote(ends[0], ends[1], n_send.at[stage, k], n_recv.at[stage, took], ends[2])

    def norm_part(k, hh, which):
        xs, zs = norm_bits(k)
        lanes = span((hh * 4 + zs * 2 + xs) * 256, 256, 256)
        rows = span(which * 640, 640, 640)
        return jnp.dot(w_ref[rows, :], turned[:, lanes], preferred_element_type=F32)

    def norm_first(k):
        if k == 0:
            loads["w"].wait()
            for m in range(3):
                for stage in range(2):
                    main_copy(stage - 2, m).wait_send()
        for hh in range(2):
            norm_spot(k, hh)[...] = norm_part(k, hh, 1 - core).astype(BF)
            norm_copy(0, k, hh).start()

    def norm_core(k):
        for hh in range(2):
            norm_copy(0, k, hh).wait_recv()
            n_core[k, hh] = (n_core[k, hh].astype(F32) + norm_part(k, hh, core)).astype(BF)
        if k < 2:
            norm_copy(1, k).start()

    def scale_copy(stage):
        where = (twin, across, xpeer, zpeer, hpeer)[stage]
        return remote(scale_ref, scale_in.at[stage], v_send.at[stage], v_recv.at[stage], where)

    def tiny(stage):
        if stage > 0:
            scale_copy(stage - 1).wait()
            scale_ref[...] += scale_in[stage - 1]
        if stage < 5:
            scale_copy(stage).start()
        else:
            given = gain_ref[2:3, :LANES]
            soft = jnp.maximum(given, 0.0) + jnp.log1p(jnp.exp(-jnp.abs(given)))
            scale_ref[0:1, :] = scale_ref[0:1, :] / (soft * (1.0 + jnp.exp(-given)))

    def norm_x(k):
        norm_copy(1, k).wait_recv()
        for hh in range(2):
            add_into(n_core.at[2 + k, hh], n_x.at[k, hh], 640, 80)
        if k == 0:
            norm_copy(2, 0).start()
            norm_copy(2, 1).start()

    def norm_far():
        norm_copy(2, 0).wait_recv()
        add_into(n_core.at[3, 1 - half], n_z.at[0], 640, 80)
        norm_copy(3, 0).start()

    def norm_near():
        norm_copy(2, 1).wait_recv()
        add_into(n_core.at[3, half], n_z.at[1], 640, 80)

        @pl.when(jnp.logical_not(mine))
        def _():
            norm_copy(3, 1).start()

    def norm_last():
        loads["x"].wait()
        loads["resid"].wait()
        @pl.when(mine)
        def _():
            n_last[core] = n_core[3, half]
            await_recv(n_last.at[0], n_recv.at[3, 2])

        @pl.when(jnp.logical_not(mine))
        def _():
            await_recv(n_last.at[0], n_recv.at[3, 0])
            await_recv(n_last.at[1], n_recv.at[3, 1])

        xf = x_ref[...].astype(F32)
        inv = lax.rsqrt(jnp.mean(xf * xf, axis=1, keepdims=True) + EPS)
        scaled = jnp.concatenate(
            [jnp.transpose(n_last[k].astype(F32)) for k in range(2)], axis=1
        ) * gain_ref[0:1, :]
        input_ref[...] = resid_grad_ref[...] + inv * (
            scaled - xf * inv * inv * jnp.mean(scaled * xf, axis=1, keepdims=True)
        )
        save(3).start()

    def head_flat(h):
        if h == 0:
            for k in range(4):
                for hh in range(2):
                    norm_copy(0, k, hh).wait_send()
        for core_k in range(2):
            for m4 in range(4):
                for j in range(3):
                    start = j * 1280 + (4 * m4 + 2 * core_k + h) * 80
                    first = start // 1920 * 640
                    sums[start % 1920 : start % 1920 + 80, first : first + 640] = gathered[
                        core_k, m4 % 2, m4 // 2, h, j * 80 : (j + 1) * 80, :
                    ]

    def save(k):
        src, dst = (
            (first_ref, first_out),
            (second_ref, second_out),
            (third_ref, third_out),
            (input_ref, input_grad_out),
            (slice_ref.at[:, pl.ds(0, 1920)], slice_out.at[:, pl.ds(0, 1920)]),
            (slice_ref.at[:, pl.ds(1920, 1920)], slice_out.at[:, pl.ds(1920, 1920)]),
        )[k]
        return pltpu.make_async_copy(src, dst, save_sem.at[k])

    def turn_all():
        for part in range(2):

            def turn(k, carry, part=part):
                rows = span(k * 384, 384, 384)
                lanes = span(part * 1920 + k * 384, 384, 384)

                @pl.when(core == 0)
                def _():
                    strip = jnp.transpose(sums[rows, part * 640 : part * 640 + 384])
                    slice_ref[:, lanes] = strip[:320]

                @pl.when(core == 1)
                def _():
                    strip = jnp.transpose(sums[rows, part * 640 + 256 : part * 640 + 640])
                    slice_ref[:, lanes] = strip[64:]

                return carry

            lax.fori_loop(0, 5, turn, 0)
            save(4 + part).start()

    tasks = {"prep": prepare, "take": take_all, "nb0": lambda: norm_x(0), "nb1": lambda: norm_x(1)}
    tasks |= {"nc_f": norm_far, "nc_n": norm_near, "nfin": norm_last, "turn": turn_all}
    for m in range(3):
        tasks[f"mt{m}"] = functools.partial(main_first, m)
        for stage in range(4):
            tasks[f"m{stage}{m}"] = functools.partial(main, stage, m)
        for stage in range(3):
            tasks[f"g{stage}{m}"] = functools.partial(main, 4 + stage, m)
        tasks[f"mw{m}"] = functools.partial(main, 7, m)
    for h in range(2):
        tasks[f"E{h}"] = functools.partial(attend_end, h)
        tasks[f"qs{h}"] = functools.partial(head_first, h)
        for stage, name in enumerate(("qa", "q0", "q1", "q2", "qc", "qw")):
            tasks[f"{name}{h}"] = functools.partial(head, 1 + stage, h)
    for k in range(4):
        tasks[f"nt{k}"] = functools.partial(norm_first, k)
        tasks[f"na{k}"] = functools.partial(norm_core, k)
    for stage in range(6):
        tasks[f"v{stage}"] = functools.partial(tiny, stage)

    normed_load(0).start()
    spot = 0
    while spot < len(PLAN):
        name = PLAN[spot]
        if name[0] != "L":
            tasks[name]()
            spot += 1
            continue
        h, step, hooks = int(name[1]), -1, {}
        while step < 7 or PLAN[spot][0] == "L":
            if PLAN[spot][0] == "L":
                step = int(PLAN[spot][2])
                if step == 7:
                    spot += 1
                    break
            else:
                hooks.setdefault(step, []).append(tasks[PLAN[spot]])
            spot += 1
        attend_head(h, hooks)

    for k in range(6):
        save(k).wait()
    def sent(block, carry):
        own_in = jnp.logical_and(mine, block == at.group)

        @pl.when(jnp.logical_not(own_in))
        def _():
            for h in range(2):
                grad_copy(block, h).wait_send()

        return carry

    lax.fori_loop(0, 8, sent, 0)
    for m in range(3):
        for stage in range(7):
            main_copy(stage, m).wait_send()
    for h in range(2):
        for stage in range(6):
            head_copy(stage, h).wait_send()
    for k in range(2):
        norm_copy(1, k).wait_send()
        norm_copy(2, k).wait_send()
    norm_copy(3, 0).wait_send()

    @pl.when(jnp.logical_not(mine))
    def _():
        norm_copy(3, 1).wait_send()


def sum_slots():
    slots = []
    for ways in SUM_WAYS:
        shape, own = [2, 320, 1280], []
        for way in ways:
            if way == "y":
                shape = shape[1:]
            else:
                shape[-1 if way == "h" else -2] //= 2
            own.append(pltpu.VMEM(tuple(shape), BF))
        slots.append(own)
    return slots


def backward(*args):
    shape = jax.ShapeDtypeStruct
    dma = pltpu.SemaphoreType.DMA
    specs = [ANY_SPEC] * 17
    for k in (8, 10, 13, 16):
        specs[k] = VMEM_SPEC
    return pl.pallas_call(
        backward_kernel,
        name="backward",
        out_shape=(
            shape((320, 1280), BF),
            shape((320, 1280), BF),
            shape((320, 1280), BF),
            shape((320, 3840), BF),
            shape((256, 1280), F32),
            shape((8, LANES), F32),
        ),
        in_specs=specs,
        out_specs=(ANY_SPEC,) * 5 + (VMEM_SPEC,),
        scratch_shapes=[
            pltpu.VMEM((320, 1280), BF),
            pltpu.VMEM((320, 1280), BF),
            pltpu.VMEM((320, 1280), BF),
            pltpu.VMEM((320, 3840), BF),
            pltpu.VMEM((256, 1280), F32),
            pltpu.VMEM((1280, 256), BF),
            pltpu.VMEM((256, 1280), BF),
            pltpu.VMEM((1280, 256), BF),
            pltpu.VMEM((256, 1280), BF),
            pltpu.VMEM((1280, 256), BF),
            pltpu.VMEM((256, 1280), BF),
            pltpu.VMEM((2048, 768), BF),
            pltpu.VMEM((160, 2048), BF),
            pltpu.VMEM((1280, 768), BF),
            pltpu.VMEM((256, 1280), BF),
            pltpu.VMEM((256, 1280), F32),
            pltpu.VMEM((2, 128, 2048), BF),
            pltpu.VMEM((2048, LANES), F32),
            pltpu.VMEM((2, 128, 2048), BF),
            pltpu.VMEM((8, 2048), F32),
            pltpu.VMEM((2048, LANES), F32),
            pltpu.VMEM((2048, LANES), F32),
            pltpu.VMEM((768, 2048), BF),
            pltpu.VMEM((2, 2048, 256), BF),
            pltpu.VMEM((4, 2, 640, 256), BF),
            pltpu.VMEM((2, 2, 640, 256), BF),
            pltpu.VMEM((2, 640, 256), BF),
            pltpu.VMEM((2, 640, 256), BF),
            pltpu.VMEM((1920, 1280), BF),
            pltpu.VMEM((3, 2, 320, 1280), BF),
            sum_slots(),
            pltpu.VMEM((2, 256, 1280), BF),
            pltpu.VMEM((2, 256, 640), BF),
            pltpu.VMEM((2, 128, 640), BF),
            pltpu.VMEM((2, 2, 2, 2, 256, 640), BF),
            pltpu.VMEM((5, 8, LANES), F32),
            dma((8, 2)),
            dma((8, 2)),
            dma((4,)),
            dma((9, 3)),
            dma((9, 3)),
            dma((6, 2)),
            dma((6, 2)),
            dma((4, 2)),
            dma((4, 2)),
            dma((4, 4)),
            dma((4, 4)),
            dma((5,)),
            dma((5,)),
            dma((11,)),
            dma((6,)),
        ],
        compiler_params=pltpu.CompilerParams(
            collective_id=1, has_side_effects=True, vmem_limit_bytes=VMEM_LIMIT
        ),
        cost_estimate=pl.CostEstimate(
            flops=30_000_000_000, bytes_accessed=60_000_000, transcendentals=8_400_000
        ),
    )(*args)


def widen_kernel(*refs):
    total = []
    for k in range(4):
        value = refs[k][...].astype(F32)
        refs[6 + k][...] = value
        if k in (0, 2):
            total.append(jnp.sum(value * refs[4 + k // 2][...].astype(F32), axis=1, keepdims=True))
    lane = lax.broadcasted_iota(jnp.int32, refs[10].shape, 1)
    refs[10][...] = jnp.where(lane == 0, total[0], total[1])


def widen(*args):
    rows = 160
    shape = jax.ShapeDtypeStruct
    specs = [pl.BlockSpec((rows, a.shape[1]), lambda k: (k, 0)) for a in args]
    return pl.pallas_call(
        widen_kernel,
        name="widen",
        grid=(args[0].shape[0] // rows,),
        out_shape=tuple(shape(a.shape, F32) for a in args[:4]) + (shape((320, LANES), F32),),
        in_specs=specs,
        out_specs=tuple(specs[:4]) + (pl.BlockSpec((rows, LANES), lambda k: (k, 0)),),
        compiler_params=pltpu.CompilerParams(vmem_limit_bytes=VMEM_LIMIT),
    )(*args)


def fast_body(
    tokens,
    lengths,
    position,
    qkv_weight,
    out_weight,
    up_weight,
    down_weight,
    attn_gain,
    mlp_gain,
    query_scale,
    cotangent,
):
    f = lax.axis_index("fsdp")
    x, dy = tokens[0], cotangent[0]
    small = jnp.zeros((16, 384), BF)
    for k, own in enumerate((attn_gain, mlp_gain, query_scale)):
        small = lax.dynamic_update_slice(small, own[None], (k, 0))
    (
        att_t, normed, qkv, lse, out, auxsum, place, w_heads,
        result, resid_grad, branch_grad, up_grad, act_t, normed_mlp_t, grad_t, mult,
    ) = forward(
        lengths, x, qkv_weight, small, position, out_weight, up_weight, down_weight, dy
    )
    g_down, g_up, g_out, g_qkv, input_grad, scale_sum = backward(
        grad_t,
        att_t,
        branch_grad,
        normed_mlp_t,
        up_grad,
        act_t,
        dy,
        qkv,
        lse,
        out,
        place,
        normed,
        w_heads,
        mult,
        x,
        resid_grad,
        auxsum,
    )
    g_qkv, g_out, g_up, g_down, sums = widen(g_qkv, g_out, g_up, g_down, qkv_weight, up_weight)
    grad_attn_gain = sums[:, 0] / attn_gain.astype(F32)
    grad_mlp_gain = sums[:, 1] / mlp_gain.astype(F32)
    return (
        result[None],
        input_grad[None],
        g_qkv,
        g_out,
        g_up,
        g_down,
        grad_attn_gain,
        grad_mlp_gain,
        lax.dynamic_slice_in_dim(scale_sum[0, :80], f * 20, 20),
    )


def solution(mesh):
    placed = (
        P("fsdp", "ctx", None),
        P("fsdp", None),
        P("fsdp", None),
        P("fsdp", None),
        P("fsdp", None),
        P("fsdp", None),
        P("fsdp", None),
        P("fsdp"),
        P("fsdp"),
        P("fsdp"),
        P("fsdp", "ctx", None),
    )
    fits = mesh.shape["ctx"] == 8 and mesh.shape["fsdp"] == 4
    return jax.shard_map(
        fast_body if fits else body,
        mesh=mesh,
        in_specs=placed,
        out_specs=(
            P("fsdp", "ctx", None),
            P("fsdp", "ctx", None),
            P("fsdp", None),
            P("fsdp", None),
            P("fsdp", None),
            P("fsdp", None),
            P("fsdp"),
            P("fsdp"),
            P("fsdp"),
        ),
        check_vma=False,
    )
```
